32 devices in a mesh: blk: 4 (over y, x), img: 8 (over z, core).
Axes of the slice: x: 2, y: 2, z: 4, core: 2. Of those that a mesh axis runs over, the one named last changes fastest.
Arguments:
- patch_tokens: bfloat16 [32, 576, 768], P('img', 'blk'), may hold values from -6 to 6
- captions: bfloat16 [400, 768], P('img'), may hold values from -6 to 6
- pair_labels: int32 [32, 400], P('img'), may hold values from 0 to 1, as said below
- master_weights: float32 [768, 12288], P(('blk', 'img')), may hold values from -0.8660254 to 0.8660254
- first_moments: float32 [768, 12288], P(('blk', 'img')), may hold values from -0.00021809896 to 0.00021809896
- second_moments: float32 [768, 12288], P(('blk', 'img')), may hold values from 5.2981906e-11 to 8.477105e-10
- master_vectors: float32 [768, 7], P(('blk', 'img')), may hold values from -6 to 6, as said below
- vector_first: float32 [768, 7], P(('blk', 'img')), may hold values from -0.0017578125 to 0.0017578125
- vector_second: float32 [768, 7], P(('blk', 'img')), may hold values from 3.390842e-09 to 5.4253472e-08
- loss_scalars: float32 [2], replicated, may hold values from -7 to 2.5
- scalar_first: float32 [2], replicated, may hold values from -0.2 to 0.2
- scalar_second: float32 [2], replicated, may hold values from 4.5e-05 to 0.00072
Outputs:
- loss: float32 [], replicated
- grad_norm: float32 [], replicated
- patch_grad: float32 [32, 576, 768], P('img', 'blk')
- new_weights: float32 [768, 12288], P(('blk', 'img'))
- new_first: float32 [768, 12288], P(('blk', 'img'))
- new_second: float32 [768, 12288], P(('blk', 'img'))
- weight_copies: bfloat16 [768, 12288], P(('blk', 'img'))
- new_vectors: float32 [768, 7], P(('blk', 'img'))
- new_vector_first: float32 [768, 7], P(('blk', 'img'))
- new_vector_second: float32 [768, 7], P(('blk', 'img'))
- vector_copies: bfloat16 [768, 7], P(('blk', 'img'))
- new_scalars: float32 [2], replicated
- new_scalar_first: float32 [2], replicated
- new_scalar_second: float32 [2], replicated
The draws below stay inside these ranges and needn't reach their ends.
Inputs may be any that keep to these rules, and one draw needn't show every extreme that they name: `pair_labels`: 1 marks a matching image and caption; images have uneven numbers of matches. `master_vectors`: gains are positive.
All inputs are finite; a program needn't handle non-finite values.
Results may differ from the reference program's by a relative error of at most 0.015.
Values may be sent and summed in bfloat16 or wider, within the bound.
A program may use at most 256 MiB of HBM per device.

```python
import math
from functools import partial
import jax
import jax.numpy as jnp
from jax import lax

D = 768
HEADS = 12
HEAD_DIM = 64
FF = 3072
PATCH = 576
STEP = 10
IMGS = 32
CAPS = 400
N_IMG = 8


def section_scales():
    return jnp.concatenate([jnp.full((3 * D,), D ** (-0.5)), jnp.full((D,), 4.0 * D ** (-0.5)), jnp.full((FF,), D ** (-0.5)), jnp.full((FF,), FF ** (-0.5)), jnp.full((D,), D ** (-0.5)), jnp.full((2 * D,), D ** (-0.5)), jnp.full((D,), 4.0 * D ** (-0.5))]).astype(jnp.float32)


def grad_size():
    return (D * (8 * D + 2 * FF)) ** (-0.5)


def spread_factor(key, shape):
    return jnp.exp(jax.random.uniform(key, shape, jnp.float32, math.log(0.5), math.log(8.0)))


def draw_pair_labels(key, part):
    key = jax.random.fold_in(key, 7)
    keys = jax.random.split(key, 2)
    rows = jnp.arange(IMGS, dtype=jnp.int32)
    rate = 2 + 6 * rows // IMGS + jax.random.randint(keys[0], (IMGS,), 0, 3)
    picks = jax.random.randint(keys[1], (IMGS, CAPS), 0, CAPS)
    return (picks < rate[:, None]).astype(jnp.int32)


def draw_master_weights(key, part):
    key = jax.random.fold_in(key, 11)
    shape = (D, 8 * D + 2 * FF)
    noise = jnp.clip(jax.random.normal(key, shape, jnp.float32), -6.0, 6.0)
    return noise * section_scales()[None, :]


def draw_first_moments(key, part):
    key = jax.random.fold_in(key, 13)
    shape = (D, 8 * D + 2 * FF)
    noise = jnp.clip(jax.random.normal(key, shape, jnp.float32), -6.0, 6.0)
    return noise * (0.111 * grad_size())


def draw_second_moments(key, part):
    key = jax.random.fold_in(key, 19)
    return spread_factor(key, (D, 8 * D + 2 * FF)) * (0.001 * grad_size() ** 2)


def draw_master_vectors(key, part):
    key = jax.random.fold_in(key, 23)
    keys = jax.random.split(key, 2)
    ramp = 0.5 + jnp.arange(D, dtype=jnp.float32) / D
    noise = jnp.clip(jax.random.normal(keys[1], (D, 7), jnp.float32), -6.0, 6.0)
    gains = ramp[:, None] * jax.random.uniform(keys[0], (D, 7), jnp.float32, 0.8, 1.2)
    column = jnp.arange(7)[None, :]
    return jnp.where((column % 2 == 0) & (column < 6), gains, jnp.where(column == 6, noise, 0.3 * noise))


def draw_vector_first(key, part):
    key = jax.random.fold_in(key, 29)
    noise = jnp.clip(jax.random.normal(key, (D, 7), jnp.float32), -6.0, 6.0)
    return noise * (0.111 * 8.0 * grad_size())


def draw_vector_second(key, part):
    key = jax.random.fold_in(key, 31)
    return spread_factor(key, (D, 7)) * (0.001 * 64.0 * grad_size() ** 2)


def draw_loss_scalars(key, part):
    key = jax.random.fold_in(key, 37)
    noise = jax.random.uniform(key, (2,), jnp.float32, -1.0, 1.0)
    return jnp.stack([2.3 + 0.2 * noise[0], -6.0 + noise[1]])


def draw_scalar_first(key, part):
    key = jax.random.fold_in(key, 41)
    return jax.random.uniform(key, (2,), jnp.float32, -1.0, 1.0) * 0.2 * jnp.array([1.0, -1.0])


def draw_scalar_second(key, part):
    key = jax.random.fold_in(key, 43)
    return spread_factor(key, (2,)) * 9e-05


def shard_levels(stream_key, extent, cuts, smallest, high):
    def one(axis_at, shards_of):
        draws = jax.random.uniform(jax.random.fold_in(jax.random.fold_in(stream_key, 6), axis_at), (shards_of,), jnp.float32, smallest / len(cuts), high / len(cuts))
        return jnp.repeat(jnp.exp(draws), extent[axis_at] // shards_of).reshape((-1,) + (1,) * (len(extent) - axis_at - 1))

    level = one(*cuts[0])
    for cut in cuts[1:]:
        level = level * one(*cut)
    return level


def bell_draw(rng, dims, scale, most, cuts=(), kind=jnp.bfloat16):
    values = jax.random.normal(rng, dims, jnp.float32) * scale
    if len(cuts) > 0:
        values = shard_levels(rng, dims, cuts, -0.22, 0.18) * values
    return jnp.clip(values, min=-most, max=most).astype(kind)


def setup_inputs(seed: int = 0) -> dict:
    streams_of = jax.random.split(jax.random.key(seed), 13)
    patch_tokens = bell_draw(streams_of[0], (IMGS, PATCH, D), 1.0, 6.0, ((0, 8), (1, 4)))
    captions = bell_draw(streams_of[1], (CAPS, D), 1.0, 6.0, ((0, 8),))
    pair_labels = draw_pair_labels(jax.random.fold_in(streams_of[12], 71), 0)
    master_weights = draw_master_weights(jax.random.fold_in(streams_of[12], 71), 0)
    first_moments = draw_first_moments(jax.random.fold_in(streams_of[12], 71), 0)
    second_moments = draw_second_moments(jax.random.fold_in(streams_of[12], 71), 0)
    master_vectors = draw_master_vectors(jax.random.fold_in(streams_of[12], 71), 0)
    vector_first = draw_vector_first(jax.random.fold_in(streams_of[12], 71), 0)
    vector_second = draw_vector_second(jax.random.fold_in(streams_of[12], 71), 0)
    loss_scalars = draw_loss_scalars(jax.random.fold_in(streams_of[12], 71), 0)
    scalar_first = draw_scalar_first(jax.random.fold_in(streams_of[12], 71), 0)
    scalar_second = draw_scalar_second(jax.random.fold_in(streams_of[12], 71), 0)
    return {"patch_tokens": patch_tokens, "captions": captions, "pair_labels": pair_labels, "master_weights": master_weights, "first_moments": first_moments, "second_moments": second_moments, "master_vectors": master_vectors, "vector_first": vector_first, "vector_second": vector_second, "loss_scalars": loss_scalars, "scalar_first": scalar_first, "scalar_second": scalar_second}


@jax.custom_vjp
def low(v):
    return lax.optimization_barrier(v.astype(jnp.bfloat16)).astype(jnp.float32)

@jax.custom_vjp
def low_back(v):
    return v

def low_keep(v):
    return (low(v), None)

def low_pass(kept, grad):
    return (grad,)

def back_keep(v):
    return (v, None)

def back_low(kept, grad):
    return (low(grad),)
low.defvjp(low_keep, low_pass)
low_back.defvjp(back_keep, back_low)
BETA_ONE = 0.9
BETA_TWO = 0.999
EPS_ADAM = 1e-08
CLIP_AT = 1.0

def layer_norm(values, gain_vec, bias_vec):
    row_mean = lax.optimization_barrier(jnp.mean(values, axis=-1, keepdims=True))
    centered = values - row_mean
    row_var = lax.optimization_barrier(jnp.mean(centered * centered, axis=-1, keepdims=True))
    return centered * lax.rsqrt(row_var + 1e-06) * gain_vec + bias_vec

def product(pattern, matrix_a, matrix_b):
    return jnp.einsum(pattern, matrix_a, matrix_b, precision=lax.Precision.HIGHEST)

def tower_group(patches, weights, vectors, probe_query):
    scale = HEAD_DIM ** (-0.5)
    groups = patches.shape[0]
    w_qkv = weights[:, :3 * D]
    w_out = weights[:, 3 * D:4 * D]
    w_up = weights[:, 4 * D:4 * D + FF]
    w_down = weights[:, 4 * D + FF:4 * D + 2 * FF]
    w_map_kv = weights[:, 5 * D + 2 * FF:7 * D + 2 * FF]
    w_map_out = weights[:, 7 * D + 2 * FF:]
    normed = low(layer_norm(patches, vectors[:, 0], vectors[:, 1]))
    qkv = low(low_back(product('gpd,dc->gpc', normed, w_qkv))).reshape(groups, PATCH, 3, HEADS, HEAD_DIM)
    scores = low_back(product('gqhe,gkhe->ghqk', qkv[:, :, 0], qkv[:, :, 1]) * scale)
    attn_probs = low(jax.nn.softmax(scores, axis=-1))
    mixed_out = low(low_back(product('ghqk,gkhe->gqhe', attn_probs, qkv[:, :, 2]))).reshape(groups, PATCH, D)
    residual = patches + low_back(product('gpd,dc->gpc', mixed_out, w_out))
    hidden = low(layer_norm(residual, vectors[:, 2], vectors[:, 3]))
    pre_act = low_back(product('gpd,df->gpf', hidden, w_up))
    activation = low(jax.nn.gelu(pre_act))
    layer_out = residual + low_back(product('gpf,df->gpd', activation, w_down))
    final_norm = low(layer_norm(layer_out, vectors[:, 4], vectors[:, 5]))
    map_kv = low(low_back(product('gpd,dc->gpc', final_norm, w_map_kv))).reshape(groups, PATCH, 2, HEADS, HEAD_DIM)
    pool_scores = low_back(product('he,gkhe->ghk', probe_query, map_kv[:, :, 0]) * scale)
    pool_probs = jax.nn.softmax(pool_scores, axis=-1)
    pooled_heads = low(low_back(product('ghk,gkhe->ghe', pool_probs, map_kv[:, :, 1]))).reshape(groups, D)
    return low_back(product('gd,dc->gc', pooled_heads, w_map_out))

def forward(patches, weights, vectors, scalars, caption_unit, signs):
    w_map_q = weights[:, 4 * D + 2 * FF:5 * D + 2 * FF]
    probe_query = low(product('d,dc->c', vectors[:, 6], w_map_q)).reshape(HEADS, HEAD_DIM)
    grouped = patches.reshape(N_IMG, IMGS // N_IMG, PATCH, D)
    pooled = lax.map(jax.checkpoint(partial(tower_group, weights=weights, vectors=vectors, probe_query=probe_query)), grouped)
    pooled = pooled.reshape(IMGS, D)
    unit_image = low(pooled * lax.rsqrt(lax.optimization_barrier(jnp.sum(pooled * pooled, axis=-1, keepdims=True)) + 1e-06))
    cosine = low_back(product('id,cd->ic', unit_image, caption_unit))
    logits = jnp.exp(scalars[0]) * cosine + scalars[1]
    return jnp.sum(jax.nn.softplus(-signs * logits)) / IMGS

def to_copy(values):
    return lax.optimization_barrier(values.astype(jnp.bfloat16)).astype(jnp.float32)

def adamw(parameter, gradient, moment_one, moment_two, step_rate, decay_rate):
    moment_one = BETA_ONE * moment_one + (1.0 - BETA_ONE) * gradient
    moment_two = BETA_TWO * moment_two + (1.0 - BETA_TWO) * gradient * gradient
    first_hat = moment_one / (1.0 - BETA_ONE ** STEP)
    second_hat = moment_two / (1.0 - BETA_TWO ** STEP)
    updated = parameter - step_rate * (first_hat / (jnp.sqrt(second_hat) + EPS_ADAM) + decay_rate * parameter)
    return (updated, moment_one, moment_two)

def reference(patch_tokens, captions, pair_labels, master_weights, first_moments, second_moments, master_vectors, vector_first, vector_second, loss_scalars, scalar_first, scalar_second):
    weights = to_copy(master_weights)
    vectors = to_copy(master_vectors)
    caption_float = captions.astype(jnp.float32)
    caption_unit = low(caption_float * lax.rsqrt(lax.optimization_barrier(jnp.sum(caption_float * caption_float, axis=-1, keepdims=True)) + 1e-06))
    signs = 2.0 * pair_labels.astype(jnp.float32) - 1.0
    patches = patch_tokens.astype(jnp.float32)
    loss, pull = jax.vjp(partial(forward, caption_unit=caption_unit, signs=signs), patches, weights, vectors, loss_scalars)
    grad_patch, grad_weights, grad_vectors, grad_scalars = pull(jnp.ones((), jnp.float32))
    grad_norm = jnp.sqrt(jnp.sum(grad_weights * grad_weights) + jnp.sum(grad_vectors * grad_vectors) + jnp.sum(grad_scalars * grad_scalars))
    factor = CLIP_AT / jnp.maximum(grad_norm, CLIP_AT)
    new_w, new_wm, new_wv = adamw(master_weights, grad_weights * factor, first_moments, second_moments, 0.03, 0.1)
    new_v, new_vm, new_vv = adamw(master_vectors, grad_vectors * factor, vector_first, vector_second, 0.3, 0.0)
    new_s, new_sm, new_sv = adamw(loss_scalars, grad_scalars * factor, scalar_first, scalar_second, 0.3, 0.0)
    return (loss, grad_norm, grad_patch, new_w, new_wm, new_wv, new_w.astype(jnp.bfloat16), new_v, new_vm, new_vv, new_v.astype(jnp.bfloat16), new_s, new_sm, new_sv)
```

```python
import jax
import jax.numpy as jnp
from jax import lax
from jax.sharding import PartitionSpec as P

D = 768
HEADS = 12
HEAD_DIM = 64
FF = 3072
STEP = 10


BETA_ONE = 0.9
BETA_TWO = 0.999
EPS_ADAM = 1e-08
CLIP_AT = 1.0


def layer_norm(values, gain_vec, bias_vec):
    row_mean = jnp.mean(values, axis=-1, keepdims=True)
    centered = values - row_mean
    row_var = jnp.mean(centered * centered, axis=-1, keepdims=True)
    return centered * lax.rsqrt(row_var + 1e-06) * gain_vec + bias_vec


def unit_rows(pooled):
    return pooled * lax.rsqrt(jnp.sum(pooled * pooled, axis=-1, keepdims=True) + 1e-06)


def attend(queries, keys_all, values_all):
    scale = HEAD_DIM ** (-0.5)
    scores = (
        jnp.einsum("iqhe,ikhe->ihqk", queries, keys_all, preferred_element_type=jnp.float32) * scale
    )
    row_max = jnp.max(scores, axis=-1, keepdims=True)
    expos = jnp.exp(scores - row_max)
    row_sum = jnp.sum(expos, axis=-1, keepdims=True)
    attn_probs = (expos / row_sum).astype(jnp.bfloat16)
    mixed_out = jnp.einsum(
        "ihqk,ikhe->iqhe", attn_probs, values_all, preferred_element_type=jnp.float32
    )
    return (mixed_out.astype(jnp.bfloat16), row_max + jnp.log(row_sum))


def attend_back(queries, keys_all, values_all, log_norm, grad_mixed):
    scale = HEAD_DIM ** (-0.5)
    scores = (
        jnp.einsum("iqhe,ikhe->ihqk", queries, keys_all, preferred_element_type=jnp.float32) * scale
    )
    attn_probs = jnp.exp(scores - log_norm)
    grad_values = jnp.einsum(
        "ihqk,iqhe->ikhe",
        attn_probs.astype(jnp.bfloat16),
        grad_mixed,
        preferred_element_type=jnp.float32,
    )
    grad_probs = jnp.einsum(
        "iqhe,ikhe->ihqk", grad_mixed, values_all, preferred_element_type=jnp.float32
    )
    centre = jnp.sum(attn_probs * grad_probs, axis=-1, keepdims=True)
    grad_scores = (attn_probs * (grad_probs - centre)).astype(jnp.bfloat16)
    grad_queries = (
        jnp.einsum("ihqk,ikhe->iqhe", grad_scores, keys_all, preferred_element_type=jnp.float32)
        * scale
    )
    grad_keys = (
        jnp.einsum("ihqk,iqhe->ikhe", grad_scores, queries, preferred_element_type=jnp.float32)
        * scale
    )
    return (grad_queries, grad_keys, grad_values)


def adamw(parameter, gradient, moment_one, moment_two, step_rate, decay_rate):
    moment_one = BETA_ONE * moment_one + (1.0 - BETA_ONE) * gradient
    moment_two = BETA_TWO * moment_two + (1.0 - BETA_TWO) * gradient * gradient
    first_hat = moment_one / (1.0 - BETA_ONE**STEP)
    second_hat = moment_two / (1.0 - BETA_TWO**STEP)
    updated = parameter - step_rate * (
        first_hat / (jnp.sqrt(second_hat) + EPS_ADAM) + decay_rate * parameter
    )
    return (updated, moment_one, moment_two)


def local(
    patch_tokens,
    captions,
    pair_labels,
    master_weights,
    first_moments,
    second_moments,
    master_vectors,
    vector_first,
    vector_second,
    loss_scalars,
    scalar_first,
    scalar_second,
):
    blocks = lax.axis_size("blk")
    block = lax.axis_index("blk")
    all_images = patch_tokens.shape[0] * lax.axis_size("img")
    images = patch_tokens.shape[0] // blocks
    length = patch_tokens.shape[1] * blocks
    scale = HEAD_DIM ** (-0.5)
    both = ("blk", "img")
    rows = master_weights.shape[0]
    first_row = lax.axis_index(both) * rows
    patch_tokens = lax.all_to_all(patch_tokens, "blk", 0, 1, tiled=True)
    pair_labels = lax.dynamic_slice_in_dim(pair_labels, block * images, images, 0)
    rounded = master_weights.astype(jnp.bfloat16)
    full_vectors = lax.all_gather(master_vectors.astype(jnp.bfloat16), both, axis=0, tiled=True)
    vectors = full_vectors.astype(jnp.float32)

    def gather(start, stop):
        return lax.all_gather(rounded[:, start:stop], both, axis=0, tiled=True)

    w_front = gather(0, 4 * D)
    w_qkv = w_front[:, : 3 * D]
    w_out = w_front[:, 3 * D :]
    w_up = gather(4 * D, 4 * D + FF)
    w_down = gather(4 * D + FF, 4 * D + 2 * FF)
    own_map_q = rounded[:, 4 * D + 2 * FF : 5 * D + 2 * FF]
    w_map = gather(5 * D + 2 * FF, 8 * D + 2 * FF)
    w_map_kv = w_map[:, : 2 * D]
    w_map_out = w_map[:, 2 * D :]
    own_vectors = master_vectors.astype(jnp.bfloat16)
    tokens = patch_tokens.astype(jnp.float32)
    normed, norm_one_pull = jax.vjp(layer_norm, tokens, vectors[:, 0], vectors[:, 1])
    normed_b = normed.astype(jnp.bfloat16)
    qkv_b = jnp.einsum("ipd,dc->ipc", normed_b, w_qkv, preferred_element_type=jnp.float32).astype(
        jnp.bfloat16
    )
    queries = qkv_b[:, :, :D].reshape(images, length, HEADS, HEAD_DIM)
    keys_all = qkv_b[:, :, D : 2 * D].reshape(images, length, HEADS, HEAD_DIM)
    values_all = qkv_b[:, :, 2 * D :].reshape(images, length, HEADS, HEAD_DIM)
    mixed_heads, log_norm = attend(queries, keys_all, values_all)
    mixed_b = mixed_heads.reshape(images, length, D)
    residual = tokens + jnp.einsum(
        "ipd,dc->ipc", mixed_b, w_out, preferred_element_type=jnp.float32
    )
    hidden, norm_two_pull = jax.vjp(layer_norm, residual, vectors[:, 2], vectors[:, 3])
    hidden_b = hidden.astype(jnp.bfloat16)
    pre_act = jnp.einsum("ipd,df->ipf", hidden_b, w_up, preferred_element_type=jnp.float32)
    activation, gelu_pull = jax.vjp(jax.nn.gelu, pre_act)
    activation_b = activation.astype(jnp.bfloat16)
    layer_out = residual + jnp.einsum(
        "ipf,df->ipd", activation_b, w_down, preferred_element_type=jnp.float32
    )
    final_norm, norm_three_pull = jax.vjp(layer_norm, layer_out, vectors[:, 4], vectors[:, 5])
    final_b = final_norm.astype(jnp.bfloat16)
    map_kv = jnp.einsum("ipd,dc->ipc", final_b, w_map_kv, preferred_element_type=jnp.float32)
    map_kv = map_kv.astype(jnp.bfloat16).reshape(images, length, 2, HEADS, HEAD_DIM)
    probe_query = lax.psum(
        jnp.dot(own_vectors[:, 6], own_map_q, preferred_element_type=jnp.float32), both
    )
    probe_query = probe_query.astype(jnp.bfloat16).reshape(HEADS, HEAD_DIM)
    pool_scores = (
        jnp.einsum("he,iphe->ihp", probe_query, map_kv[:, :, 0], preferred_element_type=jnp.float32)
        * scale
    )
    row_max = jnp.max(pool_scores, axis=-1)
    row_sum = jnp.sum(jnp.exp(pool_scores - row_max[..., None]), axis=-1)
    pool_probs = jnp.exp(pool_scores - row_max[..., None]) / row_sum[..., None]
    map_values = map_kv[:, :, 1].astype(jnp.float32)
    pooled_part = jnp.einsum(
        "ihp,iphe->ihe", pool_probs, map_values, precision=lax.Precision.HIGHEST
    )
    pooled_heads = pooled_part.reshape(images, D)
    pooled_heads_b = pooled_heads.astype(jnp.bfloat16)
    pooled = jnp.dot(pooled_heads_b, w_map_out, preferred_element_type=jnp.float32)
    caption_all = lax.all_gather(captions, "img", axis=0, tiled=True).astype(jnp.float32)
    caption_unit = unit_rows(caption_all).astype(jnp.bfloat16)
    unit_image, unit_pull = jax.vjp(unit_rows, pooled)
    cosine = jnp.einsum(
        "id,cd->ic",
        unit_image.astype(jnp.bfloat16),
        caption_unit,
        preferred_element_type=jnp.float32,
    )
    signs = 2.0 * pair_labels.astype(jnp.float32) - 1.0

    def pair_loss(cosine_in, scalars_in):
        logits = jnp.exp(scalars_in[0]) * cosine_in + scalars_in[1]
        return jnp.sum(jax.nn.softplus(-signs * logits)) / all_images

    loss_local, loss_pull = jax.vjp(pair_loss, cosine, loss_scalars)
    grad_cosine, grad_scalars = loss_pull(jnp.ones((), jnp.float32))
    loss_total, scalar_total = lax.psum((loss_local, grad_scalars), both)
    grad_unit = jnp.einsum(
        "ic,cd->id",
        grad_cosine.astype(jnp.bfloat16),
        caption_unit,
        preferred_element_type=jnp.float32,
    )
    (grad_pooled,) = unit_pull(grad_unit)
    grad_pooled_b = grad_pooled.astype(jnp.bfloat16)
    pooled_all, grad_pooled_all = (
        lax.all_gather(pooled_heads_b, both, axis=0, tiled=True),
        lax.all_gather(grad_pooled_b, both, axis=0, tiled=True),
    )
    share_map_out = jnp.einsum(
        "id,ic->dc",
        lax.dynamic_slice_in_dim(pooled_all, first_row, rows, 1),
        grad_pooled_all,
        preferred_element_type=jnp.float32,
    )
    grad_heads_b = jnp.einsum(
        "ic,dc->id", grad_pooled_b, w_map_out, preferred_element_type=jnp.float32
    )
    grad_heads_b = grad_heads_b.astype(jnp.bfloat16).reshape(images, HEADS, HEAD_DIM)
    grad_heads = grad_heads_b.astype(jnp.float32)
    centre = jnp.sum(grad_heads * pooled_heads.reshape(images, HEADS, HEAD_DIM), axis=-1)
    grad_probs = jnp.einsum(
        "ihe,iphe->ihp", grad_heads_b, map_kv[:, :, 1], preferred_element_type=jnp.float32
    )
    grad_pool_scores = (pool_probs * (grad_probs - centre[..., None])).astype(jnp.bfloat16)
    grad_map_keys = (
        jnp.einsum(
            "ihp,he->iphe", grad_pool_scores, probe_query, preferred_element_type=jnp.float32
        )
        * scale
    )
    grad_map_values = jnp.einsum(
        "ihp,ihe->iphe", pool_probs, grad_heads, precision=lax.Precision.HIGHEST
    )
    grad_probe_query = (
        jnp.einsum(
            "ihp,iphe->he", grad_pool_scores, map_kv[:, :, 0], preferred_element_type=jnp.float32
        ).reshape(D)
        * scale
    )
    grad_map_kv = (
        jnp.stack([grad_map_keys, grad_map_values], axis=2)
        .astype(jnp.bfloat16)
        .reshape(images, length, 2 * D)
    )
    grad_w_map_kv = jnp.einsum(
        "ipd,ipc->dc", final_b, grad_map_kv, preferred_element_type=jnp.float32
    )
    grad_final = jnp.einsum(
        "ipc,dc->ipd", grad_map_kv, w_map_kv, preferred_element_type=jnp.float32
    )
    grad_layer_out, grad_gain_three, grad_bias_three = norm_three_pull(grad_final)
    probe_total = lax.psum(grad_probe_query, both)
    share_map_q = jnp.outer(own_vectors[:, 6].astype(jnp.float32), probe_total)
    share_probe = jnp.dot(
        own_map_q.astype(jnp.float32), probe_total, precision=lax.Precision.HIGHEST
    )
    grad_branch_two = grad_layer_out.astype(jnp.bfloat16)
    grad_w_down = jnp.einsum(
        "ipd,ipf->df", grad_branch_two, activation_b, preferred_element_type=jnp.float32
    )
    grad_activation = jnp.einsum(
        "ipd,df->ipf", grad_branch_two, w_down, preferred_element_type=jnp.float32
    )
    (grad_pre,) = gelu_pull(grad_activation)
    grad_pre_b = grad_pre.astype(jnp.bfloat16)
    grad_w_up = jnp.einsum("ipd,ipf->df", hidden_b, grad_pre_b, preferred_element_type=jnp.float32)
    grad_hidden = jnp.einsum("ipf,df->ipd", grad_pre_b, w_up, preferred_element_type=jnp.float32)
    grad_res_part, grad_gain_two, grad_bias_two = norm_two_pull(grad_hidden)
    grad_residual = grad_layer_out + grad_res_part
    grad_branch_one = grad_residual.astype(jnp.bfloat16)
    grad_w_out = jnp.einsum(
        "ipd,ipc->dc", mixed_b, grad_branch_one, preferred_element_type=jnp.float32
    )
    grad_mixed = jnp.einsum(
        "ipc,dc->ipd", grad_branch_one, w_out, preferred_element_type=jnp.float32
    )
    grad_mixed = grad_mixed.astype(jnp.bfloat16)
    grad_queries, grad_keys, grad_values = attend_back(
        queries, keys_all, values_all, log_norm, grad_mixed.reshape(images, length, HEADS, HEAD_DIM)
    )
    grad_qkv = jnp.concatenate(
        [
            grad_queries.reshape(images, length, D),
            grad_keys.reshape(images, length, D),
            grad_values.reshape(images, length, D),
        ],
        axis=-1,
    ).astype(jnp.bfloat16)
    grad_w_qkv = jnp.einsum("ipd,ipc->dc", normed_b, grad_qkv, preferred_element_type=jnp.float32)
    grad_normed = jnp.einsum("ipc,dc->ipd", grad_qkv, w_qkv, preferred_element_type=jnp.float32)
    grad_tok_part, grad_gain_one, grad_bias_one = norm_one_pull(grad_normed)
    patch_grad = lax.all_to_all(
        (grad_residual + grad_tok_part).astype(jnp.bfloat16), "blk", 1, 0, tiled=True
    ).astype(jnp.float32)
    grad_vectors = jnp.stack(
        [
            grad_gain_one,
            grad_bias_one,
            grad_gain_two,
            grad_bias_two,
            grad_gain_three,
            grad_bias_three,
        ],
        axis=1,
    )

    def scatter(part):
        return lax.psum_scatter(
            part.astype(jnp.bfloat16), both, scatter_dimension=0, tiled=True
        ).astype(jnp.float32)

    share_map_kv = scatter(grad_w_map_kv)
    share_down = scatter(grad_w_down)
    share_up = scatter(grad_w_up)
    share_front = scatter(jnp.concatenate([grad_w_qkv, grad_w_out], axis=1))
    weight_share = jnp.concatenate(
        [share_front, share_up, share_down, share_map_q, share_map_kv, share_map_out], axis=1
    )
    vector_share = jnp.concatenate(
        [
            lax.psum_scatter(grad_vectors, both, scatter_dimension=0, tiled=True),
            share_probe[:, None],
        ],
        axis=1,
    )
    squares = jnp.sum(weight_share * weight_share) + jnp.sum(vector_share * vector_share)
    square_total = lax.psum(squares, ("blk", "img"))
    grad_norm = jnp.sqrt(square_total + jnp.sum(scalar_total * scalar_total))
    factor = CLIP_AT / jnp.maximum(grad_norm, CLIP_AT)
    new_w, new_wm, new_wv = adamw(
        master_weights, weight_share * factor, first_moments, second_moments, 0.03, 0.1
    )
    new_v, new_vm, new_vv = adamw(
        master_vectors, vector_share * factor, vector_first, vector_second, 0.3, 0.0
    )
    new_s, new_sm, new_sv = adamw(
        loss_scalars, scalar_total * factor, scalar_first, scalar_second, 0.3, 0.0
    )
    return (
        loss_total,
        grad_norm,
        patch_grad,
        new_w,
        new_wm,
        new_wv,
        new_w.astype(jnp.bfloat16),
        new_v,
        new_vm,
        new_vv,
        new_v.astype(jnp.bfloat16),
        new_s,
        new_sm,
        new_sv,
    )


def solution(mesh):
    in_specs = (
        P("img", "blk", None),
        P("img", None),
        P("img", None),
        P(("blk", "img"), None),
        P(("blk", "img"), None),
        P(("blk", "img"), None),
        P(("blk", "img"), None),
        P(("blk", "img"), None),
        P(("blk", "img"), None),
        P(),
        P(),
        P(),
    )
    out_specs = (
        P(),
        P(),
        P("img", "blk", None),
        P(("blk", "img"), None),
        P(("blk", "img"), None),
        P(("blk", "img"), None),
        P(("blk", "img"), None),
        P(("blk", "img"), None),
        P(("blk", "img"), None),
        P(("blk", "img"), None),
        P(("blk", "img"), None),
        P(),
        P(),
        P(),
    )
    return jax.shard_map(local, mesh=mesh, in_specs=in_specs, out_specs=out_specs, check_vma=False)
```

```python
import jax
import jax.numpy as jnp
from jax import lax
from jax.experimental import pallas as pl
from jax.experimental.pallas import tpu as pltpu
from jax.sharding import PartitionSpec as P

D = 768
HEADS = 12
HEAD_DIM = 64
FF = 3072
STEP = 10


BETA_ONE = 0.9
BETA_TWO = 0.999
EPS_ADAM = 1e-08
CLIP_AT = 1.0

GATHER_SKEW = 2
SCATTER_SKEW = 2
MESH = pl.DeviceIdType.MESH
CHIP_ROWS = 48
GATHER_SECTIONS = ((0, 2560), (2560, 3840), (6400, 3072), (9472, 2304))
SCATTER_SECTIONS = ((9472, 1536), (6400, 3072), (2560, 3840), (0, 2560))
GATHER_COLS = 11776
SCATTER_COLS = 11008


def aligned(value, step):
    return pl.multiple_of(value, step)


class Place:
    def __init__(self):
        self.blk = lax.axis_index("blk")
        self.img = lax.axis_index("img")
        self.x = lax.rem(self.blk, 2)
        self.y = self.blk // 2
        self.z = self.img // 2
        self.c = lax.rem(self.img, 2)
        self.chip = self.blk * 4 + self.z
        self.sibling = {"img": self.z * 2 + 1 - self.c}
        self.up = {"img": self.img + 2}
        self.down = {"img": self.img - 2}
        self.a_near = {"blk": self.block(1, 0)}
        self.b_near = {"blk": self.block(0, 1)}

    def block(self, da, db):
        flip_x = da * (1 - self.c) + db * self.c
        flip_y = db * (1 - self.c) + da * self.c
        other_x = self.x + flip_x * (1 - 2 * self.x)
        other_y = self.y + flip_y * (1 - 2 * self.y)
        return other_y * 2 + other_x


def remote(src, dst, send_sem, recv_sem, device):
    return pltpu.make_async_remote_copy(
        src_ref=src,
        dst_ref=dst,
        send_sem=send_sem,
        recv_sem=recv_sem,
        device_id=device,
        device_id_type=MESH,
    )


def greet_all(place):
    barrier = pltpu.get_barrier_semaphore()
    me = place.blk * 8 + place.img

    def greet(step, carry):
        other = lax.rem(me + step, 32)
        pl.semaphore_signal(
            barrier,
            inc=1,
            device_id={"blk": other // 8, "img": lax.rem(other, 8)},
            device_id_type=MESH,
        )
        return carry

    lax.fori_loop(1, 32, greet, 0)
    pl.semaphore_wait(barrier, 31)


class Gather:
    def __init__(self, place, buf, rows, first, width, sems):
        self.p, self.buf, self.rows, self.half = place, buf, rows, width // 2
        self.mine = aligned(first + place.c * self.half, 128)
        self.theirs = aligned(first + (1 - place.c) * self.half, 128)
        self.near_recv, self.z_recv, self.b_recv, self.near_send, self.z_send, self.b_send, self.pair = sems

    def item(self, da, db, level):
        start = aligned((self.p.block(da, db) * 4 + level) * self.rows, self.rows)
        return self.buf.at[pl.ds(start, self.rows), pl.ds(self.mine, self.half)]

    def a_copy(self):
        own = self.item(0, 0, self.p.z)
        return remote(own, own, self.near_send, self.near_recv, self.p.a_near)

    def z_copy(self, da, level, up):
        part = self.item(da, 0, level)
        device = self.p.up if up else self.p.down
        return remote(part, part, self.z_send.at[up, da, level], self.z_recv.at[da, level], device)

    def b_copy(self, da, level):
        part = self.item(da, 0, level)
        return remote(part, part, self.b_send.at[da, level], self.b_recv.at[da, level], self.p.b_near)

    def pair_copy(self, da, db, level):
        part = self.item(da, db, level)
        return remote(part, part, self.pair.at[0], self.pair.at[1], self.p.sibling)

    def onward(self, da, level, up, down):
        self.b_copy(da, level).start()
        if up:
            pl.when(self.p.z < 3)(lambda: self.z_copy(da, level, 1).start())
        if down:
            pl.when(self.p.z > 0)(lambda: self.z_copy(da, level, 0).start())
        self.pair_copy(da, 0, level).start()

    def begin(self):
        self.a_copy().start()
        self.onward(0, self.p.z, True, True)

    def near(self):
        part = self.item(1, 0, self.p.z)
        remote(part, part, self.near_send, self.near_recv, self.p.a_near).wait_recv()
        self.onward(1, self.p.z, True, True)

    def level(self, distance):
        z = self.p.z

        @pl.when(z >= distance)
        def from_below():
            for da in range(2):
                self.z_copy(da, z - distance, 1).wait_recv()
                self.onward(da, z - distance, True, False)

        @pl.when(z + distance <= 3)
        def from_above():
            for da in range(2):
                self.z_copy(da, z + distance, 0).wait_recv()
                self.onward(da, z + distance, False, True)

    def far(self):
        for level in range(4):
            for da in range(2):
                part = self.item(da, 1, level)
                remote(
                    part, part, self.b_send.at[da, level], self.b_recv.at[da, level], self.p.b_near
                ).wait_recv()
                self.pair_copy(da, 1, level).start()

    def finish(self):
        whole = self.buf.at[pl.ds(0, 16 * self.rows), pl.ds(self.theirs, self.half)]
        both = remote(whole, whole, self.pair.at[0], self.pair.at[1], self.p.sibling)
        both.wait_recv()

    def sent(self):
        z = self.p.z
        self.a_copy().wait_send()
        whole = self.buf.at[pl.ds(0, 16 * self.rows), pl.ds(self.mine, self.half)]
        remote(whole, whole, self.pair.at[0], self.pair.at[1], self.p.sibling).wait_send()
        for level in range(4):
            for da in range(2):
                self.b_copy(da, level).wait_send()
                if level < 3:
                    pl.when((z >= level) & (z < 3))(
                        lambda da=da, level=level: self.z_copy(da, level, 1).wait_send()
                    )
                if level > 0:
                    pl.when((z <= level) & (z > 0))(
                        lambda da=da, level=level: self.z_copy(da, level, 0).wait_send()
                    )

    def steps(self):
        return [
            self.begin,
            self.near,
            lambda: self.level(1),
            lambda: self.level(2),
            lambda: self.level(3),
            self.far,
        ]


def gather_sems(count):
    dma = pltpu.SemaphoreType.DMA
    return [
        dma((count,)),
        dma((count, 2, 4)),
        dma((count, 2, 4)),
        dma((count,)),
        dma((count, 2, 2, 4)),
        dma((count, 2, 4)),
        dma((count, 2)),
    ]


class Scatter:
    def __init__(self, place, buf, share, first, width, bufs, sems):
        self.p, self.buf, self.share, self.half = place, buf, share, width // 2
        self.mine = aligned(first + place.c * self.half, 128)
        self.theirs = aligned(first + (1 - place.c) * self.half, 128)
        self.pair_in, self.b_in, self.z_in, self.a_in, self.last = bufs
        self.pair, self.b_sem, self.z_send, self.z_recv, self.a_sem, self.end = sems

    def run_rows(self, da, db):
        return aligned(self.p.block(da, db) * 192, 192)

    def run(self, da, db):
        return self.buf.at[pl.ds(self.run_rows(da, db), 192), pl.ds(self.mine, self.half)]

    def level_rows(self, da, level):
        return aligned((self.p.block(da, 0) * 4 + level) * 48, 48)

    def part(self, da, level):
        return self.buf.at[pl.ds(self.level_rows(da, level), 48), pl.ds(self.mine, self.half)]

    def add(self, row, source, count, offset=0):
        def one(step, carry):
            here = aligned(row + step * 48, 48)
            there = aligned(offset + step * 48, 48)
            self.buf[pl.ds(here, 48), pl.ds(self.mine, self.half)] += source[pl.ds(there, 48), :]
            return carry

        if count == 1:
            one(0, 0)
        else:
            lax.fori_loop(0, count, one, 0)

    def pair_copy(self):
        return remote(
            self.buf.at[pl.ds(0, 768), pl.ds(self.theirs, self.half)],
            self.pair_in,
            self.pair.at[0],
            self.pair.at[1],
            self.p.sibling,
        )

    def b_copy(self, da):
        return remote(self.run(da, 1), self.b_in.at[da], self.b_sem.at[0, da], self.b_sem.at[1, da], self.p.b_near)

    def z_copy(self, da, level, up):
        return remote(
            self.part(da, level),
            self.z_in.at[up, da, level - up],
            self.z_send.at[up, da, level - up],
            self.z_recv.at[up, da, level - up],
            self.p.up if up else self.p.down,
        )

    def a_copy(self):
        return remote(self.part(1, self.p.z), self.a_in, self.a_sem.at[0], self.a_sem.at[1], self.p.a_near)

    def end_copy(self):
        return remote(
            self.last.at[pl.ds(aligned((1 - self.p.c) * 24, 8), 24), :],
            self.share.at[:, pl.ds(self.mine, self.half)],
            self.end.at[0],
            self.end.at[1],
            self.p.sibling,
        )

    def begin(self):
        self.pair_copy().start()

    def pairs_far(self):
        self.pair_copy().wait_recv()
        for da in range(2):
            row = self.run_rows(da, 1)
            self.add(row, self.pair_in, 4, row)
            self.b_copy(da).start()

    def pairs_near(self):
        for da in range(2):
            row = self.run_rows(da, 0)
            self.add(row, self.pair_in, 4, row)

    def blocks(self):
        for da in range(2):
            self.b_copy(da).wait_recv()
            self.add(self.run_rows(da, 0), self.b_in.at[da], 4)

    def z_step(self, da, level, up, holds, takes, gives):
        @pl.when(holds)
        def step():
            copy = self.z_copy(da, level, up)

            @pl.when(takes)
            def take():
                copy.wait_recv()
                self.add(self.level_rows(da, level), self.z_in.at[up, da, level - up], 1)

            if gives:
                copy.start()

    def levels(self, slot):
        z = self.p.z
        for da in range(2):
            self.z_step(
                da, 3 - slot + z, 1, (z <= slot) & (z >= slot - 2), z >= 1, slot < 3
            )
            self.z_step(
                da, slot - 3 + z, 0, (z >= 3 - slot) & (z <= 5 - slot), z <= 2, slot < 3
            )

    def across(self):
        self.a_copy().start()

    def close(self):
        self.a_copy().wait_recv()
        rows = self.level_rows(0, self.p.z)
        self.last[...] = self.buf[pl.ds(rows, 48), pl.ds(self.mine, self.half)].astype(
            jnp.float32
        ) + self.a_in[...].astype(jnp.float32)
        self.end_copy().start()
        self.share[:, pl.ds(self.mine, self.half)] = self.last[
            pl.ds(aligned(self.p.c * 24, 8), 24), :
        ]

    def finish(self):
        z = self.p.z
        theirs = self.share.at[:, pl.ds(self.theirs, self.half)]
        remote(theirs, theirs, self.end.at[0], self.end.at[1], self.p.sibling).wait_recv()
        self.end_copy().wait_send()
        self.a_copy().wait_send()
        self.pair_copy().wait_send()
        for da in range(2):
            self.b_copy(da).wait_send()
            for number in range(3):
                up, down = self.z_copy(da, 3 - number, 1), self.z_copy(da, number, 0)
                pl.when(z < 3 - number)(lambda up=up: up.wait_send())
                pl.when(z > number)(lambda down=down: down.wait_send())

    def steps(self):
        return [
            self.begin,
            self.pairs_far,
            self.pairs_near,
            self.blocks,
            lambda: self.levels(0),
            lambda: self.levels(1),
            lambda: self.levels(2),
            lambda: self.levels(3),
            self.across,
            self.close,
        ]


class Swap:
    def __init__(self, place, own, buf, first_buf_row, rows, first, width, offset, sems):
        self.p, self.rows, self.half = place, rows, width // 2
        self.own, self.buf, self.sems, self.offset = own, buf, sems, offset
        self.mine = aligned(first + place.c * self.half, 128)
        self.theirs = aligned(first + (1 - place.c) * self.half, 128)
        self.row = aligned(first_buf_row + place.c * rows, rows)
        self.other_row = aligned(first_buf_row + (1 - place.c) * rows, rows)

    def columns(self, start):
        return pl.ds(start, self.half) if self.offset is None else pl.ds(self.offset, self.half)

    def away(self):
        return remote(
            self.own.at[:, pl.ds(self.theirs, self.half)],
            self.buf.at[pl.ds(self.row, self.rows), self.columns(self.theirs)],
            self.sems.at[0],
            self.sems.at[1],
            self.p.sibling,
        )

    def here(self):
        return pltpu.make_async_copy(
            self.own.at[:, pl.ds(self.mine, self.half)],
            self.buf.at[pl.ds(self.row, self.rows), self.columns(self.mine)],
            self.sems.at[2],
        )

    def begin(self):
        self.away().start()
        self.here().start()

    def finish(self):
        landed = self.buf.at[pl.ds(self.other_row, self.rows), self.columns(self.mine)]
        remote(landed, landed, self.sems.at[0], self.sems.at[1], self.p.sibling).wait_recv()
        self.here().wait()
        self.away().wait_send()


def gather_kernel(own, tokens, caps, w_out, x, cap_all, w, stage, swap_sems, token_sems, *sems):
    p = Place()
    greet_all(p)
    sections = []
    swaps = []
    for number, (first, width) in enumerate(GATHER_SECTIONS):
        swap = Swap(p, own, stage, 0, 24, first, width, first // 2, swap_sems.at[number])
        swap.begin()
        swaps.append(swap)
        sections.append(
            Gather(p, w, CHIP_ROWS, first, width, [s.at[number] for s in sems])
        )
    count = len(GATHER_SECTIONS)
    cap_swap = Swap(p, caps, cap_all, p.chip * 32, 16, 0, 768, None, swap_sems.at[count])
    cap_swap.begin()
    sections.append(Gather(p, cap_all, 32, 0, 768, [s.at[count] for s in sems]))
    token_copies = []
    for step in range(1, 4):
        to = lax.rem(p.blk + step, 4)
        copy = remote(
            tokens.at[to],
            x.at[pl.ds(aligned(p.blk * 144, 144), 144), :],
            token_sems.at[0, step - 1],
            token_sems.at[1, step - 1],
            {"blk": to},
        )
        copy.start()
        token_copies.append(copy)
    own_tokens = pltpu.make_async_copy(
        tokens.at[p.blk], x.at[pl.ds(aligned(p.blk * 144, 144), 144), :], token_sems.at[0, 3]
    )
    own_tokens.start()

    def ready(number):
        swaps[number].finish()
        first, width = GATHER_SECTIONS[number]
        w[
            pl.ds(aligned(p.chip * 48, 48), 48), pl.ds(sections[number].mine, width // 2)
        ] = stage[:, first // 2 : first // 2 + width // 2].astype(jnp.bfloat16)

    plans = []
    for number, section in enumerate(sections):
        steps = section.steps()
        if number < count:
            steps[0] = lambda number=number, begin=steps[0]: (ready(number), begin())
        else:
            steps[0] = lambda begin=steps[0]: (cap_swap.finish(), begin())
        plans.append(steps)
    skew = GATHER_SKEW
    last = max(len(s) + skew * n for n, s in enumerate(plans))
    outs = []
    for tick in range(last + 1):
        for number, steps in enumerate(plans):
            at = tick - skew * number
            if 0 <= at < len(steps):
                steps[at]()
    for number, section in enumerate(sections):
        section.finish()
        if number < count:
            first, width = GATHER_SECTIONS[number]
            out = pltpu.make_async_copy(
                w.at[:, first : first + width],
                w_out.at[:, first : first + width],
                swap_sems.at[number, 3],
            )
            out.start()
            outs.append(out)
    for step, copy in enumerate(token_copies):
        source = lax.rem(p.blk + 3 - step, 4)
        landed = x.at[pl.ds(aligned(source * 144, 144), 144), :]
        remote(
            landed, landed, token_sems.at[0, step], token_sems.at[1, step], {"blk": source}
        ).wait_recv()
        copy.wait_send()
    own_tokens.wait()
    for section in sections:
        section.sent()
    for out in outs:
        out.wait()


def gather_call(own, tokens, caps):
    count = len(GATHER_SECTIONS) + 1
    dma = pltpu.SemaphoreType.DMA
    return pl.pallas_call(
        gather_kernel,
        out_shape=(
            jax.ShapeDtypeStruct((768, GATHER_COLS), jnp.bfloat16),
            jax.ShapeDtypeStruct((576, 768), jnp.bfloat16),
            jax.ShapeDtypeStruct((512, 768), jnp.bfloat16),
        ),
        in_specs=[
            pl.BlockSpec(memory_space=pl.ANY),
            pl.BlockSpec(memory_space=pl.ANY),
            pl.BlockSpec(memory_space=pltpu.VMEM),
        ],
        out_specs=(
            pl.BlockSpec(memory_space=pl.ANY),
            pl.BlockSpec(memory_space=pltpu.VMEM),
            pl.BlockSpec(memory_space=pltpu.VMEM),
        ),
        scratch_shapes=[
            pltpu.VMEM((768, GATHER_COLS), jnp.bfloat16),
            pltpu.VMEM((48, GATHER_COLS // 2), jnp.float32),
            dma((count, 4)),
            dma((2, 4)),
            *gather_sems(count),
        ],
        compiler_params=pltpu.CompilerParams(
            collective_id=0, has_side_effects=True, vmem_limit_bytes=60 * 2**20
        ),
        name="gather_weights",
    )(own, tokens, caps)


class Spread:
    def __init__(self, place, mine, everyone, send_sem, recv_sem):
        self.p, self.mine, self.everyone = place, mine, everyone
        self.send_sem, self.recv_sem = send_sem, recv_sem
        self.me = place.blk * 8 + place.img

    def copy(self, step):
        other = lax.rem(self.me + step, 32)
        return remote(
            self.mine,
            self.everyone.at[step - 1],
            self.send_sem,
            self.recv_sem,
            {"blk": other // 8, "img": lax.rem(other, 8)},
        )

    def begin(self, tile):
        self.mine[...] = tile

        def start(step, carry):
            self.copy(step).start()
            return carry

        lax.fori_loop(1, 32, start, 0)

    def total(self):
        remote(
            self.everyone, self.everyone, self.send_sem, self.recv_sem, self.p.sibling
        ).wait()
        return self.mine[...] + jnp.sum(self.everyone[...], axis=0)


def small_tail(p, small, map_q, probe, share, spread):
    everything = small[...]
    as_rows = everything.astype(jnp.bfloat16)
    sums = jnp.sum(everything.reshape(32, 8, 768), axis=0)
    query, scalars = sums[2:3], sums[3:4]
    device = lax.broadcasted_iota(jnp.int32, (32, 256), 0) * 8
    row = lax.broadcasted_iota(jnp.int32, (32, 256), 1)

    def rows_of(kind):
        pick = (row == device + kind).astype(jnp.float32).astype(jnp.bfloat16)
        return jnp.dot(pick, as_rows, preferred_element_type=jnp.float32).astype(jnp.bfloat16)

    pooled, grads = rows_of(0), rows_of(1)
    first = (p.blk * 8 + p.img) * 24
    picks = (
        lax.broadcasted_iota(jnp.int32, (24, 768), 1)
        == lax.broadcasted_iota(jnp.int32, (24, 768), 0) + first
    ).astype(jnp.float32).astype(jnp.bfloat16)
    rows = lax.dot_general(
        picks, pooled, (((1,), (1,)), ((), ())), preferred_element_type=jnp.float32
    ).astype(jnp.bfloat16)
    map_out = jnp.dot(rows, grads, preferred_element_type=jnp.float32)
    map_q_share = probe * query
    probe_share = jnp.sum(map_q * query, axis=1, keepdims=True)
    square = (
        jnp.sum(map_out * map_out)
        + jnp.sum(map_q_share * map_q_share)
        + jnp.sum(probe_share * probe_share)
    )

    def one(step, total):
        part = share[:, pl.ds(aligned(step * 256, 256), 256)]
        return total + jnp.sum(part * part)

    square = lax.fori_loop(0, SCATTER_COLS // 256, one, square)
    spread.begin(jnp.full((8, 128), square, jnp.float32))
    total = spread.total()
    one_lane = lax.broadcasted_iota(jnp.int32, (1, 768), 1)
    scalar_square = jnp.sum(
        jnp.where((one_lane == 1) | (one_lane == 2), scalars * scalars, 0.0)
    )
    norm = jnp.sqrt(total + scalar_square)
    return map_out, map_q_share, probe_share, scalars, norm


def scatter_kernel(
    grads, small_own, map_q, probe, patch, share, map_out, map_q_share, probe_share, facts, patch_out,
    w, small, pair_in, b_in, z_in, a_in, last, mine, everyone,
    load_sems, swap_sems, patch_sems, send_sem, recv_sem, *sems,
):
    p = Place()
    loads = []
    for number, (first, width) in enumerate(SCATTER_SECTIONS):
        load = pltpu.make_async_copy(
            grads.at[:, first : first + width], w.at[:, first : first + width], load_sems.at[number]
        )
        load.start()
        loads.append(load)
    greet_all(p)
    gather, sems = sems[:7], sems[7:]
    swap = Swap(p, small_own, small, p.chip * 16, 8, 0, 768, None, swap_sems)
    swap.begin()
    small_gather = Gather(p, small, 16, 0, 768, [s.at[0] for s in gather])
    patch_copies = []
    for step in range(1, 4):
        to = lax.rem(p.blk + step, 4)
        copy = remote(
            patch.at[pl.ds(aligned(to * 144, 144), 144), :],
            patch_out.at[p.blk],
            patch_sems.at[0, step - 1],
            patch_sems.at[1, step - 1],
            {"blk": to},
        )
        copy.start()
        patch_copies.append(copy)
    own_patch = pltpu.make_async_copy(
        patch.at[pl.ds(aligned(p.blk * 144, 144), 144), :], patch_out.at[p.blk], patch_sems.at[0, 3]
    )
    own_patch.start()
    plans = []
    sections = []
    for number, (first, width) in enumerate(SCATTER_SECTIONS):
        half = width // 2
        bufs = (pair_in[number], b_in[number], z_in[number], a_in[number], last[number])
        section = Scatter(p, w, share, first, width, bufs, [s.at[number] for s in sems])
        sections.append(section)
        steps = section.steps()
        steps[0] = lambda begin=steps[0], load=loads[number]: (load.wait(), begin())
        plans.append(steps)
    small_steps = small_gather.steps()
    small_steps[0] = lambda begin=small_steps[0]: (swap.finish(), begin())
    plans.insert(1, small_steps)
    skew = SCATTER_SKEW
    last_tick = max(len(s) + skew * n for n, s in enumerate(plans))
    for tick in range(last_tick + 1):
        for number, steps in enumerate(plans):
            at = tick - skew * number
            if 0 <= at < len(steps):
                steps[at]()
    for section in sections:
        section.finish()
    small_gather.finish()
    small_gather.sent()
    for step, copy in enumerate(patch_copies):
        source = lax.rem(p.blk + 3 - step, 4)
        landed = patch_out.at[source]
        remote(
            landed, landed, patch_sems.at[0, step], patch_sems.at[1, step], {"blk": source}
        ).wait_recv()
        copy.wait_send()
    own_patch.wait()
    spread = Spread(p, mine, everyone, send_sem, recv_sem)
    out = small_tail(p, small, map_q[...], probe[...], share, spread)
    map_out[...], map_q_share[...] = out[0], out[1]
    probe_share[...] = jnp.broadcast_to(out[2], (24, 128))
    facts[...] = jnp.concatenate(
        [jnp.broadcast_to(out[3][:, :128], (7, 128)), out[4][:1]], axis=0
    )


def scatter_call(grads, small_own, map_q, probe, patch):
    dma = pltpu.SemaphoreType.DMA
    count = len(SCATTER_SECTIONS)
    widths = [w // 2 for _, w in SCATTER_SECTIONS]
    vm = lambda *shape, dt=jnp.bfloat16: pltpu.VMEM(shape, dt)
    f32 = jnp.float32
    return pl.pallas_call(
        scatter_kernel,
        out_shape=(
            jax.ShapeDtypeStruct((24, SCATTER_COLS), f32),
            jax.ShapeDtypeStruct((24, 768), f32),
            jax.ShapeDtypeStruct((24, 768), f32),
            jax.ShapeDtypeStruct((24, 128), f32),
            jax.ShapeDtypeStruct((8, 128), f32),
            jax.ShapeDtypeStruct((4, 144, 768), jnp.bfloat16),
        ),
        in_specs=[pl.BlockSpec(memory_space=pl.ANY)]
        + [pl.BlockSpec(memory_space=pltpu.VMEM)] * 4,
        out_specs=tuple([pl.BlockSpec(memory_space=pltpu.VMEM)] * 6),
        scratch_shapes=[
            vm(768, SCATTER_COLS),
            vm(256, 768, dt=f32),
            [vm(768, w) for w in widths],
            [vm(2, 192, w) for w in widths],
            [vm(2, 2, 3, 48, w) for w in widths],
            [vm(48, w) for w in widths],
            [vm(48, w, dt=f32) for w in widths],
            vm(8, 128, dt=f32),
            vm(31, 8, 128, dt=f32),
            dma((count,)),
            dma((4,)),
            dma((2, 4)),
            dma,
            dma,
            *gather_sems(1),
            dma((count, 2)),
            dma((count, 2, 2)),
            dma((count, 2, 2, 3)),
            dma((count, 2, 2, 3)),
            dma((count, 2)),
            dma((count, 2)),
        ],
        compiler_params=pltpu.CompilerParams(
            collective_id=1, has_side_effects=True, vmem_limit_bytes=62 * 2**20
        ),
        name="scatter_grads",
    )(grads, small_own, map_q, probe, patch)


def layer_norm(values, gain_vec, bias_vec):
    row_mean = jnp.mean(values, axis=-1, keepdims=True)
    centered = values - row_mean
    row_var = jnp.mean(centered * centered, axis=-1, keepdims=True)
    return centered * lax.rsqrt(row_var + 1e-06) * gain_vec + bias_vec


def unit_rows(pooled):
    return pooled * lax.rsqrt(jnp.sum(pooled * pooled, axis=-1, keepdims=True) + 1e-06)


def attend(queries, keys_all, values_all):
    scale = HEAD_DIM ** (-0.5)
    scores = (
        jnp.einsum("iqhe,ikhe->ihqk", queries, keys_all, preferred_element_type=jnp.float32) * scale
    )
    row_max = jnp.max(scores, axis=-1, keepdims=True)
    expos = jnp.exp(scores - row_max)
    row_sum = jnp.sum(expos, axis=-1, keepdims=True)
    attn_probs = (expos / row_sum).astype(jnp.bfloat16)
    mixed_out = jnp.einsum(
        "ihqk,ikhe->iqhe", attn_probs, values_all, preferred_element_type=jnp.float32
    )
    return (mixed_out.astype(jnp.bfloat16), row_max + jnp.log(row_sum))


def attend_back(queries, keys_all, values_all, log_norm, grad_mixed):
    scale = HEAD_DIM ** (-0.5)
    scores = (
        jnp.einsum("iqhe,ikhe->ihqk", queries, keys_all, preferred_element_type=jnp.float32) * scale
    )
    attn_probs = jnp.exp(scores - log_norm)
    grad_values = jnp.einsum(
        "ihqk,iqhe->ikhe",
        attn_probs.astype(jnp.bfloat16),
        grad_mixed,
        preferred_element_type=jnp.float32,
    )
    grad_probs = jnp.einsum(
        "iqhe,ikhe->ihqk", grad_mixed, values_all, preferred_element_type=jnp.float32
    )
    centre = jnp.sum(attn_probs * grad_probs, axis=-1, keepdims=True)
    grad_scores = (attn_probs * (grad_probs - centre)).astype(jnp.bfloat16)
    grad_queries = (
        jnp.einsum("ihqk,ikhe->iqhe", grad_scores, keys_all, preferred_element_type=jnp.float32)
        * scale
    )
    grad_keys = (
        jnp.einsum("ihqk,iqhe->ikhe", grad_scores, queries, preferred_element_type=jnp.float32)
        * scale
    )
    return (grad_queries, grad_keys, grad_values)


def adamw(parameter, gradient, moment_one, moment_two, step_rate, decay_rate):
    moment_one = BETA_ONE * moment_one + (1.0 - BETA_ONE) * gradient
    moment_two = BETA_TWO * moment_two + (1.0 - BETA_TWO) * gradient * gradient
    first_hat = moment_one / (1.0 - BETA_ONE**STEP)
    second_hat = moment_two / (1.0 - BETA_TWO**STEP)
    updated = parameter - step_rate * (
        first_hat / (jnp.sqrt(second_hat) + EPS_ADAM) + decay_rate * parameter
    )
    return (updated, moment_one, moment_two)


def local(
    patch_tokens,
    captions,
    pair_labels,
    master_weights,
    first_moments,
    second_moments,
    master_vectors,
    vector_first,
    vector_second,
    loss_scalars,
    scalar_first,
    scalar_second,
):
    blocks = lax.axis_size("blk")
    block = lax.axis_index("blk")
    all_images = patch_tokens.shape[0] * lax.axis_size("img")
    images = patch_tokens.shape[0] // blocks
    length = patch_tokens.shape[1] * blocks
    scale = HEAD_DIM ** (-0.5)
    both = ("blk", "img")
    rows = master_weights.shape[0]
    first_row = lax.axis_index(both) * rows
    patch_tokens = lax.all_to_all(patch_tokens, "blk", 0, 1, tiled=True)
    pair_labels = lax.dynamic_slice_in_dim(pair_labels, block * images, images, 0)
    rounded = master_weights.astype(jnp.bfloat16)
    full_vectors = lax.all_gather(master_vectors.astype(jnp.bfloat16), both, axis=0, tiled=True)
    vectors = full_vectors.astype(jnp.float32)

    def gather(start, stop):
        return lax.all_gather(rounded[:, start:stop], both, axis=0, tiled=True)

    w_front = gather(0, 4 * D)
    w_qkv = w_front[:, : 3 * D]
    w_out = w_front[:, 3 * D :]
    w_up = gather(4 * D, 4 * D + FF)
    w_down = gather(4 * D + FF, 4 * D + 2 * FF)
    own_map_q = rounded[:, 4 * D + 2 * FF : 5 * D + 2 * FF]
    w_map = gather(5 * D + 2 * FF, 8 * D + 2 * FF)
    w_map_kv = w_map[:, : 2 * D]
    w_map_out = w_map[:, 2 * D :]
    own_vectors = master_vectors.astype(jnp.bfloat16)
    tokens = patch_tokens.astype(jnp.float32)
    normed, norm_one_pull = jax.vjp(layer_norm, tokens, vectors[:, 0], vectors[:, 1])
    normed_b = normed.astype(jnp.bfloat16)
    qkv_b = jnp.einsum("ipd,dc->ipc", normed_b, w_qkv, preferred_element_type=jnp.float32).astype(
        jnp.bfloat16
    )
    queries = qkv_b[:, :, :D].reshape(images, length, HEADS, HEAD_DIM)
    keys_all = qkv_b[:, :, D : 2 * D].reshape(images, length, HEADS, HEAD_DIM)
    values_all = qkv_b[:, :, 2 * D :].reshape(images, length, HEADS, HEAD_DIM)
    mixed_heads, log_norm = attend(queries, keys_all, values_all)
    mixed_b = mixed_heads.reshape(images, length, D)
    residual = tokens + jnp.einsum(
        "ipd,dc->ipc", mixed_b, w_out, preferred_element_type=jnp.float32
    )
    hidden, norm_two_pull = jax.vjp(layer_norm, residual, vectors[:, 2], vectors[:, 3])
    hidden_b = hidden.astype(jnp.bfloat16)
    pre_act = jnp.einsum("ipd,df->ipf", hidden_b, w_up, preferred_element_type=jnp.float32)
    activation, gelu_pull = jax.vjp(jax.nn.gelu, pre_act)
    activation_b = activation.astype(jnp.bfloat16)
    layer_out = residual + jnp.einsum(
        "ipf,df->ipd", activation_b, w_down, preferred_element_type=jnp.float32
    )
    final_norm, norm_three_pull = jax.vjp(layer_norm, layer_out, vectors[:, 4], vectors[:, 5])
    final_b = final_norm.astype(jnp.bfloat16)
    map_kv = jnp.einsum("ipd,dc->ipc", final_b, w_map_kv, preferred_element_type=jnp.float32)
    map_kv = map_kv.astype(jnp.bfloat16).reshape(images, length, 2, HEADS, HEAD_DIM)
    probe_query = lax.psum(
        jnp.dot(own_vectors[:, 6], own_map_q, preferred_element_type=jnp.float32), both
    )
    probe_query = probe_query.astype(jnp.bfloat16).reshape(HEADS, HEAD_DIM)
    pool_scores = (
        jnp.einsum("he,iphe->ihp", probe_query, map_kv[:, :, 0], preferred_element_type=jnp.float32)
        * scale
    )
    row_max = jnp.max(pool_scores, axis=-1)
    row_sum = jnp.sum(jnp.exp(pool_scores - row_max[..., None]), axis=-1)
    pool_probs = jnp.exp(pool_scores - row_max[..., None]) / row_sum[..., None]
    map_values = map_kv[:, :, 1].astype(jnp.float32)
    pooled_part = jnp.einsum(
        "ihp,iphe->ihe", pool_probs, map_values, precision=lax.Precision.HIGHEST
    )
    pooled_heads = pooled_part.reshape(images, D)
    pooled_heads_b = pooled_heads.astype(jnp.bfloat16)
    pooled = jnp.dot(pooled_heads_b, w_map_out, preferred_element_type=jnp.float32)
    caption_all = lax.all_gather(captions, "img", axis=0, tiled=True).astype(jnp.float32)
    caption_unit = unit_rows(caption_all).astype(jnp.bfloat16)
    unit_image, unit_pull = jax.vjp(unit_rows, pooled)
    cosine = jnp.einsum(
        "id,cd->ic",
        unit_image.astype(jnp.bfloat16),
        caption_unit,
        preferred_element_type=jnp.float32,
    )
    signs = 2.0 * pair_labels.astype(jnp.float32) - 1.0

    def pair_loss(cosine_in, scalars_in):
        logits = jnp.exp(scalars_in[0]) * cosine_in + scalars_in[1]
        return jnp.sum(jax.nn.softplus(-signs * logits)) / all_images

    loss_local, loss_pull = jax.vjp(pair_loss, cosine, loss_scalars)
    grad_cosine, grad_scalars = loss_pull(jnp.ones((), jnp.float32))
    loss_total, scalar_total = lax.psum((loss_local, grad_scalars), both)
    grad_unit = jnp.einsum(
        "ic,cd->id",
        grad_cosine.astype(jnp.bfloat16),
        caption_unit,
        preferred_element_type=jnp.float32,
    )
    (grad_pooled,) = unit_pull(grad_unit)
    grad_pooled_b = grad_pooled.astype(jnp.bfloat16)
    pooled_all, grad_pooled_all = (
        lax.all_gather(pooled_heads_b, both, axis=0, tiled=True),
        lax.all_gather(grad_pooled_b, both, axis=0, tiled=True),
    )
    share_map_out = jnp.einsum(
        "id,ic->dc",
        lax.dynamic_slice_in_dim(pooled_all, first_row, rows, 1),
        grad_pooled_all,
        preferred_element_type=jnp.float32,
    )
    grad_heads_b = jnp.einsum(
        "ic,dc->id", grad_pooled_b, w_map_out, preferred_element_type=jnp.float32
    )
    grad_heads_b = grad_heads_b.astype(jnp.bfloat16).reshape(images, HEADS, HEAD_DIM)
    grad_heads = grad_heads_b.astype(jnp.float32)
    centre = jnp.sum(grad_heads * pooled_heads.reshape(images, HEADS, HEAD_DIM), axis=-1)
    grad_probs = jnp.einsum(
        "ihe,iphe->ihp", grad_heads_b, map_kv[:, :, 1], preferred_element_type=jnp.float32
    )
    grad_pool_scores = (pool_probs * (grad_probs - centre[..., None])).astype(jnp.bfloat16)
    grad_map_keys = (
        jnp.einsum(
            "ihp,he->iphe", grad_pool_scores, probe_query, preferred_element_type=jnp.float32
        )
        * scale
    )
    grad_map_values = jnp.einsum(
        "ihp,ihe->iphe", pool_probs, grad_heads, precision=lax.Precision.HIGHEST
    )
    grad_probe_query = (
        jnp.einsum(
            "ihp,iphe->he", grad_pool_scores, map_kv[:, :, 0], preferred_element_type=jnp.float32
        ).reshape(D)
        * scale
    )
    grad_map_kv = (
        jnp.stack([grad_map_keys, grad_map_values], axis=2)
        .astype(jnp.bfloat16)
        .reshape(images, length, 2 * D)
    )
    grad_w_map_kv = jnp.einsum(
        "ipd,ipc->dc", final_b, grad_map_kv, preferred_element_type=jnp.float32
    )
    grad_final = jnp.einsum(
        "ipc,dc->ipd", grad_map_kv, w_map_kv, preferred_element_type=jnp.float32
    )
    grad_layer_out, grad_gain_three, grad_bias_three = norm_three_pull(grad_final)
    probe_total = lax.psum(grad_probe_query, both)
    share_map_q = jnp.outer(own_vectors[:, 6].astype(jnp.float32), probe_total)
    share_probe = jnp.dot(
        own_map_q.astype(jnp.float32), probe_total, precision=lax.Precision.HIGHEST
    )
    grad_branch_two = grad_layer_out.astype(jnp.bfloat16)
    grad_w_down = jnp.einsum(
        "ipd,ipf->df", grad_branch_two, activation_b, preferred_element_type=jnp.float32
    )
    grad_activation = jnp.einsum(
        "ipd,df->ipf", grad_branch_two, w_down, preferred_element_type=jnp.float32
    )
    (grad_pre,) = gelu_pull(grad_activation)
    grad_pre_b = grad_pre.astype(jnp.bfloat16)
    grad_w_up = jnp.einsum("ipd,ipf->df", hidden_b, grad_pre_b, preferred_element_type=jnp.float32)
    grad_hidden = jnp.einsum("ipf,df->ipd", grad_pre_b, w_up, preferred_element_type=jnp.float32)
    grad_res_part, grad_gain_two, grad_bias_two = norm_two_pull(grad_hidden)
    grad_residual = grad_layer_out + grad_res_part
    grad_branch_one = grad_residual.astype(jnp.bfloat16)
    grad_w_out = jnp.einsum(
        "ipd,ipc->dc", mixed_b, grad_branch_one, preferred_element_type=jnp.float32
    )
    grad_mixed = jnp.einsum(
        "ipc,dc->ipd", grad_branch_one, w_out, preferred_element_type=jnp.float32
    )
    grad_mixed = grad_mixed.astype(jnp.bfloat16)
    grad_queries, grad_keys, grad_values = attend_back(
        queries, keys_all, values_all, log_norm, grad_mixed.reshape(images, length, HEADS, HEAD_DIM)
    )
    grad_qkv = jnp.concatenate(
        [
            grad_queries.reshape(images, length, D),
            grad_keys.reshape(images, length, D),
            grad_values.reshape(images, length, D),
        ],
        axis=-1,
    ).astype(jnp.bfloat16)
    grad_w_qkv = jnp.einsum("ipd,ipc->dc", normed_b, grad_qkv, preferred_element_type=jnp.float32)
    grad_normed = jnp.einsum("ipc,dc->ipd", grad_qkv, w_qkv, preferred_element_type=jnp.float32)
    grad_tok_part, grad_gain_one, grad_bias_one = norm_one_pull(grad_normed)
    patch_grad = lax.all_to_all(
        (grad_residual + grad_tok_part).astype(jnp.bfloat16), "blk", 1, 0, tiled=True
    ).astype(jnp.float32)
    grad_vectors = jnp.stack(
        [
            grad_gain_one,
            grad_bias_one,
            grad_gain_two,
            grad_bias_two,
            grad_gain_three,
            grad_bias_three,
        ],
        axis=1,
    )

    def scatter(part):
        return lax.psum_scatter(
            part.astype(jnp.bfloat16), both, scatter_dimension=0, tiled=True
        ).astype(jnp.float32)

    share_map_kv = scatter(grad_w_map_kv)
    share_down = scatter(grad_w_down)
    share_up = scatter(grad_w_up)
    share_front = scatter(jnp.concatenate([grad_w_qkv, grad_w_out], axis=1))
    weight_share = jnp.concatenate(
        [share_front, share_up, share_down, share_map_q, share_map_kv, share_map_out], axis=1
    )
    vector_share = jnp.concatenate(
        [
            lax.psum_scatter(grad_vectors, both, scatter_dimension=0, tiled=True),
            share_probe[:, None],
        ],
        axis=1,
    )
    squares = jnp.sum(weight_share * weight_share) + jnp.sum(vector_share * vector_share)
    square_total = lax.psum(squares, ("blk", "img"))
    grad_norm = jnp.sqrt(square_total + jnp.sum(scalar_total * scalar_total))
    factor = CLIP_AT / jnp.maximum(grad_norm, CLIP_AT)
    new_w, new_wm, new_wv = adamw(
        master_weights, weight_share * factor, first_moments, second_moments, 0.03, 0.1
    )
    new_v, new_vm, new_vv = adamw(
        master_vectors, vector_share * factor, vector_first, vector_second, 0.3, 0.0
    )
    new_s, new_sm, new_sv = adamw(
        loss_scalars, scalar_total * factor, scalar_first, scalar_second, 0.3, 0.0
    )
    return (
        loss_total,
        grad_norm,
        patch_grad,
        new_w,
        new_wm,
        new_wv,
        new_w.astype(jnp.bfloat16),
        new_v,
        new_vm,
        new_vv,
        new_v.astype(jnp.bfloat16),
        new_s,
        new_sm,
        new_sv,
    )


def local_kernels(
    patch_tokens,
    captions,
    pair_labels,
    master_weights,
    first_moments,
    second_moments,
    master_vectors,
    vector_first,
    vector_second,
    loss_scalars,
    scalar_first,
    scalar_second,
):
    blocks = lax.axis_size("blk")
    block = lax.axis_index("blk")
    all_images = patch_tokens.shape[0] * lax.axis_size("img")
    images = patch_tokens.shape[0] // blocks
    length = patch_tokens.shape[1] * blocks
    scale = HEAD_DIM ** (-0.5)
    pair_labels = lax.dynamic_slice_in_dim(pair_labels, block, 1, 0)
    rounded = master_weights.astype(jnp.bfloat16)
    own_map_q = rounded[:, 4 * D + 2 * FF : 5 * D + 2 * FF]
    own_vectors = master_vectors.astype(jnp.bfloat16)
    query_part = jnp.dot(own_vectors[:, 6], own_map_q, preferred_element_type=jnp.float32)
    query_high = query_part.astype(jnp.bfloat16).astype(jnp.float32)
    query_rows = jnp.concatenate(
        [
            query_high.reshape(6, 128),
            (query_part - query_high).reshape(6, 128),
            jnp.zeros((12, 128), jnp.float32),
        ]
    )
    own_all = jnp.concatenate(
        [
            master_weights[:, : 3 * D],
            jnp.pad(own_vectors.astype(jnp.float32), ((0, 0), (0, 121))),
            query_rows,
            master_weights[:, 3 * D : 4 * D + 2 * FF],
            master_weights[:, 5 * D + 2 * FF :],
        ],
        axis=1,
    )
    caption_rows = unit_rows(captions.astype(jnp.float32)).astype(jnp.bfloat16)
    caption_rows = jnp.pad(caption_rows, ((0, 14), (0, 0)))
    caption_rows = lax.dynamic_slice_in_dim(caption_rows, block * 16, 16, 0)
    weights, patch_tokens, caption_unit = gather_call(own_all, patch_tokens, caption_rows)
    patch_tokens = patch_tokens[None]
    w_qkv = weights[:, : 3 * D]
    vectors = weights[:, 2304:2432].astype(jnp.float32)
    query_all = weights[:, 2432:2560].astype(jnp.float32).reshape(32, 24, 128)
    w_out = weights[:, 2560:3328]
    w_up = weights[:, 3328:6400]
    w_down = weights[:, 6400:9472]
    w_map_kv = weights[:, 9472:11008]
    w_map_out = weights[:, 11008:]
    tokens = patch_tokens.astype(jnp.float32)
    normed, norm_one_pull = jax.vjp(layer_norm, tokens, vectors[:, 0], vectors[:, 1])
    normed_b = normed.astype(jnp.bfloat16)
    qkv_b = jnp.einsum("ipd,dc->ipc", normed_b, w_qkv, preferred_element_type=jnp.float32).astype(
        jnp.bfloat16
    )
    queries = qkv_b[:, :, :D].reshape(images, length, HEADS, HEAD_DIM)
    keys_all = qkv_b[:, :, D : 2 * D].reshape(images, length, HEADS, HEAD_DIM)
    values_all = qkv_b[:, :, 2 * D :].reshape(images, length, HEADS, HEAD_DIM)
    mixed_heads, log_norm = attend(queries, keys_all, values_all)
    mixed_b = mixed_heads.reshape(images, length, D)
    residual = tokens + jnp.einsum(
        "ipd,dc->ipc", mixed_b, w_out, preferred_element_type=jnp.float32
    )
    hidden, norm_two_pull = jax.vjp(layer_norm, residual, vectors[:, 2], vectors[:, 3])
    hidden_b = hidden.astype(jnp.bfloat16)
    pre_act = jnp.einsum("ipd,df->ipf", hidden_b, w_up, preferred_element_type=jnp.float32)
    activation, gelu_pull = jax.vjp(jax.nn.gelu, pre_act)
    activation_b = activation.astype(jnp.bfloat16)
    layer_out = residual + jnp.einsum(
        "ipf,df->ipd", activation_b, w_down, preferred_element_type=jnp.float32
    )
    final_norm, norm_three_pull = jax.vjp(layer_norm, layer_out, vectors[:, 4], vectors[:, 5])
    final_b = final_norm.astype(jnp.bfloat16)
    map_kv = jnp.einsum("ipd,dc->ipc", final_b, w_map_kv, preferred_element_type=jnp.float32)
    map_kv = map_kv.astype(jnp.bfloat16).reshape(images, length, 2, HEADS, HEAD_DIM)
    query_total = jnp.sum(query_all, axis=0)
    probe_query = (query_total[:6] + query_total[6:12]).reshape(D)
    probe_query = probe_query.astype(jnp.bfloat16).reshape(HEADS, HEAD_DIM)
    pool_scores = (
        jnp.einsum("he,iphe->ihp", probe_query, map_kv[:, :, 0], preferred_element_type=jnp.float32)
        * scale
    )
    row_max = jnp.max(pool_scores, axis=-1)
    row_sum = jnp.sum(jnp.exp(pool_scores - row_max[..., None]), axis=-1)
    pool_probs = jnp.exp(pool_scores - row_max[..., None]) / row_sum[..., None]
    map_values = map_kv[:, :, 1].astype(jnp.float32)
    pooled_part = jnp.einsum(
        "ihp,iphe->ihe", pool_probs, map_values, precision=lax.Precision.HIGHEST
    )
    pooled_heads = pooled_part.reshape(images, D)
    pooled_heads_b = pooled_heads.astype(jnp.bfloat16)
    pooled = jnp.dot(pooled_heads_b, w_map_out, preferred_element_type=jnp.float32)
    unit_image, unit_pull = jax.vjp(unit_rows, pooled)
    cosine = jnp.einsum(
        "id,cd->ic",
        unit_image.astype(jnp.bfloat16),
        caption_unit,
        preferred_element_type=jnp.float32,
    )
    signs = 2.0 * pair_labels.astype(jnp.float32) - 1.0
    signs = jnp.pad(signs.reshape(8, 50), ((0, 0), (0, 14))).reshape(8, 4, 16)
    signs = signs.transpose(1, 0, 2).reshape(1, 512)

    def pair_loss(cosine_in, scalars_in):
        logits = jnp.exp(scalars_in[0]) * cosine_in + scalars_in[1]
        return jnp.sum(jnp.where(signs == 0, 0.0, jax.nn.softplus(-signs * logits))) / all_images

    loss_local, loss_pull = jax.vjp(pair_loss, cosine, loss_scalars)
    grad_cosine, grad_scalars = loss_pull(jnp.ones((), jnp.float32))
    grad_unit = jnp.einsum(
        "ic,cd->id",
        grad_cosine.astype(jnp.bfloat16),
        caption_unit,
        preferred_element_type=jnp.float32,
    )
    (grad_pooled,) = unit_pull(grad_unit)
    grad_pooled_b = grad_pooled.astype(jnp.bfloat16)
    grad_heads_b = jnp.einsum(
        "ic,dc->id", grad_pooled_b, w_map_out, preferred_element_type=jnp.float32
    )
    grad_heads_b = grad_heads_b.astype(jnp.bfloat16).reshape(images, HEADS, HEAD_DIM)
    grad_heads = grad_heads_b.astype(jnp.float32)
    centre = jnp.sum(grad_heads * pooled_heads.reshape(images, HEADS, HEAD_DIM), axis=-1)
    grad_probs = jnp.einsum(
        "ihe,iphe->ihp", grad_heads_b, map_kv[:, :, 1], preferred_element_type=jnp.float32
    )
    grad_pool_scores = (pool_probs * (grad_probs - centre[..., None])).astype(jnp.bfloat16)
    grad_map_keys = (
        jnp.einsum(
            "ihp,he->iphe", grad_pool_scores, probe_query, preferred_element_type=jnp.float32
        )
        * scale
    )
    grad_map_values = jnp.einsum(
        "ihp,ihe->iphe", pool_probs, grad_heads, precision=lax.Precision.HIGHEST
    )
    grad_probe_query = (
        jnp.einsum(
            "ihp,iphe->he", grad_pool_scores, map_kv[:, :, 0], preferred_element_type=jnp.float32
        ).reshape(D)
        * scale
    )
    grad_map_kv = (
        jnp.stack([grad_map_keys, grad_map_values], axis=2)
        .astype(jnp.bfloat16)
        .reshape(images, length, 2 * D)
    )
    grad_w_map_kv = jnp.einsum(
        "ipd,ipc->dc", final_b, grad_map_kv, preferred_element_type=jnp.float32
    )
    grad_final = jnp.einsum(
        "ipc,dc->ipd", grad_map_kv, w_map_kv, preferred_element_type=jnp.float32
    )
    grad_layer_out, grad_gain_three, grad_bias_three = norm_three_pull(grad_final)
    grad_branch_two = grad_layer_out.astype(jnp.bfloat16)
    grad_w_down = jnp.einsum(
        "ipd,ipf->df", grad_branch_two, activation_b, preferred_element_type=jnp.float32
    )
    grad_activation = jnp.einsum(
        "ipd,df->ipf", grad_branch_two, w_down, preferred_element_type=jnp.float32
    )
    (grad_pre,) = gelu_pull(grad_activation)
    grad_pre_b = grad_pre.astype(jnp.bfloat16)
    grad_w_up = jnp.einsum("ipd,ipf->df", hidden_b, grad_pre_b, preferred_element_type=jnp.float32)
    grad_hidden = jnp.einsum("ipf,df->ipd", grad_pre_b, w_up, preferred_element_type=jnp.float32)
    grad_res_part, grad_gain_two, grad_bias_two = norm_two_pull(grad_hidden)
    grad_residual = grad_layer_out + grad_res_part
    grad_branch_one = grad_residual.astype(jnp.bfloat16)
    grad_w_out = jnp.einsum(
        "ipd,ipc->dc", mixed_b, grad_branch_one, preferred_element_type=jnp.float32
    )
    grad_mixed = jnp.einsum(
        "ipc,dc->ipd", grad_branch_one, w_out, preferred_element_type=jnp.float32
    )
    grad_mixed = grad_mixed.astype(jnp.bfloat16)
    grad_queries, grad_keys, grad_values = attend_back(
        queries, keys_all, values_all, log_norm, grad_mixed.reshape(images, length, HEADS, HEAD_DIM)
    )
    grad_qkv = jnp.concatenate(
        [
            grad_queries.reshape(images, length, D),
            grad_keys.reshape(images, length, D),
            grad_values.reshape(images, length, D),
        ],
        axis=-1,
    ).astype(jnp.bfloat16)
    grad_w_qkv = jnp.einsum("ipd,ipc->dc", normed_b, grad_qkv, preferred_element_type=jnp.float32)
    grad_normed = jnp.einsum("ipc,dc->ipd", grad_qkv, w_qkv, preferred_element_type=jnp.float32)
    grad_tok_part, grad_gain_one, grad_bias_one = norm_one_pull(grad_normed)
    grad_vectors = jnp.stack(
        [
            grad_gain_one,
            grad_bias_one,
            grad_gain_two,
            grad_bias_two,
            grad_gain_three,
            grad_bias_three,
        ],
        axis=1,
    )
    to_send = jnp.concatenate(
        [
            part.astype(jnp.bfloat16)
            for part in (
                grad_w_qkv,
                jnp.pad(grad_vectors, ((0, 0), (0, 250))),
                grad_w_out,
                grad_w_up,
                grad_w_down,
                grad_w_map_kv,
            )
        ],
        axis=1,
    )
    small_own = jnp.concatenate(
        [
            pooled_heads_b.astype(jnp.float32),
            grad_pooled_b.astype(jnp.float32),
            grad_probe_query[None],
            jnp.pad(jnp.stack([loss_local, grad_scalars[0], grad_scalars[1]]), (0, D - 3))[None],
            jnp.zeros((4, D), jnp.float32),
        ]
    )
    share, share_map_out, share_map_q, share_probe, facts, patch_grad = scatter_call(
        to_send,
        small_own,
        own_map_q.astype(jnp.float32),
        own_vectors[:, 6:7].astype(jnp.float32),
        (grad_residual + grad_tok_part)[0].astype(jnp.bfloat16),
    )
    patch_grad = patch_grad.astype(jnp.float32)
    loss_total, scalar_total, grad_norm = facts[0, 0], facts[0, 1:3], facts[7, 0]
    weight_share = jnp.concatenate(
        [
            share[:, :2304],
            share[:, 2560:9472],
            share_map_q,
            share[:, 9472:],
            share_map_out,
        ],
        axis=1,
    )
    vector_share = jnp.concatenate([share[:, 2304:2310], share_probe[:, :1]], axis=1)
    factor = CLIP_AT / jnp.maximum(grad_norm, CLIP_AT)
    new_w, new_wm, new_wv = adamw(
        master_weights, weight_share * factor, first_moments, second_moments, 0.03, 0.1
    )
    new_v, new_vm, new_vv = adamw(
        master_vectors, vector_share * factor, vector_first, vector_second, 0.3, 0.0
    )
    new_s, new_sm, new_sv = adamw(
        loss_scalars, scalar_total * factor, scalar_first, scalar_second, 0.3, 0.0
    )
    return (
        loss_total,
        grad_norm,
        patch_grad,
        new_w,
        new_wm,
        new_wv,
        new_w.astype(jnp.bfloat16),
        new_v,
        new_vm,
        new_vv,
        new_v.astype(jnp.bfloat16),
        new_s,
        new_sm,
        new_sv,
    )


def solution(mesh):
    in_specs = (
        P("img", "blk", None),
        P("img", None),
        P("img", None),
        P(("blk", "img"), None),
        P(("blk", "img"), None),
        P(("blk", "img"), None),
        P(("blk", "img"), None),
        P(("blk", "img"), None),
        P(("blk", "img"), None),
        P(),
        P(),
        P(),
    )
    out_specs = (
        P(),
        P(),
        P("img", "blk", None),
        P(("blk", "img"), None),
        P(("blk", "img"), None),
        P(("blk", "img"), None),
        P(("blk", "img"), None),
        P(("blk", "img"), None),
        P(("blk", "img"), None),
        P(("blk", "img"), None),
        P(("blk", "img"), None),
        P(),
        P(),
        P(),
    )
    body = local_kernels if tuple(mesh.shape.values()) == (4, 8) else local
    return jax.shard_map(body, mesh=mesh, in_specs=in_specs, out_specs=out_specs, check_vma=False)
```

```python
import functools

import jax
import jax.numpy as jnp
from jax import lax
from jax.experimental import pallas as pl
from jax.experimental.pallas import tpu as pltpu
from jax.sharding import PartitionSpec as P

D = 768
HEADS = 12
HEAD_DIM = 64
FF = 3072
STEP = 10


BETA_ONE = 0.9
BETA_TWO = 0.999
EPS_ADAM = 1e-08
CLIP_AT = 1.0


def layer_norm(values, gain_vec, bias_vec):
    row_mean = jnp.mean(values, axis=-1, keepdims=True)
    centered = values - row_mean
    row_var = jnp.mean(centered * centered, axis=-1, keepdims=True)
    return centered * lax.rsqrt(row_var + 1e-06) * gain_vec + bias_vec


def unit_rows(pooled):
    return pooled * lax.rsqrt(jnp.sum(pooled * pooled, axis=-1, keepdims=True) + 1e-06)


def attend(queries, keys_all, values_all):
    scale = HEAD_DIM ** (-0.5)
    scores = (
        jnp.einsum("iqhe,ikhe->ihqk", queries, keys_all, preferred_element_type=jnp.float32) * scale
    )
    row_max = jnp.max(scores, axis=-1, keepdims=True)
    expos = jnp.exp(scores - row_max)
    row_sum = jnp.sum(expos, axis=-1, keepdims=True)
    attn_probs = (expos / row_sum).astype(jnp.bfloat16)
    mixed_out = jnp.einsum(
        "ihqk,ikhe->iqhe", attn_probs, values_all, preferred_element_type=jnp.float32
    )
    return (mixed_out.astype(jnp.bfloat16), row_max + jnp.log(row_sum))


def attend_back(queries, keys_all, values_all, log_norm, grad_mixed):
    scale = HEAD_DIM ** (-0.5)
    scores = (
        jnp.einsum("iqhe,ikhe->ihqk", queries, keys_all, preferred_element_type=jnp.float32) * scale
    )
    attn_probs = jnp.exp(scores - log_norm)
    grad_values = jnp.einsum(
        "ihqk,iqhe->ikhe",
        attn_probs.astype(jnp.bfloat16),
        grad_mixed,
        preferred_element_type=jnp.float32,
    )
    grad_probs = jnp.einsum(
        "iqhe,ikhe->ihqk", grad_mixed, values_all, preferred_element_type=jnp.float32
    )
    centre = jnp.sum(attn_probs * grad_probs, axis=-1, keepdims=True)
    grad_scores = (attn_probs * (grad_probs - centre)).astype(jnp.bfloat16)
    grad_queries = (
        jnp.einsum("ihqk,ikhe->iqhe", grad_scores, keys_all, preferred_element_type=jnp.float32)
        * scale
    )
    grad_keys = (
        jnp.einsum("ihqk,iqhe->ikhe", grad_scores, queries, preferred_element_type=jnp.float32)
        * scale
    )
    return (grad_queries, grad_keys, grad_values)


def adamw(parameter, gradient, moment_one, moment_two, step_rate, decay_rate):
    moment_one = BETA_ONE * moment_one + (1.0 - BETA_ONE) * gradient
    moment_two = BETA_TWO * moment_two + (1.0 - BETA_TWO) * gradient * gradient
    first_hat = moment_one / (1.0 - BETA_ONE**STEP)
    second_hat = moment_two / (1.0 - BETA_TWO**STEP)
    updated = parameter - step_rate * (
        first_hat / (jnp.sqrt(second_hat) + EPS_ADAM) + decay_rate * parameter
    )
    return (updated, moment_one, moment_two)


def local(
    patch_tokens,
    captions,
    pair_labels,
    master_weights,
    first_moments,
    second_moments,
    master_vectors,
    vector_first,
    vector_second,
    loss_scalars,
    scalar_first,
    scalar_second,
):
    blocks = lax.axis_size("blk")
    block = lax.axis_index("blk")
    all_images = patch_tokens.shape[0] * lax.axis_size("img")
    images = patch_tokens.shape[0] // blocks
    length = patch_tokens.shape[1] * blocks
    scale = HEAD_DIM ** (-0.5)
    both = ("blk", "img")
    rows = master_weights.shape[0]
    first_row = lax.axis_index(both) * rows
    patch_tokens = lax.all_to_all(patch_tokens, "blk", 0, 1, tiled=True)
    pair_labels = lax.dynamic_slice_in_dim(pair_labels, block * images, images, 0)
    rounded = master_weights.astype(jnp.bfloat16)
    full_vectors = lax.all_gather(master_vectors.astype(jnp.bfloat16), both, axis=0, tiled=True)
    vectors = full_vectors.astype(jnp.float32)

    def gather(start, stop):
        return lax.all_gather(rounded[:, start:stop], both, axis=0, tiled=True)

    w_front = gather(0, 4 * D)
    w_qkv = w_front[:, : 3 * D]
    w_out = w_front[:, 3 * D :]
    w_up = gather(4 * D, 4 * D + FF)
    w_down = gather(4 * D + FF, 4 * D + 2 * FF)
    own_map_q = rounded[:, 4 * D + 2 * FF : 5 * D + 2 * FF]
    w_map = gather(5 * D + 2 * FF, 8 * D + 2 * FF)
    w_map_kv = w_map[:, : 2 * D]
    w_map_out = w_map[:, 2 * D :]
    own_vectors = master_vectors.astype(jnp.bfloat16)
    tokens = patch_tokens.astype(jnp.float32)
    normed, norm_one_pull = jax.vjp(layer_norm, tokens, vectors[:, 0], vectors[:, 1])
    normed_b = normed.astype(jnp.bfloat16)
    qkv_b = jnp.einsum("ipd,dc->ipc", normed_b, w_qkv, preferred_element_type=jnp.float32).astype(
        jnp.bfloat16
    )
    queries = qkv_b[:, :, :D].reshape(images, length, HEADS, HEAD_DIM)
    keys_all = qkv_b[:, :, D : 2 * D].reshape(images, length, HEADS, HEAD_DIM)
    values_all = qkv_b[:, :, 2 * D :].reshape(images, length, HEADS, HEAD_DIM)
    mixed_heads, log_norm = attend(queries, keys_all, values_all)
    mixed_b = mixed_heads.reshape(images, length, D)
    residual = tokens + jnp.einsum(
        "ipd,dc->ipc", mixed_b, w_out, preferred_element_type=jnp.float32
    )
    hidden, norm_two_pull = jax.vjp(layer_norm, residual, vectors[:, 2], vectors[:, 3])
    hidden_b = hidden.astype(jnp.bfloat16)
    pre_act = jnp.einsum("ipd,df->ipf", hidden_b, w_up, preferred_element_type=jnp.float32)
    activation, gelu_pull = jax.vjp(jax.nn.gelu, pre_act)
    activation_b = activation.astype(jnp.bfloat16)
    layer_out = residual + jnp.einsum(
        "ipf,df->ipd", activation_b, w_down, preferred_element_type=jnp.float32
    )
    final_norm, norm_three_pull = jax.vjp(layer_norm, layer_out, vectors[:, 4], vectors[:, 5])
    final_b = final_norm.astype(jnp.bfloat16)
    map_kv = jnp.einsum("ipd,dc->ipc", final_b, w_map_kv, preferred_element_type=jnp.float32)
    map_kv = map_kv.astype(jnp.bfloat16).reshape(images, length, 2, HEADS, HEAD_DIM)
    probe_query = lax.psum(
        jnp.dot(own_vectors[:, 6], own_map_q, preferred_element_type=jnp.float32), both
    )
    probe_query = probe_query.astype(jnp.bfloat16).reshape(HEADS, HEAD_DIM)
    pool_scores = (
        jnp.einsum("he,iphe->ihp", probe_query, map_kv[:, :, 0], preferred_element_type=jnp.float32)
        * scale
    )
    row_max = jnp.max(pool_scores, axis=-1)
    row_sum = jnp.sum(jnp.exp(pool_scores - row_max[..., None]), axis=-1)
    pool_probs = jnp.exp(pool_scores - row_max[..., None]) / row_sum[..., None]
    map_values = map_kv[:, :, 1].astype(jnp.float32)
    pooled_part = jnp.einsum(
        "ihp,iphe->ihe", pool_probs, map_values, precision=lax.Precision.HIGHEST
    )
    pooled_heads = pooled_part.reshape(images, D)
    pooled_heads_b = pooled_heads.astype(jnp.bfloat16)
    pooled = jnp.dot(pooled_heads_b, w_map_out, preferred_element_type=jnp.float32)
    caption_all = lax.all_gather(captions, "img", axis=0, tiled=True).astype(jnp.float32)
    caption_unit = unit_rows(caption_all).astype(jnp.bfloat16)
    unit_image, unit_pull = jax.vjp(unit_rows, pooled)
    cosine = jnp.einsum(
        "id,cd->ic",
        unit_image.astype(jnp.bfloat16),
        caption_unit,
        preferred_element_type=jnp.float32,
    )
    signs = 2.0 * pair_labels.astype(jnp.float32) - 1.0

    def pair_loss(cosine_in, scalars_in):
        logits = jnp.exp(scalars_in[0]) * cosine_in + scalars_in[1]
        return jnp.sum(jax.nn.softplus(-signs * logits)) / all_images

    loss_local, loss_pull = jax.vjp(pair_loss, cosine, loss_scalars)
    grad_cosine, grad_scalars = loss_pull(jnp.ones((), jnp.float32))
    loss_total, scalar_total = lax.psum((loss_local, grad_scalars), both)
    grad_unit = jnp.einsum(
        "ic,cd->id",
        grad_cosine.astype(jnp.bfloat16),
        caption_unit,
        preferred_element_type=jnp.float32,
    )
    (grad_pooled,) = unit_pull(grad_unit)
    grad_pooled_b = grad_pooled.astype(jnp.bfloat16)
    pooled_all, grad_pooled_all = (
        lax.all_gather(pooled_heads_b, both, axis=0, tiled=True),
        lax.all_gather(grad_pooled_b, both, axis=0, tiled=True),
    )
    share_map_out = jnp.einsum(
        "id,ic->dc",
        lax.dynamic_slice_in_dim(pooled_all, first_row, rows, 1),
        grad_pooled_all,
        preferred_element_type=jnp.float32,
    )
    grad_heads_b = jnp.einsum(
        "ic,dc->id", grad_pooled_b, w_map_out, preferred_element_type=jnp.float32
    )
    grad_heads_b = grad_heads_b.astype(jnp.bfloat16).reshape(images, HEADS, HEAD_DIM)
    grad_heads = grad_heads_b.astype(jnp.float32)
    centre = jnp.sum(grad_heads * pooled_heads.reshape(images, HEADS, HEAD_DIM), axis=-1)
    grad_probs = jnp.einsum(
        "ihe,iphe->ihp", grad_heads_b, map_kv[:, :, 1], preferred_element_type=jnp.float32
    )
    grad_pool_scores = (pool_probs * (grad_probs - centre[..., None])).astype(jnp.bfloat16)
    grad_map_keys = (
        jnp.einsum(
            "ihp,he->iphe", grad_pool_scores, probe_query, preferred_element_type=jnp.float32
        )
        * scale
    )
    grad_map_values = jnp.einsum(
        "ihp,ihe->iphe", pool_probs, grad_heads, precision=lax.Precision.HIGHEST
    )
    grad_probe_query = (
        jnp.einsum(
            "ihp,iphe->he", grad_pool_scores, map_kv[:, :, 0], preferred_element_type=jnp.float32
        ).reshape(D)
        * scale
    )
    grad_map_kv = (
        jnp.stack([grad_map_keys, grad_map_values], axis=2)
        .astype(jnp.bfloat16)
        .reshape(images, length, 2 * D)
    )
    grad_w_map_kv = jnp.einsum(
        "ipd,ipc->dc", final_b, grad_map_kv, preferred_element_type=jnp.float32
    )
    grad_final = jnp.einsum(
        "ipc,dc->ipd", grad_map_kv, w_map_kv, preferred_element_type=jnp.float32
    )
    grad_layer_out, grad_gain_three, grad_bias_three = norm_three_pull(grad_final)
    probe_total = lax.psum(grad_probe_query, both)
    share_map_q = jnp.outer(own_vectors[:, 6].astype(jnp.float32), probe_total)
    share_probe = jnp.dot(
        own_map_q.astype(jnp.float32), probe_total, precision=lax.Precision.HIGHEST
    )
    grad_branch_two = grad_layer_out.astype(jnp.bfloat16)
    grad_w_down = jnp.einsum(
        "ipd,ipf->df", grad_branch_two, activation_b, preferred_element_type=jnp.float32
    )
    grad_activation = jnp.einsum(
        "ipd,df->ipf", grad_branch_two, w_down, preferred_element_type=jnp.float32
    )
    (grad_pre,) = gelu_pull(grad_activation)
    grad_pre_b = grad_pre.astype(jnp.bfloat16)
    grad_w_up = jnp.einsum("ipd,ipf->df", hidden_b, grad_pre_b, preferred_element_type=jnp.float32)
    grad_hidden = jnp.einsum("ipf,df->ipd", grad_pre_b, w_up, preferred_element_type=jnp.float32)
    grad_res_part, grad_gain_two, grad_bias_two = norm_two_pull(grad_hidden)
    grad_residual = grad_layer_out + grad_res_part
    grad_branch_one = grad_residual.astype(jnp.bfloat16)
    grad_w_out = jnp.einsum(
        "ipd,ipc->dc", mixed_b, grad_branch_one, preferred_element_type=jnp.float32
    )
    grad_mixed = jnp.einsum(
        "ipc,dc->ipd", grad_branch_one, w_out, preferred_element_type=jnp.float32
    )
    grad_mixed = grad_mixed.astype(jnp.bfloat16)
    grad_queries, grad_keys, grad_values = attend_back(
        queries, keys_all, values_all, log_norm, grad_mixed.reshape(images, length, HEADS, HEAD_DIM)
    )
    grad_qkv = jnp.concatenate(
        [
            grad_queries.reshape(images, length, D),
            grad_keys.reshape(images, length, D),
            grad_values.reshape(images, length, D),
        ],
        axis=-1,
    ).astype(jnp.bfloat16)
    grad_w_qkv = jnp.einsum("ipd,ipc->dc", normed_b, grad_qkv, preferred_element_type=jnp.float32)
    grad_normed = jnp.einsum("ipc,dc->ipd", grad_qkv, w_qkv, preferred_element_type=jnp.float32)
    grad_tok_part, grad_gain_one, grad_bias_one = norm_one_pull(grad_normed)
    patch_grad = lax.all_to_all(
        (grad_residual + grad_tok_part).astype(jnp.bfloat16), "blk", 1, 0, tiled=True
    ).astype(jnp.float32)
    grad_vectors = jnp.stack(
        [
            grad_gain_one,
            grad_bias_one,
            grad_gain_two,
            grad_bias_two,
            grad_gain_three,
            grad_bias_three,
        ],
        axis=1,
    )

    def scatter(part):
        return lax.psum_scatter(
            part.astype(jnp.bfloat16), both, scatter_dimension=0, tiled=True
        ).astype(jnp.float32)

    share_map_kv = scatter(grad_w_map_kv)
    share_down = scatter(grad_w_down)
    share_up = scatter(grad_w_up)
    share_front = scatter(jnp.concatenate([grad_w_qkv, grad_w_out], axis=1))
    weight_share = jnp.concatenate(
        [share_front, share_up, share_down, share_map_q, share_map_kv, share_map_out], axis=1
    )
    vector_share = jnp.concatenate(
        [
            lax.psum_scatter(grad_vectors, both, scatter_dimension=0, tiled=True),
            share_probe[:, None],
        ],
        axis=1,
    )
    squares = jnp.sum(weight_share * weight_share) + jnp.sum(vector_share * vector_share)
    square_total = lax.psum(squares, ("blk", "img"))
    grad_norm = jnp.sqrt(square_total + jnp.sum(scalar_total * scalar_total))
    factor = CLIP_AT / jnp.maximum(grad_norm, CLIP_AT)
    new_w, new_wm, new_wv = adamw(
        master_weights, weight_share * factor, first_moments, second_moments, 0.03, 0.1
    )
    new_v, new_vm, new_vv = adamw(
        master_vectors, vector_share * factor, vector_first, vector_second, 0.3, 0.0
    )
    new_s, new_sm, new_sv = adamw(
        loss_scalars, scalar_total * factor, scalar_first, scalar_second, 0.3, 0.0
    )
    return (
        loss_total,
        grad_norm,
        patch_grad,
        new_w,
        new_wm,
        new_wv,
        new_w.astype(jnp.bfloat16),
        new_v,
        new_vm,
        new_vv,
        new_v.astype(jnp.bfloat16),
        new_s,
        new_sm,
        new_sv,
    )


LINK_SPEED = (1.0, 2.0)


def gather_key(number, at):
    return 0 if at == 0 else at + number


MESH = pl.DeviceIdType.MESH
CHIP_ROWS = 48
GATHER_SECTIONS = ((0, 2560), (2560, 3840), (6400, 3072), (9472, 2304))
SCATTER_SECTIONS = (
    (9472, 1536, True),
    (6400, 3072, False),
    (2560, 3840, True),
    (0, 1280, False),
    (1280, 1280, False),
)
GATHER_COLS = 11776
SCATTER_COLS = 11008


def aligned(value, step):
    return pl.multiple_of(value, step)


class Place:
    def __init__(self):
        self.blk = lax.axis_index("blk")
        self.img = lax.axis_index("img")
        self.x = lax.rem(self.blk, 2)
        self.y = self.blk // 2
        self.z = self.img // 2
        self.c = lax.rem(self.img, 2)
        self.chip = self.blk * 4 + self.z
        self.sibling = {"img": self.z * 2 + 1 - self.c}
        self.up = {"img": self.img + 2}
        self.down = {"img": self.img - 2}
        self.a_near = {"blk": self.block(1, 0)}
        self.b_near = {"blk": self.block(0, 1)}

    def block(self, da, db):
        flip_x = da * (1 - self.c) + db * self.c
        flip_y = db * (1 - self.c) + da * self.c
        other_x = self.x + flip_x * (1 - 2 * self.x)
        other_y = self.y + flip_y * (1 - 2 * self.y)
        return other_y * 2 + other_x


def remote(src, dst, send_sem, recv_sem, device):
    return pltpu.make_async_remote_copy(
        src_ref=src,
        dst_ref=dst,
        send_sem=send_sem,
        recv_sem=recv_sem,
        device_id=device,
        device_id_type=MESH,
    )


def greet_all(place):
    barrier = pltpu.get_barrier_semaphore()
    me = place.blk * 8 + place.img

    def greet(step, carry):
        other = lax.rem(me + step, 32)
        pl.semaphore_signal(
            barrier,
            inc=1,
            device_id={"blk": other // 8, "img": lax.rem(other, 8)},
            device_id_type=MESH,
        )
        return carry

    lax.fori_loop(1, 32, greet, 0)
    pl.semaphore_wait(barrier, 31)


class Gather:
    def __init__(self, place, buf, rows, first, width, sems):
        self.p, self.buf, self.rows, self.half = place, buf, rows, width // 2
        self.mine = aligned(first + place.c * self.half, 128)
        self.theirs = aligned(first + (1 - place.c) * self.half, 128)
        self.near_recv, self.z_recv, self.b_recv, self.near_send, self.z_send, self.b_send, self.pair = sems

    def item(self, da, db, level):
        start = aligned((self.p.block(da, db) * 4 + level) * self.rows, self.rows)
        return self.buf.at[pl.ds(start, self.rows), pl.ds(self.mine, self.half)]

    def a_copy(self):
        own = self.item(0, 0, self.p.z)
        return remote(own, own, self.near_send, self.near_recv, self.p.a_near)

    def z_copy(self, da, level, up):
        part = self.item(da, 0, level)
        device = self.p.up if up else self.p.down
        return remote(part, part, self.z_send.at[up, da, level], self.z_recv.at[da, level], device)

    def b_copy(self, da, level):
        part = self.item(da, 0, level)
        return remote(part, part, self.b_send.at[da, level], self.b_recv.at[da, level], self.p.b_near)

    def pair_copy(self, da, db, level):
        part = self.item(da, db, level)
        return remote(part, part, self.pair.at[0], self.pair.at[1], self.p.sibling)

    def onward(self, da, level, up, down):
        self.b_copy(da, level).start()
        if up:
            pl.when(self.p.z < 3)(lambda: self.z_copy(da, level, 1).start())
        if down:
            pl.when(self.p.z > 0)(lambda: self.z_copy(da, level, 0).start())
        self.pair_copy(da, 0, level).start()

    def begin(self):
        self.a_copy().start()
        self.onward(0, self.p.z, True, True)

    def near(self):
        part = self.item(1, 0, self.p.z)
        remote(part, part, self.near_send, self.near_recv, self.p.a_near).wait_recv()
        self.onward(1, self.p.z, True, True)

    def level(self, distance):
        z = self.p.z

        @pl.when(z >= distance)
        def from_below():
            for da in range(2):
                self.z_copy(da, z - distance, 1).wait_recv()
                self.onward(da, z - distance, True, False)

        @pl.when(z + distance <= 3)
        def from_above():
            for da in range(2):
                self.z_copy(da, z + distance, 0).wait_recv()
                self.onward(da, z + distance, False, True)

    def far(self):
        for level in range(4):
            for da in range(2):
                part = self.item(da, 1, level)
                remote(
                    part, part, self.b_send.at[da, level], self.b_recv.at[da, level], self.p.b_near
                ).wait_recv()
                self.pair_copy(da, 1, level).start()

    def finish(self):
        whole = self.buf.at[pl.ds(0, 16 * self.rows), pl.ds(self.theirs, self.half)]
        both = remote(whole, whole, self.pair.at[0], self.pair.at[1], self.p.sibling)
        both.wait_recv()

    def sent(self):
        z = self.p.z
        self.a_copy().wait_send()
        whole = self.buf.at[pl.ds(0, 16 * self.rows), pl.ds(self.mine, self.half)]
        remote(whole, whole, self.pair.at[0], self.pair.at[1], self.p.sibling).wait_send()
        for level in range(4):
            for da in range(2):
                self.b_copy(da, level).wait_send()
                if level < 3:
                    pl.when((z >= level) & (z < 3))(
                        lambda da=da, level=level: self.z_copy(da, level, 1).wait_send()
                    )
                if level > 0:
                    pl.when((z <= level) & (z > 0))(
                        lambda da=da, level=level: self.z_copy(da, level, 0).wait_send()
                    )

    def steps(self):
        return [
            self.begin,
            self.near,
            lambda: self.level(1),
            lambda: self.level(2),
            lambda: self.level(3),
            self.far,
        ]


def gather_sems(count):
    dma = pltpu.SemaphoreType.DMA
    return [
        dma((count,)),
        dma((count, 2, 4)),
        dma((count, 2, 4)),
        dma((count,)),
        dma((count, 2, 2, 4)),
        dma((count, 2, 4)),
        dma((count, 2)),
    ]


class Scatter:
    def __init__(self, place, buf, share, first, width, z_first, bufs, sems):
        self.p, self.buf, self.share, self.half = place, buf, share, width // 2
        self.z_first = z_first
        self.sides = 2 if z_first else 1
        self.mine = aligned(first + place.c * self.half, 128)
        self.theirs = aligned(first + (1 - place.c) * self.half, 128)
        self.pair_in, self.b_in, self.z_in, self.a_in, self.last = bufs
        self.pair, self.b_sem, self.z_send, self.z_recv, self.a_sem, self.end = sems

    def run_rows(self, da, db):
        return aligned(self.p.block(da, db) * 192, 192)

    def run(self, da, db):
        return self.buf.at[pl.ds(self.run_rows(da, db), 192), pl.ds(self.mine, self.half)]

    def level_rows(self, da, level):
        return aligned((self.p.block(da, 0) * 4 + level) * 48, 48)

    def part(self, da, level):
        return self.buf.at[pl.ds(self.level_rows(da, level), 48), pl.ds(self.mine, self.half)]

    def add(self, row, source, count, offset=0):
        def one(step, carry):
            here = aligned(row + step * 48, 48)
            there = aligned(offset + step * 48, 48)
            self.buf[pl.ds(here, 48), pl.ds(self.mine, self.half)] += source[pl.ds(there, 48), :]
            return carry

        if count == 1:
            one(0, 0)
        else:
            lax.fori_loop(0, count, one, 0)

    def pair_copy(self):
        return remote(
            self.buf.at[pl.ds(0, 768), pl.ds(self.theirs, self.half)],
            self.pair_in,
            self.pair.at[0],
            self.pair.at[1],
            self.p.sibling,
        )

    def b_copy(self, da):
        return remote(
            self.run(da, 1),
            self.b_in.at[da * 192 : da * 192 + 192, :],
            self.b_sem.at[0, da],
            self.b_sem.at[1, da],
            self.p.b_near,
        )

    def z_slot(self, da, level, up):
        return aligned(((up * self.sides + da) * 3 + level - up) * 48, 48)

    def z_copy(self, da, level, up):
        return remote(
            self.part(da, level),
            self.z_in.at[pl.ds(self.z_slot(da, level, up), 48), :],
            self.z_send.at[up, da, level - up],
            self.z_recv.at[up, da, level - up],
            self.p.up if up else self.p.down,
        )

    def a_copy(self):
        source = self.part(1, self.p.z) if self.z_first else self.run(1, 0)
        return remote(source, self.a_in, self.a_sem.at[0], self.a_sem.at[1], self.p.a_near)

    def end_copy(self):
        return remote(
            self.last.at[pl.ds(aligned((1 - self.p.c) * 24, 8), 24), :],
            self.share.at[:, pl.ds(self.mine, self.half)],
            self.end.at[0],
            self.end.at[1],
            self.p.sibling,
        )

    def begin(self):
        self.pair_copy().start()

    def pairs_far(self):
        self.pair_copy().wait_recv()
        for da in range(2):
            row = self.run_rows(da, 1)
            self.add(row, self.pair_in, 4, row)
            self.b_copy(da).start()

    def pairs_near(self):
        for da in range(2):
            row = self.run_rows(da, 0)
            self.add(row, self.pair_in, 4, row)

    def blocks(self):
        for da in (1, 0):
            self.b_copy(da).wait_recv()
            self.add(self.run_rows(da, 0), self.b_in, 4, da * 192)
            if da == 1 and not self.z_first:
                self.a_copy().start()

    def z_step(self, da, level, up, holds, takes, gives):
        @pl.when(holds)
        def step():
            copy = self.z_copy(da, level, up)

            @pl.when(takes)
            def take():
                copy.wait_recv()
                self.add(self.level_rows(da, level), self.z_in, 1, self.z_slot(da, level, up))

            if gives:
                copy.start()

    def levels(self, slot):
        z = self.p.z
        for da in range(self.sides):
            self.z_step(da, 3 - slot + z, 1, (z <= slot) & (z >= slot - 2), z >= 1, slot < 3)
            self.z_step(da, slot - 3 + z, 0, (z >= 3 - slot) & (z <= 5 - slot), z <= 2, slot < 3)

    def across(self):
        self.a_copy().start()

    def joined(self):
        self.a_copy().wait_recv()
        self.add(self.run_rows(0, 0), self.a_in, 4)

    def close(self):
        rows = self.level_rows(0, self.p.z)
        total = self.buf[pl.ds(rows, 48), pl.ds(self.mine, self.half)].astype(jnp.float32)
        if self.z_first:
            self.a_copy().wait_recv()
            total += self.a_in[...].astype(jnp.float32)
        self.last[...] = total
        self.end_copy().start()
        self.share[:, pl.ds(self.mine, self.half)] = self.last[
            pl.ds(aligned(self.p.c * 24, 8), 24), :
        ]

    def finish(self):
        z = self.p.z
        theirs = self.share.at[:, pl.ds(self.theirs, self.half)]
        remote(theirs, theirs, self.end.at[0], self.end.at[1], self.p.sibling).wait_recv()
        self.end_copy().wait_send()
        self.a_copy().wait_send()
        self.pair_copy().wait_send()
        for da in range(2):
            self.b_copy(da).wait_send()
        for da in range(self.sides):
            for number in range(3):
                up, down = self.z_copy(da, 3 - number, 1), self.z_copy(da, number, 0)
                pl.when(z < 3 - number)(lambda up=up: up.wait_send())
                pl.when(z > number)(lambda down=down: down.wait_send())


class Links:
    def __init__(self, slow=1.0, hop=2.0):
        self.flat = self.high = 0.0
        self.slow, self.hop = slow, hop

    def use(self, name, start, time):
        start = max(start, getattr(self, name))
        setattr(self, name, start + time * self.slow)
        return start + time * self.slow + self.hop

    def steps(self, section, start, width):
        size = width / 256
        out = []
        now = start + 0.35 * size * self.slow + 1.0
        out += [(now, section.pairs_far), (now + 0.5, section.pairs_near)]
        now = self.use("flat", now + 0.5, 1.01 * size)
        out.append((now, section.blocks))
        if not section.z_first:
            now = self.use("flat", now, 0.5 * size)
            out.append((now, section.joined))
        for slot in range(4):
            out.append((now, functools.partial(section.levels, slot)))
            if slot < 3:
                now = self.use("high", now, 0.2525 * section.sides * size)
        if section.z_first:
            out.append((now, section.across))
            now = self.use("flat", now, 0.13 * size)
        out.append((now, section.close))
        return out


class Program:
    def __init__(self):
        self.now, self.places, self.wanted = 0.0, [], []
        self.plans = {}
        self.tail = []

    def loop(self, name, count, each):
        self.plans[name] = {}
        for index in range(count):
            self.now += each
            self.places.append((self.now, name, index))

    def gap(self, time):
        self.now += time

    def want(self, steps):
        self.wanted += [(time, len(self.wanted) + n, step) for n, (time, step) in enumerate(steps)]

    def settle(self):
        for time, _, step in sorted(self.wanted, key=lambda entry: entry[:2]):
            for place, name, index in self.places:
                if place >= time:
                    self.plans[name].setdefault(index, []).append(step)
                    break
            else:
                self.tail.append(step)


class Swap:
    def __init__(self, place, pieces, buf, first_buf_row, rows, first, width, offset, sems):
        self.p, self.rows, self.half = place, rows, width // 2
        self.buf, self.sems = buf, sems
        self.row = aligned(first_buf_row + place.c * rows, rows)
        self.other_row = aligned(first_buf_row + (1 - place.c) * rows, rows)
        self.halves = []
        for core in range(2):
            low, here = first + core * self.half, []
            for array, source, target, size in pieces:
                start, stop = max(low, target), min(low + self.half, target + size)
                if start < stop:
                    at = start - low + offset if offset is not None else start
                    here.append((array, source + start - target, at, stop - start))
            self.halves.append(here)
        self.at = (
            pl.ds(aligned(first + place.c * self.half, 128), self.half)
            if offset is None
            else pl.ds(offset, self.half)
        )
        self.away_at = (
            pl.ds(aligned(first + (1 - place.c) * self.half, 128), self.half)
            if offset is None
            else pl.ds(offset, self.half)
        )

    def begin(self, late=None):
        for core in range(2):
            for array, source, at, size in self.halves[core]:
                if late is not None and (array is late[0]) != late[1]:
                    continue
                part = array.at[:, source : source + size]
                goal = self.buf.at[pl.ds(self.row, self.rows), at : at + size]

                @pl.when(self.p.c == core)
                def here(part=part, goal=goal):
                    pltpu.make_async_copy(part, goal, self.sems.at[2]).start()

                @pl.when(self.p.c != core)
                def away(part=part, goal=goal):
                    remote(part, goal, self.sems.at[0], self.sems.at[1], self.p.sibling).start()

    def finish(self):
        landed = self.buf.at[pl.ds(self.other_row, self.rows), self.at]
        own = self.buf.at[pl.ds(self.row, self.rows), self.at]
        gone = self.buf.at[pl.ds(self.row, self.rows), self.away_at]
        remote(landed, landed, self.sems.at[0], self.sems.at[1], self.p.sibling).wait_recv()
        pltpu.make_async_copy(own, own, self.sems.at[2]).wait()
        remote(gone, gone, self.sems.at[0], self.sems.at[1], self.p.sibling).wait_send()


class Spread:
    def __init__(self, place, mine, everyone, send_sem, recv_sem):
        self.p, self.mine, self.everyone = place, mine, everyone
        self.send_sem, self.recv_sem = send_sem, recv_sem
        self.me = place.blk * 8 + place.img

    def copy(self, step):
        other = lax.rem(self.me + step, 32)
        return remote(
            self.mine,
            self.everyone.at[step - 1],
            self.send_sem,
            self.recv_sem,
            {"blk": other // 8, "img": lax.rem(other, 8)},
        )

    def begin(self, tile):
        self.mine[...] = tile

        def start(step, carry):
            self.copy(step).start()
            return carry

        lax.fori_loop(1, 32, start, 0)

    def finish(self):
        lane = lax.broadcasted_iota(jnp.int32, (1, 768), 1)
        scalars = self.sums
        square = jnp.sum(jnp.where((lane == 1) | (lane == 2), scalars * scalars, 0.0))
        return scalars, jnp.sqrt(self.total() + square)

    def total(self):
        remote(
            self.everyone, self.everyone, self.send_sem, self.recv_sem, self.p.sibling
        ).wait()
        return self.mine[...] + jnp.sum(self.everyone[...], axis=0)


def small_tail(p, small, map_q, probe, share, spread, map_out_ref, map_q_ref):
    everything = small[...]
    as_rows = everything.astype(jnp.bfloat16)
    sums = jnp.sum(everything.reshape(32, 8, 768), axis=0)
    query, scalars = sums[2:3], sums[3:4]
    device = lax.broadcasted_iota(jnp.int32, (32, 256), 0) * 8
    row = lax.broadcasted_iota(jnp.int32, (32, 256), 1)

    def rows_of(kind):
        pick = (row == device + kind).astype(jnp.float32).astype(jnp.bfloat16)
        return jnp.dot(pick, as_rows, preferred_element_type=jnp.float32).astype(jnp.bfloat16)

    pooled, grads = rows_of(0), rows_of(1)
    first = (p.blk * 8 + p.img) * 24
    picks = (
        lax.broadcasted_iota(jnp.int32, (24, 768), 1)
        == lax.broadcasted_iota(jnp.int32, (24, 768), 0) + first
    ).astype(jnp.float32).astype(jnp.bfloat16)
    rows = lax.dot_general(
        picks, pooled, (((1,), (1,)), ((), ())), preferred_element_type=jnp.float32
    ).astype(jnp.bfloat16)
    map_out = jnp.dot(rows, grads, preferred_element_type=jnp.float32)
    map_q_share = probe * query
    probe_share = jnp.sum(map_q * query, axis=1, keepdims=True)
    square = (
        jnp.sum(map_out * map_out)
        + jnp.sum(map_q_share * map_q_share)
        + jnp.sum(probe_share * probe_share)
    )

    def one(step, total):
        part = share[:, pl.ds(aligned(step * 256, 256), 256)]
        return total + jnp.sum(part * part)

    square = lax.fori_loop(0, SCATTER_COLS // 256, one, square)
    spread.begin(jnp.full((8, 128), square, jnp.float32))
    spread.sums = scalars
    map_out_ref[...], map_q_ref[...] = map_out, map_q_share
    return probe_share


COL_VECTORS = 2304
COL_QUERY = 2432
COL_OUT = 2560
COL_UP = 3328
COL_DOWN = 6400
COL_MAP_KV = 9472
COL_MAP_OUT = 11008
TOKENS = 576
CHUNK = 96
TILE = 256
SCALE = 0.125
GELU_A = 0.7978845608028654
GELU_B = 0.044715
NT = (((1,), (1,)), ((), ()))
TN = (((0,), (0,)), ((), ()))


def dot(lhs, rhs, dims=(((1,), (0,)), ((), ()))):
    return lax.dot_general(lhs, rhs, dims, preferred_element_type=jnp.float32)


def loop(count, body, plan=None):
    def one(index, carry):
        body(index)
        for at, steps in (plan or {}).items():

            @pl.when(index == at)
            def run(steps=steps):
                for step in steps:
                    step()

        return carry

    lax.fori_loop(0, count, one, 0)


def columns(index, first=0, width=TILE):
    return pl.ds(aligned(first + index * width, 128), width)


def chunk_rows(index):
    return pl.ds(aligned(index * CHUNK, 32), CHUNK)


def normalize(values):
    row_mean = jnp.mean(values, axis=-1, keepdims=True)
    centered = values - row_mean
    row_var = jnp.mean(centered * centered, axis=-1, keepdims=True)
    rate = lax.rsqrt(row_var + 1e-06)
    return centered * rate, rate


def normalize_back(scaled, rate, grad, gain):
    inner = grad * gain
    first = jnp.mean(inner, axis=-1, keepdims=True)
    second = jnp.mean(inner * scaled, axis=-1, keepdims=True)
    return (
        rate * (inner - first - scaled * second),
        jnp.sum(grad * scaled, axis=0, keepdims=True),
        jnp.sum(grad, axis=0, keepdims=True),
    )


class Tower:
    def __init__(self, **refs):
        self.__dict__.update(refs)

    def unpack(self):
        turned = jnp.transpose(self.w[:, COL_VECTORS : COL_VECTORS + 128].astype(jnp.float32))
        self.vec[0:8, :] = turned[0:8]
        packed = self.w[:, COL_QUERY : COL_QUERY + 128].astype(jnp.float32)
        total = jnp.sum(packed.reshape(32, 24, 128), axis=0)
        query = total[0:6] + total[6:12]
        row = jnp.concatenate([query[i : i + 1] for i in range(6)], axis=1)
        self.vec[8:16, :] = jnp.broadcast_to(row, (8, 768)).astype(jnp.bfloat16).astype(jnp.float32)

    def norm(self, source, gain, bias, out):
        def body(index):
            rows = chunk_rows(index)
            scaled, _ = normalize(source[rows, :].astype(jnp.float32))
            out[rows, :] = (scaled * gain + bias).astype(jnp.bfloat16)

        loop(TOKENS // CHUNK, body)

    def first_norm(self):
        self.norm(self.x, self.vec[0:1, :], self.vec[1:2, :], self.h)

    def project(self, plan=None):
        def body(index):
            self.qkv[:, columns(index)] = dot(self.h[...], self.w[:, columns(index)]).astype(jnp.bfloat16)

        loop(9, body, plan)

    def pair_of(self, pair, which):
        return self.qkv[:, columns(pair, which * D, 128)]

    def attend(self, plan=None):
        lanes = lax.broadcasted_iota(jnp.int32, (TOKENS, 128), 1)

        def body(pair):
            queries = self.pair_of(pair, 0) * jnp.bfloat16(SCALE)
            keys = self.pair_of(pair, 1)
            values_turned = jnp.transpose(self.pair_of(pair, 2))
            mixed = []
            for head in range(2):
                mine = (lanes < 64) if head == 0 else (lanes >= 64)
                masked = jnp.where(mine, queries, jnp.bfloat16(0))
                scores = dot(keys, masked, NT)
                most = jnp.max(scores, axis=0, keepdims=True)
                expos = jnp.exp(scores - most)
                total = jnp.sum(expos, axis=0, keepdims=True)
                part = dot(values_turned[head * 64 : head * 64 + 64], expos.astype(jnp.bfloat16))
                mixed.append(part * (1.0 / total))
                self.lse[pl.ds(pair * 2 + head, 1), :] = most + jnp.log(total)
            self.a[:, columns(pair, 0, 128)] = jnp.transpose(
                jnp.concatenate(mixed, axis=0)
            ).astype(jnp.bfloat16)

        loop(6, body, plan)

    def attend_out(self, plan=None):
        def body(index):
            self.r[:, columns(index)] = self.x[:, columns(index)].astype(jnp.float32) + dot(
                self.a[...], self.w[:, columns(index, COL_OUT)]
            )

        loop(3, body, plan)
        self.norm(self.r, self.vec[2:3, :], self.vec[3:4, :], self.h2)

    def feed_up(self, plan=None):
        def body(index):
            value = dot(self.h2[...], self.w[:, columns(index, COL_UP)])
            square = value * value
            bend = jnp.tanh(GELU_A * value * (1.0 + GELU_B * square))
            half = 0.5 + 0.5 * bend
            self.g[:, columns(index)] = (value * half).astype(jnp.bfloat16)
            slope = half + 0.5 * value * (1.0 - bend * bend) * (
                GELU_A + 3.0 * GELU_A * GELU_B * square
            )
            self.gp[:, columns(index)] = slope.astype(jnp.bfloat16)

        loop(12, body, plan)

    def feed_down(self, plan=None):
        def body(index):
            self.y[:, columns(index)] = self.r[:, columns(index)] + dot(
                self.g[...], self.w[columns(index), COL_DOWN : COL_DOWN + FF], NT
            )

        loop(3, body, plan)
        self.norm(self.y, self.vec[4:5, :], self.vec[5:6, :], self.f)

    def pool_project(self, plan=None):
        def body(index):
            self.kvp[:, columns(index)] = dot(
                self.f[...], self.w[:, columns(index, COL_MAP_KV)]
            ).astype(jnp.bfloat16)

        loop(6, body, plan)

    def pool(self, signs, temperature, offset, images):
        head = lax.broadcasted_iota(jnp.int32, (16, D), 0)
        owner = lax.broadcasted_iota(jnp.int32, (16, D), 1) // HEAD_DIM
        own = head == owner
        heads_query = jnp.where(own, self.vec[8:9, :], 0.0).astype(jnp.bfloat16)
        keys, values = self.kvp[:, :D], self.kvp[:, D:]
        scores = dot(heads_query, keys, NT) * SCALE
        expos = jnp.exp(scores - jnp.max(scores, axis=1, keepdims=True))
        probs = expos / jnp.sum(expos, axis=1, keepdims=True)
        probs_high = probs.astype(jnp.bfloat16)
        probs_low = (probs - probs_high.astype(jnp.float32)).astype(jnp.bfloat16)
        spread = dot(probs_high, values) + dot(probs_low, values)
        pooled = jnp.sum(jnp.where(own, spread, 0.0), axis=0, keepdims=True)
        pooled_b = pooled.astype(jnp.bfloat16)
        w_out = self.w[:, COL_MAP_OUT : COL_MAP_OUT + D]
        many = jnp.broadcast_to(pooled, (16, D)).astype(jnp.bfloat16)
        embed = dot(many, w_out)[0:1]
        rate = lax.rsqrt(jnp.sum(embed * embed, axis=1, keepdims=True) + 1e-06)
        unit = jnp.broadcast_to(embed * rate, (16, D)).astype(jnp.bfloat16)
        cosine = dot(unit, self.cap[...], NT)[0:1]
        heat = jnp.exp(temperature)
        logits = heat * cosine + offset
        turned = -signs * logits
        losses = jnp.maximum(turned, 0.0) + jnp.log1p(jnp.exp(-jnp.abs(turned)))
        loss = jnp.sum(jnp.where(signs == 0.0, 0.0, losses), axis=1, keepdims=True) / images
        grad_logits = -signs * (1.0 / (1.0 + jnp.exp(-turned))) / images
        grad_heat = jnp.sum(grad_logits * cosine * heat, axis=1, keepdims=True)
        grad_offset = jnp.sum(grad_logits, axis=1, keepdims=True)
        grad_cosine = jnp.broadcast_to(grad_logits * heat, (16, cosine.shape[1])).astype(jnp.bfloat16)
        grad_unit = dot(grad_cosine, self.cap[...])[0:1]
        grad_embed = rate * grad_unit - embed * (
            rate * rate * rate * jnp.sum(grad_unit * embed, axis=1, keepdims=True)
        )
        grad_many = jnp.broadcast_to(grad_embed, (16, D)).astype(jnp.bfloat16)
        grad_pooled = dot(grad_many, w_out, NT).astype(jnp.bfloat16).astype(jnp.float32)
        heads_grad = jnp.where(own, grad_pooled, 0.0).astype(jnp.bfloat16)
        grad_probs = dot(heads_grad, values, NT)
        centre = jnp.sum(probs * grad_probs, axis=1, keepdims=True)
        grad_scores = (probs * (grad_probs - centre)).astype(jnp.bfloat16)
        query_spread = dot(grad_scores, keys) * SCALE
        grad_query = jnp.sum(jnp.where(own, query_spread, 0.0), axis=0, keepdims=True)
        self.small_own[0:1, :] = pooled_b.astype(jnp.float32)
        self.small_own[1:2, :] = grad_many[0:1].astype(jnp.float32)
        self.small_own[2:3, :] = grad_query
        lane = lax.broadcasted_iota(jnp.int32, (1, D), 1)
        self.small_own[3:4, :] = jnp.where(
            lane == 0, loss, jnp.where(lane == 1, grad_heat, jnp.where(lane == 2, grad_offset, 0.0))
        )
        self.small_own[4:8, :] = jnp.zeros((4, D), jnp.float32)
        self.kvp[:, :D] = (dot(grad_scores, heads_query, TN) * SCALE).astype(jnp.bfloat16)
        both_probs = jnp.concatenate([probs_high, probs_low], axis=0)
        both_grads = jnp.concatenate([heads_grad, heads_grad], axis=0)
        self.kvp[:, D:] = dot(both_probs, both_grads, TN).astype(jnp.bfloat16)

    def turn(self, source):
        def body(index):
            self.turned[columns(index), :] = jnp.transpose(source[:, columns(index)])

        loop(3, body)

    def weight_grad(self, first, source, tiles, plan=None):
        def body(index):
            self.w[:, columns(index, first)] = dot(
                self.turned[...], source[:, columns(index)]
            ).astype(jnp.bfloat16)

        loop(tiles, body, plan)

    def input_grad(self, source, first, width, plan=None):
        def body(index):
            self.acc[:, columns(index)] = dot(
                source[...], self.w[columns(index), first : first + width], NT
            )

        loop(3, body, plan)

    def norm_back(self, source, added, number, out, rounded):
        gain = self.vec[2 * number : 2 * number + 1, :]

        def body(index, carry):
            rows = chunk_rows(index)
            scaled, rate = normalize(source[rows, :].astype(jnp.float32))
            grad, grad_gain, grad_bias = normalize_back(scaled, rate, self.acc[rows, :], gain)
            if added is not None:
                grad = grad + added[rows, :]
            if out is not None:
                out[rows, :] = grad
            rounded[rows, :] = grad.astype(jnp.bfloat16)
            return carry[0] + grad_gain, carry[1] + grad_bias

        zero = jnp.zeros((1, D), jnp.float32)
        grad_gain, grad_bias = lax.fori_loop(0, TOKENS // CHUNK, body, (zero, zero))
        self.vec_grad[2 * number : 2 * number + 1, :] = grad_gain
        self.vec_grad[2 * number + 1 : 2 * number + 2, :] = grad_bias

    def pool_back(self, plan=None, after=None):
        self.input_grad(self.kvp, COL_MAP_KV, 2 * D)
        self.turn(self.f)
        self.weight_grad(COL_MAP_KV, self.kvp, 6, plan)
        if after is not None:
            after()
        self.norm_back(self.y, None, 2, self.y, self.f)

    def down_back(self, plan=None):
        self.turn(self.f)

        def body(index):
            here = columns(index)
            grad = dot(self.f[...], self.w[:, columns(index, COL_DOWN)])
            self.gp[:, here] = (grad * self.gp[:, here].astype(jnp.float32)).astype(jnp.bfloat16)
            self.w[:, columns(index, COL_DOWN)] = dot(self.turned[...], self.g[:, here]).astype(
                jnp.bfloat16
            )

        loop(12, body, plan)

    def up_input(self, plan=None):
        self.input_grad(self.gp, COL_UP, FF, plan)

    def up_weight(self, plan=None):
        self.turn(self.h2)
        self.weight_grad(COL_UP, self.gp, 12, plan)

    def up_norm(self):
        self.norm_back(self.r, self.y, 1, self.r, self.f)

    def out_back(self, plan=None):
        self.turn(self.a)

        def body(index):
            self.a[:, columns(index)] = dot(
                self.f[...], self.w[columns(index), COL_OUT : COL_OUT + D], NT
            ).astype(jnp.bfloat16)

        loop(3, body)
        self.weight_grad(COL_OUT, self.f, 3, plan)

    def attend_back(self, plan=None):
        lanes = lax.broadcasted_iota(jnp.int32, (TOKENS, 128), 1)

        def body(pair):
            queries = self.pair_of(pair, 0) * jnp.bfloat16(SCALE)
            keys, values = self.pair_of(pair, 1), self.pair_of(pair, 2)
            grads = self.a[:, columns(pair, 0, 128)]
            keys_turned = jnp.transpose(keys)
            grad_queries = []
            grad_keys = None
            for head in range(2):
                mine = (lanes < 64) if head == 0 else (lanes >= 64)
                masked = jnp.where(mine, queries, jnp.bfloat16(0))
                masked_grads = jnp.where(mine, grads, jnp.bfloat16(0))
                scores = dot(keys, masked, NT)
                probs = jnp.exp(scores - self.lse[pl.ds(pair * 2 + head, 1), :])
                value_part = dot(probs.astype(jnp.bfloat16), masked_grads)
                grad_probs = dot(values, masked_grads, NT)
                centre = jnp.sum(probs * grad_probs, axis=0, keepdims=True)
                grad_scores = (probs * (grad_probs - centre)).astype(jnp.bfloat16)
                key_part = dot(grad_scores, masked)
                grad_queries.append(dot(keys_turned[head * 64 : head * 64 + 64], grad_scores))
                if head == 0:
                    grad_keys, grad_values = key_part, value_part
                else:
                    grad_keys, grad_values = grad_keys + key_part, grad_values + value_part
            self.qkv[:, columns(pair, 0, 128)] = (
                jnp.transpose(jnp.concatenate(grad_queries, axis=0)) * SCALE
            ).astype(jnp.bfloat16)
            self.qkv[:, columns(pair, D, 128)] = grad_keys.astype(jnp.bfloat16)
            self.qkv[:, columns(pair, 2 * D, 128)] = grad_values.astype(jnp.bfloat16)

        loop(6, body, plan)

    def project_input(self, plan=None):
        self.first_norm()
        self.input_grad(self.qkv, 0, 3 * D, plan)
        self.turn(self.h)
        self.norm_back(self.x, self.r, 0, None, self.h)

    def project_weight(self, start, tiles, plan=None):
        def body(index):
            self.w[:, columns(index, start * TILE)] = dot(
                self.turned[...], self.qkv[:, columns(index, start * TILE)]
            ).astype(jnp.bfloat16)

        loop(tiles, body, plan)

    def vectors_back(self):
        packed = jnp.concatenate([self.vec_grad[...], jnp.zeros((120, D), jnp.float32)], axis=0)
        self.w[:, COL_VECTORS : COL_VECTORS + 128] = jnp.transpose(packed).astype(jnp.bfloat16)
        self.w[:, COL_QUERY : COL_QUERY + 128] = jnp.zeros((D, 128), jnp.bfloat16)


def spread_steps(steps, count):
    plan = {}
    for at, step in enumerate(steps):
        plan.setdefault(min(count - 1, at * count // max(len(steps), 1)), []).append(step)
    return plan


TOWER_REFS = (
    ("w", "x", "cap", "h", "qkv", "a", "r", "h2", "g", "gp", "y", "f", "kvp", "lse", "turned", "acc", "vec", "vec_grad", "small_own")
)


def layer_kernel(
    master, tokens, captions, vectors, labels, scalars,
    share_out, vector_out, facts, patch_out, *scratch,
):
    p = Place()
    t = Tower(**dict(zip(TOWER_REFS, scratch)))
    scratch = scratch[len(TOWER_REFS) :]
    stage, small, pair_a, pair_b, b_in, z_in, a_in, last, mine, everyone = scratch[:10]
    share, extra, caps, map_q, map_out, map_q_share, signs = scratch[10:17]
    swap_sems, token_sems, patch_sems, own_sems, send_sem, recv_sem, grant = scratch[17:24]
    gather_s, scatter_s = scratch[24:31], scratch[31:]
    map_q_at = 4 * D + 2 * FF
    map_q_copy = pltpu.make_async_copy(
        master.at[:, map_q_at : map_q_at + D], map_q, own_sems.at[0]
    )
    map_q_copy.start()
    greet_all(p)

    count = len(GATHER_SECTIONS)
    gathers, swaps = [], []
    pieces = (
        (master, 0, 0, 3 * D),
        (extra, 0, 3 * D, 256),
        (master, 3 * D, COL_OUT, D + 2 * FF),
        (master, map_q_at + D, COL_MAP_KV, 3 * D),
    )
    for number, (first, width) in enumerate(GATHER_SECTIONS):
        swaps.append(
            Swap(p, pieces, stage, 0, 24, first, width, first // 2, swap_sems.at[number])
        )
        swaps[-1].begin((extra, False))
        gathers.append(Gather(p, t.w, CHIP_ROWS, first, width, [s.at[number] for s in gather_s]))
    own_vectors = vectors[...].astype(jnp.bfloat16).astype(jnp.float32)
    map_q_copy.wait()
    map_q[...] = map_q[...].astype(jnp.bfloat16).astype(jnp.float32)
    part = jnp.sum(own_vectors[:, 6:7] * map_q[...], axis=0, keepdims=True)
    high = part.astype(jnp.bfloat16).astype(jnp.float32)
    for side in range(6):
        lanes = slice(side * 128, side * 128 + 128)
        extra[side : side + 1, 128:256] = high[:, lanes]
        extra[6 + side : 7 + side, 128:256] = (part - high)[:, lanes]
    extra[12:24, 128:256] = jnp.zeros((12, 128), jnp.float32)
    extra[:, 0:128] = jnp.concatenate([own_vectors, jnp.zeros((24, 121), jnp.float32)], axis=1)
    swaps[0].begin((extra, True))
    each = captions.shape[0]
    caps[...] = jnp.concatenate(
        [unit_rows(captions[...].astype(jnp.float32)), jnp.zeros((64 - each, D), jnp.float32)], axis=0
    ).astype(jnp.bfloat16)
    own_caps = caps.at[pl.ds(aligned(p.blk * 16, 16), 16), :]
    swaps.append(
        Swap(p, ((own_caps, 0, 0, D),), t.cap, p.chip * 32, 16, 0, D, None, swap_sems.at[count])
    )
    swaps[-1].begin()
    gathers.append(Gather(p, t.cap, 32, 0, D, [s.at[count] for s in gather_s]))
    token_copies = []
    for step in range(1, 4):
        to = lax.rem(p.blk + step, 4)
        token_copies.append(
            remote(
                tokens.at[to],
                t.x.at[pl.ds(aligned(p.blk * 144, 144), 144), :],
                token_sems.at[0, step - 1],
                token_sems.at[1, step - 1],
                {"blk": to},
            )
        )
        token_copies[-1].start()
    own_tokens = pltpu.make_async_copy(
        tokens.at[p.blk], t.x.at[pl.ds(aligned(p.blk * 144, 144), 144), :], token_sems.at[0, 3]
    )
    own_tokens.start()

    def ready(number):
        swaps[number].finish()
        if number < count:
            first, width = GATHER_SECTIONS[number]
            t.w[
                pl.ds(aligned(p.chip * 48, 48), 48), pl.ds(gathers[number].mine, width // 2)
            ] = stage[:, first // 2 : first // 2 + width // 2].astype(jnp.bfloat16)
        gathers[number].begin()

    order = []
    for number, gather in enumerate(gathers):
        for at, step in enumerate(gather.steps()):
            call = step if at else (lambda number=number: ready(number))
            order.append((gather_key(number, at), number, at, call))
    order.sort(key=lambda entry: entry[:3])
    ends = [
        max(i for i, entry in enumerate(order) if entry[1] <= number)
        for number in range(count + 1)
    ]

    def between(number):
        return [entry[3] for entry in order[ends[number - 1] + 1 : ends[number] + 1]]

    for entry in order[: ends[0] + 1]:
        entry[3]()
    slot = lax.broadcasted_iota(jnp.int32, (8 * each, 512), 1)
    within = (slot >> 7) * 16 + (slot & 15)
    source = ((slot >> 5) & 3) * (2 * each) + ((slot >> 4) & 1) * each + within
    label = lax.broadcasted_iota(jnp.int32, (8 * each, 512), 0)
    pick = ((label == source) & (within < each)).astype(jnp.float32).astype(jnp.bfloat16)
    row = 2.0 * labels[pl.ds(p.blk, 1), :].astype(jnp.float32) - 1.0
    signs[...] = dot(jnp.broadcast_to(row, (16, 8 * each)).astype(jnp.bfloat16), pick)
    for step in range(3):
        source = lax.rem(p.blk + 3 - step, 4)
        landed = t.x.at[pl.ds(aligned(source * 144, 144), 144), :]
        remote(
            landed, landed, token_sems.at[0, step], token_sems.at[1, step], {"blk": source}
        ).wait_recv()
    own_tokens.wait()
    gathers[0].finish()

    t.unpack()
    t.first_norm()
    t.project()
    t.attend(spread_steps(between(1), 6))
    gathers[1].finish()
    t.attend_out()
    t.feed_up(spread_steps(between(2), 12))
    gathers[2].finish()
    t.feed_down(spread_steps(between(3), 3))
    gathers[3].finish()
    t.pool_project(spread_steps(between(4), 6))
    gathers[4].finish()
    t.vec_grad[...] = jnp.zeros((8, D), jnp.float32)
    images = tokens.shape[0] * 8
    t.pool(signs[0:1, :], jnp.full((1, 512), scalars[0], jnp.float32), scalars[1], images)
    swap = Swap(
        p, ((t.small_own, 0, 0, D),), small, p.chip * 16, 8, 0, D, None, swap_sems.at[count + 1]
    )
    swap.begin()
    small_gather = Gather(p, small, 16, 0, D, [s.at[count + 1] for s in gather_s])
    small_steps = small_gather.steps()
    for gather in gathers:
        gather.sent()
    for copy in token_copies:
        copy.wait_send()

    sections = []
    for number, (first, width, z_first) in enumerate(SCATTER_SECTIONS):
        half = width // 2
        rest = (number - 3) * 640
        bufs = (
            (pair_b if number in (1, 3, 4) else pair_a).at[
                :, (half if number == 4 else 0) : (2 * half if number == 4 else half)
            ],
            b_in[number] if number < 3 else t.g.at[0:384, rest : rest + half],
            z_in[number]
            if number < 2
            else (t.gp.at[:, 0:half] if number == 2 else t.g.at[0:288, 1280 + rest : 1280 + rest + half]),
            a_in[number] if number < 3 else t.g.at[384:576, rest : rest + half],
            last[number],
        )
        sections.append(
            Scatter(p, t.w, share, first, width, z_first, bufs, [s.at[number] for s in scatter_s])
        )
    pool_part, down_part, up_part, front_part, end_part = sections

    def small_begin():
        swap.finish()
        small_steps[0]()

    links, program = Links(*LINK_SPEED), Program()
    timed = []

    def leaves(section, number):
        timed.append((section, program.now, SCATTER_SECTIONS[number][1]))

    leaves(pool_part, 0)
    program.want(zip((0.5, 1.5, 4.5, 7.0, 9.5, 12.0), [small_begin] + small_steps[1:]))
    program.gap(2.0)
    program.loop("down", 12, 0.75)
    leaves(down_part, 1)
    program.loop("up_input", 3, 1.4)
    program.loop("up_weight", 12, 0.46)
    program.gap(1.7)
    program.loop("out", 3, 1.1)
    leaves(up_part, 2)
    program.loop("attend", 6, 2.05)
    program.gap(1.0)
    program.loop("project_input", 3, 1.0)
    program.gap(2.2)
    program.loop("front", 5, 0.5)
    leaves(front_part, 3)
    program.loop("end", 4, 0.5)
    program.gap(1.0)
    leaves(end_part, 4)
    for entry in timed:
        program.want(links.steps(*entry))
    program.settle()
    plans = program.plans
    t.pool_back(None, pool_part.begin)
    t.down_back(plans["down"])
    down_part.begin()
    t.up_input(plans["up_input"])
    t.up_weight(plans["up_weight"])
    near = (p.z < 3).astype(jnp.int32) + (p.z > 0).astype(jnp.int32)
    for device in (p.sibling, p.a_near, p.b_near):
        pl.semaphore_signal(grant, inc=1, device_id=device, device_id_type=MESH)
    pl.when(p.z < 3)(
        lambda: pl.semaphore_signal(grant, inc=1, device_id=p.up, device_id_type=MESH)
    )
    pl.when(p.z > 0)(
        lambda: pl.semaphore_signal(grant, inc=1, device_id=p.down, device_id_type=MESH)
    )
    t.up_norm()
    t.out_back(plans["out"])
    pl.semaphore_wait(grant, 3 + near)
    up_part.begin()
    t.attend_back(plans["attend"])
    t.project_input(plans["project_input"])
    patch_copies = []
    for step in range(1, 4):
        to = lax.rem(p.blk + step, 4)
        patch_copies.append(
            remote(
                t.h.at[pl.ds(aligned(to * 144, 144), 144), :],
                patch_out.at[p.blk],
                patch_sems.at[0, step - 1],
                patch_sems.at[1, step - 1],
                {"blk": to},
            )
        )
        patch_copies[-1].start()
    own_patch = pltpu.make_async_copy(
        t.h.at[pl.ds(aligned(p.blk * 144, 144), 144), :], patch_out.at[p.blk], patch_sems.at[0, 3]
    )
    own_patch.start()
    t.project_weight(0, 5, plans["front"])
    front_part.begin()
    t.project_weight(5, 4, plans["end"])
    t.vectors_back()
    end_part.begin()
    for step in program.tail:
        step()
    for section in sections:
        section.finish()
    outs = [
        pltpu.make_async_copy(
            share.at[:, source : source + width],
            share_out.at[:, target : target + width],
            own_sems.at[1 + number],
        )
        for number, (source, target, width) in enumerate(
            (
                (0, 0, 3 * D),
                (COL_OUT, 3 * D, D + 2 * FF),
                (COL_MAP_KV, map_q_at + D, 2 * D),
            )
        )
    ]
    for out in outs:
        out.start()
    small_gather.finish()
    small_gather.sent()
    for step, copy in enumerate(patch_copies):
        source = lax.rem(p.blk + 3 - step, 4)
        landed = patch_out.at[source]
        remote(
            landed, landed, patch_sems.at[0, step], patch_sems.at[1, step], {"blk": source}
        ).wait_recv()
        copy.wait_send()
    own_patch.wait()
    spread = Spread(p, mine, everyone, send_sem, recv_sem)
    tail = small_tail(p, small, map_q[...], own_vectors[:, 6:7], share, spread, map_out, map_q_share)
    for number, (source, target) in enumerate(((map_q_share, map_q_at), (map_out, map_q_at + 3 * D))):
        outs.append(
            pltpu.make_async_copy(
                source, share_out.at[:, target : target + D], own_sems.at[4 + number]
            )
        )
        outs[-1].start()
    lane = lax.broadcasted_iota(jnp.int32, (24, 128), 1)
    vector_out[...] = jnp.where(lane == 6, tail, share[:, COL_VECTORS : COL_VECTORS + 128])
    sums, norm = spread.finish()
    facts[...] = jnp.concatenate([jnp.broadcast_to(sums[:, :128], (7, 128)), norm[:1]], axis=0)
    for out in outs:
        out.wait()


def layer_call(master, tokens, captions, vectors, labels, scalars):
    dma = pltpu.SemaphoreType.DMA
    f32 = jnp.float32
    gathers = len(GATHER_SECTIONS) + 2
    count = len(SCATTER_SECTIONS)
    widths = [entry[1] // 2 for entry in SCATTER_SECTIONS]

    def vm(*shape, dt=jnp.bfloat16):
        return pltpu.VMEM(shape, dt)

    vmem = pl.BlockSpec(memory_space=pltpu.VMEM)
    return pl.pallas_call(
        layer_kernel,
        out_shape=(
            jax.ShapeDtypeStruct((24, 8 * D + 2 * FF), f32),
            jax.ShapeDtypeStruct((24, 128), f32),
            jax.ShapeDtypeStruct((8, 128), f32),
            jax.ShapeDtypeStruct((4, 144, D), jnp.bfloat16),
        ),
        in_specs=[
            pl.BlockSpec(memory_space=pl.ANY),
            pl.BlockSpec(memory_space=pl.ANY),
            vmem,
            vmem,
            vmem,
            pl.BlockSpec(memory_space=pltpu.SMEM),
        ],
        out_specs=(
            pl.BlockSpec(memory_space=pl.ANY),
            vmem,
            vmem,
            pl.BlockSpec(memory_space=pl.ANY),
        ),
        scratch_shapes=[
            vm(D, GATHER_COLS),
            vm(TOKENS, D),
            vm(512, D),
            vm(TOKENS, D),
            vm(TOKENS, 3 * D),
            vm(TOKENS, D),
            vm(TOKENS, D, dt=f32),
            vm(TOKENS, D),
            vm(TOKENS, FF),
            vm(TOKENS, FF),
            vm(TOKENS, D, dt=f32),
            vm(TOKENS, D),
            vm(TOKENS, 2 * D),
            vm(16, TOKENS, dt=f32),
            vm(D, TOKENS),
            vm(TOKENS, D, dt=f32),
            vm(16, D, dt=f32),
            vm(8, D, dt=f32),
            vm(8, D, dt=f32),
            vm(48, GATHER_COLS // 2, dt=f32),
            vm(256, D, dt=f32),
            vm(D, widths[2]),
            vm(D, widths[1]),
            [vm(384, w) for w in widths[:3]],
            [vm(576, widths[0]), vm(288, widths[1])],
            [vm(48, widths[0]), vm(192, widths[1]), vm(48, widths[2])],
            [vm(48, w, dt=f32) for w in widths],
            vm(8, 128, dt=f32),
            vm(31, 8, 128, dt=f32),
            vm(24, SCATTER_COLS, dt=f32),
            vm(24, 256, dt=f32),
            vm(64, D),
            vm(24, D, dt=f32),
            vm(24, D, dt=f32),
            vm(24, D, dt=f32),
            vm(16, 512, dt=f32),
            dma((gathers, 4)),
            dma((2, 4)),
            dma((2, 4)),
            dma((6,)),
            dma,
            dma,
            pltpu.SemaphoreType.REGULAR,
            *gather_sems(gathers),
            dma((count, 2)),
            dma((count, 2, 2)),
            dma((count, 2, 2, 3)),
            dma((count, 2, 2, 3)),
            dma((count, 2)),
            dma((count, 2)),
        ],
        compiler_params=pltpu.CompilerParams(
            collective_id=0, has_side_effects=True, vmem_limit_bytes=63 * 2**20
        ),
        name="layer_step",
    )(master, tokens, captions, vectors, labels, scalars)


def local_kernel(
    patch_tokens,
    captions,
    pair_labels,
    master_weights,
    first_moments,
    second_moments,
    master_vectors,
    vector_first,
    vector_second,
    loss_scalars,
    scalar_first,
    scalar_second,
):
    weight_share, vector_share, facts, patch_grad = layer_call(
        master_weights, patch_tokens, captions, master_vectors, pair_labels, loss_scalars
    )
    vector_share = vector_share[:, :7]
    patch_grad = patch_grad.astype(jnp.float32)
    loss_total, scalar_total, grad_norm = facts[0, 0], facts[0, 1:3], facts[7, 0]
    factor = CLIP_AT / jnp.maximum(grad_norm, CLIP_AT)
    new_w, new_wm, new_wv = adamw(
        master_weights, weight_share * factor, first_moments, second_moments, 0.03, 0.1
    )
    new_v, new_vm, new_vv = adamw(
        master_vectors, vector_share * factor, vector_first, vector_second, 0.3, 0.0
    )
    new_s, new_sm, new_sv = adamw(
        loss_scalars, scalar_total * factor, scalar_first, scalar_second, 0.3, 0.0
    )
    return (
        loss_total,
        grad_norm,
        patch_grad,
        new_w,
        new_wm,
        new_wv,
        new_w.astype(jnp.bfloat16),
        new_v,
        new_vm,
        new_vv,
        new_v.astype(jnp.bfloat16),
        new_s,
        new_sm,
        new_sv,
    )


def solution(mesh):
    in_specs = (
        P("img", "blk", None),
        P("img", None),
        P("img", None),
        P(("blk", "img"), None),
        P(("blk", "img"), None),
        P(("blk", "img"), None),
        P(("blk", "img"), None),
        P(("blk", "img"), None),
        P(("blk", "img"), None),
        P(),
        P(),
        P(),
    )
    out_specs = (
        P(),
        P(),
        P("img", "blk", None),
        P(("blk", "img"), None),
        P(("blk", "img"), None),
        P(("blk", "img"), None),
        P(("blk", "img"), None),
        P(("blk", "img"), None),
        P(("blk", "img"), None),
        P(("blk", "img"), None),
        P(("blk", "img"), None),
        P(),
        P(),
        P(),
    )
    body = local_kernel if tuple(mesh.shape.values()) == (4, 8) else local
    return jax.shard_map(body, mesh=mesh, in_specs=in_specs, out_specs=out_specs, check_vma=False)
```

```python
import functools

import jax
import jax.numpy as jnp
from jax import lax
from jax.experimental import pallas as pl
from jax.experimental.pallas import tpu as pltpu
from jax.sharding import PartitionSpec as P

D = 768
HEADS = 12
HEAD_DIM = 64
FF = 3072
STEP = 10


BETA_ONE = 0.9
BETA_TWO = 0.999
EPS_ADAM = 1e-08
CLIP_AT = 1.0


def layer_norm(values, gain_vec, bias_vec):
    row_mean = jnp.mean(values, axis=-1, keepdims=True)
    centered = values - row_mean
    row_var = jnp.mean(centered * centered, axis=-1, keepdims=True)
    return centered * lax.rsqrt(row_var + 1e-06) * gain_vec + bias_vec


def unit_rows(pooled):
    return pooled * lax.rsqrt(jnp.sum(pooled * pooled, axis=-1, keepdims=True) + 1e-06)


def attend(queries, keys_all, values_all):
    scale = HEAD_DIM ** (-0.5)
    scores = (
        jnp.einsum("iqhe,ikhe->ihqk", queries, keys_all, preferred_element_type=jnp.float32) * scale
    )
    row_max = jnp.max(scores, axis=-1, keepdims=True)
    expos = jnp.exp(scores - row_max)
    row_sum = jnp.sum(expos, axis=-1, keepdims=True)
    attn_probs = (expos / row_sum).astype(jnp.bfloat16)
    mixed_out = jnp.einsum(
        "ihqk,ikhe->iqhe", attn_probs, values_all, preferred_element_type=jnp.float32
    )
    return (mixed_out.astype(jnp.bfloat16), row_max + jnp.log(row_sum))


def attend_back(queries, keys_all, values_all, log_norm, grad_mixed):
    scale = HEAD_DIM ** (-0.5)
    scores = (
        jnp.einsum("iqhe,ikhe->ihqk", queries, keys_all, preferred_element_type=jnp.float32) * scale
    )
    attn_probs = jnp.exp(scores - log_norm)
    grad_values = jnp.einsum(
        "ihqk,iqhe->ikhe",
        attn_probs.astype(jnp.bfloat16),
        grad_mixed,
        preferred_element_type=jnp.float32,
    )
    grad_probs = jnp.einsum(
        "iqhe,ikhe->ihqk", grad_mixed, values_all, preferred_element_type=jnp.float32
    )
    centre = jnp.sum(attn_probs * grad_probs, axis=-1, keepdims=True)
    grad_scores = (attn_probs * (grad_probs - centre)).astype(jnp.bfloat16)
    grad_queries = (
        jnp.einsum("ihqk,ikhe->iqhe", grad_scores, keys_all, preferred_element_type=jnp.float32)
        * scale
    )
    grad_keys = (
        jnp.einsum("ihqk,iqhe->ikhe", grad_scores, queries, preferred_element_type=jnp.float32)
        * scale
    )
    return (grad_queries, grad_keys, grad_values)


def adamw(parameter, gradient, moment_one, moment_two, step_rate, decay_rate):
    moment_one = BETA_ONE * moment_one + (1.0 - BETA_ONE) * gradient
    moment_two = BETA_TWO * moment_two + (1.0 - BETA_TWO) * gradient * gradient
    first_hat = moment_one / (1.0 - BETA_ONE**STEP)
    second_hat = moment_two / (1.0 - BETA_TWO**STEP)
    updated = parameter - step_rate * (
        first_hat / (jnp.sqrt(second_hat) + EPS_ADAM) + decay_rate * parameter
    )
    return (updated, moment_one, moment_two)


def local(
    patch_tokens,
    captions,
    pair_labels,
    master_weights,
    first_moments,
    second_moments,
    master_vectors,
    vector_first,
    vector_second,
    loss_scalars,
    scalar_first,
    scalar_second,
):
    blocks = lax.axis_size("blk")
    block = lax.axis_index("blk")
    all_images = patch_tokens.shape[0] * lax.axis_size("img")
    images = patch_tokens.shape[0] // blocks
    length = patch_tokens.shape[1] * blocks
    scale = HEAD_DIM ** (-0.5)
    both = ("blk", "img")
    rows = master_weights.shape[0]
    first_row = lax.axis_index(both) * rows
    patch_tokens = lax.all_to_all(patch_tokens, "blk", 0, 1, tiled=True)
    pair_labels = lax.dynamic_slice_in_dim(pair_labels, block * images, images, 0)
    rounded = master_weights.astype(jnp.bfloat16)
    full_vectors = lax.all_gather(master_vectors.astype(jnp.bfloat16), both, axis=0, tiled=True)
    vectors = full_vectors.astype(jnp.float32)

    def gather(start, stop):
        return lax.all_gather(rounded[:, start:stop], both, axis=0, tiled=True)

    w_front = gather(0, 4 * D)
    w_qkv = w_front[:, : 3 * D]
    w_out = w_front[:, 3 * D :]
    w_up = gather(4 * D, 4 * D + FF)
    w_down = gather(4 * D + FF, 4 * D + 2 * FF)
    own_map_q = rounded[:, 4 * D + 2 * FF : 5 * D + 2 * FF]
    w_map = gather(5 * D + 2 * FF, 8 * D + 2 * FF)
    w_map_kv = w_map[:, : 2 * D]
    w_map_out = w_map[:, 2 * D :]
    own_vectors = master_vectors.astype(jnp.bfloat16)
    tokens = patch_tokens.astype(jnp.float32)
    normed, norm_one_pull = jax.vjp(layer_norm, tokens, vectors[:, 0], vectors[:, 1])
    normed_b = normed.astype(jnp.bfloat16)
    qkv_b = jnp.einsum("ipd,dc->ipc", normed_b, w_qkv, preferred_element_type=jnp.float32).astype(
        jnp.bfloat16
    )
    queries = qkv_b[:, :, :D].reshape(images, length, HEADS, HEAD_DIM)
    keys_all = qkv_b[:, :, D : 2 * D].reshape(images, length, HEADS, HEAD_DIM)
    values_all = qkv_b[:, :, 2 * D :].reshape(images, length, HEADS, HEAD_DIM)
    mixed_heads, log_norm = attend(queries, keys_all, values_all)
    mixed_b = mixed_heads.reshape(images, length, D)
    residual = tokens + jnp.einsum(
        "ipd,dc->ipc", mixed_b, w_out, preferred_element_type=jnp.float32
    )
    hidden, norm_two_pull = jax.vjp(layer_norm, residual, vectors[:, 2], vectors[:, 3])
    hidden_b = hidden.astype(jnp.bfloat16)
    pre_act = jnp.einsum("ipd,df->ipf", hidden_b, w_up, preferred_element_type=jnp.float32)
    activation, gelu_pull = jax.vjp(jax.nn.gelu, pre_act)
    activation_b = activation.astype(jnp.bfloat16)
    layer_out = residual + jnp.einsum(
        "ipf,df->ipd", activation_b, w_down, preferred_element_type=jnp.float32
    )
    final_norm, norm_three_pull = jax.vjp(layer_norm, layer_out, vectors[:, 4], vectors[:, 5])
    final_b = final_norm.astype(jnp.bfloat16)
    map_kv = jnp.einsum("ipd,dc->ipc", final_b, w_map_kv, preferred_element_type=jnp.float32)
    map_kv = map_kv.astype(jnp.bfloat16).reshape(images, length, 2, HEADS, HEAD_DIM)
    probe_query = lax.psum(
        jnp.dot(own_vectors[:, 6], own_map_q, preferred_element_type=jnp.float32), both
    )
    probe_query = probe_query.astype(jnp.bfloat16).reshape(HEADS, HEAD_DIM)
    pool_scores = (
        jnp.einsum("he,iphe->ihp", probe_query, map_kv[:, :, 0], preferred_element_type=jnp.float32)
        * scale
    )
    row_max = jnp.max(pool_scores, axis=-1)
    row_sum = jnp.sum(jnp.exp(pool_scores - row_max[..., None]), axis=-1)
    pool_probs = jnp.exp(pool_scores - row_max[..., None]) / row_sum[..., None]
    map_values = map_kv[:, :, 1].astype(jnp.float32)
    pooled_part = jnp.einsum(
        "ihp,iphe->ihe", pool_probs, map_values, precision=lax.Precision.HIGHEST
    )
    pooled_heads = pooled_part.reshape(images, D)
    pooled_heads_b = pooled_heads.astype(jnp.bfloat16)
    pooled = jnp.dot(pooled_heads_b, w_map_out, preferred_element_type=jnp.float32)
    caption_all = lax.all_gather(captions, "img", axis=0, tiled=True).astype(jnp.float32)
    caption_unit = unit_rows(caption_all).astype(jnp.bfloat16)
    unit_image, unit_pull = jax.vjp(unit_rows, pooled)
    cosine = jnp.einsum(
        "id,cd->ic",
        unit_image.astype(jnp.bfloat16),
        caption_unit,
        preferred_element_type=jnp.float32,
    )
    signs = 2.0 * pair_labels.astype(jnp.float32) - 1.0

    def pair_loss(cosine_in, scalars_in):
        logits = jnp.exp(scalars_in[0]) * cosine_in + scalars_in[1]
        return jnp.sum(jax.nn.softplus(-signs * logits)) / all_images

    loss_local, loss_pull = jax.vjp(pair_loss, cosine, loss_scalars)
    grad_cosine, grad_scalars = loss_pull(jnp.ones((), jnp.float32))
    loss_total, scalar_total = lax.psum((loss_local, grad_scalars), both)
    grad_unit = jnp.einsum(
        "ic,cd->id",
        grad_cosine.astype(jnp.bfloat16),
        caption_unit,
        preferred_element_type=jnp.float32,
    )
    (grad_pooled,) = unit_pull(grad_unit)
    grad_pooled_b = grad_pooled.astype(jnp.bfloat16)
    pooled_all, grad_pooled_all = (
        lax.all_gather(pooled_heads_b, both, axis=0, tiled=True),
        lax.all_gather(grad_pooled_b, both, axis=0, tiled=True),
    )
    share_map_out = jnp.einsum(
        "id,ic->dc",
        lax.dynamic_slice_in_dim(pooled_all, first_row, rows, 1),
        grad_pooled_all,
        preferred_element_type=jnp.float32,
    )
    grad_heads_b = jnp.einsum(
        "ic,dc->id", grad_pooled_b, w_map_out, preferred_element_type=jnp.float32
    )
    grad_heads_b = grad_heads_b.astype(jnp.bfloat16).reshape(images, HEADS, HEAD_DIM)
    grad_heads = grad_heads_b.astype(jnp.float32)
    centre = jnp.sum(grad_heads * pooled_heads.reshape(images, HEADS, HEAD_DIM), axis=-1)
    grad_probs = jnp.einsum(
        "ihe,iphe->ihp", grad_heads_b, map_kv[:, :, 1], preferred_element_type=jnp.float32
    )
    grad_pool_scores = (pool_probs * (grad_probs - centre[..., None])).astype(jnp.bfloat16)
    grad_map_keys = (
        jnp.einsum(
            "ihp,he->iphe", grad_pool_scores, probe_query, preferred_element_type=jnp.float32
        )
        * scale
    )
    grad_map_values = jnp.einsum(
        "ihp,ihe->iphe", pool_probs, grad_heads, precision=lax.Precision.HIGHEST
    )
    grad_probe_query = (
        jnp.einsum(
            "ihp,iphe->he", grad_pool_scores, map_kv[:, :, 0], preferred_element_type=jnp.float32
        ).reshape(D)
        * scale
    )
    grad_map_kv = (
        jnp.stack([grad_map_keys, grad_map_values], axis=2)
        .astype(jnp.bfloat16)
        .reshape(images, length, 2 * D)
    )
    grad_w_map_kv = jnp.einsum(
        "ipd,ipc->dc", final_b, grad_map_kv, preferred_element_type=jnp.float32
    )
    grad_final = jnp.einsum(
        "ipc,dc->ipd", grad_map_kv, w_map_kv, preferred_element_type=jnp.float32
    )
    grad_layer_out, grad_gain_three, grad_bias_three = norm_three_pull(grad_final)
    probe_total = lax.psum(grad_probe_query, both)
    share_map_q = jnp.outer(own_vectors[:, 6].astype(jnp.float32), probe_total)
    share_probe = jnp.dot(
        own_map_q.astype(jnp.float32), probe_total, precision=lax.Precision.HIGHEST
    )
    grad_branch_two = grad_layer_out.astype(jnp.bfloat16)
    grad_w_down = jnp.einsum(
        "ipd,ipf->df", grad_branch_two, activation_b, preferred_element_type=jnp.float32
    )
    grad_activation = jnp.einsum(
        "ipd,df->ipf", grad_branch_two, w_down, preferred_element_type=jnp.float32
    )
    (grad_pre,) = gelu_pull(grad_activation)
    grad_pre_b = grad_pre.astype(jnp.bfloat16)
    grad_w_up = jnp.einsum("ipd,ipf->df", hidden_b, grad_pre_b, preferred_element_type=jnp.float32)
    grad_hidden = jnp.einsum("ipf,df->ipd", grad_pre_b, w_up, preferred_element_type=jnp.float32)
    grad_res_part, grad_gain_two, grad_bias_two = norm_two_pull(grad_hidden)
    grad_residual = grad_layer_out + grad_res_part
    grad_branch_one = grad_residual.astype(jnp.bfloat16)
    grad_w_out = jnp.einsum(
        "ipd,ipc->dc", mixed_b, grad_branch_one, preferred_element_type=jnp.float32
    )
    grad_mixed = jnp.einsum(
        "ipc,dc->ipd", grad_branch_one, w_out, preferred_element_type=jnp.float32
    )
    grad_mixed = grad_mixed.astype(jnp.bfloat16)
    grad_queries, grad_keys, grad_values = attend_back(
        queries, keys_all, values_all, log_norm, grad_mixed.reshape(images, length, HEADS, HEAD_DIM)
    )
    grad_qkv = jnp.concatenate(
        [
            grad_queries.reshape(images, length, D),
            grad_keys.reshape(images, length, D),
            grad_values.reshape(images, length, D),
        ],
        axis=-1,
    ).astype(jnp.bfloat16)
    grad_w_qkv = jnp.einsum("ipd,ipc->dc", normed_b, grad_qkv, preferred_element_type=jnp.float32)
    grad_normed = jnp.einsum("ipc,dc->ipd", grad_qkv, w_qkv, preferred_element_type=jnp.float32)
    grad_tok_part, grad_gain_one, grad_bias_one = norm_one_pull(grad_normed)
    patch_grad = lax.all_to_all(
        (grad_residual + grad_tok_part).astype(jnp.bfloat16), "blk", 1, 0, tiled=True
    ).astype(jnp.float32)
    grad_vectors = jnp.stack(
        [
            grad_gain_one,
            grad_bias_one,
            grad_gain_two,
            grad_bias_two,
            grad_gain_three,
            grad_bias_three,
        ],
        axis=1,
    )

    def scatter(part):
        return lax.psum_scatter(
            part.astype(jnp.bfloat16), both, scatter_dimension=0, tiled=True
        ).astype(jnp.float32)

    share_map_kv = scatter(grad_w_map_kv)
    share_down = scatter(grad_w_down)
    share_up = scatter(grad_w_up)
    share_front = scatter(jnp.concatenate([grad_w_qkv, grad_w_out], axis=1))
    weight_share = jnp.concatenate(
        [share_front, share_up, share_down, share_map_q, share_map_kv, share_map_out], axis=1
    )
    vector_share = jnp.concatenate(
        [
            lax.psum_scatter(grad_vectors, both, scatter_dimension=0, tiled=True),
            share_probe[:, None],
        ],
        axis=1,
    )
    squares = jnp.sum(weight_share * weight_share) + jnp.sum(vector_share * vector_share)
    square_total = lax.psum(squares, ("blk", "img"))
    grad_norm = jnp.sqrt(square_total + jnp.sum(scalar_total * scalar_total))
    factor = CLIP_AT / jnp.maximum(grad_norm, CLIP_AT)
    new_w, new_wm, new_wv = adamw(
        master_weights, weight_share * factor, first_moments, second_moments, 0.03, 0.1
    )
    new_v, new_vm, new_vv = adamw(
        master_vectors, vector_share * factor, vector_first, vector_second, 0.3, 0.0
    )
    new_s, new_sm, new_sv = adamw(
        loss_scalars, scalar_total * factor, scalar_first, scalar_second, 0.3, 0.0
    )
    return (
        loss_total,
        grad_norm,
        patch_grad,
        new_w,
        new_wm,
        new_wv,
        new_w.astype(jnp.bfloat16),
        new_v,
        new_vm,
        new_vv,
        new_v.astype(jnp.bfloat16),
        new_s,
        new_sm,
        new_sv,
    )


LINK_SPEED = (1.1, 3.0)


def gather_key(number, at):
    return 0 if at == 0 else at + number


MESH = pl.DeviceIdType.MESH
CHIP_ROWS = 48
GATHER_SECTIONS = ((0, 2560), (2560, 3840), (6400, 3072), (9472, 2304))
SCATTER_SECTIONS = (
    (9472, 1536),
    (6400, 1536),
    (7936, 1536),
    (3328, 1536),
    (4864, 1536),
    (2560, 768),
    (0, 1280),
    (1280, 1280),
)
PAIR_PLACES = ((0, 0), (0, 768), (1, 0), (1, 768), (0, 0), (0, 1536), (0, 768), (1, 0))
LATE_PLACES = (0, 768, 1152, 1792)
GATHER_COLS = 11776
SCATTER_COLS = 11008


def aligned(value, step):
    return pl.multiple_of(value, step)


class Place:
    def __init__(self):
        self.blk = lax.axis_index("blk")
        self.img = lax.axis_index("img")
        self.x = lax.rem(self.blk, 2)
        self.y = self.blk // 2
        self.z = self.img // 2
        self.c = lax.rem(self.img, 2)
        self.chip = self.blk * 4 + self.z
        self.sibling = {"img": self.z * 2 + 1 - self.c}
        self.up = {"img": self.img + 2}
        self.down = {"img": self.img - 2}
        self.a_near = {"blk": self.block(1, 0)}
        self.b_near = {"blk": self.block(0, 1)}

    def on_level(self, level):
        return {"img": level * 2 + self.c}

    def block(self, da, db):
        flip_x = da * (1 - self.c) + db * self.c
        flip_y = db * (1 - self.c) + da * self.c
        other_x = self.x + flip_x * (1 - 2 * self.x)
        other_y = self.y + flip_y * (1 - 2 * self.y)
        return other_y * 2 + other_x


def remote(src, dst, send_sem, recv_sem, device):
    return pltpu.make_async_remote_copy(
        src_ref=src,
        dst_ref=dst,
        send_sem=send_sem,
        recv_sem=recv_sem,
        device_id=device,
        device_id_type=MESH,
    )


def greet_all(place):
    barrier = pltpu.get_barrier_semaphore()
    me = place.blk * 8 + place.img

    def greet(step, carry):
        other = lax.rem(me + step, 32)
        pl.semaphore_signal(
            barrier,
            inc=1,
            device_id={"blk": other // 8, "img": lax.rem(other, 8)},
            device_id_type=MESH,
        )
        return carry

    lax.fori_loop(1, 32, greet, 0)
    pl.semaphore_wait(barrier, 31)


class Gather:
    def __init__(self, place, buf, rows, first, width, sems):
        self.p, self.buf, self.rows, self.half = place, buf, rows, width // 2
        self.mine = aligned(first + place.c * self.half, 128)
        self.theirs = aligned(first + (1 - place.c) * self.half, 128)
        self.near_recv, self.z_recv, self.b_recv, self.near_send, self.z_send, self.b_send, self.pair = sems

    def item(self, da, db, level):
        start = aligned((self.p.block(da, db) * 4 + level) * self.rows, self.rows)
        return self.buf.at[pl.ds(start, self.rows), pl.ds(self.mine, self.half)]

    def a_copy(self):
        own = self.item(0, 0, self.p.z)
        return remote(own, own, self.near_send, self.near_recv, self.p.a_near)

    def z_copy(self, da, level, up):
        part = self.item(da, 0, level)
        device = self.p.up if up else self.p.down
        return remote(part, part, self.z_send.at[up, da, level], self.z_recv.at[da, level], device)

    def b_copy(self, da, level):
        part = self.item(da, 0, level)
        return remote(part, part, self.b_send.at[da, level], self.b_recv.at[da, level], self.p.b_near)

    def pair_copy(self, da, db, level):
        part = self.item(da, db, level)
        return remote(part, part, self.pair.at[0], self.pair.at[1], self.p.sibling)

    def onward(self, da, level, up, down):
        self.b_copy(da, level).start()
        if up:
            pl.when(self.p.z < 3)(lambda: self.z_copy(da, level, 1).start())
        if down:
            pl.when(self.p.z > 0)(lambda: self.z_copy(da, level, 0).start())
        self.pair_copy(da, 0, level).start()

    def begin(self):
        self.a_copy().start()
        self.onward(0, self.p.z, True, True)

    def near(self):
        part = self.item(1, 0, self.p.z)
        remote(part, part, self.near_send, self.near_recv, self.p.a_near).wait_recv()
        self.onward(1, self.p.z, True, True)

    def level(self, distance):
        z = self.p.z

        @pl.when(z >= distance)
        def from_below():
            for da in range(2):
                self.z_copy(da, z - distance, 1).wait_recv()
                self.onward(da, z - distance, True, False)

        @pl.when(z + distance <= 3)
        def from_above():
            for da in range(2):
                self.z_copy(da, z + distance, 0).wait_recv()
                self.onward(da, z + distance, False, True)

    def far(self):
        for level in range(4):
            for da in range(2):
                part = self.item(da, 1, level)
                remote(
                    part, part, self.b_send.at[da, level], self.b_recv.at[da, level], self.p.b_near
                ).wait_recv()
                self.pair_copy(da, 1, level).start()

    def finish(self):
        whole = self.buf.at[pl.ds(0, 16 * self.rows), pl.ds(self.theirs, self.half)]
        both = remote(whole, whole, self.pair.at[0], self.pair.at[1], self.p.sibling)
        both.wait_recv()

    def sent(self):
        z = self.p.z
        self.a_copy().wait_send()
        whole = self.buf.at[pl.ds(0, 16 * self.rows), pl.ds(self.mine, self.half)]
        remote(whole, whole, self.pair.at[0], self.pair.at[1], self.p.sibling).wait_send()
        for level in range(4):
            for da in range(2):
                self.b_copy(da, level).wait_send()
                if level < 3:
                    pl.when((z >= level) & (z < 3))(
                        lambda da=da, level=level: self.z_copy(da, level, 1).wait_send()
                    )
                if level > 0:
                    pl.when((z <= level) & (z > 0))(
                        lambda da=da, level=level: self.z_copy(da, level, 0).wait_send()
                    )

    def steps(self):
        return [
            self.begin,
            self.near,
            lambda: self.level(1),
            lambda: self.level(2),
            lambda: self.level(3),
            self.far,
        ]


def gather_sems(count):
    dma = pltpu.SemaphoreType.DMA
    return [
        dma((count,)),
        dma((count, 2, 4)),
        dma((count, 2, 4)),
        dma((count,)),
        dma((count, 2, 2, 4)),
        dma((count, 2, 4)),
        dma((count, 2)),
    ]


class Scatter:
    def __init__(self, place, buf, share, first, width, bufs, sems):
        self.p, self.buf, self.share, self.half = place, buf, share, width // 2
        self.mine = aligned(first + place.c * self.half, 128)
        self.theirs = aligned(first + (1 - place.c) * self.half, 128)
        self.pair_in, self.b_in, self.a_in, self.z_in, self.last = bufs
        self.pair, self.b_sem, self.a_sem, self.z_sem, self.end = sems

    def run_rows(self, da, db):
        return aligned(self.p.block(da, db) * 192, 192)

    def run(self, da, db):
        return self.buf.at[pl.ds(self.run_rows(da, db), 192), pl.ds(self.mine, self.half)]

    def level_rows(self, da, level):
        return aligned((self.p.block(da, 0) * 4 + level) * 48, 48)

    def part(self, da, level):
        return self.buf.at[pl.ds(self.level_rows(da, level), 48), pl.ds(self.mine, self.half)]

    def add(self, row, source, count, offset=0):
        def one(step, carry):
            here = aligned(row + step * 48, 48)
            there = aligned(offset + step * 48, 48)
            self.buf[pl.ds(here, 48), pl.ds(self.mine, self.half)] += source[pl.ds(there, 48), :]
            return carry

        if count == 1:
            one(0, 0)
        else:
            lax.fori_loop(0, count, one, 0)

    def pair_copy(self):
        return remote(
            self.buf.at[pl.ds(0, 768), pl.ds(self.theirs, self.half)],
            self.pair_in,
            self.pair.at[0],
            self.pair.at[1],
            self.p.sibling,
        )

    def b_copy(self, da):
        return remote(
            self.run(da, 1),
            self.b_in.at[da * 192 : da * 192 + 192, :],
            self.b_sem.at[0, da],
            self.b_sem.at[1, da],
            self.p.b_near,
        )

    def a_copy(self):
        return remote(self.run(1, 0), self.a_in, self.a_sem.at[0], self.a_sem.at[1], self.p.a_near)

    def z_copy(self, step):
        level = lax.rem(self.p.z + step, 4)
        return remote(
            self.part(0, level),
            self.z_in.at[(3 - step) * 48 : (4 - step) * 48, :],
            self.z_sem.at[0, 3 - step],
            self.z_sem.at[1, 3 - step],
            self.p.on_level(level),
        )

    def end_copy(self):
        return remote(
            self.last.at[pl.ds(aligned((1 - self.p.c) * 24, 8), 24), :],
            self.share.at[:, pl.ds(self.mine, self.half)],
            self.end.at[0],
            self.end.at[1],
            self.p.sibling,
        )

    def begin(self):
        self.pair_copy().start()

    def pairs_far(self):
        self.pair_copy().wait_recv()
        for da in range(2):
            row = self.run_rows(da, 1)
            self.add(row, self.pair_in, 4, row)
            self.b_copy(da).start()

    def pairs_near(self):
        for da in range(2):
            row = self.run_rows(da, 0)
            self.add(row, self.pair_in, 4, row)

    def blocks(self):
        for da in (1, 0):
            self.b_copy(da).wait_recv()
            self.add(self.run_rows(da, 0), self.b_in, 4, da * 192)
            if da == 1:
                self.a_copy().start()

    def joined(self):
        self.a_copy().wait_recv()
        self.add(self.run_rows(0, 0), self.a_in, 4)
        for step in (2, 1, 3):
            self.z_copy(step).start()

    def close(self):
        total = self.buf[pl.ds(self.level_rows(0, self.p.z), 48), pl.ds(self.mine, self.half)]
        total = total.astype(jnp.float32)
        for step in (1, 3, 2):
            self.z_copy(step).wait_recv()
            total += self.z_in[(3 - step) * 48 : (4 - step) * 48, :].astype(jnp.float32)
        self.last[...] = total
        self.end_copy().start()
        self.share[:, pl.ds(self.mine, self.half)] = self.last[
            pl.ds(aligned(self.p.c * 24, 8), 24), :
        ]

    def finish(self):
        theirs = self.share.at[:, pl.ds(self.theirs, self.half)]
        remote(theirs, theirs, self.end.at[0], self.end.at[1], self.p.sibling).wait_recv()
        self.end_copy().wait_send()
        self.a_copy().wait_send()
        self.pair_copy().wait_send()
        for da in range(2):
            self.b_copy(da).wait_send()
        for step in range(1, 4):
            self.z_copy(step).wait_send()


class Links:
    def __init__(self, slow=1.0, hop=2.0):
        self.flat = self.high = 0.0
        self.slow, self.hop = slow, hop

    def use(self, name, start, time):
        start = max(start, getattr(self, name))
        setattr(self, name, start + time * self.slow)
        return start + time * self.slow + self.hop

    def steps(self, section, start, width):
        size = width / 256
        out = []
        now = start + 0.35 * size * self.slow + 1.0
        out += [(now, section.pairs_far), (now + 0.5, section.pairs_near)]
        now = self.use("flat", now + 0.5, 1.01 * size)
        out.append((now, section.blocks))
        now = self.use("flat", now, 0.5 * size)
        out.append((now, section.joined))
        now = self.use("high", now, 1.01 * size)
        out.append((now, section.close))
        return out


class Program:
    def __init__(self):
        self.now, self.places, self.wanted = 0.0, [], []
        self.plans = {}
        self.tail = []

    def loop(self, name, count, each):
        self.plans[name] = {}
        for index in range(count):
            self.now += each
            self.places.append((self.now, name, index))

    def gap(self, time):
        self.now += time

    def want(self, steps):
        self.wanted += [(time, len(self.wanted) + n, step) for n, (time, step) in enumerate(steps)]

    def settle(self):
        for time, _, step in sorted(self.wanted, key=lambda entry: entry[:2]):
            for place, name, index in self.places:
                if place >= time:
                    self.plans[name].setdefault(index, []).append(step)
                    break
            else:
                self.tail.append(step)


class Swap:
    def __init__(self, place, pieces, buf, first_buf_row, rows, first, width, offset, sems):
        self.p, self.rows, self.half = place, rows, width // 2
        self.buf, self.sems = buf, sems
        self.row = aligned(first_buf_row + place.c * rows, rows)
        self.other_row = aligned(first_buf_row + (1 - place.c) * rows, rows)
        self.halves = []
        for core in range(2):
            low, here = first + core * self.half, []
            for array, source, target, size in pieces:
                start, stop = max(low, target), min(low + self.half, target + size)
                if start < stop:
                    at = start - low + offset if offset is not None else start
                    here.append((array, source + start - target, at, stop - start))
            self.halves.append(here)
        self.at = (
            pl.ds(aligned(first + place.c * self.half, 128), self.half)
            if offset is None
            else pl.ds(offset, self.half)
        )
        self.away_at = (
            pl.ds(aligned(first + (1 - place.c) * self.half, 128), self.half)
            if offset is None
            else pl.ds(offset, self.half)
        )

    def begin(self, late=None):
        for core in range(2):
            for array, source, at, size in self.halves[core]:
                if late is not None and (array is late[0]) != late[1]:
                    continue
                part = array.at[:, source : source + size]
                goal = self.buf.at[pl.ds(self.row, self.rows), at : at + size]

                @pl.when(self.p.c == core)
                def here(part=part, goal=goal):
                    pltpu.make_async_copy(part, goal, self.sems.at[2]).start()

                @pl.when(self.p.c != core)
                def away(part=part, goal=goal):
                    remote(part, goal, self.sems.at[0], self.sems.at[1], self.p.sibling).start()

    def finish(self):
        landed = self.buf.at[pl.ds(self.other_row, self.rows), self.at]
        own = self.buf.at[pl.ds(self.row, self.rows), self.at]
        gone = self.buf.at[pl.ds(self.row, self.rows), self.away_at]
        remote(landed, landed, self.sems.at[0], self.sems.at[1], self.p.sibling).wait_recv()
        pltpu.make_async_copy(own, own, self.sems.at[2]).wait()
        remote(gone, gone, self.sems.at[0], self.sems.at[1], self.p.sibling).wait_send()


class Spread:
    def __init__(self, place, mine, everyone, send_sem, recv_sem):
        self.p, self.mine, self.everyone = place, mine, everyone
        self.send_sem, self.recv_sem = send_sem, recv_sem
        self.me = place.blk * 8 + place.img

    def copy(self, step):
        other = lax.rem(self.me + step, 32)
        return remote(
            self.mine,
            self.everyone.at[step - 1],
            self.send_sem,
            self.recv_sem,
            {"blk": other // 8, "img": lax.rem(other, 8)},
        )

    def begin(self, tile):
        self.mine[...] = tile

        def start(step, carry):
            self.copy(step).start()
            return carry

        lax.fori_loop(1, 32, start, 0)

    def finish(self):
        lane = lax.broadcasted_iota(jnp.int32, (1, 768), 1)
        scalars = self.sums
        square = jnp.sum(jnp.where((lane == 1) | (lane == 2), scalars * scalars, 0.0))
        return scalars, jnp.sqrt(self.total() + square)

    def total(self):
        remote(
            self.everyone, self.everyone, self.send_sem, self.recv_sem, self.p.sibling
        ).wait()
        return self.mine[...] + jnp.sum(self.everyone[...], axis=0)


def small_tail(p, small, map_q, probe, share, spread, map_out_ref, map_q_ref):
    everything = small[...]
    as_rows = everything.astype(jnp.bfloat16)
    sums = jnp.sum(everything.reshape(32, 8, 768), axis=0)
    query, scalars = sums[2:3], sums[3:4]
    device = lax.broadcasted_iota(jnp.int32, (32, 256), 0) * 8
    row = lax.broadcasted_iota(jnp.int32, (32, 256), 1)

    def rows_of(kind):
        pick = (row == device + kind).astype(jnp.float32).astype(jnp.bfloat16)
        return jnp.dot(pick, as_rows, preferred_element_type=jnp.float32).astype(jnp.bfloat16)

    pooled, grads = rows_of(0), rows_of(1)
    first = (p.blk * 8 + p.img) * 24
    picks = (
        lax.broadcasted_iota(jnp.int32, (24, 768), 1)
        == lax.broadcasted_iota(jnp.int32, (24, 768), 0) + first
    ).astype(jnp.float32).astype(jnp.bfloat16)
    rows = lax.dot_general(
        picks, pooled, (((1,), (1,)), ((), ())), preferred_element_type=jnp.float32
    ).astype(jnp.bfloat16)
    map_out = jnp.dot(rows, grads, preferred_element_type=jnp.float32)
    map_q_share = probe * query
    probe_share = jnp.sum(map_q * query, axis=1, keepdims=True)
    square = (
        jnp.sum(map_out * map_out)
        + jnp.sum(map_q_share * map_q_share)
        + jnp.sum(probe_share * probe_share)
    )

    def one(step, total):
        part = share[:, pl.ds(aligned(step * 256, 256), 256)]
        return total + jnp.sum(part * part)

    square = lax.fori_loop(0, SCATTER_COLS // 256, one, square)
    spread.begin(jnp.full((8, 128), square, jnp.float32))
    spread.sums = scalars
    map_out_ref[...], map_q_ref[...] = map_out, map_q_share
    return probe_share


COL_VECTORS = 2304
COL_QUERY = 2432
COL_OUT = 2560
COL_UP = 3328
COL_DOWN = 6400
COL_MAP_KV = 9472
COL_MAP_OUT = 11008
TOKENS = 576
CHUNK = 96
TILE = 256
SCALE = 0.125
GELU_A = 0.7978845608028654
GELU_B = 0.044715
NT = (((1,), (1,)), ((), ()))
TN = (((0,), (0,)), ((), ()))


def dot(lhs, rhs, dims=(((1,), (0,)), ((), ()))):
    return lax.dot_general(lhs, rhs, dims, preferred_element_type=jnp.float32)


def loop(count, body, plan=None):
    def one(index, carry):
        body(index)
        for at, steps in (plan or {}).items():

            @pl.when(index == at)
            def run(steps=steps):
                for step in steps:
                    step()

        return carry

    lax.fori_loop(0, count, one, 0)


def columns(index, first=0, width=TILE):
    return pl.ds(aligned(first + index * width, 128), width)


def chunk_rows(index):
    return pl.ds(aligned(index * CHUNK, 32), CHUNK)


def normalize(values):
    row_mean = jnp.mean(values, axis=-1, keepdims=True)
    centered = values - row_mean
    row_var = jnp.mean(centered * centered, axis=-1, keepdims=True)
    rate = lax.rsqrt(row_var + 1e-06)
    return centered * rate, rate


def normalize_back(scaled, rate, grad, gain):
    inner = grad * gain
    first = jnp.mean(inner, axis=-1, keepdims=True)
    second = jnp.mean(inner * scaled, axis=-1, keepdims=True)
    return (
        rate * (inner - first - scaled * second),
        jnp.sum(grad * scaled, axis=0, keepdims=True),
        jnp.sum(grad, axis=0, keepdims=True),
    )


class Tower:
    def __init__(self, **refs):
        self.__dict__.update(refs)

    def unpack(self):
        turned = jnp.transpose(self.w[:, COL_VECTORS : COL_VECTORS + 128].astype(jnp.float32))
        self.vec[0:8, :] = turned[0:8]
        packed = self.w[:, COL_QUERY : COL_QUERY + 128].astype(jnp.float32)
        total = jnp.sum(packed.reshape(32, 24, 128), axis=0)
        query = total[0:6] + total[6:12]
        row = jnp.concatenate([query[i : i + 1] for i in range(6)], axis=1)
        self.vec[8:16, :] = jnp.broadcast_to(row, (8, 768)).astype(jnp.bfloat16).astype(jnp.float32)

    def norm(self, source, gain, bias, out):
        def body(index):
            rows = chunk_rows(index)
            scaled, _ = normalize(source[rows, :].astype(jnp.float32))
            out[rows, :] = (scaled * gain + bias).astype(jnp.bfloat16)

        loop(TOKENS // CHUNK, body)

    def first_norm(self):
        self.norm(self.x, self.vec[0:1, :], self.vec[1:2, :], self.h)

    def project(self, plan=None):
        def body(index):
            self.qkv[:, columns(index)] = dot(self.h[...], self.w[:, columns(index)]).astype(jnp.bfloat16)

        loop(9, body, plan)

    def pair_of(self, pair, which):
        return self.qkv[:, columns(pair, which * D, 128)]

    def attend(self, plan=None):
        lanes = lax.broadcasted_iota(jnp.int32, (TOKENS, 128), 1)

        def body(pair):
            queries = self.pair_of(pair, 0) * jnp.bfloat16(SCALE)
            keys = self.pair_of(pair, 1)
            values_turned = jnp.transpose(self.pair_of(pair, 2))
            mixed = []
            for head in range(2):
                mine = (lanes < 64) if head == 0 else (lanes >= 64)
                masked = jnp.where(mine, queries, jnp.bfloat16(0))
                scores = dot(keys, masked, NT)
                most = jnp.max(scores, axis=0, keepdims=True)
                expos = jnp.exp(scores - most)
                total = jnp.sum(expos, axis=0, keepdims=True)
                part = dot(values_turned[head * 64 : head * 64 + 64], expos.astype(jnp.bfloat16))
                mixed.append(part * (1.0 / total))
                self.lse[pl.ds(pair * 2 + head, 1), :] = most + jnp.log(total)
            self.a[:, columns(pair, 0, 128)] = jnp.transpose(
                jnp.concatenate(mixed, axis=0)
            ).astype(jnp.bfloat16)

        loop(6, body, plan)

    def attend_out(self, plan=None):
        def body(index):
            self.r[:, columns(index)] = self.x[:, columns(index)].astype(jnp.float32) + dot(
                self.a[...], self.w[:, columns(index, COL_OUT)]
            )

        loop(3, body, plan)
        self.norm(self.r, self.vec[2:3, :], self.vec[3:4, :], self.h2)

    def feed_up(self, plan=None):
        def body(index):
            value = dot(self.h2[...], self.w[:, columns(index, COL_UP)])
            square = value * value
            bend = jnp.tanh(GELU_A * value * (1.0 + GELU_B * square))
            half = 0.5 + 0.5 * bend
            self.g[:, columns(index)] = (value * half).astype(jnp.bfloat16)
            slope = half + 0.5 * value * (1.0 - bend * bend) * (
                GELU_A + 3.0 * GELU_A * GELU_B * square
            )
            self.gp[:, columns(index)] = slope.astype(jnp.bfloat16)

        loop(12, body, plan)

    def feed_down(self, plan=None):
        def body(index):
            self.y[:, columns(index)] = self.r[:, columns(index)] + dot(
                self.g[...], self.w[columns(index), COL_DOWN : COL_DOWN + FF], NT
            )

        loop(3, body, plan)
        self.norm(self.y, self.vec[4:5, :], self.vec[5:6, :], self.f)

    def pool_project(self, plan=None):
        def body(index):
            self.kvp[:, columns(index)] = dot(
                self.f[...], self.w[:, columns(index, COL_MAP_KV)]
            ).astype(jnp.bfloat16)

        loop(6, body, plan)

    def pool(self, signs, temperature, offset, images):
        head = lax.broadcasted_iota(jnp.int32, (16, D), 0)
        owner = lax.broadcasted_iota(jnp.int32, (16, D), 1) // HEAD_DIM
        own = head == owner
        heads_query = jnp.where(own, self.vec[8:9, :], 0.0).astype(jnp.bfloat16)
        keys, values = self.kvp[:, :D], self.kvp[:, D:]
        scores = dot(heads_query, keys, NT) * SCALE
        expos = jnp.exp(scores - jnp.max(scores, axis=1, keepdims=True))
        probs = expos / jnp.sum(expos, axis=1, keepdims=True)
        probs_high = probs.astype(jnp.bfloat16)
        probs_low = (probs - probs_high.astype(jnp.float32)).astype(jnp.bfloat16)
        spread = dot(probs_high, values) + dot(probs_low, values)
        pooled = jnp.sum(jnp.where(own, spread, 0.0), axis=0, keepdims=True)
        pooled_b = pooled.astype(jnp.bfloat16)
        w_out = self.w[:, COL_MAP_OUT : COL_MAP_OUT + D]
        many = jnp.broadcast_to(pooled, (16, D)).astype(jnp.bfloat16)
        embed = dot(many, w_out)[0:1]
        rate = lax.rsqrt(jnp.sum(embed * embed, axis=1, keepdims=True) + 1e-06)
        unit = jnp.broadcast_to(embed * rate, (16, D)).astype(jnp.bfloat16)
        cosine = dot(unit, self.cap[...], NT)[0:1]
        heat = jnp.exp(temperature)
        logits = heat * cosine + offset
        turned = -signs * logits
        losses = jnp.maximum(turned, 0.0) + jnp.log1p(jnp.exp(-jnp.abs(turned)))
        loss = jnp.sum(jnp.where(signs == 0.0, 0.0, losses), axis=1, keepdims=True) / images
        grad_logits = -signs * (1.0 / (1.0 + jnp.exp(-turned))) / images
        grad_heat = jnp.sum(grad_logits * cosine * heat, axis=1, keepdims=True)
        grad_offset = jnp.sum(grad_logits, axis=1, keepdims=True)
        grad_cosine = jnp.broadcast_to(grad_logits * heat, (16, cosine.shape[1])).astype(jnp.bfloat16)
        grad_unit = dot(grad_cosine, self.cap[...])[0:1]
        grad_embed = rate * grad_unit - embed * (
            rate * rate * rate * jnp.sum(grad_unit * embed, axis=1, keepdims=True)
        )
        grad_many = jnp.broadcast_to(grad_embed, (16, D)).astype(jnp.bfloat16)
        grad_pooled = dot(grad_many, w_out, NT).astype(jnp.bfloat16).astype(jnp.float32)
        heads_grad = jnp.where(own, grad_pooled, 0.0).astype(jnp.bfloat16)
        grad_probs = dot(heads_grad, values, NT)
        centre = jnp.sum(probs * grad_probs, axis=1, keepdims=True)
        grad_scores = (probs * (grad_probs - centre)).astype(jnp.bfloat16)
        query_spread = dot(grad_scores, keys) * SCALE
        grad_query = jnp.sum(jnp.where(own, query_spread, 0.0), axis=0, keepdims=True)
        self.small_own[0:1, :] = pooled_b.astype(jnp.float32)
        self.small_own[1:2, :] = grad_many[0:1].astype(jnp.float32)
        self.small_own[2:3, :] = grad_query
        lane = lax.broadcasted_iota(jnp.int32, (1, D), 1)
        self.small_own[3:4, :] = jnp.where(
            lane == 0, loss, jnp.where(lane == 1, grad_heat, jnp.where(lane == 2, grad_offset, 0.0))
        )
        self.small_own[4:8, :] = jnp.zeros((4, D), jnp.float32)
        self.kvp[:, :D] = (dot(grad_scores, heads_query, TN) * SCALE).astype(jnp.bfloat16)
        both_probs = jnp.concatenate([probs_high, probs_low], axis=0)
        both_grads = jnp.concatenate([heads_grad, heads_grad], axis=0)
        self.kvp[:, D:] = dot(both_probs, both_grads, TN).astype(jnp.bfloat16)

    def turn(self, source):
        def body(index):
            self.turned[columns(index), :] = jnp.transpose(source[:, columns(index)])

        loop(3, body)

    def weight_grad(self, first, source, tiles, plan=None):
        def body(index):
            self.w[:, columns(index, first)] = dot(
                self.turned[...], source[:, columns(index)]
            ).astype(jnp.bfloat16)

        loop(tiles, body, plan)

    def input_grad(self, source, first, width, plan=None):
        def body(index):
            self.acc[:, columns(index)] = dot(
                source[...], self.w[columns(index), first : first + width], NT
            )

        loop(3, body, plan)

    def norm_back(self, source, added, number, out, rounded):
        gain = self.vec[2 * number : 2 * number + 1, :]

        def body(index, carry):
            rows = chunk_rows(index)
            scaled, rate = normalize(source[rows, :].astype(jnp.float32))
            grad, grad_gain, grad_bias = normalize_back(scaled, rate, self.acc[rows, :], gain)
            if added is not None:
                grad = grad + added[rows, :]
            if out is not None:
                out[rows, :] = grad
            rounded[rows, :] = grad.astype(jnp.bfloat16)
            return carry[0] + grad_gain, carry[1] + grad_bias

        zero = jnp.zeros((1, D), jnp.float32)
        grad_gain, grad_bias = lax.fori_loop(0, TOKENS // CHUNK, body, (zero, zero))
        self.vec_grad[2 * number : 2 * number + 1, :] = grad_gain
        self.vec_grad[2 * number + 1 : 2 * number + 2, :] = grad_bias

    def pool_back(self, plan=None, after=None):
        self.input_grad(self.kvp, COL_MAP_KV, 2 * D)
        self.turn(self.f)
        self.weight_grad(COL_MAP_KV, self.kvp, 6, plan)
        if after is not None:
            after()
        self.norm_back(self.y, None, 2, self.y, self.f)

    def down_back(self, start, tiles, plan=None):
        def body(step):
            index = start + step
            here = columns(index)
            grad = dot(self.f[...], self.w[:, columns(index, COL_DOWN)])
            self.gp[:, here] = (grad * self.gp[:, here].astype(jnp.float32)).astype(jnp.bfloat16)
            self.w[:, columns(index, COL_DOWN)] = dot(self.turned[...], self.g[:, here]).astype(
                jnp.bfloat16
            )

        loop(tiles, body, plan)

    def up_input(self, plan=None):
        self.input_grad(self.gp, COL_UP, FF, plan)

    def up_weight(self, start, tiles, plan=None):
        def body(step):
            index = start + step
            self.w[:, columns(index, COL_UP)] = dot(
                self.turned[...], self.gp[:, columns(index)]
            ).astype(jnp.bfloat16)

        loop(tiles, body, plan)

    def up_norm(self):
        self.norm_back(self.r, self.y, 1, self.r, self.f)

    def out_back(self, plan=None):
        self.turn(self.a)

        def body(index):
            self.a[:, columns(index)] = dot(
                self.f[...], self.w[columns(index), COL_OUT : COL_OUT + D], NT
            ).astype(jnp.bfloat16)

        loop(3, body)
        self.weight_grad(COL_OUT, self.f, 3, plan)

    def attend_back(self, plan=None):
        lanes = lax.broadcasted_iota(jnp.int32, (TOKENS, 128), 1)

        def body(pair):
            queries = self.pair_of(pair, 0) * jnp.bfloat16(SCALE)
            keys, values = self.pair_of(pair, 1), self.pair_of(pair, 2)
            grads = self.a[:, columns(pair, 0, 128)]
            keys_turned = jnp.transpose(keys)
            grad_queries = []
            grad_keys = None
            for head in range(2):
                mine = (lanes < 64) if head == 0 else (lanes >= 64)
                masked = jnp.where(mine, queries, jnp.bfloat16(0))
                masked_grads = jnp.where(mine, grads, jnp.bfloat16(0))
                scores = dot(keys, masked, NT)
                probs = jnp.exp(scores - self.lse[pl.ds(pair * 2 + head, 1), :])
                value_part = dot(probs.astype(jnp.bfloat16), masked_grads)
                grad_probs = dot(values, masked_grads, NT)
                centre = jnp.sum(probs * grad_probs, axis=0, keepdims=True)
                grad_scores = (probs * (grad_probs - centre)).astype(jnp.bfloat16)
                key_part = dot(grad_scores, masked)
                grad_queries.append(dot(keys_turned[head * 64 : head * 64 + 64], grad_scores))
                if head == 0:
                    grad_keys, grad_values = key_part, value_part
                else:
                    grad_keys, grad_values = grad_keys + key_part, grad_values + value_part
            self.qkv[:, columns(pair, 0, 128)] = (
                jnp.transpose(jnp.concatenate(grad_queries, axis=0)) * SCALE
            ).astype(jnp.bfloat16)
            self.qkv[:, columns(pair, D, 128)] = grad_keys.astype(jnp.bfloat16)
            self.qkv[:, columns(pair, 2 * D, 128)] = grad_values.astype(jnp.bfloat16)

        loop(6, body, plan)

    def project_input(self, plan=None):
        self.first_norm()
        self.input_grad(self.qkv, 0, 3 * D, plan)
        self.turn(self.h)
        self.norm_back(self.x, self.r, 0, None, self.h)

    def project_weight(self, start, tiles, plan=None):
        def body(index):
            self.w[:, columns(index, start * TILE)] = dot(
                self.turned[...], self.qkv[:, columns(index, start * TILE)]
            ).astype(jnp.bfloat16)

        loop(tiles, body, plan)

    def vectors_back(self):
        packed = jnp.concatenate([self.vec_grad[...], jnp.zeros((120, D), jnp.float32)], axis=0)
        self.w[:, COL_VECTORS : COL_VECTORS + 128] = jnp.transpose(packed).astype(jnp.bfloat16)
        self.w[:, COL_QUERY : COL_QUERY + 128] = jnp.zeros((D, 128), jnp.bfloat16)


def spread_steps(steps, count):
    plan = {}
    for at, step in enumerate(steps):
        plan.setdefault(min(count - 1, at * count // max(len(steps), 1)), []).append(step)
    return plan


TOWER_REFS = (
    ("w", "x", "cap", "h", "qkv", "a", "r", "h2", "g", "gp", "y", "f", "kvp", "lse", "turned", "acc", "vec", "vec_grad", "small_own")
)


def layer_kernel(
    master, tokens, captions, vectors, labels, scalars,
    share_out, vector_out, facts, patch_out, *scratch,
):
    p = Place()
    t = Tower(**dict(zip(TOWER_REFS, scratch)))
    scratch = scratch[len(TOWER_REFS) :]
    stage, small, pair_a, pair_b, b_in, z_in, a_in, last, mine, everyone = scratch[:10]
    share, extra, caps, map_q, map_out, map_q_share, signs = scratch[10:17]
    swap_sems, token_sems, patch_sems, own_sems, send_sem, recv_sem, grant = scratch[17:24]
    gather_s, scatter_s = scratch[24:31], scratch[31:]
    map_q_at = 4 * D + 2 * FF
    map_q_copy = pltpu.make_async_copy(
        master.at[:, map_q_at : map_q_at + D], map_q, own_sems.at[0]
    )
    map_q_copy.start()
    greet_all(p)

    count = len(GATHER_SECTIONS)
    gathers, swaps = [], []
    pieces = (
        (master, 0, 0, 3 * D),
        (extra, 0, 3 * D, 256),
        (master, 3 * D, COL_OUT, D + 2 * FF),
        (master, map_q_at + D, COL_MAP_KV, 3 * D),
    )
    for number, (first, width) in enumerate(GATHER_SECTIONS):
        swaps.append(
            Swap(p, pieces, stage, 0, 24, first, width, first // 2, swap_sems.at[number])
        )
        swaps[-1].begin((extra, False))
        gathers.append(Gather(p, t.w, CHIP_ROWS, first, width, [s.at[number] for s in gather_s]))
    own_vectors = vectors[...].astype(jnp.bfloat16).astype(jnp.float32)
    map_q_copy.wait()
    map_q[...] = map_q[...].astype(jnp.bfloat16).astype(jnp.float32)
    part = jnp.sum(own_vectors[:, 6:7] * map_q[...], axis=0, keepdims=True)
    high = part.astype(jnp.bfloat16).astype(jnp.float32)
    for side in range(6):
        lanes = slice(side * 128, side * 128 + 128)
        extra[side : side + 1, 128:256] = high[:, lanes]
        extra[6 + side : 7 + side, 128:256] = (part - high)[:, lanes]
    extra[12:24, 128:256] = jnp.zeros((12, 128), jnp.float32)
    extra[:, 0:128] = jnp.concatenate([own_vectors, jnp.zeros((24, 121), jnp.float32)], axis=1)
    swaps[0].begin((extra, True))
    each = captions.shape[0]
    caps[...] = jnp.concatenate(
        [unit_rows(captions[...].astype(jnp.float32)), jnp.zeros((64 - each, D), jnp.float32)], axis=0
    ).astype(jnp.bfloat16)
    own_caps = caps.at[pl.ds(aligned(p.blk * 16, 16), 16), :]
    swaps.append(
        Swap(p, ((own_caps, 0, 0, D),), t.cap, p.chip * 32, 16, 0, D, None, swap_sems.at[count])
    )
    swaps[-1].begin()
    gathers.append(Gather(p, t.cap, 32, 0, D, [s.at[count] for s in gather_s]))
    token_copies = []
    for step in range(1, 4):
        to = lax.rem(p.blk + step, 4)
        token_copies.append(
            remote(
                tokens.at[to],
                t.x.at[pl.ds(aligned(p.blk * 144, 144), 144), :],
                token_sems.at[0, step - 1],
                token_sems.at[1, step - 1],
                {"blk": to},
            )
        )
        token_copies[-1].start()
    own_tokens = pltpu.make_async_copy(
        tokens.at[p.blk], t.x.at[pl.ds(aligned(p.blk * 144, 144), 144), :], token_sems.at[0, 3]
    )
    own_tokens.start()

    def ready(number):
        swaps[number].finish()
        if number < count:
            first, width = GATHER_SECTIONS[number]
            t.w[
                pl.ds(aligned(p.chip * 48, 48), 48), pl.ds(gathers[number].mine, width // 2)
            ] = stage[:, first // 2 : first // 2 + width // 2].astype(jnp.bfloat16)
        gathers[number].begin()

    order = []
    for number, gather in enumerate(gathers):
        for at, step in enumerate(gather.steps()):
            call = step if at else (lambda number=number: ready(number))
            order.append((gather_key(number, at), number, at, call))
    order.sort(key=lambda entry: entry[:3])
    ends = [
        max(i for i, entry in enumerate(order) if entry[1] <= number)
        for number in range(count + 1)
    ]

    def between(number):
        return [entry[3] for entry in order[ends[number - 1] + 1 : ends[number] + 1]]

    for entry in order[: ends[0] + 1]:
        entry[3]()
    slot = lax.broadcasted_iota(jnp.int32, (8 * each, 512), 1)
    within = (slot >> 7) * 16 + (slot & 15)
    source = ((slot >> 5) & 3) * (2 * each) + ((slot >> 4) & 1) * each + within
    label = lax.broadcasted_iota(jnp.int32, (8 * each, 512), 0)
    pick = ((label == source) & (within < each)).astype(jnp.float32).astype(jnp.bfloat16)
    row = 2.0 * labels[pl.ds(p.blk, 1), :].astype(jnp.float32) - 1.0
    signs[...] = dot(jnp.broadcast_to(row, (16, 8 * each)).astype(jnp.bfloat16), pick)
    for step in range(3):
        source = lax.rem(p.blk + 3 - step, 4)
        landed = t.x.at[pl.ds(aligned(source * 144, 144), 144), :]
        remote(
            landed, landed, token_sems.at[0, step], token_sems.at[1, step], {"blk": source}
        ).wait_recv()
    own_tokens.wait()
    gathers[0].finish()

    t.unpack()
    t.first_norm()
    t.project()
    t.attend(spread_steps(between(1), 6))
    gathers[1].finish()
    t.attend_out()
    t.feed_up(spread_steps(between(2), 12))
    gathers[2].finish()
    t.feed_down(spread_steps(between(3), 3))
    gathers[3].finish()
    t.pool_project(spread_steps(between(4), 6))
    gathers[4].finish()
    t.vec_grad[...] = jnp.zeros((8, D), jnp.float32)
    images = tokens.shape[0] * 8
    t.pool(signs[0:1, :], jnp.full((1, 512), scalars[0], jnp.float32), scalars[1], images)
    swap = Swap(
        p, ((t.small_own, 0, 0, D),), small, p.chip * 16, 8, 0, D, None, swap_sems.at[count + 1]
    )
    swap.begin()
    small_gather = Gather(p, small, 16, 0, D, [s.at[count + 1] for s in gather_s])
    small_steps = small_gather.steps()
    for gather in gathers:
        gather.sent()
    for copy in token_copies:
        copy.wait_send()

    sections = []
    for number, (first, width) in enumerate(SCATTER_SECTIONS):
        half = width // 2
        which, at = PAIR_PLACES[number]
        pair_in = (pair_a, pair_b)[which].at[:, at : at + half]
        if number < 4:
            others = (b_in[number], a_in[number], z_in[number])
        else:
            here = slice(LATE_PLACES[number - 4], LATE_PLACES[number - 4] + half)
            others = (
                t.g.at[0:384, here],
                t.g.at[384:576, here],
                t.gp.at[0:144, here],
            )
        bufs = (pair_in, *others, last[number])
        sections.append(
            Scatter(p, t.w, share, first, width, bufs, [s.at[number] for s in scatter_s])
        )

    def small_begin():
        swap.finish()
        small_steps[0]()

    links, program = Links(*LINK_SPEED), Program()
    timed = []

    def leaves(section, number):
        timed.append((section, program.now, SCATTER_SECTIONS[number][1]))

    leaves(sections[0], 0)
    program.want(zip((0.5, 1.5, 4.5, 7.0, 9.5, 12.0), [small_begin] + small_steps[1:]))
    program.gap(2.5)
    program.loop("down_first", 6, 0.75)
    leaves(sections[1], 1)
    program.loop("down_second", 6, 0.75)
    leaves(sections[2], 2)
    program.loop("up_input", 3, 1.4)
    program.gap(0.5)
    program.loop("up_first", 6, 0.46)
    leaves(sections[3], 3)
    program.loop("up_second", 6, 0.46)
    program.gap(1.7)
    leaves(sections[4], 4)
    program.loop("out", 3, 1.1)
    leaves(sections[5], 5)
    program.loop("attend", 6, 2.05)
    program.gap(1.0)
    program.loop("project_input", 3, 1.0)
    program.gap(2.2)
    program.loop("front", 5, 0.5)
    leaves(sections[6], 6)
    program.loop("end", 4, 0.5)
    program.gap(1.0)
    leaves(sections[7], 7)
    for entry in timed:
        program.want(links.steps(*entry))
    program.settle()
    plans = program.plans
    t.pool_back(None, sections[0].begin)
    t.turn(t.f)
    t.down_back(0, 6, plans["down_first"])
    sections[1].begin()
    t.down_back(6, 6, plans["down_second"])
    sections[2].begin()
    t.up_input(plans["up_input"])
    t.turn(t.h2)
    t.up_weight(0, 6, plans["up_first"])
    sections[3].begin()
    t.up_weight(6, 6, plans["up_second"])
    levels = [p.on_level(lax.rem(p.z + step, 4)) for step in range(1, 4)]
    for device in (p.sibling, p.a_near, p.b_near, *levels):
        pl.semaphore_signal(grant, inc=1, device_id=device, device_id_type=MESH)
    t.up_norm()
    pl.semaphore_wait(grant, 6)
    sections[4].begin()
    t.out_back(plans["out"])
    sections[5].begin()
    t.attend_back(plans["attend"])
    t.project_input(plans["project_input"])
    patch_copies = []
    for step in range(1, 4):
        to = lax.rem(p.blk + step, 4)
        patch_copies.append(
            remote(
                t.h.at[pl.ds(aligned(to * 144, 144), 144), :],
                patch_out.at[p.blk],
                patch_sems.at[0, step - 1],
                patch_sems.at[1, step - 1],
                {"blk": to},
            )
        )
        patch_copies[-1].start()
    own_patch = pltpu.make_async_copy(
        t.h.at[pl.ds(aligned(p.blk * 144, 144), 144), :], patch_out.at[p.blk], patch_sems.at[0, 3]
    )
    own_patch.start()
    t.project_weight(0, 5, plans["front"])
    sections[6].begin()
    t.project_weight(5, 4, plans["end"])
    t.vectors_back()
    sections[7].begin()
    for step in program.tail:
        step()
    for section in sections:
        section.finish()
    outs = [
        pltpu.make_async_copy(
            share.at[:, source : source + width],
            share_out.at[:, target : target + width],
            own_sems.at[1 + number],
        )
        for number, (source, target, width) in enumerate(
            (
                (0, 0, 3 * D),
                (COL_OUT, 3 * D, D + 2 * FF),
                (COL_MAP_KV, map_q_at + D, 2 * D),
            )
        )
    ]
    for out in outs:
        out.start()
    small_gather.finish()
    small_gather.sent()
    for step, copy in enumerate(patch_copies):
        source = lax.rem(p.blk + 3 - step, 4)
        landed = patch_out.at[source]
        remote(
            landed, landed, patch_sems.at[0, step], patch_sems.at[1, step], {"blk": source}
        ).wait_recv()
        copy.wait_send()
    own_patch.wait()
    spread = Spread(p, mine, everyone, send_sem, recv_sem)
    tail = small_tail(p, small, map_q[...], own_vectors[:, 6:7], share, spread, map_out, map_q_share)
    for number, (source, target) in enumerate(((map_q_share, map_q_at), (map_out, map_q_at + 3 * D))):
        outs.append(
            pltpu.make_async_copy(
                source, share_out.at[:, target : target + D], own_sems.at[4 + number]
            )
        )
        outs[-1].start()
    lane = lax.broadcasted_iota(jnp.int32, (24, 128), 1)
    vector_out[...] = jnp.where(lane == 6, tail, share[:, COL_VECTORS : COL_VECTORS + 128])
    sums, norm = spread.finish()
    facts[...] = jnp.concatenate([jnp.broadcast_to(sums[:, :128], (7, 128)), norm[:1]], axis=0)
    for out in outs:
        out.wait()


def layer_call(master, tokens, captions, vectors, labels, scalars):
    dma = pltpu.SemaphoreType.DMA
    f32 = jnp.float32
    gathers = len(GATHER_SECTIONS) + 2
    count = len(SCATTER_SECTIONS)
    widths = [entry[1] // 2 for entry in SCATTER_SECTIONS]

    def vm(*shape, dt=jnp.bfloat16):
        return pltpu.VMEM(shape, dt)

    vmem = pl.BlockSpec(memory_space=pltpu.VMEM)
    return pl.pallas_call(
        layer_kernel,
        out_shape=(
            jax.ShapeDtypeStruct((24, 8 * D + 2 * FF), f32),
            jax.ShapeDtypeStruct((24, 128), f32),
            jax.ShapeDtypeStruct((8, 128), f32),
            jax.ShapeDtypeStruct((4, 144, D), jnp.bfloat16),
        ),
        in_specs=[
            pl.BlockSpec(memory_space=pl.ANY),
            pl.BlockSpec(memory_space=pl.ANY),
            vmem,
            vmem,
            vmem,
            pl.BlockSpec(memory_space=pltpu.SMEM),
        ],
        out_specs=(
            pl.BlockSpec(memory_space=pl.ANY),
            vmem,
            vmem,
            pl.BlockSpec(memory_space=pl.ANY),
        ),
        scratch_shapes=[
            vm(D, GATHER_COLS),
            vm(TOKENS, D),
            vm(512, D),
            vm(TOKENS, D),
            vm(TOKENS, 3 * D),
            vm(TOKENS, D),
            vm(TOKENS, D, dt=f32),
            vm(TOKENS, D),
            vm(TOKENS, FF),
            vm(TOKENS, FF),
            vm(TOKENS, D, dt=f32),
            vm(TOKENS, D),
            vm(TOKENS, 2 * D),
            vm(16, TOKENS, dt=f32),
            vm(D, TOKENS),
            vm(TOKENS, D, dt=f32),
            vm(16, D, dt=f32),
            vm(8, D, dt=f32),
            vm(8, D, dt=f32),
            vm(48, GATHER_COLS // 2, dt=f32),
            vm(256, D, dt=f32),
            vm(D, 1920),
            vm(D, 1536),
            [vm(384, w) for w in widths[:4]],
            [vm(144, w) for w in widths[:4]],
            [vm(192, w) for w in widths[:4]],
            [vm(48, w, dt=f32) for w in widths],
            vm(8, 128, dt=f32),
            vm(31, 8, 128, dt=f32),
            vm(24, SCATTER_COLS, dt=f32),
            vm(24, 256, dt=f32),
            vm(64, D),
            vm(24, D, dt=f32),
            vm(24, D, dt=f32),
            vm(24, D, dt=f32),
            vm(16, 512, dt=f32),
            dma((gathers, 4)),
            dma((2, 4)),
            dma((2, 4)),
            dma((6,)),
            dma,
            dma,
            pltpu.SemaphoreType.REGULAR,
            *gather_sems(gathers),
            dma((count, 2)),
            dma((count, 2, 2)),
            dma((count, 2)),
            dma((count, 2, 3)),
            dma((count, 2)),
        ],
        compiler_params=pltpu.CompilerParams(
            collective_id=0, has_side_effects=True, vmem_limit_bytes=63 * 2**20
        ),
        name="layer_step",
    )(master, tokens, captions, vectors, labels, scalars)


def local_kernel(
    patch_tokens,
    captions,
    pair_labels,
    master_weights,
    first_moments,
    second_moments,
    master_vectors,
    vector_first,
    vector_second,
    loss_scalars,
    scalar_first,
    scalar_second,
):
    weight_share, vector_share, facts, patch_grad = layer_call(
        master_weights, patch_tokens, captions, master_vectors, pair_labels, loss_scalars
    )
    vector_share = vector_share[:, :7]
    patch_grad = patch_grad.astype(jnp.float32)
    loss_total, scalar_total, grad_norm = facts[0, 0], facts[0, 1:3], facts[7, 0]
    factor = CLIP_AT / jnp.maximum(grad_norm, CLIP_AT)
    new_w, new_wm, new_wv = adamw(
        master_weights, weight_share * factor, first_moments, second_moments, 0.03, 0.1
    )
    new_v, new_vm, new_vv = adamw(
        master_vectors, vector_share * factor, vector_first, vector_second, 0.3, 0.0
    )
    new_s, new_sm, new_sv = adamw(
        loss_scalars, scalar_total * factor, scalar_first, scalar_second, 0.3, 0.0
    )
    return (
        loss_total,
        grad_norm,
        patch_grad,
        new_w,
        new_wm,
        new_wv,
        new_w.astype(jnp.bfloat16),
        new_v,
        new_vm,
        new_vv,
        new_v.astype(jnp.bfloat16),
        new_s,
        new_sm,
        new_sv,
    )


def solution(mesh):
    in_specs = (
        P("img", "blk", None),
        P("img", None),
        P("img", None),
        P(("blk", "img"), None),
        P(("blk", "img"), None),
        P(("blk", "img"), None),
        P(("blk", "img"), None),
        P(("blk", "img"), None),
        P(("blk", "img"), None),
        P(),
        P(),
        P(),
    )
    out_specs = (
        P(),
        P(),
        P("img", "blk", None),
        P(("blk", "img"), None),
        P(("blk", "img"), None),
        P(("blk", "img"), None),
        P(("blk", "img"), None),
        P(("blk", "img"), None),
        P(("blk", "img"), None),
        P(("blk", "img"), None),
        P(("blk", "img"), None),
        P(),
        P(),
        P(),
    )
    body = local_kernel if tuple(mesh.shape.values()) == (4, 8) else local
    return jax.shard_map(body, mesh=mesh, in_specs=in_specs, out_specs=out_specs, check_vma=False)
```

```python
import functools

import jax
import jax.numpy as jnp
from jax import lax
from jax.experimental import pallas as pl
from jax.experimental.pallas import tpu as pltpu
from jax.sharding import PartitionSpec as P

D = 768
HEADS = 12
HEAD_DIM = 64
FF = 3072
STEP = 10


BETA_ONE = 0.9
BETA_TWO = 0.999
EPS_ADAM = 1e-08
CLIP_AT = 1.0


def layer_norm(values, gain_vec, bias_vec):
    row_mean = jnp.mean(values, axis=-1, keepdims=True)
    centered = values - row_mean
    row_var = jnp.mean(centered * centered, axis=-1, keepdims=True)
    return centered * lax.rsqrt(row_var + 1e-06) * gain_vec + bias_vec


def unit_rows(pooled):
    return pooled * lax.rsqrt(jnp.sum(pooled * pooled, axis=-1, keepdims=True) + 1e-06)


def attend(queries, keys_all, values_all):
    scale = HEAD_DIM ** (-0.5)
    scores = (
        jnp.einsum("iqhe,ikhe->ihqk", queries, keys_all, preferred_element_type=jnp.float32) * scale
    )
    row_max = jnp.max(scores, axis=-1, keepdims=True)
    expos = jnp.exp(scores - row_max)
    row_sum = jnp.sum(expos, axis=-1, keepdims=True)
    attn_probs = (expos / row_sum).astype(jnp.bfloat16)
    mixed_out = jnp.einsum(
        "ihqk,ikhe->iqhe", attn_probs, values_all, preferred_element_type=jnp.float32
    )
    return (mixed_out.astype(jnp.bfloat16), row_max + jnp.log(row_sum))


def attend_back(queries, keys_all, values_all, log_norm, grad_mixed):
    scale = HEAD_DIM ** (-0.5)
    scores = (
        jnp.einsum("iqhe,ikhe->ihqk", queries, keys_all, preferred_element_type=jnp.float32) * scale
    )
    attn_probs = jnp.exp(scores - log_norm)
    grad_values = jnp.einsum(
        "ihqk,iqhe->ikhe",
        attn_probs.astype(jnp.bfloat16),
        grad_mixed,
        preferred_element_type=jnp.float32,
    )
    grad_probs = jnp.einsum(
        "iqhe,ikhe->ihqk", grad_mixed, values_all, preferred_element_type=jnp.float32
    )
    centre = jnp.sum(attn_probs * grad_probs, axis=-1, keepdims=True)
    grad_scores = (attn_probs * (grad_probs - centre)).astype(jnp.bfloat16)
    grad_queries = (
        jnp.einsum("ihqk,ikhe->iqhe", grad_scores, keys_all, preferred_element_type=jnp.float32)
        * scale
    )
    grad_keys = (
        jnp.einsum("ihqk,iqhe->ikhe", grad_scores, queries, preferred_element_type=jnp.float32)
        * scale
    )
    return (grad_queries, grad_keys, grad_values)


def adamw(parameter, gradient, moment_one, moment_two, step_rate, decay_rate):
    moment_one = BETA_ONE * moment_one + (1.0 - BETA_ONE) * gradient
    moment_two = BETA_TWO * moment_two + (1.0 - BETA_TWO) * gradient * gradient
    first_hat = moment_one / (1.0 - BETA_ONE**STEP)
    second_hat = moment_two / (1.0 - BETA_TWO**STEP)
    updated = parameter - step_rate * (
        first_hat / (jnp.sqrt(second_hat) + EPS_ADAM) + decay_rate * parameter
    )
    return (updated, moment_one, moment_two)


def local(
    patch_tokens,
    captions,
    pair_labels,
    master_weights,
    first_moments,
    second_moments,
    master_vectors,
    vector_first,
    vector_second,
    loss_scalars,
    scalar_first,
    scalar_second,
):
    blocks = lax.axis_size("blk")
    block = lax.axis_index("blk")
    all_images = patch_tokens.shape[0] * lax.axis_size("img")
    images = patch_tokens.shape[0] // blocks
    length = patch_tokens.shape[1] * blocks
    scale = HEAD_DIM ** (-0.5)
    both = ("blk", "img")
    rows = master_weights.shape[0]
    first_row = lax.axis_index(both) * rows
    patch_tokens = lax.all_to_all(patch_tokens, "blk", 0, 1, tiled=True)
    pair_labels = lax.dynamic_slice_in_dim(pair_labels, block * images, images, 0)
    rounded = master_weights.astype(jnp.bfloat16)
    full_vectors = lax.all_gather(master_vectors.astype(jnp.bfloat16), both, axis=0, tiled=True)
    vectors = full_vectors.astype(jnp.float32)

    def gather(start, stop):
        return lax.all_gather(rounded[:, start:stop], both, axis=0, tiled=True)

    w_front = gather(0, 4 * D)
    w_qkv = w_front[:, : 3 * D]
    w_out = w_front[:, 3 * D :]
    w_up = gather(4 * D, 4 * D + FF)
    w_down = gather(4 * D + FF, 4 * D + 2 * FF)
    own_map_q = rounded[:, 4 * D + 2 * FF : 5 * D + 2 * FF]
    w_map = gather(5 * D + 2 * FF, 8 * D + 2 * FF)
    w_map_kv = w_map[:, : 2 * D]
    w_map_out = w_map[:, 2 * D :]
    own_vectors = master_vectors.astype(jnp.bfloat16)
    tokens = patch_tokens.astype(jnp.float32)
    normed, norm_one_pull = jax.vjp(layer_norm, tokens, vectors[:, 0], vectors[:, 1])
    normed_b = normed.astype(jnp.bfloat16)
    qkv_b = jnp.einsum("ipd,dc->ipc", normed_b, w_qkv, preferred_element_type=jnp.float32).astype(
        jnp.bfloat16
    )
    queries = qkv_b[:, :, :D].reshape(images, length, HEADS, HEAD_DIM)
    keys_all = qkv_b[:, :, D : 2 * D].reshape(images, length, HEADS, HEAD_DIM)
    values_all = qkv_b[:, :, 2 * D :].reshape(images, length, HEADS, HEAD_DIM)
    mixed_heads, log_norm = attend(queries, keys_all, values_all)
    mixed_b = mixed_heads.reshape(images, length, D)
    residual = tokens + jnp.einsum(
        "ipd,dc->ipc", mixed_b, w_out, preferred_element_type=jnp.float32
    )
    hidden, norm_two_pull = jax.vjp(layer_norm, residual, vectors[:, 2], vectors[:, 3])
    hidden_b = hidden.astype(jnp.bfloat16)
    pre_act = jnp.einsum("ipd,df->ipf", hidden_b, w_up, preferred_element_type=jnp.float32)
    activation, gelu_pull = jax.vjp(jax.nn.gelu, pre_act)
    activation_b = activation.astype(jnp.bfloat16)
    layer_out = residual + jnp.einsum(
        "ipf,df->ipd", activation_b, w_down, preferred_element_type=jnp.float32
    )
    final_norm, norm_three_pull = jax.vjp(layer_norm, layer_out, vectors[:, 4], vectors[:, 5])
    final_b = final_norm.astype(jnp.bfloat16)
    map_kv = jnp.einsum("ipd,dc->ipc", final_b, w_map_kv, preferred_element_type=jnp.float32)
    map_kv = map_kv.astype(jnp.bfloat16).reshape(images, length, 2, HEADS, HEAD_DIM)
    probe_query = lax.psum(
        jnp.dot(own_vectors[:, 6], own_map_q, preferred_element_type=jnp.float32), both
    )
    probe_query = probe_query.astype(jnp.bfloat16).reshape(HEADS, HEAD_DIM)
    pool_scores = (
        jnp.einsum("he,iphe->ihp", probe_query, map_kv[:, :, 0], preferred_element_type=jnp.float32)
        * scale
    )
    row_max = jnp.max(pool_scores, axis=-1)
    row_sum = jnp.sum(jnp.exp(pool_scores - row_max[..., None]), axis=-1)
    pool_probs = jnp.exp(pool_scores - row_max[..., None]) / row_sum[..., None]
    map_values = map_kv[:, :, 1].astype(jnp.float32)
    pooled_part = jnp.einsum(
        "ihp,iphe->ihe", pool_probs, map_values, precision=lax.Precision.HIGHEST
    )
    pooled_heads = pooled_part.reshape(images, D)
    pooled_heads_b = pooled_heads.astype(jnp.bfloat16)
    pooled = jnp.dot(pooled_heads_b, w_map_out, preferred_element_type=jnp.float32)
    caption_all = lax.all_gather(captions, "img", axis=0, tiled=True).astype(jnp.float32)
    caption_unit = unit_rows(caption_all).astype(jnp.bfloat16)
    unit_image, unit_pull = jax.vjp(unit_rows, pooled)
    cosine = jnp.einsum(
        "id,cd->ic",
        unit_image.astype(jnp.bfloat16),
        caption_unit,
        preferred_element_type=jnp.float32,
    )
    signs = 2.0 * pair_labels.astype(jnp.float32) - 1.0

    def pair_loss(cosine_in, scalars_in):
        logits = jnp.exp(scalars_in[0]) * cosine_in + scalars_in[1]
        return jnp.sum(jax.nn.softplus(-signs * logits)) / all_images

    loss_local, loss_pull = jax.vjp(pair_loss, cosine, loss_scalars)
    grad_cosine, grad_scalars = loss_pull(jnp.ones((), jnp.float32))
    loss_total, scalar_total = lax.psum((loss_local, grad_scalars), both)
    grad_unit = jnp.einsum(
        "ic,cd->id",
        grad_cosine.astype(jnp.bfloat16),
        caption_unit,
        preferred_element_type=jnp.float32,
    )
    (grad_pooled,) = unit_pull(grad_unit)
    grad_pooled_b = grad_pooled.astype(jnp.bfloat16)
    pooled_all, grad_pooled_all = (
        lax.all_gather(pooled_heads_b, both, axis=0, tiled=True),
        lax.all_gather(grad_pooled_b, both, axis=0, tiled=True),
    )
    share_map_out = jnp.einsum(
        "id,ic->dc",
        lax.dynamic_slice_in_dim(pooled_all, first_row, rows, 1),
        grad_pooled_all,
        preferred_element_type=jnp.float32,
    )
    grad_heads_b = jnp.einsum(
        "ic,dc->id", grad_pooled_b, w_map_out, preferred_element_type=jnp.float32
    )
    grad_heads_b = grad_heads_b.astype(jnp.bfloat16).reshape(images, HEADS, HEAD_DIM)
    grad_heads = grad_heads_b.astype(jnp.float32)
    centre = jnp.sum(grad_heads * pooled_heads.reshape(images, HEADS, HEAD_DIM), axis=-1)
    grad_probs = jnp.einsum(
        "ihe,iphe->ihp", grad_heads_b, map_kv[:, :, 1], preferred_element_type=jnp.float32
    )
    grad_pool_scores = (pool_probs * (grad_probs - centre[..., None])).astype(jnp.bfloat16)
    grad_map_keys = (
        jnp.einsum(
            "ihp,he->iphe", grad_pool_scores, probe_query, preferred_element_type=jnp.float32
        )
        * scale
    )
    grad_map_values = jnp.einsum(
        "ihp,ihe->iphe", pool_probs, grad_heads, precision=lax.Precision.HIGHEST
    )
    grad_probe_query = (
        jnp.einsum(
            "ihp,iphe->he", grad_pool_scores, map_kv[:, :, 0], preferred_element_type=jnp.float32
        ).reshape(D)
        * scale
    )
    grad_map_kv = (
        jnp.stack([grad_map_keys, grad_map_values], axis=2)
        .astype(jnp.bfloat16)
        .reshape(images, length, 2 * D)
    )
    grad_w_map_kv = jnp.einsum(
        "ipd,ipc->dc", final_b, grad_map_kv, preferred_element_type=jnp.float32
    )
    grad_final = jnp.einsum(
        "ipc,dc->ipd", grad_map_kv, w_map_kv, preferred_element_type=jnp.float32
    )
    grad_layer_out, grad_gain_three, grad_bias_three = norm_three_pull(grad_final)
    probe_total = lax.psum(grad_probe_query, both)
    share_map_q = jnp.outer(own_vectors[:, 6].astype(jnp.float32), probe_total)
    share_probe = jnp.dot(
        own_map_q.astype(jnp.float32), probe_total, precision=lax.Precision.HIGHEST
    )
    grad_branch_two = grad_layer_out.astype(jnp.bfloat16)
    grad_w_down = jnp.einsum(
        "ipd,ipf->df", grad_branch_two, activation_b, preferred_element_type=jnp.float32
    )
    grad_activation = jnp.einsum(
        "ipd,df->ipf", grad_branch_two, w_down, preferred_element_type=jnp.float32
    )
    (grad_pre,) = gelu_pull(grad_activation)
    grad_pre_b = grad_pre.astype(jnp.bfloat16)
    grad_w_up = jnp.einsum("ipd,ipf->df", hidden_b, grad_pre_b, preferred_element_type=jnp.float32)
    grad_hidden = jnp.einsum("ipf,df->ipd", grad_pre_b, w_up, preferred_element_type=jnp.float32)
    grad_res_part, grad_gain_two, grad_bias_two = norm_two_pull(grad_hidden)
    grad_residual = grad_layer_out + grad_res_part
    grad_branch_one = grad_residual.astype(jnp.bfloat16)
    grad_w_out = jnp.einsum(
        "ipd,ipc->dc", mixed_b, grad_branch_one, preferred_element_type=jnp.float32
    )
    grad_mixed = jnp.einsum(
        "ipc,dc->ipd", grad_branch_one, w_out, preferred_element_type=jnp.float32
    )
    grad_mixed = grad_mixed.astype(jnp.bfloat16)
    grad_queries, grad_keys, grad_values = attend_back(
        queries, keys_all, values_all, log_norm, grad_mixed.reshape(images, length, HEADS, HEAD_DIM)
    )
    grad_qkv = jnp.concatenate(
        [
            grad_queries.reshape(images, length, D),
            grad_keys.reshape(images, length, D),
            grad_values.reshape(images, length, D),
        ],
        axis=-1,
    ).astype(jnp.bfloat16)
    grad_w_qkv = jnp.einsum("ipd,ipc->dc", normed_b, grad_qkv, preferred_element_type=jnp.float32)
    grad_normed = jnp.einsum("ipc,dc->ipd", grad_qkv, w_qkv, preferred_element_type=jnp.float32)
    grad_tok_part, grad_gain_one, grad_bias_one = norm_one_pull(grad_normed)
    patch_grad = lax.all_to_all(
        (grad_residual + grad_tok_part).astype(jnp.bfloat16), "blk", 1, 0, tiled=True
    ).astype(jnp.float32)
    grad_vectors = jnp.stack(
        [
            grad_gain_one,
            grad_bias_one,
            grad_gain_two,
            grad_bias_two,
            grad_gain_three,
            grad_bias_three,
        ],
        axis=1,
    )

    def scatter(part):
        return lax.psum_scatter(
            part.astype(jnp.bfloat16), both, scatter_dimension=0, tiled=True
        ).astype(jnp.float32)

    share_map_kv = scatter(grad_w_map_kv)
    share_down = scatter(grad_w_down)
    share_up = scatter(grad_w_up)
    share_front = scatter(jnp.concatenate([grad_w_qkv, grad_w_out], axis=1))
    weight_share = jnp.concatenate(
        [share_front, share_up, share_down, share_map_q, share_map_kv, share_map_out], axis=1
    )
    vector_share = jnp.concatenate(
        [
            lax.psum_scatter(grad_vectors, both, scatter_dimension=0, tiled=True),
            share_probe[:, None],
        ],
        axis=1,
    )
    squares = jnp.sum(weight_share * weight_share) + jnp.sum(vector_share * vector_share)
    square_total = lax.psum(squares, ("blk", "img"))
    grad_norm = jnp.sqrt(square_total + jnp.sum(scalar_total * scalar_total))
    factor = CLIP_AT / jnp.maximum(grad_norm, CLIP_AT)
    new_w, new_wm, new_wv = adamw(
        master_weights, weight_share * factor, first_moments, second_moments, 0.03, 0.1
    )
    new_v, new_vm, new_vv = adamw(
        master_vectors, vector_share * factor, vector_first, vector_second, 0.3, 0.0
    )
    new_s, new_sm, new_sv = adamw(
        loss_scalars, scalar_total * factor, scalar_first, scalar_second, 0.3, 0.0
    )
    return (
        loss_total,
        grad_norm,
        patch_grad,
        new_w,
        new_wm,
        new_wv,
        new_w.astype(jnp.bfloat16),
        new_v,
        new_vm,
        new_vv,
        new_v.astype(jnp.bfloat16),
        new_s,
        new_sm,
        new_sv,
    )


LINK_SPEED = (1.1, 3.0)


def gather_key(number, at):
    return 0 if at == 0 else at + number


MESH = pl.DeviceIdType.MESH
CHIP_ROWS = 48
GATHER_SECTIONS = ((0, 2560, False), (2560, 3840, True), (6400, 3072, False), (9472, 2304, False))
SCATTER_SECTIONS = (
    (9472, 1536, False),
    (6400, 1536, False),
    (7936, 1536, False),
    (3328, 1536, False),
    (4864, 1536, False),
    (2560, 768, False),
    (0, 1280, False),
    (1280, 1280, False),
)
PAIR_PLACES = ((0, 0), (0, 768), (1, 0), (1, 768), (0, 0), (0, 1536), (0, 768), (1, 0))
LATE_PLACES = (0, 768, 1152, 1792)
GATHER_COLS = 11776
SCATTER_COLS = 11008


def aligned(value, step):
    return pl.multiple_of(value, step)


class Place:
    def __init__(self):
        self.blk = lax.axis_index("blk")
        self.img = lax.axis_index("img")
        self.x = lax.rem(self.blk, 2)
        self.y = self.blk // 2
        self.z = self.img // 2
        self.c = lax.rem(self.img, 2)
        self.chip = self.blk * 4 + self.z
        self.sibling = {"img": self.z * 2 + 1 - self.c}
        self.up = {"img": self.img + 2}
        self.down = {"img": self.img - 2}
        self.a_near = {"blk": self.block(1, 0)}
        self.b_near = {"blk": self.block(0, 1)}

    def on_level(self, level):
        return {"img": level * 2 + self.c}

    def block(self, da, db):
        flip_x = da * (1 - self.c) + db * self.c
        flip_y = db * (1 - self.c) + da * self.c
        other_x = self.x + flip_x * (1 - 2 * self.x)
        other_y = self.y + flip_y * (1 - 2 * self.y)
        return other_y * 2 + other_x


def remote(src, dst, send_sem, recv_sem, device):
    return pltpu.make_async_remote_copy(
        src_ref=src,
        dst_ref=dst,
        send_sem=send_sem,
        recv_sem=recv_sem,
        device_id=device,
        device_id_type=MESH,
    )


def greet_all(place):
    barrier = pltpu.get_barrier_semaphore()
    me = place.blk * 8 + place.img

    def greet(step, carry):
        other = lax.rem(me + step, 32)
        pl.semaphore_signal(
            barrier,
            inc=1,
            device_id={"blk": other // 8, "img": lax.rem(other, 8)},
            device_id_type=MESH,
        )
        return carry

    lax.fori_loop(1, 32, greet, 0)


def all_greeted():
    pl.semaphore_wait(pltpu.get_barrier_semaphore(), 31)


class Gather:
    def __init__(self, place, buf, rows, first, width, z_first, sems):
        self.p, self.buf, self.rows, self.half = place, buf, rows, width // 2
        self.z_first = z_first
        self.mine = aligned(first + place.c * self.half, 128)
        self.theirs = aligned(first + (1 - place.c) * self.half, 128)
        self.near_recv, self.z_recv, self.b_recv, self.near_send, self.z_send, self.b_send, self.pair = sems

    def item(self, da, db, level):
        start = aligned((self.p.block(da, db) * 4 + level) * self.rows, self.rows)
        return self.buf.at[pl.ds(start, self.rows), pl.ds(self.mine, self.half)]

    def a_copy(self, level, da=0):
        part = self.item(da, 0, level)
        return remote(part, part, self.near_send.at[level], self.near_recv.at[level], self.p.a_near)

    def z_copy(self, da, level, up):
        part = self.item(da, 0, level)
        device = self.p.up if up else self.p.down
        return remote(part, part, self.z_send.at[up, da, level], self.z_recv.at[da, level], device)

    def b_copy(self, da, level):
        part = self.item(da, 0, level)
        return remote(part, part, self.b_send.at[da, level], self.b_recv.at[da, level], self.p.b_near)

    def pair_copy(self, da, db):
        start = aligned(self.p.block(da, db) * (4 * self.rows), 4 * self.rows)
        part = self.buf.at[pl.ds(start, 4 * self.rows), pl.ds(self.mine, self.half)]
        return remote(part, part, self.pair.at[0], self.pair.at[1], self.p.sibling)

    def onward(self, da, level, up, down):
        if self.z_first and da == 0:
            self.a_copy(level).start()
        self.b_copy(da, level).start()
        if up:
            pl.when(self.p.z < 3)(lambda: self.z_copy(da, level, 1).start())
        if down:
            pl.when(self.p.z > 0)(lambda: self.z_copy(da, level, 0).start())

    def begin(self):
        if not self.z_first:
            self.a_copy(self.p.z).start()
        self.onward(0, self.p.z, True, True)

    def near(self):
        z = self.p.z
        if not self.z_first:
            self.a_copy(z, 1).wait_recv()
            self.onward(1, z, True, True)
            return
        for step in range(4):
            level = lax.rem(z + step, 4)
            self.a_copy(level, 1).wait_recv()
            self.onward(1, level, False, False)
        self.pair_copy(1, 0).start()

    def level(self, distance):
        z = self.p.z
        sides = 1 if self.z_first else 2

        @pl.when(z >= distance)
        def from_below():
            for da in range(sides):
                self.z_copy(da, z - distance, 1).wait_recv()
                self.onward(da, z - distance, True, False)

        @pl.when(z + distance <= 3)
        def from_above():
            for da in range(sides):
                self.z_copy(da, z + distance, 0).wait_recv()
                self.onward(da, z + distance, False, True)

        if distance == 3:
            for da in range(sides):
                self.pair_copy(da, 0).start()

    def far(self):
        for da in range(2):
            for level in range(4):
                part = self.item(da, 1, level)
                remote(
                    part, part, self.b_send.at[da, level], self.b_recv.at[da, level], self.p.b_near
                ).wait_recv()
            self.pair_copy(da, 1).start()

    def finish(self):
        whole = self.buf.at[pl.ds(0, 16 * self.rows), pl.ds(self.theirs, self.half)]
        both = remote(whole, whole, self.pair.at[0], self.pair.at[1], self.p.sibling)
        both.wait_recv()

    def sent(self):
        z = self.p.z
        whole = self.buf.at[pl.ds(0, 16 * self.rows), pl.ds(self.mine, self.half)]
        remote(whole, whole, self.pair.at[0], self.pair.at[1], self.p.sibling).wait_send()
        if not self.z_first:
            self.a_copy(z).wait_send()
        for level in range(4):
            if self.z_first:
                self.a_copy(level).wait_send()
            for da in range(2):
                self.b_copy(da, level).wait_send()
            for da in range(1 if self.z_first else 2):
                if level < 3:
                    pl.when((z >= level) & (z < 3))(
                        lambda da=da, level=level: self.z_copy(da, level, 1).wait_send()
                    )
                if level > 0:
                    pl.when((z <= level) & (z > 0))(
                        lambda da=da, level=level: self.z_copy(da, level, 0).wait_send()
                    )

    def steps(self):
        levels = [functools.partial(self.level, distance) for distance in (1, 2, 3)]
        if self.z_first:
            return [self.begin, *levels, self.near, self.far]
        return [self.begin, self.near, *levels, self.far]


def gather_sems(count):
    dma = pltpu.SemaphoreType.DMA
    return [
        dma((count, 4)),
        dma((count, 2, 4)),
        dma((count, 2, 4)),
        dma((count, 4)),
        dma((count, 2, 2, 4)),
        dma((count, 2, 4)),
        dma((count, 2)),
    ]


class Scatter:
    def __init__(self, place, buf, share, first, width, z_first, bufs, sems):
        self.p, self.buf, self.share, self.half = place, buf, share, width // 2
        self.z_first = z_first
        self.mine = aligned(first + place.c * self.half, 128)
        self.theirs = aligned(first + (1 - place.c) * self.half, 128)
        self.pair_in, self.b_in, self.a_in, self.z_in, self.last = bufs
        self.pair, self.b_sem, self.a_sem, self.z_sem, self.end = sems

    def run_rows(self, da, db):
        return aligned(self.p.block(da, db) * 192, 192)

    def run(self, da, db):
        return self.buf.at[pl.ds(self.run_rows(da, db), 192), pl.ds(self.mine, self.half)]

    def level_rows(self, da, level):
        return aligned((self.p.block(da, 0) * 4 + level) * 48, 48)

    def part(self, da, level):
        return self.buf.at[pl.ds(self.level_rows(da, level), 48), pl.ds(self.mine, self.half)]

    def add(self, row, source, count, offset=0):
        def one(step, carry):
            here = aligned(row + step * 48, 48)
            there = aligned(offset + step * 48, 48)
            self.buf[pl.ds(here, 48), pl.ds(self.mine, self.half)] += source[pl.ds(there, 48), :]
            return carry

        if count == 1:
            one(0, 0)
        else:
            lax.fori_loop(0, count, one, 0)

    def pair_copy(self):
        return remote(
            self.buf.at[pl.ds(0, 768), pl.ds(self.theirs, self.half)],
            self.pair_in,
            self.pair.at[0],
            self.pair.at[1],
            self.p.sibling,
        )

    def b_copy(self, da):
        return remote(
            self.run(da, 1),
            self.b_in.at[da * 192 : da * 192 + 192, :],
            self.b_sem.at[0, da],
            self.b_sem.at[1, da],
            self.p.b_near,
        )

    def a_copy(self):
        source = self.part(1, self.p.z) if self.z_first else self.run(1, 0)
        return remote(source, self.a_in, self.a_sem.at[0], self.a_sem.at[1], self.p.a_near)

    def z_slot(self, da, step):
        return slice(da * 144 + (3 - step) * 48, da * 144 + (4 - step) * 48)

    def z_copy(self, da, step):
        level = lax.rem(self.p.z + step, 4)
        return remote(
            self.part(da, level),
            self.z_in.at[self.z_slot(da, step), :],
            self.z_sem.at[0, da, 3 - step],
            self.z_sem.at[1, da, 3 - step],
            self.p.on_level(level),
        )

    def z_start(self, da):
        for step in (2, 1, 3):
            self.z_copy(da, step).start()

    def z_total(self, da):
        total = self.buf[pl.ds(self.level_rows(da, self.p.z), 48), pl.ds(self.mine, self.half)]
        total = total.astype(jnp.float32)
        for step in (1, 3, 2):
            self.z_copy(da, step).wait_recv()
            total += self.z_in[self.z_slot(da, step), :].astype(jnp.float32)
        return total

    def end_copy(self):
        return remote(
            self.last.at[pl.ds(aligned((1 - self.p.c) * 24, 8), 24), :],
            self.share.at[:, pl.ds(self.mine, self.half)],
            self.end.at[0],
            self.end.at[1],
            self.p.sibling,
        )

    def begin(self):
        self.pair_copy().start()

    def pairs_far(self):
        self.pair_copy().wait_recv()
        for da in range(2):
            row = self.run_rows(da, 1)
            self.add(row, self.pair_in, 4, row)
            self.b_copy(da).start()

    def pairs_near(self):
        for da in range(2):
            row = self.run_rows(da, 0)
            self.add(row, self.pair_in, 4, row)

    def blocks(self):
        for da in (1, 0):
            self.b_copy(da).wait_recv()
            self.add(self.run_rows(da, 0), self.b_in, 4, da * 192)
            if self.z_first:
                self.z_start(da)
            elif da == 1:
                self.a_copy().start()

    def joined(self):
        if self.z_first:
            self.buf[pl.ds(self.level_rows(1, self.p.z), 48), pl.ds(self.mine, self.half)] = (
                self.z_total(1).astype(jnp.bfloat16)
            )
            self.a_copy().start()
        else:
            self.a_copy().wait_recv()
            self.add(self.run_rows(0, 0), self.a_in, 4)
            self.z_start(0)

    def close(self):
        total = self.z_total(0)
        if self.z_first:
            self.a_copy().wait_recv()
            total += self.a_in[...].astype(jnp.float32)
        self.last[...] = total
        self.end_copy().start()
        self.share[:, pl.ds(self.mine, self.half)] = self.last[
            pl.ds(aligned(self.p.c * 24, 8), 24), :
        ]

    def finish(self):
        theirs = self.share.at[:, pl.ds(self.theirs, self.half)]
        remote(theirs, theirs, self.end.at[0], self.end.at[1], self.p.sibling).wait_recv()
        self.end_copy().wait_send()
        self.a_copy().wait_send()
        self.pair_copy().wait_send()
        for da in range(2):
            self.b_copy(da).wait_send()
        for da in range(2 if self.z_first else 1):
            for step in range(1, 4):
                self.z_copy(da, step).wait_send()


class Links:
    def __init__(self, slow=1.0, hop=2.0):
        self.flat = self.high = 0.0
        self.slow, self.hop = slow, hop

    def use(self, name, start, time):
        start = max(start, getattr(self, name))
        setattr(self, name, start + time * self.slow)
        return start + time * self.slow + self.hop

    def steps(self, section, start, width):
        size = width / 256
        out = []
        now = start + 0.35 * size * self.slow + 1.0
        out += [(now, section.pairs_far), (now + 0.5, section.pairs_near)]
        now = self.use("flat", now + 0.5, 1.01 * size)
        out.append((now, section.blocks))
        if section.z_first:
            now = self.use("high", now, 2.02 * size)
            out.append((now, section.joined))
            now = self.use("flat", now, 0.13 * size)
        else:
            now = self.use("flat", now, 0.5 * size)
            out.append((now, section.joined))
            now = self.use("high", now, 1.01 * size)
        out += [(now, section.close), (now + 4.0, section.finish)]
        return out


class Program:
    def __init__(self):
        self.now, self.places, self.wanted = 0.0, [], []
        self.plans = {}
        self.tail = []

    def loop(self, name, count, each):
        self.plans[name] = {}
        for index in range(count):
            self.now += each
            self.places.append((self.now, name, index))

    def gap(self, time):
        self.now += time

    def want(self, steps):
        self.wanted += [(time, len(self.wanted) + n, step) for n, (time, step) in enumerate(steps)]

    def settle(self):
        for time, _, step in sorted(self.wanted, key=lambda entry: entry[:2]):
            for place, name, index in self.places:
                if place >= time:
                    self.plans[name].setdefault(index, []).append(step)
                    break
            else:
                self.tail.append(step)


class Swap:
    def __init__(self, place, pieces, buf, first_buf_row, rows, first, width, offset, sems):
        self.p, self.rows, self.half = place, rows, width // 2
        self.buf, self.sems = buf, sems
        self.row = aligned(first_buf_row + place.c * rows, rows)
        self.other_row = aligned(first_buf_row + (1 - place.c) * rows, rows)
        self.halves = []
        for core in range(2):
            low, here = first + core * self.half, []
            for array, source, target, size in pieces:
                start, stop = max(low, target), min(low + self.half, target + size)
                if start < stop:
                    at = start - low + offset if offset is not None else start
                    here.append((array, source + start - target, at, stop - start))
            self.halves.append(here)
        self.at = (
            pl.ds(aligned(first + place.c * self.half, 128), self.half)
            if offset is None
            else pl.ds(offset, self.half)
        )
        self.away_at = (
            pl.ds(aligned(first + (1 - place.c) * self.half, 128), self.half)
            if offset is None
            else pl.ds(offset, self.half)
        )

    def begin(self, late=None):
        for core in range(2):
            for array, source, at, size in self.halves[core]:
                if late is not None and (array is late[0]) != late[1]:
                    continue
                part = array.at[:, source : source + size]
                goal = self.buf.at[pl.ds(self.row, self.rows), at : at + size]

                @pl.when(self.p.c == core)
                def here(part=part, goal=goal):
                    pltpu.make_async_copy(part, goal, self.sems.at[2]).start()

                @pl.when(self.p.c != core)
                def away(part=part, goal=goal):
                    remote(part, goal, self.sems.at[0], self.sems.at[1], self.p.sibling).start()

    def finish(self):
        landed = self.buf.at[pl.ds(self.other_row, self.rows), self.at]
        own = self.buf.at[pl.ds(self.row, self.rows), self.at]
        gone = self.buf.at[pl.ds(self.row, self.rows), self.away_at]
        remote(landed, landed, self.sems.at[0], self.sems.at[1], self.p.sibling).wait_recv()
        pltpu.make_async_copy(own, own, self.sems.at[2]).wait()
        remote(gone, gone, self.sems.at[0], self.sems.at[1], self.p.sibling).wait_send()


class Spread:
    def __init__(self, place, mine, everyone, send_sem, recv_sem):
        self.p, self.mine, self.everyone = place, mine, everyone
        self.send_sem, self.recv_sem = send_sem, recv_sem
        self.me = place.blk * 8 + place.img

    def copy(self, step):
        other = lax.rem(self.me + step, 32)
        return remote(
            self.mine,
            self.everyone.at[step - 1],
            self.send_sem,
            self.recv_sem,
            {"blk": other // 8, "img": lax.rem(other, 8)},
        )

    def begin(self, tile):
        self.mine[...] = tile

        def start(step, carry):
            self.copy(step).start()
            return carry

        lax.fori_loop(1, 32, start, 0)

    def finish(self, small):
        scalars = jnp.sum(small[...].reshape(32, 8, 768), axis=0)[3:4]
        lane = lax.broadcasted_iota(jnp.int32, (1, 768), 1)
        square = jnp.sum(jnp.where((lane == 1) | (lane == 2), scalars * scalars, 0.0))
        return scalars, jnp.sqrt(self.total() + square)

    def total(self):
        remote(
            self.everyone, self.everyone, self.send_sem, self.recv_sem, self.p.sibling
        ).wait()
        return self.mine[...] + jnp.sum(self.everyone[...], axis=0)


def small_tail(p, small, map_q, probe, map_out_ref, map_q_ref):
    everything = small[...]
    as_rows = everything.astype(jnp.bfloat16)
    sums = jnp.sum(everything.reshape(32, 8, 768), axis=0)
    query = sums[2:3]
    device = lax.broadcasted_iota(jnp.int32, (32, 256), 0) * 8
    row = lax.broadcasted_iota(jnp.int32, (32, 256), 1)

    def rows_of(kind):
        pick = (row == device + kind).astype(jnp.float32).astype(jnp.bfloat16)
        return jnp.dot(pick, as_rows, preferred_element_type=jnp.float32).astype(jnp.bfloat16)

    pooled, grads = rows_of(0), rows_of(1)
    first = (p.blk * 8 + p.img) * 24
    picks = (
        lax.broadcasted_iota(jnp.int32, (24, 768), 1)
        == lax.broadcasted_iota(jnp.int32, (24, 768), 0) + first
    ).astype(jnp.float32).astype(jnp.bfloat16)
    rows = lax.dot_general(
        picks, pooled, (((1,), (1,)), ((), ())), preferred_element_type=jnp.float32
    ).astype(jnp.bfloat16)
    map_out = jnp.dot(rows, grads, preferred_element_type=jnp.float32)
    map_q_share = probe * query
    probe_share = jnp.sum(map_q * query, axis=1, keepdims=True)
    square = (
        jnp.sum(map_out * map_out)
        + jnp.sum(map_q_share * map_q_share)
        + jnp.sum(probe_share * probe_share)
    )
    map_out_ref[...], map_q_ref[...] = map_out, map_q_share
    return probe_share, square


def square_share(share, square, start, stop):
    def one(step, total):
        part = share[:, pl.ds(aligned(step * 256, 256), 256)]
        return total + jnp.sum(part * part)

    return lax.fori_loop(start, stop, one, square)


COL_VECTORS = 2304
COL_QUERY = 2432
COL_OUT = 2560
COL_UP = 3328
COL_DOWN = 6400
COL_MAP_KV = 9472
COL_MAP_OUT = 11008
TOKENS = 576
CHUNK = 96
TILE = 256
SCALE = 0.125
GELU_A = 0.7978845608028654
GELU_B = 0.044715
NT = (((1,), (1,)), ((), ()))
TN = (((0,), (0,)), ((), ()))


def dot(lhs, rhs, dims=(((1,), (0,)), ((), ()))):
    return lax.dot_general(lhs, rhs, dims, preferred_element_type=jnp.float32)


def loop(count, body, plan=None):
    def one(index, carry):
        body(index)
        for at, steps in (plan or {}).items():

            @pl.when(index == at)
            def run(steps=steps):
                for step in steps:
                    step()

        return carry

    lax.fori_loop(0, count, one, 0)


def columns(index, first=0, width=TILE):
    return pl.ds(aligned(first + index * width, 128), width)


def chunk_rows(index):
    return pl.ds(aligned(index * CHUNK, 32), CHUNK)


def normalize(values):
    row_mean = jnp.mean(values, axis=-1, keepdims=True)
    centered = values - row_mean
    row_var = jnp.mean(centered * centered, axis=-1, keepdims=True)
    rate = lax.rsqrt(row_var + 1e-06)
    return centered * rate, rate


def normalize_back(scaled, rate, grad, gain):
    inner = grad * gain
    first = jnp.mean(inner, axis=-1, keepdims=True)
    second = jnp.mean(inner * scaled, axis=-1, keepdims=True)
    return (
        rate * (inner - first - scaled * second),
        jnp.sum(grad * scaled, axis=0, keepdims=True),
        jnp.sum(grad, axis=0, keepdims=True),
    )


class Tower:
    def __init__(self, **refs):
        self.__dict__.update(refs)

    def unpack(self):
        turned = jnp.transpose(self.w[:, COL_VECTORS : COL_VECTORS + 128].astype(jnp.float32))
        self.vec[0:8, :] = turned[0:8]
        packed = self.w[:, COL_QUERY : COL_QUERY + 128].astype(jnp.float32)
        total = jnp.sum(packed.reshape(32, 24, 128), axis=0)
        query = total[0:6] + total[6:12]
        row = jnp.concatenate([query[i : i + 1] for i in range(6)], axis=1)
        self.vec[8:16, :] = jnp.broadcast_to(row, (8, 768)).astype(jnp.bfloat16).astype(jnp.float32)

    def norm(self, source, gain, bias, out):
        def body(index):
            rows = chunk_rows(index)
            scaled, _ = normalize(source[rows, :].astype(jnp.float32))
            out[rows, :] = (scaled * gain + bias).astype(jnp.bfloat16)

        loop(TOKENS // CHUNK, body)

    def first_norm(self):
        self.norm(self.x, self.vec[0:1, :], self.vec[1:2, :], self.h)

    def project(self, plan=None):
        def body(index):
            self.qkv[:, columns(index)] = dot(self.h[...], self.w[:, columns(index)]).astype(jnp.bfloat16)

        loop(9, body, plan)

    def pair_of(self, pair, which):
        return self.qkv[:, columns(pair, which * D, 128)]

    def attend(self, plan=None):
        lanes = lax.broadcasted_iota(jnp.int32, (TOKENS, 128), 1)

        def body(pair):
            queries = self.pair_of(pair, 0) * jnp.bfloat16(SCALE)
            keys = self.pair_of(pair, 1)
            values_turned = jnp.transpose(self.pair_of(pair, 2))
            mixed = []
            for head in range(2):
                mine = (lanes < 64) if head == 0 else (lanes >= 64)
                masked = jnp.where(mine, queries, jnp.bfloat16(0))
                scores = dot(keys, masked, NT)
                most = jnp.max(scores, axis=0, keepdims=True)
                expos = jnp.exp(scores - most)
                total = jnp.sum(expos, axis=0, keepdims=True)
                part = dot(values_turned[head * 64 : head * 64 + 64], expos.astype(jnp.bfloat16))
                mixed.append(part * (1.0 / total))
                self.lse[pl.ds(pair * 2 + head, 1), :] = most + jnp.log(total)
            self.a[:, columns(pair, 0, 128)] = jnp.transpose(
                jnp.concatenate(mixed, axis=0)
            ).astype(jnp.bfloat16)

        loop(6, body, plan)

    def attend_out(self, plan=None):
        def body(index):
            self.r[:, columns(index)] = self.x[:, columns(index)].astype(jnp.float32) + dot(
                self.a[...], self.w[:, columns(index, COL_OUT)]
            )

        loop(3, body, plan)
        self.norm(self.r, self.vec[2:3, :], self.vec[3:4, :], self.h2)

    def feed_up(self, plan=None):
        def body(index):
            value = dot(self.h2[...], self.w[:, columns(index, COL_UP)])
            square = value * value
            bend = jnp.tanh(GELU_A * value * (1.0 + GELU_B * square))
            half = 0.5 + 0.5 * bend
            self.g[:, columns(index)] = (value * half).astype(jnp.bfloat16)
            slope = half + 0.5 * value * (1.0 - bend * bend) * (
                GELU_A + 3.0 * GELU_A * GELU_B * square
            )
            self.gp[:, columns(index)] = slope.astype(jnp.bfloat16)

        loop(12, body, plan)

    def feed_down(self, plan=None):
        def body(index):
            self.y[:, columns(index)] = self.r[:, columns(index)] + dot(
                self.g[...], self.w[columns(index), COL_DOWN : COL_DOWN + FF], NT
            )

        loop(3, body, plan)
        self.norm(self.y, self.vec[4:5, :], self.vec[5:6, :], self.f)

    def pool_project(self, plan=None):
        def body(index):
            self.kvp[:, columns(index)] = dot(
                self.f[...], self.w[:, columns(index, COL_MAP_KV)]
            ).astype(jnp.bfloat16)

        loop(6, body, plan)

    def pool(self, signs, temperature, offset, images):
        head = lax.broadcasted_iota(jnp.int32, (16, D), 0)
        owner = lax.broadcasted_iota(jnp.int32, (16, D), 1) // HEAD_DIM
        own = head == owner
        heads_query = jnp.where(own, self.vec[8:9, :], 0.0).astype(jnp.bfloat16)
        keys, values = self.kvp[:, :D], self.kvp[:, D:]
        scores = dot(heads_query, keys, NT) * SCALE
        expos = jnp.exp(scores - jnp.max(scores, axis=1, keepdims=True))
        probs = expos / jnp.sum(expos, axis=1, keepdims=True)
        probs_high = probs.astype(jnp.bfloat16)
        probs_low = (probs - probs_high.astype(jnp.float32)).astype(jnp.bfloat16)
        spread = dot(probs_high, values) + dot(probs_low, values)
        pooled = jnp.sum(jnp.where(own, spread, 0.0), axis=0, keepdims=True)
        pooled_b = pooled.astype(jnp.bfloat16)
        w_out = self.w[:, COL_MAP_OUT : COL_MAP_OUT + D]
        many = jnp.broadcast_to(pooled, (16, D)).astype(jnp.bfloat16)
        embed = dot(many, w_out)[0:1]
        rate = lax.rsqrt(jnp.sum(embed * embed, axis=1, keepdims=True) + 1e-06)
        unit = jnp.broadcast_to(embed * rate, (16, D)).astype(jnp.bfloat16)
        cosine = dot(unit, self.cap[...], NT)[0:1]
        heat = jnp.exp(temperature)
        logits = heat * cosine + offset
        turned = -signs * logits
        losses = jnp.maximum(turned, 0.0) + jnp.log1p(jnp.exp(-jnp.abs(turned)))
        loss = jnp.sum(jnp.where(signs == 0.0, 0.0, losses), axis=1, keepdims=True) / images
        grad_logits = -signs * (1.0 / (1.0 + jnp.exp(-turned))) / images
        grad_heat = jnp.sum(grad_logits * cosine * heat, axis=1, keepdims=True)
        grad_offset = jnp.sum(grad_logits, axis=1, keepdims=True)
        grad_cosine = jnp.broadcast_to(grad_logits * heat, (16, cosine.shape[1])).astype(jnp.bfloat16)
        grad_unit = dot(grad_cosine, self.cap[...])[0:1]
        grad_embed = rate * grad_unit - embed * (
            rate * rate * rate * jnp.sum(grad_unit * embed, axis=1, keepdims=True)
        )
        grad_many = jnp.broadcast_to(grad_embed, (16, D)).astype(jnp.bfloat16)
        grad_pooled = dot(grad_many, w_out, NT).astype(jnp.bfloat16).astype(jnp.float32)
        heads_grad = jnp.where(own, grad_pooled, 0.0).astype(jnp.bfloat16)
        grad_probs = dot(heads_grad, values, NT)
        centre = jnp.sum(probs * grad_probs, axis=1, keepdims=True)
        grad_scores = (probs * (grad_probs - centre)).astype(jnp.bfloat16)
        query_spread = dot(grad_scores, keys) * SCALE
        grad_query = jnp.sum(jnp.where(own, query_spread, 0.0), axis=0, keepdims=True)
        self.small_own[0:1, :] = pooled_b.astype(jnp.float32)
        self.small_own[1:2, :] = grad_many[0:1].astype(jnp.float32)
        self.small_own[2:3, :] = grad_query
        lane = lax.broadcasted_iota(jnp.int32, (1, D), 1)
        self.small_own[3:4, :] = jnp.where(
            lane == 0, loss, jnp.where(lane == 1, grad_heat, jnp.where(lane == 2, grad_offset, 0.0))
        )
        self.small_own[4:8, :] = jnp.zeros((4, D), jnp.float32)
        self.kvp[:, :D] = (dot(grad_scores, heads_query, TN) * SCALE).astype(jnp.bfloat16)
        both_probs = jnp.concatenate([probs_high, probs_low], axis=0)
        both_grads = jnp.concatenate([heads_grad, heads_grad], axis=0)
        self.kvp[:, D:] = dot(both_probs, both_grads, TN).astype(jnp.bfloat16)

    def turn(self, source):
        def body(index):
            self.turned[columns(index), :] = jnp.transpose(source[:, columns(index)])

        loop(3, body)

    def weight_grad(self, first, source, tiles, plan=None):
        def body(index):
            self.w[:, columns(index, first)] = dot(
                self.turned[...], source[:, columns(index)]
            ).astype(jnp.bfloat16)

        loop(tiles, body, plan)

    def input_grad(self, source, first, width, plan=None):
        def body(index):
            self.acc[:, columns(index)] = dot(
                source[...], self.w[columns(index), first : first + width], NT
            )

        loop(3, body, plan)

    def norm_back(self, source, added, number, out, rounded):
        gain = self.vec[2 * number : 2 * number + 1, :]

        def body(index, carry):
            rows = chunk_rows(index)
            scaled, rate = normalize(source[rows, :].astype(jnp.float32))
            grad, grad_gain, grad_bias = normalize_back(scaled, rate, self.acc[rows, :], gain)
            if added is not None:
                grad = grad + added[rows, :]
            if out is not None:
                out[rows, :] = grad
            rounded[rows, :] = grad.astype(jnp.bfloat16)
            return carry[0] + grad_gain, carry[1] + grad_bias

        zero = jnp.zeros((1, D), jnp.float32)
        grad_gain, grad_bias = lax.fori_loop(0, TOKENS // CHUNK, body, (zero, zero))
        self.vec_grad[2 * number : 2 * number + 1, :] = grad_gain
        self.vec_grad[2 * number + 1 : 2 * number + 2, :] = grad_bias

    def pool_back(self, plan=None, after=None):
        self.input_grad(self.kvp, COL_MAP_KV, 2 * D)
        self.turn(self.f)
        self.weight_grad(COL_MAP_KV, self.kvp, 6, plan)
        if after is not None:
            after()
        self.norm_back(self.y, None, 2, self.y, self.f)

    def down_back(self, start, tiles, plan=None):
        def body(step):
            index = start + step
            here = columns(index)
            grad = dot(self.f[...], self.w[:, columns(index, COL_DOWN)])
            self.gp[:, here] = (grad * self.gp[:, here].astype(jnp.float32)).astype(jnp.bfloat16)
            self.w[:, columns(index, COL_DOWN)] = dot(self.turned[...], self.g[:, here]).astype(
                jnp.bfloat16
            )

        loop(tiles, body, plan)

    def up_input(self, plan=None):
        self.input_grad(self.gp, COL_UP, FF, plan)

    def up_weight(self, start, tiles, plan=None):
        def body(step):
            index = start + step
            self.w[:, columns(index, COL_UP)] = dot(
                self.turned[...], self.gp[:, columns(index)]
            ).astype(jnp.bfloat16)

        loop(tiles, body, plan)

    def up_norm(self):
        self.norm_back(self.r, self.y, 1, self.r, self.f)

    def out_back(self, plan=None):
        self.turn(self.a)

        def body(index):
            self.a[:, columns(index)] = dot(
                self.f[...], self.w[columns(index), COL_OUT : COL_OUT + D], NT
            ).astype(jnp.bfloat16)

        loop(3, body)
        self.weight_grad(COL_OUT, self.f, 3, plan)

    def attend_back(self, plan=None):
        lanes = lax.broadcasted_iota(jnp.int32, (TOKENS, 128), 1)

        def body(pair):
            queries = self.pair_of(pair, 0) * jnp.bfloat16(SCALE)
            keys, values = self.pair_of(pair, 1), self.pair_of(pair, 2)
            grads = self.a[:, columns(pair, 0, 128)]
            keys_turned = jnp.transpose(keys)
            grad_queries = []
            grad_keys = None
            for head in range(2):
                mine = (lanes < 64) if head == 0 else (lanes >= 64)
                masked = jnp.where(mine, queries, jnp.bfloat16(0))
                masked_grads = jnp.where(mine, grads, jnp.bfloat16(0))
                scores = dot(keys, masked, NT)
                probs = jnp.exp(scores - self.lse[pl.ds(pair * 2 + head, 1), :])
                value_part = dot(probs.astype(jnp.bfloat16), masked_grads)
                grad_probs = dot(values, masked_grads, NT)
                centre = jnp.sum(probs * grad_probs, axis=0, keepdims=True)
                grad_scores = (probs * (grad_probs - centre)).astype(jnp.bfloat16)
                key_part = dot(grad_scores, masked)
                grad_queries.append(dot(keys_turned[head * 64 : head * 64 + 64], grad_scores))
                if head == 0:
                    grad_keys, grad_values = key_part, value_part
                else:
                    grad_keys, grad_values = grad_keys + key_part, grad_values + value_part
            self.qkv[:, columns(pair, 0, 128)] = (
                jnp.transpose(jnp.concatenate(grad_queries, axis=0)) * SCALE
            ).astype(jnp.bfloat16)
            self.qkv[:, columns(pair, D, 128)] = grad_keys.astype(jnp.bfloat16)
            self.qkv[:, columns(pair, 2 * D, 128)] = grad_values.astype(jnp.bfloat16)

        loop(6, body, plan)

    def project_input(self, plan=None):
        self.first_norm()
        self.input_grad(self.qkv, 0, 3 * D, plan)
        self.turn(self.h)
        self.norm_back(self.x, self.r, 0, None, self.h)

    def project_weight(self, start, tiles, plan=None):
        def body(index):
            self.w[:, columns(index, start * TILE)] = dot(
                self.turned[...], self.qkv[:, columns(index, start * TILE)]
            ).astype(jnp.bfloat16)

        loop(tiles, body, plan)

    def vectors_back(self):
        packed = jnp.concatenate([self.vec_grad[...], jnp.zeros((120, D), jnp.float32)], axis=0)
        self.w[:, COL_VECTORS : COL_VECTORS + 128] = jnp.transpose(packed).astype(jnp.bfloat16)
        self.w[:, COL_QUERY : COL_QUERY + 128] = jnp.zeros((D, 128), jnp.bfloat16)


def spread_steps(steps, count):
    plan = {}
    for at, step in enumerate(steps):
        plan.setdefault(min(count - 1, at * count // max(len(steps), 1)), []).append(step)
    return plan


TOWER_REFS = (
    ("w", "x", "cap", "h", "qkv", "a", "r", "h2", "g", "gp", "y", "f", "kvp", "lse", "turned", "acc", "vec", "vec_grad", "small_own")
)


def layer_kernel(
    master, tokens, captions, vectors, labels, scalars,
    share_out, vector_out, facts, patch_out, *scratch,
):
    p = Place()
    t = Tower(**dict(zip(TOWER_REFS, scratch)))
    scratch = scratch[len(TOWER_REFS) :]
    stage, small, pair_a, pair_b, b_in, z_in, a_in, last, mine, everyone = scratch[:10]
    share, extra, caps, map_q, map_out, map_q_share, signs = scratch[10:17]
    swap_sems, token_sems, patch_sems, own_sems, send_sem, recv_sem, grant = scratch[17:24]
    gather_s, scatter_s = scratch[24:31], scratch[31:]
    map_q_at = 4 * D + 2 * FF
    map_q_copy = pltpu.make_async_copy(
        master.at[:, map_q_at : map_q_at + D], map_q, own_sems.at[0]
    )
    map_q_copy.start()
    greet_all(p)

    own_vectors = jnp.transpose(
        jnp.concatenate([vectors[...], jnp.zeros((121, 24), jnp.float32)], axis=0)
    )
    own_vectors = own_vectors.astype(jnp.bfloat16).astype(jnp.float32)
    map_q_copy.wait()
    map_q[...] = map_q[...].astype(jnp.bfloat16).astype(jnp.float32)
    part = jnp.sum(own_vectors[:, 6:7] * map_q[...], axis=0, keepdims=True)
    high = part.astype(jnp.bfloat16).astype(jnp.float32)
    for side in range(6):
        lanes = slice(side * 128, side * 128 + 128)
        extra[side : side + 1, 128:256] = high[:, lanes]
        extra[6 + side : 7 + side, 128:256] = (part - high)[:, lanes]
    extra[12:24, 128:256] = jnp.zeros((12, 128), jnp.float32)
    extra[:, 0:128] = own_vectors
    each = captions.shape[0]
    caps[...] = jnp.concatenate(
        [unit_rows(captions[...].astype(jnp.float32)), jnp.zeros((64 - each, D), jnp.float32)], axis=0
    ).astype(jnp.bfloat16)
    slot = lax.broadcasted_iota(jnp.int32, (8 * each, 512), 1)
    within = (slot >> 7) * 16 + (slot & 15)
    source = ((slot >> 5) & 3) * (2 * each) + ((slot >> 4) & 1) * each + within
    label = lax.broadcasted_iota(jnp.int32, (8 * each, 512), 0)
    pick = ((label == source) & (within < each)).astype(jnp.float32).astype(jnp.bfloat16)
    row = 2.0 * labels[pl.ds(p.blk, 1), :].astype(jnp.float32) - 1.0
    signs[...] = dot(jnp.broadcast_to(row, (16, 8 * each)).astype(jnp.bfloat16), pick)
    all_greeted()

    count = len(GATHER_SECTIONS)
    gathers, swaps = [], []
    pieces = (
        (master, 0, 0, 3 * D),
        (extra, 0, 3 * D, 256),
        (master, 3 * D, COL_OUT, D + 2 * FF),
        (master, map_q_at + D, COL_MAP_KV, 3 * D),
    )
    for number, (first, width, z_first) in enumerate(GATHER_SECTIONS):
        swaps.append(
            Swap(p, pieces, stage, 0, 24, first, width, first // 2, swap_sems.at[number])
        )
        swaps[-1].begin()
        gathers.append(
            Gather(p, t.w, CHIP_ROWS, first, width, z_first, [s.at[number] for s in gather_s])
        )
    own_caps = caps.at[pl.ds(aligned(p.blk * 16, 16), 16), :]
    swaps.append(
        Swap(p, ((own_caps, 0, 0, D),), t.cap, p.chip * 32, 16, 0, D, None, swap_sems.at[count])
    )
    swaps[-1].begin()
    gathers.append(Gather(p, t.cap, 32, 0, D, True, [s.at[count] for s in gather_s]))
    token_copies = []
    for step in range(1, 4):
        to = lax.rem(p.blk + step, 4)
        token_copies.append(
            remote(
                tokens.at[to],
                t.x.at[pl.ds(aligned(p.blk * 144, 144), 144), :],
                token_sems.at[0, step - 1],
                token_sems.at[1, step - 1],
                {"blk": to},
            )
        )
        token_copies[-1].start()
    own_tokens = pltpu.make_async_copy(
        tokens.at[p.blk], t.x.at[pl.ds(aligned(p.blk * 144, 144), 144), :], token_sems.at[0, 3]
    )
    own_tokens.start()

    def ready(number):
        swaps[number].finish()
        if number < count:
            first, width, _ = GATHER_SECTIONS[number]
            t.w[
                pl.ds(aligned(p.chip * 48, 48), 48), pl.ds(gathers[number].mine, width // 2)
            ] = stage[:, first // 2 : first // 2 + width // 2].astype(jnp.bfloat16)
        gathers[number].begin()

    order = []
    for number, gather in enumerate(gathers):
        for at, step in enumerate(gather.steps()):
            call = step if at else (lambda number=number: ready(number))
            order.append((gather_key(number, at), number, at, call))
    order.sort(key=lambda entry: entry[:3])
    ends = [
        max(i for i, entry in enumerate(order) if entry[1] <= number)
        for number in range(count + 1)
    ]

    def between(number):
        return [entry[3] for entry in order[ends[number - 1] + 1 : ends[number] + 1]]

    for entry in order[: ends[0] + 1]:
        entry[3]()
    for step in range(3):
        source = lax.rem(p.blk + 3 - step, 4)
        landed = t.x.at[pl.ds(aligned(source * 144, 144), 144), :]
        remote(
            landed, landed, token_sems.at[0, step], token_sems.at[1, step], {"blk": source}
        ).wait_recv()
    own_tokens.wait()
    gathers[0].finish()

    t.unpack()
    t.first_norm()
    t.project()
    t.attend(spread_steps(between(1), 6))
    gathers[1].finish()
    t.attend_out()
    t.feed_up(spread_steps(between(2), 12))
    gathers[2].finish()
    t.feed_down(spread_steps(between(3), 3))
    gathers[3].finish()
    t.pool_project(spread_steps(between(4), 6))
    gathers[4].finish()
    t.vec_grad[...] = jnp.zeros((8, D), jnp.float32)
    images = tokens.shape[0] * 8
    t.pool(signs[0:1, :], jnp.full((1, 512), scalars[0], jnp.float32), scalars[1], images)
    swap = Swap(
        p, ((t.small_own, 0, 0, D),), small, p.chip * 16, 8, 0, D, None, swap_sems.at[count + 1]
    )
    swap.begin()
    small_gather = Gather(p, small, 16, 0, D, True, [s.at[count + 1] for s in gather_s])
    small_steps = small_gather.steps()
    gathers[3].sent()

    sections = []
    for number, (first, width, z_first) in enumerate(SCATTER_SECTIONS):
        half = width // 2
        which, at = PAIR_PLACES[number]
        pair_in = (pair_a, pair_b)[which].at[:, at : at + half]
        if number < 4:
            others = (b_in[number], a_in[number], z_in[number])
        else:
            here = slice(LATE_PLACES[number - 4], LATE_PLACES[number - 4] + half)
            others = (
                t.g.at[0:384, here],
                t.g.at[384 : 432 if z_first else 576, here],
                t.gp.at[0 : 288 if z_first else 144, here],
            )
        bufs = (pair_in, *others, last[number])
        sections.append(
            Scatter(p, t.w, share, first, width, z_first, bufs, [s.at[number] for s in scatter_s])
        )

    def small_begin():
        swap.finish()
        small_steps[0]()

    links, program = Links(*LINK_SPEED), Program()
    timed = []

    def leaves(section, number):
        timed.append((section, program.now, SCATTER_SECTIONS[number][1]))

    leaves(sections[0], 0)
    program.want(zip((0.5, 1.5, 4.5, 7.0, 9.5, 12.0), [small_begin] + small_steps[1:]))
    program.gap(2.5)
    program.loop("down_first", 6, 0.75)
    leaves(sections[1], 1)
    program.loop("down_second", 6, 0.75)
    leaves(sections[2], 2)
    program.loop("up_input", 3, 1.4)
    program.gap(0.5)
    program.loop("up_first", 6, 0.46)
    leaves(sections[3], 3)
    program.loop("up_second", 6, 0.46)
    program.gap(1.7)
    leaves(sections[4], 4)
    program.loop("out", 3, 1.1)
    leaves(sections[5], 5)
    program.loop("attend", 6, 2.05)
    program.gap(1.0)
    program.loop("project_input", 3, 1.0)
    program.gap(2.2)
    program.loop("front", 5, 0.5)
    leaves(sections[6], 6)
    program.loop("end", 4, 0.5)
    program.gap(1.0)
    leaves(sections[7], 7)
    for entry in timed:
        program.want(links.steps(*entry))
    program.settle()
    plans = program.plans
    t.pool_back(None, sections[0].begin)
    t.turn(t.f)
    gathers[2].sent()
    t.down_back(0, 6, plans["down_first"])
    sections[1].begin()
    t.down_back(6, 6, plans["down_second"])
    sections[2].begin()
    t.up_input(plans["up_input"])
    t.turn(t.h2)
    gathers[1].sent()
    t.up_weight(0, 6, plans["up_first"])
    sections[3].begin()
    t.up_weight(6, 6, plans["up_second"])
    levels = [p.on_level(lax.rem(p.z + step, 4)) for step in range(1, 4)]
    for device in (p.sibling, p.a_near, p.b_near, *levels):
        pl.semaphore_signal(grant, inc=1, device_id=device, device_id_type=MESH)
    t.up_norm()
    pl.semaphore_wait(grant, 6)
    sections[4].begin()
    t.out_back(plans["out"])
    sections[5].begin()
    t.attend_back(plans["attend"])
    t.project_input(plans["project_input"])
    patch_copies = []
    for step in range(1, 4):
        to = lax.rem(p.blk + step, 4)
        patch_copies.append(
            remote(
                t.h.at[pl.ds(aligned(to * 144, 144), 144), :],
                patch_out.at[p.blk],
                patch_sems.at[0, step - 1],
                patch_sems.at[1, step - 1],
                {"blk": to},
            )
        )
        patch_copies[-1].start()
    own_patch = pltpu.make_async_copy(
        t.h.at[pl.ds(aligned(p.blk * 144, 144), 144), :], patch_out.at[p.blk], patch_sems.at[0, 3]
    )
    own_patch.start()
    gathers[0].sent()
    t.project_weight(0, 5, plans["front"])
    sections[6].begin()
    t.project_weight(5, 4, plans["end"])
    t.vectors_back()
    sections[7].begin()
    small_gather.finish()
    probe_share, square = small_tail(
        p, small, map_q[...], own_vectors[:, 6:7], map_out, map_q_share
    )
    small_gather.sent()
    gathers[4].sent()
    for copy in token_copies:
        copy.wait_send()
    outs = [
        pltpu.make_async_copy(source, share_out.at[:, target : target + D], own_sems.at[4 + number])
        for number, (source, target) in enumerate(
            ((map_q_share, map_q_at), (map_out, map_q_at + 3 * D))
        )
    ]
    for out in outs:
        out.start()
    for step in program.tail[:-2]:
        step()
    for step, copy in enumerate(patch_copies):
        source = lax.rem(p.blk + 3 - step, 4)
        landed = patch_out.at[source]
        remote(
            landed, landed, patch_sems.at[0, step], patch_sems.at[1, step], {"blk": source}
        ).wait_recv()
        copy.wait_send()
    own_patch.wait()
    square = square_share(share, square, COL_OUT // 256, SCATTER_COLS // 256)
    for step in program.tail[-2:]:
        step()
    spread = Spread(p, mine, everyone, send_sem, recv_sem)
    spread.begin(jnp.full((8, 128), square_share(share, square, 0, COL_OUT // 256), jnp.float32))
    for number, (source, target, width) in enumerate(
        ((0, 0, 3 * D), (COL_OUT, 3 * D, D + 2 * FF), (COL_MAP_KV, map_q_at + D, 2 * D))
    ):
        outs.append(
            pltpu.make_async_copy(
                share.at[:, source : source + width],
                share_out.at[:, target : target + width],
                own_sems.at[1 + number],
            )
        )
        outs[-1].start()
    lane = lax.broadcasted_iota(jnp.int32, (24, 128), 1)
    vector_out[...] = jnp.transpose(
        jnp.where(lane == 6, probe_share, share[:, COL_VECTORS : COL_VECTORS + 128])
    )[0:8]
    sums, norm = spread.finish(small)
    facts[...] = jnp.concatenate([jnp.broadcast_to(sums[:, :128], (7, 128)), norm[:1]], axis=0)
    for out in outs:
        out.wait()


def layer_call(master, tokens, captions, vectors, labels, scalars):
    dma = pltpu.SemaphoreType.DMA
    f32 = jnp.float32
    gathers = len(GATHER_SECTIONS) + 2
    count = len(SCATTER_SECTIONS)
    widths = [entry[1] // 2 for entry in SCATTER_SECTIONS]

    def vm(*shape, dt=jnp.bfloat16):
        return pltpu.VMEM(shape, dt)

    vmem = pl.BlockSpec(memory_space=pltpu.VMEM)
    return pl.pallas_call(
        layer_kernel,
        out_shape=(
            jax.ShapeDtypeStruct((24, 8 * D + 2 * FF), f32),
            jax.ShapeDtypeStruct((8, 24), f32),
            jax.ShapeDtypeStruct((8, 128), f32),
            jax.ShapeDtypeStruct((4, 144, D), jnp.bfloat16),
        ),
        in_specs=[
            pl.BlockSpec(memory_space=pl.ANY),
            pl.BlockSpec(memory_space=pl.ANY),
            vmem,
            vmem,
            vmem,
            pl.BlockSpec(memory_space=pltpu.SMEM),
        ],
        out_specs=(
            pl.BlockSpec(memory_space=pl.ANY),
            vmem,
            vmem,
            pl.BlockSpec(memory_space=pl.ANY),
        ),
        scratch_shapes=[
            vm(D, GATHER_COLS),
            vm(TOKENS, D),
            vm(512, D),
            vm(TOKENS, D),
            vm(TOKENS, 3 * D),
            vm(TOKENS, D),
            vm(TOKENS, D, dt=f32),
            vm(TOKENS, D),
            vm(TOKENS, FF),
            vm(TOKENS, FF),
            vm(TOKENS, D, dt=f32),
            vm(TOKENS, D),
            vm(TOKENS, 2 * D),
            vm(16, TOKENS, dt=f32),
            vm(D, TOKENS),
            vm(TOKENS, D, dt=f32),
            vm(16, D, dt=f32),
            vm(8, D, dt=f32),
            vm(8, D, dt=f32),
            vm(48, GATHER_COLS // 2, dt=f32),
            vm(256, D, dt=f32),
            vm(D, 1920),
            vm(D, 1536),
            [vm(384, w) for w in widths[:4]],
            [vm(288 if entry[2] else 144, entry[1] // 2) for entry in SCATTER_SECTIONS[:4]],
            [vm(48 if entry[2] else 192, entry[1] // 2) for entry in SCATTER_SECTIONS[:4]],
            [vm(48, w, dt=f32) for w in widths],
            vm(8, 128, dt=f32),
            vm(31, 8, 128, dt=f32),
            vm(24, SCATTER_COLS, dt=f32),
            vm(24, 256, dt=f32),
            vm(64, D),
            vm(24, D, dt=f32),
            vm(24, D, dt=f32),
            vm(24, D, dt=f32),
            vm(16, 512, dt=f32),
            dma((gathers, 4)),
            dma((2, 4)),
            dma((2, 4)),
            dma((6,)),
            dma,
            dma,
            pltpu.SemaphoreType.REGULAR,
            *gather_sems(gathers),
            dma((count, 2)),
            dma((count, 2, 2)),
            dma((count, 2)),
            dma((count, 2, 2, 3)),
            dma((count, 2)),
        ],
        compiler_params=pltpu.CompilerParams(
            collective_id=0, has_side_effects=True, vmem_limit_bytes=63 * 2**20
        ),
        name="layer_step",
    )(master, tokens, captions, vectors, labels, scalars)


def local_kernel(
    patch_tokens,
    captions,
    pair_labels,
    master_weights,
    first_moments,
    second_moments,
    master_vectors,
    vector_first,
    vector_second,
    loss_scalars,
    scalar_first,
    scalar_second,
):
    weight_share, vector_share, facts, patch_grad = layer_call(
        master_weights, patch_tokens, captions, master_vectors.T, pair_labels, loss_scalars
    )
    vector_share = vector_share[:7].T
    patch_grad = patch_grad.astype(jnp.float32)
    loss_total, scalar_total, grad_norm = facts[0, 0], facts[0, 1:3], facts[7, 0]
    factor = CLIP_AT / jnp.maximum(grad_norm, CLIP_AT)
    new_w, new_wm, new_wv = adamw(
        master_weights, weight_share * factor, first_moments, second_moments, 0.03, 0.1
    )
    new_v, new_vm, new_vv = adamw(
        master_vectors, vector_share * factor, vector_first, vector_second, 0.3, 0.0
    )
    new_s, new_sm, new_sv = adamw(
        loss_scalars, scalar_total * factor, scalar_first, scalar_second, 0.3, 0.0
    )
    return (
        loss_total,
        grad_norm,
        patch_grad,
        new_w,
        new_wm,
        new_wv,
        new_w.astype(jnp.bfloat16),
        new_v,
        new_vm,
        new_vv,
        new_v.astype(jnp.bfloat16),
        new_s,
        new_sm,
        new_sv,
    )


def solution(mesh):
    in_specs = (
        P("img", "blk", None),
        P("img", None),
        P("img", None),
        P(("blk", "img"), None),
        P(("blk", "img"), None),
        P(("blk", "img"), None),
        P(("blk", "img"), None),
        P(("blk", "img"), None),
        P(("blk", "img"), None),
        P(),
        P(),
        P(),
    )
    out_specs = (
        P(),
        P(),
        P("img", "blk", None),
        P(("blk", "img"), None),
        P(("blk", "img"), None),
        P(("blk", "img"), None),
        P(("blk", "img"), None),
        P(("blk", "img"), None),
        P(("blk", "img"), None),
        P(("blk", "img"), None),
        P(("blk", "img"), None),
        P(),
        P(),
        P(),
    )
    body = local_kernel if tuple(mesh.shape.values()) == (4, 8) else local
    return jax.shard_map(body, mesh=mesh, in_specs=in_specs, out_specs=out_specs, check_vma=False)
```

```python
import functools

import jax
import jax.numpy as jnp
from jax import lax
from jax.experimental import pallas as pl
from jax.experimental.pallas import tpu as pltpu
from jax.sharding import PartitionSpec as P

D = 768
HEADS = 12
HEAD_DIM = 64
FF = 3072
STEP = 10


BETA_ONE = 0.9
BETA_TWO = 0.999
EPS_ADAM = 1e-08
CLIP_AT = 1.0


def layer_norm(values, gain_vec, bias_vec):
    row_mean = jnp.mean(values, axis=-1, keepdims=True)
    centered = values - row_mean
    row_var = jnp.mean(centered * centered, axis=-1, keepdims=True)
    return centered * lax.rsqrt(row_var + 1e-06) * gain_vec + bias_vec


def unit_rows(pooled):
    return pooled * lax.rsqrt(jnp.sum(pooled * pooled, axis=-1, keepdims=True) + 1e-06)


def attend(queries, keys_all, values_all):
    scale = HEAD_DIM ** (-0.5)
    scores = (
        jnp.einsum("iqhe,ikhe->ihqk", queries, keys_all, preferred_element_type=jnp.float32) * scale
    )
    row_max = jnp.max(scores, axis=-1, keepdims=True)
    expos = jnp.exp(scores - row_max)
    row_sum = jnp.sum(expos, axis=-1, keepdims=True)
    attn_probs = (expos / row_sum).astype(jnp.bfloat16)
    mixed_out = jnp.einsum(
        "ihqk,ikhe->iqhe", attn_probs, values_all, preferred_element_type=jnp.float32
    )
    return (mixed_out.astype(jnp.bfloat16), row_max + jnp.log(row_sum))


def attend_back(queries, keys_all, values_all, log_norm, grad_mixed):
    scale = HEAD_DIM ** (-0.5)
    scores = (
        jnp.einsum("iqhe,ikhe->ihqk", queries, keys_all, preferred_element_type=jnp.float32) * scale
    )
    attn_probs = jnp.exp(scores - log_norm)
    grad_values = jnp.einsum(
        "ihqk,iqhe->ikhe",
        attn_probs.astype(jnp.bfloat16),
        grad_mixed,
        preferred_element_type=jnp.float32,
    )
    grad_probs = jnp.einsum(
        "iqhe,ikhe->ihqk", grad_mixed, values_all, preferred_element_type=jnp.float32
    )
    centre = jnp.sum(attn_probs * grad_probs, axis=-1, keepdims=True)
    grad_scores = (attn_probs * (grad_probs - centre)).astype(jnp.bfloat16)
    grad_queries = (
        jnp.einsum("ihqk,ikhe->iqhe", grad_scores, keys_all, preferred_element_type=jnp.float32)
        * scale
    )
    grad_keys = (
        jnp.einsum("ihqk,iqhe->ikhe", grad_scores, queries, preferred_element_type=jnp.float32)
        * scale
    )
    return (grad_queries, grad_keys, grad_values)


def adamw(parameter, gradient, moment_one, moment_two, step_rate, decay_rate):
    moment_one = BETA_ONE * moment_one + (1.0 - BETA_ONE) * gradient
    moment_two = BETA_TWO * moment_two + (1.0 - BETA_TWO) * gradient * gradient
    first_hat = moment_one / (1.0 - BETA_ONE**STEP)
    second_hat = moment_two / (1.0 - BETA_TWO**STEP)
    updated = parameter - step_rate * (
        first_hat / (jnp.sqrt(second_hat) + EPS_ADAM) + decay_rate * parameter
    )
    return (updated, moment_one, moment_two)


def local(
    patch_tokens,
    captions,
    pair_labels,
    master_weights,
    first_moments,
    second_moments,
    master_vectors,
    vector_first,
    vector_second,
    loss_scalars,
    scalar_first,
    scalar_second,
):
    blocks = lax.axis_size("blk")
    block = lax.axis_index("blk")
    all_images = patch_tokens.shape[0] * lax.axis_size("img")
    images = patch_tokens.shape[0] // blocks
    length = patch_tokens.shape[1] * blocks
    scale = HEAD_DIM ** (-0.5)
    both = ("blk", "img")
    rows = master_weights.shape[0]
    first_row = lax.axis_index(both) * rows
    patch_tokens = lax.all_to_all(patch_tokens, "blk", 0, 1, tiled=True)
    pair_labels = lax.dynamic_slice_in_dim(pair_labels, block * images, images, 0)
    rounded = master_weights.astype(jnp.bfloat16)
    full_vectors = lax.all_gather(master_vectors.astype(jnp.bfloat16), both, axis=0, tiled=True)
    vectors = full_vectors.astype(jnp.float32)

    def gather(start, stop):
        return lax.all_gather(rounded[:, start:stop], both, axis=0, tiled=True)

    w_front = gather(0, 4 * D)
    w_qkv = w_front[:, : 3 * D]
    w_out = w_front[:, 3 * D :]
    w_up = gather(4 * D, 4 * D + FF)
    w_down = gather(4 * D + FF, 4 * D + 2 * FF)
    own_map_q = rounded[:, 4 * D + 2 * FF : 5 * D + 2 * FF]
    w_map = gather(5 * D + 2 * FF, 8 * D + 2 * FF)
    w_map_kv = w_map[:, : 2 * D]
    w_map_out = w_map[:, 2 * D :]
    own_vectors = master_vectors.astype(jnp.bfloat16)
    tokens = patch_tokens.astype(jnp.float32)
    normed, norm_one_pull = jax.vjp(layer_norm, tokens, vectors[:, 0], vectors[:, 1])
    normed_b = normed.astype(jnp.bfloat16)
    qkv_b = jnp.einsum("ipd,dc->ipc", normed_b, w_qkv, preferred_element_type=jnp.float32).astype(
        jnp.bfloat16
    )
    queries = qkv_b[:, :, :D].reshape(images, length, HEADS, HEAD_DIM)
    keys_all = qkv_b[:, :, D : 2 * D].reshape(images, length, HEADS, HEAD_DIM)
    values_all = qkv_b[:, :, 2 * D :].reshape(images, length, HEADS, HEAD_DIM)
    mixed_heads, log_norm = attend(queries, keys_all, values_all)
    mixed_b = mixed_heads.reshape(images, length, D)
    residual = tokens + jnp.einsum(
        "ipd,dc->ipc", mixed_b, w_out, preferred_element_type=jnp.float32
    )
    hidden, norm_two_pull = jax.vjp(layer_norm, residual, vectors[:, 2], vectors[:, 3])
    hidden_b = hidden.astype(jnp.bfloat16)
    pre_act = jnp.einsum("ipd,df->ipf", hidden_b, w_up, preferred_element_type=jnp.float32)
    activation, gelu_pull = jax.vjp(jax.nn.gelu, pre_act)
    activation_b = activation.astype(jnp.bfloat16)
    layer_out = residual + jnp.einsum(
        "ipf,df->ipd", activation_b, w_down, preferred_element_type=jnp.float32
    )
    final_norm, norm_three_pull = jax.vjp(layer_norm, layer_out, vectors[:, 4], vectors[:, 5])
    final_b = final_norm.astype(jnp.bfloat16)
    map_kv = jnp.einsum("ipd,dc->ipc", final_b, w_map_kv, preferred_element_type=jnp.float32)
    map_kv = map_kv.astype(jnp.bfloat16).reshape(images, length, 2, HEADS, HEAD_DIM)
    probe_query = lax.psum(
        jnp.dot(own_vectors[:, 6], own_map_q, preferred_element_type=jnp.float32), both
    )
    probe_query = probe_query.astype(jnp.bfloat16).reshape(HEADS, HEAD_DIM)
    pool_scores = (
        jnp.einsum("he,iphe->ihp", probe_query, map_kv[:, :, 0], preferred_element_type=jnp.float32)
        * scale
    )
    row_max = jnp.max(pool_scores, axis=-1)
    row_sum = jnp.sum(jnp.exp(pool_scores - row_max[..., None]), axis=-1)
    pool_probs = jnp.exp(pool_scores - row_max[..., None]) / row_sum[..., None]
    map_values = map_kv[:, :, 1].astype(jnp.float32)
    pooled_part = jnp.einsum(
        "ihp,iphe->ihe", pool_probs, map_values, precision=lax.Precision.HIGHEST
    )
    pooled_heads = pooled_part.reshape(images, D)
    pooled_heads_b = pooled_heads.astype(jnp.bfloat16)
    pooled = jnp.dot(pooled_heads_b, w_map_out, preferred_element_type=jnp.float32)
    caption_all = lax.all_gather(captions, "img", axis=0, tiled=True).astype(jnp.float32)
    caption_unit = unit_rows(caption_all).astype(jnp.bfloat16)
    unit_image, unit_pull = jax.vjp(unit_rows, pooled)
    cosine = jnp.einsum(
        "id,cd->ic",
        unit_image.astype(jnp.bfloat16),
        caption_unit,
        preferred_element_type=jnp.float32,
    )
    signs = 2.0 * pair_labels.astype(jnp.float32) - 1.0

    def pair_loss(cosine_in, scalars_in):
        logits = jnp.exp(scalars_in[0]) * cosine_in + scalars_in[1]
        return jnp.sum(jax.nn.softplus(-signs * logits)) / all_images

    loss_local, loss_pull = jax.vjp(pair_loss, cosine, loss_scalars)
    grad_cosine, grad_scalars = loss_pull(jnp.ones((), jnp.float32))
    loss_total, scalar_total = lax.psum((loss_local, grad_scalars), both)
    grad_unit = jnp.einsum(
        "ic,cd->id",
        grad_cosine.astype(jnp.bfloat16),
        caption_unit,
        preferred_element_type=jnp.float32,
    )
    (grad_pooled,) = unit_pull(grad_unit)
    grad_pooled_b = grad_pooled.astype(jnp.bfloat16)
    pooled_all, grad_pooled_all = (
        lax.all_gather(pooled_heads_b, both, axis=0, tiled=True),
        lax.all_gather(grad_pooled_b, both, axis=0, tiled=True),
    )
    share_map_out = jnp.einsum(
        "id,ic->dc",
        lax.dynamic_slice_in_dim(pooled_all, first_row, rows, 1),
        grad_pooled_all,
        preferred_element_type=jnp.float32,
    )
    grad_heads_b = jnp.einsum(
        "ic,dc->id", grad_pooled_b, w_map_out, preferred_element_type=jnp.float32
    )
    grad_heads_b = grad_heads_b.astype(jnp.bfloat16).reshape(images, HEADS, HEAD_DIM)
    grad_heads = grad_heads_b.astype(jnp.float32)
    centre = jnp.sum(grad_heads * pooled_heads.reshape(images, HEADS, HEAD_DIM), axis=-1)
    grad_probs = jnp.einsum(
        "ihe,iphe->ihp", grad_heads_b, map_kv[:, :, 1], preferred_element_type=jnp.float32
    )
    grad_pool_scores = (pool_probs * (grad_probs - centre[..., None])).astype(jnp.bfloat16)
    grad_map_keys = (
        jnp.einsum(
            "ihp,he->iphe", grad_pool_scores, probe_query, preferred_element_type=jnp.float32
        )
        * scale
    )
    grad_map_values = jnp.einsum(
        "ihp,ihe->iphe", pool_probs, grad_heads, precision=lax.Precision.HIGHEST
    )
    grad_probe_query = (
        jnp.einsum(
            "ihp,iphe->he", grad_pool_scores, map_kv[:, :, 0], preferred_element_type=jnp.float32
        ).reshape(D)
        * scale
    )
    grad_map_kv = (
        jnp.stack([grad_map_keys, grad_map_values], axis=2)
        .astype(jnp.bfloat16)
        .reshape(images, length, 2 * D)
    )
    grad_w_map_kv = jnp.einsum(
        "ipd,ipc->dc", final_b, grad_map_kv, preferred_element_type=jnp.float32
    )
    grad_final = jnp.einsum(
        "ipc,dc->ipd", grad_map_kv, w_map_kv, preferred_element_type=jnp.float32
    )
    grad_layer_out, grad_gain_three, grad_bias_three = norm_three_pull(grad_final)
    probe_total = lax.psum(grad_probe_query, both)
    share_map_q = jnp.outer(own_vectors[:, 6].astype(jnp.float32), probe_total)
    share_probe = jnp.dot(
        own_map_q.astype(jnp.float32), probe_total, precision=lax.Precision.HIGHEST
    )
    grad_branch_two = grad_layer_out.astype(jnp.bfloat16)
    grad_w_down = jnp.einsum(
        "ipd,ipf->df", grad_branch_two, activation_b, preferred_element_type=jnp.float32
    )
    grad_activation = jnp.einsum(
        "ipd,df->ipf", grad_branch_two, w_down, preferred_element_type=jnp.float32
    )
    (grad_pre,) = gelu_pull(grad_activation)
    grad_pre_b = grad_pre.astype(jnp.bfloat16)
    grad_w_up = jnp.einsum("ipd,ipf->df", hidden_b, grad_pre_b, preferred_element_type=jnp.float32)
    grad_hidden = jnp.einsum("ipf,df->ipd", grad_pre_b, w_up, preferred_element_type=jnp.float32)
    grad_res_part, grad_gain_two, grad_bias_two = norm_two_pull(grad_hidden)
    grad_residual = grad_layer_out + grad_res_part
    grad_branch_one = grad_residual.astype(jnp.bfloat16)
    grad_w_out = jnp.einsum(
        "ipd,ipc->dc", mixed_b, grad_branch_one, preferred_element_type=jnp.float32
    )
    grad_mixed = jnp.einsum(
        "ipc,dc->ipd", grad_branch_one, w_out, preferred_element_type=jnp.float32
    )
    grad_mixed = grad_mixed.astype(jnp.bfloat16)
    grad_queries, grad_keys, grad_values = attend_back(
        queries, keys_all, values_all, log_norm, grad_mixed.reshape(images, length, HEADS, HEAD_DIM)
    )
    grad_qkv = jnp.concatenate(
        [
            grad_queries.reshape(images, length, D),
            grad_keys.reshape(images, length, D),
            grad_values.reshape(images, length, D),
        ],
        axis=-1,
    ).astype(jnp.bfloat16)
    grad_w_qkv = jnp.einsum("ipd,ipc->dc", normed_b, grad_qkv, preferred_element_type=jnp.float32)
    grad_normed = jnp.einsum("ipc,dc->ipd", grad_qkv, w_qkv, preferred_element_type=jnp.float32)
    grad_tok_part, grad_gain_one, grad_bias_one = norm_one_pull(grad_normed)
    patch_grad = lax.all_to_all(
        (grad_residual + grad_tok_part).astype(jnp.bfloat16), "blk", 1, 0, tiled=True
    ).astype(jnp.float32)
    grad_vectors = jnp.stack(
        [
            grad_gain_one,
            grad_bias_one,
            grad_gain_two,
            grad_bias_two,
            grad_gain_three,
            grad_bias_three,
        ],
        axis=1,
    )

    def scatter(part):
        return lax.psum_scatter(
            part.astype(jnp.bfloat16), both, scatter_dimension=0, tiled=True
        ).astype(jnp.float32)

    share_map_kv = scatter(grad_w_map_kv)
    share_down = scatter(grad_w_down)
    share_up = scatter(grad_w_up)
    share_front = scatter(jnp.concatenate([grad_w_qkv, grad_w_out], axis=1))
    weight_share = jnp.concatenate(
        [share_front, share_up, share_down, share_map_q, share_map_kv, share_map_out], axis=1
    )
    vector_share = jnp.concatenate(
        [
            lax.psum_scatter(grad_vectors, both, scatter_dimension=0, tiled=True),
            share_probe[:, None],
        ],
        axis=1,
    )
    squares = jnp.sum(weight_share * weight_share) + jnp.sum(vector_share * vector_share)
    square_total = lax.psum(squares, ("blk", "img"))
    grad_norm = jnp.sqrt(square_total + jnp.sum(scalar_total * scalar_total))
    factor = CLIP_AT / jnp.maximum(grad_norm, CLIP_AT)
    new_w, new_wm, new_wv = adamw(
        master_weights, weight_share * factor, first_moments, second_moments, 0.03, 0.1
    )
    new_v, new_vm, new_vv = adamw(
        master_vectors, vector_share * factor, vector_first, vector_second, 0.3, 0.0
    )
    new_s, new_sm, new_sv = adamw(
        loss_scalars, scalar_total * factor, scalar_first, scalar_second, 0.3, 0.0
    )
    return (
        loss_total,
        grad_norm,
        patch_grad,
        new_w,
        new_wm,
        new_wv,
        new_w.astype(jnp.bfloat16),
        new_v,
        new_vm,
        new_vv,
        new_v.astype(jnp.bfloat16),
        new_s,
        new_sm,
        new_sv,
    )


LINK_SPEED = (1.1, 4.0)


def gather_key(number, at):
    return 0 if at == 0 else at + number


MESH = pl.DeviceIdType.MESH
CHIP_ROWS = 48
GATHER_SECTIONS = ((0, 2560, False), (2560, 3840, True), (6400, 3072, False), (9472, 2304, False))
SCATTER_SECTIONS = (
    (9472, 1536, False),
    (6400, 1536, False),
    (7936, 1536, False),
    (3328, 1536, False),
    (4864, 1536, False),
    (2560, 768, False),
    (0, 1280, False),
    (1280, 1280, False),
)
PAIR_PLACES = ((0, 0), (0, 768), (1, 0), (1, 768), (0, 0), (0, 1536), (0, 768), (1, 0))
LATE_PLACES = (0, 768, 1152, 1792)
GATHER_COLS = 11776
SCATTER_COLS = 11008


def aligned(value, step):
    return pl.multiple_of(value, step)


class Place:
    def __init__(self):
        self.blk = lax.axis_index("blk")
        self.img = lax.axis_index("img")
        self.x = lax.rem(self.blk, 2)
        self.y = self.blk // 2
        self.z = self.img // 2
        self.c = lax.rem(self.img, 2)
        self.chip = self.blk * 4 + self.z
        self.sibling = {"img": self.z * 2 + 1 - self.c}
        self.up = {"img": self.img + 2}
        self.down = {"img": self.img - 2}
        self.a_near = {"blk": self.block(1, 0)}
        self.b_near = {"blk": self.block(0, 1)}

    def on_level(self, level):
        return {"img": level * 2 + self.c}

    def block(self, da, db):
        flip_x = da * (1 - self.c) + db * self.c
        flip_y = db * (1 - self.c) + da * self.c
        other_x = self.x + flip_x * (1 - 2 * self.x)
        other_y = self.y + flip_y * (1 - 2 * self.y)
        return other_y * 2 + other_x


def remote(src, dst, send_sem, recv_sem, device):
    return pltpu.make_async_remote_copy(
        src_ref=src,
        dst_ref=dst,
        send_sem=send_sem,
        recv_sem=recv_sem,
        device_id=device,
        device_id_type=MESH,
    )


def greet_all(place):
    barrier = pltpu.get_barrier_semaphore()
    me = place.blk * 8 + place.img

    def greet(step, carry):
        other = lax.rem(me + step, 32)
        pl.semaphore_signal(
            barrier,
            inc=1,
            device_id={"blk": other // 8, "img": lax.rem(other, 8)},
            device_id_type=MESH,
        )
        return carry

    lax.fori_loop(1, 32, greet, 0)


def all_greeted():
    pl.semaphore_wait(pltpu.get_barrier_semaphore(), 31)


class Gather:
    def __init__(self, place, buf, rows, first, width, z_first, sems):
        self.p, self.buf, self.rows, self.half = place, buf, rows, width // 2
        self.z_first = z_first
        self.mine = aligned(first + place.c * self.half, 128)
        self.theirs = aligned(first + (1 - place.c) * self.half, 128)
        self.near_recv, self.z_recv, self.b_recv, self.near_send, self.z_send, self.b_send, self.pair = sems

    def item(self, da, db, level):
        start = aligned((self.p.block(da, db) * 4 + level) * self.rows, self.rows)
        return self.buf.at[pl.ds(start, self.rows), pl.ds(self.mine, self.half)]

    def a_copy(self, level, da=0):
        part = self.item(da, 0, level)
        return remote(part, part, self.near_send.at[level], self.near_recv.at[level], self.p.a_near)

    def z_copy(self, da, level, up):
        part = self.item(da, 0, level)
        device = self.p.up if up else self.p.down
        return remote(part, part, self.z_send.at[up, da, level], self.z_recv.at[da, level], device)

    def b_copy(self, da, level):
        part = self.item(da, 0, level)
        return remote(part, part, self.b_send.at[da, level], self.b_recv.at[da, level], self.p.b_near)

    def pair_copy(self, da, db):
        start = aligned(self.p.block(da, db) * (4 * self.rows), 4 * self.rows)
        part = self.buf.at[pl.ds(start, 4 * self.rows), pl.ds(self.mine, self.half)]
        return remote(part, part, self.pair.at[0], self.pair.at[1], self.p.sibling)

    def onward(self, da, level, up, down):
        if self.z_first and da == 0:
            self.a_copy(level).start()
        self.b_copy(da, level).start()
        if up:
            pl.when(self.p.z < 3)(lambda: self.z_copy(da, level, 1).start())
        if down:
            pl.when(self.p.z > 0)(lambda: self.z_copy(da, level, 0).start())

    def begin(self):
        if not self.z_first:
            self.a_copy(self.p.z).start()
        self.onward(0, self.p.z, True, True)

    def near(self):
        z = self.p.z
        if not self.z_first:
            self.a_copy(z, 1).wait_recv()
            self.onward(1, z, True, True)
            return
        for step in range(4):
            level = lax.rem(z + step, 4)
            self.a_copy(level, 1).wait_recv()
            self.onward(1, level, False, False)
        self.pair_copy(1, 0).start()

    def level(self, distance):
        z = self.p.z
        sides = 1 if self.z_first else 2

        @pl.when(z >= distance)
        def from_below():
            for da in range(sides):
                self.z_copy(da, z - distance, 1).wait_recv()
                self.onward(da, z - distance, True, False)

        @pl.when(z + distance <= 3)
        def from_above():
            for da in range(sides):
                self.z_copy(da, z + distance, 0).wait_recv()
                self.onward(da, z + distance, False, True)

        if distance == 3:
            for da in range(sides):
                self.pair_copy(da, 0).start()

    def far(self):
        for da in range(2):
            for level in range(4):
                part = self.item(da, 1, level)
                remote(
                    part, part, self.b_send.at[da, level], self.b_recv.at[da, level], self.p.b_near
                ).wait_recv()
            self.pair_copy(da, 1).start()

    def finish(self):
        whole = self.buf.at[pl.ds(0, 16 * self.rows), pl.ds(self.theirs, self.half)]
        both = remote(whole, whole, self.pair.at[0], self.pair.at[1], self.p.sibling)
        both.wait_recv()

    def sent(self):
        z = self.p.z
        whole = self.buf.at[pl.ds(0, 16 * self.rows), pl.ds(self.mine, self.half)]
        remote(whole, whole, self.pair.at[0], self.pair.at[1], self.p.sibling).wait_send()
        if not self.z_first:
            self.a_copy(z).wait_send()
        for level in range(4):
            if self.z_first:
                self.a_copy(level).wait_send()
            for da in range(2):
                self.b_copy(da, level).wait_send()
            for da in range(1 if self.z_first else 2):
                if level < 3:
                    pl.when((z >= level) & (z < 3))(
                        lambda da=da, level=level: self.z_copy(da, level, 1).wait_send()
                    )
                if level > 0:
                    pl.when((z <= level) & (z > 0))(
                        lambda da=da, level=level: self.z_copy(da, level, 0).wait_send()
                    )

    def steps(self):
        levels = [functools.partial(self.level, distance) for distance in (1, 2, 3)]
        if self.z_first:
            return [self.begin, *levels, self.near, self.far]
        return [self.begin, self.near, *levels, self.far]


def gather_sems(count):
    dma = pltpu.SemaphoreType.DMA
    return [
        dma((count, 4)),
        dma((count, 2, 4)),
        dma((count, 2, 4)),
        dma((count, 4)),
        dma((count, 2, 2, 4)),
        dma((count, 2, 4)),
        dma((count, 2)),
    ]


class Scatter:
    def __init__(self, place, buf, share, first, width, z_first, bufs, sems):
        self.p, self.buf, self.share, self.half = place, buf, share, width // 2
        self.z_first = z_first
        self.mine = aligned(first + place.c * self.half, 128)
        self.theirs = aligned(first + (1 - place.c) * self.half, 128)
        self.pair_in, self.b_in, self.a_in, self.z_in, self.last = bufs
        self.pair, self.b_sem, self.a_sem, self.z_sem, self.end = sems

    def run_rows(self, da, db):
        return aligned(self.p.block(da, db) * 192, 192)

    def run(self, da, db):
        return self.buf.at[pl.ds(self.run_rows(da, db), 192), pl.ds(self.mine, self.half)]

    def level_rows(self, da, level):
        return aligned((self.p.block(da, 0) * 4 + level) * 48, 48)

    def part(self, da, level):
        return self.buf.at[pl.ds(self.level_rows(da, level), 48), pl.ds(self.mine, self.half)]

    def add(self, row, source, count, offset=0):
        def one(step, carry):
            here = aligned(row + step * 48, 48)
            there = aligned(offset + step * 48, 48)
            self.buf[pl.ds(here, 48), pl.ds(self.mine, self.half)] += source[pl.ds(there, 48), :]
            return carry

        if count == 1:
            one(0, 0)
        else:
            lax.fori_loop(0, count, one, 0)

    def pair_copy(self):
        return remote(
            self.buf.at[pl.ds(0, 768), pl.ds(self.theirs, self.half)],
            self.pair_in,
            self.pair.at[0],
            self.pair.at[1],
            self.p.sibling,
        )

    def b_copy(self, da):
        return remote(
            self.run(da, 1),
            self.b_in.at[da * 192 : da * 192 + 192, :],
            self.b_sem.at[0, da],
            self.b_sem.at[1, da],
            self.p.b_near,
        )

    def a_copy(self):
        source = self.part(1, self.p.z) if self.z_first else self.run(1, 0)
        return remote(source, self.a_in, self.a_sem.at[0], self.a_sem.at[1], self.p.a_near)

    def z_slot(self, da, step):
        return slice(da * 144 + (3 - step) * 48, da * 144 + (4 - step) * 48)

    def z_copy(self, da, step):
        level = lax.rem(self.p.z + step, 4)
        return remote(
            self.part(da, level),
            self.z_in.at[self.z_slot(da, step), :],
            self.z_sem.at[0, da, 3 - step],
            self.z_sem.at[1, da, 3 - step],
            self.p.on_level(level),
        )

    def z_start(self, da):
        for step in (2, 1, 3):
            self.z_copy(da, step).start()

    def z_total(self, da):
        total = self.buf[pl.ds(self.level_rows(da, self.p.z), 48), pl.ds(self.mine, self.half)]
        total = total.astype(jnp.float32)
        for step in (1, 3, 2):
            self.z_copy(da, step).wait_recv()
            total += self.z_in[self.z_slot(da, step), :].astype(jnp.float32)
        return total

    def end_copy(self):
        return remote(
            self.last.at[pl.ds(aligned((1 - self.p.c) * 24, 8), 24), :],
            self.share.at[:, pl.ds(self.mine, self.half)],
            self.end.at[0],
            self.end.at[1],
            self.p.sibling,
        )

    def begin(self):
        self.pair_copy().start()

    def pairs_far(self):
        self.pair_copy().wait_recv()
        for da in range(2):
            row = self.run_rows(da, 1)
            self.add(row, self.pair_in, 4, row)
            self.b_copy(da).start()

    def pairs_near(self):
        for da in range(2):
            row = self.run_rows(da, 0)
            self.add(row, self.pair_in, 4, row)

    def blocks(self):
        for da in (1, 0):
            self.b_copy(da).wait_recv()
            self.add(self.run_rows(da, 0), self.b_in, 4, da * 192)
            if self.z_first:
                self.z_start(da)
            elif da == 1:
                self.a_copy().start()

    def joined(self):
        if self.z_first:
            self.buf[pl.ds(self.level_rows(1, self.p.z), 48), pl.ds(self.mine, self.half)] = (
                self.z_total(1).astype(jnp.bfloat16)
            )
            self.a_copy().start()
        else:
            self.a_copy().wait_recv()
            self.add(self.run_rows(0, 0), self.a_in, 4)
            self.z_start(0)

    def close(self):
        total = self.z_total(0)
        if self.z_first:
            self.a_copy().wait_recv()
            total += self.a_in[...].astype(jnp.float32)
        self.last[...] = total
        self.end_copy().start()
        self.share[:, pl.ds(self.mine, self.half)] = self.last[
            pl.ds(aligned(self.p.c * 24, 8), 24), :
        ]

    def finish(self):
        theirs = self.share.at[:, pl.ds(self.theirs, self.half)]
        remote(theirs, theirs, self.end.at[0], self.end.at[1], self.p.sibling).wait_recv()
        self.end_copy().wait_send()
        self.a_copy().wait_send()
        self.pair_copy().wait_send()
        for da in range(2):
            self.b_copy(da).wait_send()
        for da in range(2 if self.z_first else 1):
            for step in range(1, 4):
                self.z_copy(da, step).wait_send()


class Links:
    def __init__(self, slow=1.0, hop=2.0):
        self.flat = self.high = 0.0
        self.slow, self.hop = slow, hop

    def use(self, name, start, time):
        start = max(start, getattr(self, name))
        setattr(self, name, start + time * self.slow)
        return start + time * self.slow + self.hop

    def steps(self, section, start, width):
        size = width / 256
        out = []
        now = start + 0.35 * size * self.slow + 1.0
        out += [(now, section.pairs_far), (now + 0.5, section.pairs_near)]
        now = self.use("flat", now + 0.5, 1.01 * size)
        out.append((now, section.blocks))
        if section.z_first:
            now = self.use("high", now, 2.02 * size)
            out.append((now, section.joined))
            now = self.use("flat", now, 0.13 * size)
        else:
            now = self.use("flat", now, 0.5 * size)
            out.append((now, section.joined))
            now = self.use("high", now, 1.01 * size)
        out += [(now, section.close), (now + 4.0, section.finish)]
        return out


class Program:
    def __init__(self):
        self.now, self.places, self.wanted = 0.0, [], []
        self.plans = {}
        self.tail = []

    def loop(self, name, count, each):
        self.plans[name] = {}
        for index in range(count):
            self.now += each
            self.places.append((self.now, name, index))

    def gap(self, time):
        self.now += time

    def want(self, steps):
        self.wanted += [(time, len(self.wanted) + n, step) for n, (time, step) in enumerate(steps)]

    def settle(self):
        for time, _, step in sorted(self.wanted, key=lambda entry: entry[:2]):
            for place, name, index in self.places:
                if place >= time:
                    self.plans[name].setdefault(index, []).append(step)
                    break
            else:
                self.tail.append(step)


class Swap:
    def __init__(self, place, pieces, buf, first_buf_row, rows, first, width, offset, sems):
        self.p, self.rows, self.half = place, rows, width // 2
        self.buf, self.sems = buf, sems
        self.row = aligned(first_buf_row + place.c * rows, rows)
        self.other_row = aligned(first_buf_row + (1 - place.c) * rows, rows)
        self.halves = []
        for core in range(2):
            low, here = first + core * self.half, []
            for array, source, target, size in pieces:
                start, stop = max(low, target), min(low + self.half, target + size)
                if start < stop:
                    at = start - low + offset if offset is not None else start
                    here.append((array, source + start - target, at, stop - start))
            self.halves.append(here)
        self.at = (
            pl.ds(aligned(first + place.c * self.half, 128), self.half)
            if offset is None
            else pl.ds(offset, self.half)
        )
        self.away_at = (
            pl.ds(aligned(first + (1 - place.c) * self.half, 128), self.half)
            if offset is None
            else pl.ds(offset, self.half)
        )

    def begin(self, late=None):
        for core in range(2):
            for array, source, at, size in self.halves[core]:
                if late is not None and (array is late[0]) != late[1]:
                    continue
                part = array.at[:, source : source + size]
                goal = self.buf.at[pl.ds(self.row, self.rows), at : at + size]

                @pl.when(self.p.c == core)
                def here(part=part, goal=goal):
                    pltpu.make_async_copy(part, goal, self.sems.at[2]).start()

                @pl.when(self.p.c != core)
                def away(part=part, goal=goal):
                    remote(part, goal, self.sems.at[0], self.sems.at[1], self.p.sibling).start()

    def finish(self):
        landed = self.buf.at[pl.ds(self.other_row, self.rows), self.at]
        own = self.buf.at[pl.ds(self.row, self.rows), self.at]
        gone = self.buf.at[pl.ds(self.row, self.rows), self.away_at]
        remote(landed, landed, self.sems.at[0], self.sems.at[1], self.p.sibling).wait_recv()
        pltpu.make_async_copy(own, own, self.sems.at[2]).wait()
        remote(gone, gone, self.sems.at[0], self.sems.at[1], self.p.sibling).wait_send()


class Spread:
    def __init__(self, place, mine, everyone, send_sem, recv_sem):
        self.p, self.mine, self.everyone = place, mine, everyone
        self.send_sem, self.recv_sem = send_sem, recv_sem
        self.me = place.blk * 8 + place.img

    def copy(self, step):
        other = lax.rem(self.me + step, 32)
        return remote(
            self.mine,
            self.everyone.at[step - 1],
            self.send_sem,
            self.recv_sem,
            {"blk": other // 8, "img": lax.rem(other, 8)},
        )

    def begin(self, tile):
        self.mine[...] = tile

        def start(step, carry):
            self.copy(step).start()
            return carry

        lax.fori_loop(1, 32, start, 0)

    def finish(self, small):
        scalars = jnp.sum(small[...].reshape(32, 8, 768), axis=0)[3:4]
        lane = lax.broadcasted_iota(jnp.int32, (1, 768), 1)
        square = jnp.sum(jnp.where((lane == 1) | (lane == 2), scalars * scalars, 0.0))
        return scalars, jnp.sqrt(self.total() + square)

    def total(self):
        remote(
            self.everyone, self.everyone, self.send_sem, self.recv_sem, self.p.sibling
        ).wait()
        return self.mine[...] + jnp.sum(self.everyone[...], axis=0)


def small_tail(p, small, map_q, probe, map_out_ref, map_q_ref):
    everything = small[...]
    as_rows = everything.astype(jnp.bfloat16)
    sums = jnp.sum(everything.reshape(32, 8, 768), axis=0)
    query = sums[2:3]
    device = lax.broadcasted_iota(jnp.int32, (32, 256), 0) * 8
    row = lax.broadcasted_iota(jnp.int32, (32, 256), 1)

    def rows_of(kind):
        pick = (row == device + kind).astype(jnp.float32).astype(jnp.bfloat16)
        return jnp.dot(pick, as_rows, preferred_element_type=jnp.float32).astype(jnp.bfloat16)

    pooled, grads = rows_of(0), rows_of(1)
    first = (p.blk * 8 + p.img) * 24
    picks = (
        lax.broadcasted_iota(jnp.int32, (24, 768), 1)
        == lax.broadcasted_iota(jnp.int32, (24, 768), 0) + first
    ).astype(jnp.float32).astype(jnp.bfloat16)
    rows = lax.dot_general(
        picks, pooled, (((1,), (1,)), ((), ())), preferred_element_type=jnp.float32
    ).astype(jnp.bfloat16)
    map_out = jnp.dot(rows, grads, preferred_element_type=jnp.float32)
    map_q_share = probe * query
    probe_share = jnp.sum(map_q * query, axis=1, keepdims=True)
    square = (
        jnp.sum(map_out * map_out)
        + jnp.sum(map_q_share * map_q_share)
        + jnp.sum(probe_share * probe_share)
    )
    map_out_ref[...], map_q_ref[...] = map_out, map_q_share
    return probe_share, square


def square_share(share, square, start, stop):
    def one(step, total):
        part = share[:, pl.ds(aligned(step * 256, 256), 256)]
        return total + jnp.sum(part * part)

    return lax.fori_loop(start, stop, one, square)


COL_VECTORS = 2304
COL_QUERY = 2432
COL_OUT = 2560
COL_UP = 3328
COL_DOWN = 6400
COL_MAP_KV = 9472
COL_MAP_OUT = 11008
TOKENS = 576
CHUNK = 96
TILE = 256
SCALE = 0.125
GELU_A = 0.7978845608028654
GELU_B = 0.044715
NT = (((1,), (1,)), ((), ()))
TN = (((0,), (0,)), ((), ()))


def dot(lhs, rhs, dims=(((1,), (0,)), ((), ()))):
    return lax.dot_general(lhs, rhs, dims, preferred_element_type=jnp.float32)


def loop(count, body, plan=None):
    def one(index, carry):
        body(index)
        for at, steps in (plan or {}).items():

            @pl.when(index == at)
            def run(steps=steps):
                for step in steps:
                    step()

        return carry

    lax.fori_loop(0, count, one, 0)


def columns(index, first=0, width=TILE):
    return pl.ds(aligned(first + index * width, 128), width)


def chunk_rows(index):
    return pl.ds(aligned(index * CHUNK, 32), CHUNK)


def normalize(values):
    row_mean = jnp.mean(values, axis=-1, keepdims=True)
    centered = values - row_mean
    row_var = jnp.mean(centered * centered, axis=-1, keepdims=True)
    rate = lax.rsqrt(row_var + 1e-06)
    return centered * rate, rate


def normalize_back(scaled, rate, grad, gain):
    inner = grad * gain
    first = jnp.mean(inner, axis=-1, keepdims=True)
    second = jnp.mean(inner * scaled, axis=-1, keepdims=True)
    return (
        rate * (inner - first - scaled * second),
        jnp.sum(grad * scaled, axis=0, keepdims=True),
        jnp.sum(grad, axis=0, keepdims=True),
    )


class Tower:
    def __init__(self, **refs):
        self.__dict__.update(refs)

    def unpack(self):
        turned = jnp.transpose(self.w[:, COL_VECTORS : COL_VECTORS + 128].astype(jnp.float32))
        self.vec[0:8, :] = turned[0:8]
        packed = self.w[:, COL_QUERY : COL_QUERY + 128].astype(jnp.float32)
        total = jnp.sum(packed.reshape(32, 24, 128), axis=0)
        query = total[0:6] + total[6:12]
        row = jnp.concatenate([query[i : i + 1] for i in range(6)], axis=1)
        self.vec[8:16, :] = jnp.broadcast_to(row, (8, 768)).astype(jnp.bfloat16).astype(jnp.float32)

    def norm(self, source, gain, bias, out):
        def body(index):
            rows = chunk_rows(index)
            scaled, _ = normalize(source[rows, :].astype(jnp.float32))
            out[rows, :] = (scaled * gain + bias).astype(jnp.bfloat16)

        loop(TOKENS // CHUNK, body)

    def first_norm(self):
        self.norm(self.x, self.vec[0:1, :], self.vec[1:2, :], self.h)

    def project(self, plan=None):
        def body(index):
            self.qkv[:, columns(index)] = dot(self.h[...], self.w[:, columns(index)]).astype(jnp.bfloat16)

        loop(9, body, plan)

    def pair_of(self, pair, which):
        return self.qkv[:, columns(pair, which * D, 128)]

    def attend(self, plan=None):
        lanes = lax.broadcasted_iota(jnp.int32, (TOKENS, 128), 1)

        def body(pair):
            queries = self.pair_of(pair, 0) * jnp.bfloat16(SCALE)
            keys = self.pair_of(pair, 1)
            values_turned = jnp.transpose(self.pair_of(pair, 2))
            mixed = []
            for head in range(2):
                mine = (lanes < 64) if head == 0 else (lanes >= 64)
                masked = jnp.where(mine, queries, jnp.bfloat16(0))
                scores = dot(keys, masked, NT)
                most = jnp.max(scores, axis=0, keepdims=True)
                expos = jnp.exp(scores - most)
                total = jnp.sum(expos, axis=0, keepdims=True)
                part = dot(values_turned[head * 64 : head * 64 + 64], expos.astype(jnp.bfloat16))
                mixed.append(part * (1.0 / total))
                self.lse[pl.ds(pair * 2 + head, 1), :] = most + jnp.log(total)
            self.a[:, columns(pair, 0, 128)] = jnp.transpose(
                jnp.concatenate(mixed, axis=0)
            ).astype(jnp.bfloat16)

        loop(6, body, plan)

    def attend_out(self, plan=None):
        def body(index):
            self.r[:, columns(index)] = self.x[:, columns(index)].astype(jnp.float32) + dot(
                self.a[...], self.w[:, columns(index, COL_OUT)]
            )

        loop(3, body, plan)
        self.norm(self.r, self.vec[2:3, :], self.vec[3:4, :], self.h2)

    def feed_up(self, plan=None):
        def body(index):
            value = dot(self.h2[...], self.w[:, columns(index, COL_UP)])
            square = value * value
            bend = jnp.tanh(GELU_A * value * (1.0 + GELU_B * square))
            half = 0.5 + 0.5 * bend
            self.g[:, columns(index)] = (value * half).astype(jnp.bfloat16)
            slope = half + 0.5 * value * (1.0 - bend * bend) * (
                GELU_A + 3.0 * GELU_A * GELU_B * square
            )
            self.gp[:, columns(index)] = slope.astype(jnp.bfloat16)

        loop(12, body, plan)

    def feed_down(self, plan=None):
        def body(index):
            self.y[:, columns(index)] = self.r[:, columns(index)] + dot(
                self.g[...], self.w[columns(index), COL_DOWN : COL_DOWN + FF], NT
            )

        loop(3, body, plan)
        self.norm(self.y, self.vec[4:5, :], self.vec[5:6, :], self.f)

    def pool_project(self, plan=None):
        def body(index):
            self.kvp[:, columns(index)] = dot(
                self.f[...], self.w[:, columns(index, COL_MAP_KV)]
            ).astype(jnp.bfloat16)

        loop(6, body, plan)

    def pool(self, signs, temperature, offset, images):
        head = lax.broadcasted_iota(jnp.int32, (16, D), 0)
        owner = lax.broadcasted_iota(jnp.int32, (16, D), 1) // HEAD_DIM
        own = head == owner
        heads_query = jnp.where(own, self.vec[8:9, :], 0.0).astype(jnp.bfloat16)
        keys, values = self.kvp[:, :D], self.kvp[:, D:]
        scores = dot(heads_query, keys, NT) * SCALE
        expos = jnp.exp(scores - jnp.max(scores, axis=1, keepdims=True))
        probs = expos / jnp.sum(expos, axis=1, keepdims=True)
        probs_high = probs.astype(jnp.bfloat16)
        probs_low = (probs - probs_high.astype(jnp.float32)).astype(jnp.bfloat16)
        spread = dot(probs_high, values) + dot(probs_low, values)
        pooled = jnp.sum(jnp.where(own, spread, 0.0), axis=0, keepdims=True)
        pooled_b = pooled.astype(jnp.bfloat16)
        w_out = self.w[:, COL_MAP_OUT : COL_MAP_OUT + D]
        many = jnp.broadcast_to(pooled, (16, D)).astype(jnp.bfloat16)
        embed = dot(many, w_out)[0:1]
        rate = lax.rsqrt(jnp.sum(embed * embed, axis=1, keepdims=True) + 1e-06)
        unit = jnp.broadcast_to(embed * rate, (16, D)).astype(jnp.bfloat16)
        cosine = dot(unit, self.cap[...], NT)[0:1]
        heat = jnp.exp(temperature)
        logits = heat * cosine + offset
        turned = -signs * logits
        losses = jnp.maximum(turned, 0.0) + jnp.log1p(jnp.exp(-jnp.abs(turned)))
        loss = jnp.sum(jnp.where(signs == 0.0, 0.0, losses), axis=1, keepdims=True) / images
        grad_logits = -signs * (1.0 / (1.0 + jnp.exp(-turned))) / images
        grad_heat = jnp.sum(grad_logits * cosine * heat, axis=1, keepdims=True)
        grad_offset = jnp.sum(grad_logits, axis=1, keepdims=True)
        grad_cosine = jnp.broadcast_to(grad_logits * heat, (16, cosine.shape[1])).astype(jnp.bfloat16)
        grad_unit = dot(grad_cosine, self.cap[...])[0:1]
        grad_embed = rate * grad_unit - embed * (
            rate * rate * rate * jnp.sum(grad_unit * embed, axis=1, keepdims=True)
        )
        grad_many = jnp.broadcast_to(grad_embed, (16, D)).astype(jnp.bfloat16)
        grad_pooled = dot(grad_many, w_out, NT).astype(jnp.bfloat16).astype(jnp.float32)
        heads_grad = jnp.where(own, grad_pooled, 0.0).astype(jnp.bfloat16)
        grad_probs = dot(heads_grad, values, NT)
        centre = jnp.sum(probs * grad_probs, axis=1, keepdims=True)
        grad_scores = (probs * (grad_probs - centre)).astype(jnp.bfloat16)
        query_spread = dot(grad_scores, keys) * SCALE
        grad_query = jnp.sum(jnp.where(own, query_spread, 0.0), axis=0, keepdims=True)
        self.small_own[0:1, :] = pooled_b.astype(jnp.float32)
        self.small_own[1:2, :] = grad_many[0:1].astype(jnp.float32)
        self.small_own[2:3, :] = grad_query
        lane = lax.broadcasted_iota(jnp.int32, (1, D), 1)
        self.small_own[3:4, :] = jnp.where(
            lane == 0, loss, jnp.where(lane == 1, grad_heat, jnp.where(lane == 2, grad_offset, 0.0))
        )
        self.small_own[4:8, :] = jnp.zeros((4, D), jnp.float32)
        self.kvp[:, :D] = (dot(grad_scores, heads_query, TN) * SCALE).astype(jnp.bfloat16)
        both_probs = jnp.concatenate([probs_high, probs_low], axis=0)
        both_grads = jnp.concatenate([heads_grad, heads_grad], axis=0)
        self.kvp[:, D:] = dot(both_probs, both_grads, TN).astype(jnp.bfloat16)

    def turn(self, source):
        def body(index):
            self.turned[columns(index), :] = jnp.transpose(source[:, columns(index)])

        loop(3, body)

    def weight_grad(self, first, source, tiles, plan=None):
        def body(index):
            self.w[:, columns(index, first)] = dot(
                self.turned[...], source[:, columns(index)]
            ).astype(jnp.bfloat16)

        loop(tiles, body, plan)

    def input_grad(self, source, first, width, plan=None):
        def body(index):
            self.acc[:, columns(index)] = dot(
                source[...], self.w[columns(index), first : first + width], NT
            )

        loop(3, body, plan)

    def norm_back(self, source, added, number, out, rounded):
        gain = self.vec[2 * number : 2 * number + 1, :]

        def body(index, carry):
            rows = chunk_rows(index)
            scaled, rate = normalize(source[rows, :].astype(jnp.float32))
            grad, grad_gain, grad_bias = normalize_back(scaled, rate, self.acc[rows, :], gain)
            if added is not None:
                grad = grad + added[rows, :]
            if out is not None:
                out[rows, :] = grad
            rounded[rows, :] = grad.astype(jnp.bfloat16)
            return carry[0] + grad_gain, carry[1] + grad_bias

        zero = jnp.zeros((1, D), jnp.float32)
        grad_gain, grad_bias = lax.fori_loop(0, TOKENS // CHUNK, body, (zero, zero))
        self.vec_grad[2 * number : 2 * number + 1, :] = grad_gain
        self.vec_grad[2 * number + 1 : 2 * number + 2, :] = grad_bias

    def pool_back(self, plan=None, after=None):
        self.input_grad(self.kvp, COL_MAP_KV, 2 * D)
        self.turn(self.f)
        self.weight_grad(COL_MAP_KV, self.kvp, 6, plan)
        if after is not None:
            after()
        self.norm_back(self.y, None, 2, self.y, self.f)

    def down_back(self, start, tiles, plan=None):
        def body(step):
            index = start + step
            here = columns(index)
            grad = dot(self.f[...], self.w[:, columns(index, COL_DOWN)])
            self.gp[:, here] = (grad * self.gp[:, here].astype(jnp.float32)).astype(jnp.bfloat16)
            self.w[:, columns(index, COL_DOWN)] = dot(self.turned[...], self.g[:, here]).astype(
                jnp.bfloat16
            )

        loop(tiles, body, plan)

    def up_input(self, plan=None):
        self.input_grad(self.gp, COL_UP, FF, plan)

    def up_weight(self, start, tiles, plan=None):
        def body(step):
            index = start + step
            self.w[:, columns(index, COL_UP)] = dot(
                self.turned[...], self.gp[:, columns(index)]
            ).astype(jnp.bfloat16)

        loop(tiles, body, plan)

    def up_norm(self):
        self.norm_back(self.r, self.y, 1, self.r, self.f)

    def out_back(self, plan=None):
        self.turn(self.a)

        def body(index):
            self.a[:, columns(index)] = dot(
                self.f[...], self.w[columns(index), COL_OUT : COL_OUT + D], NT
            ).astype(jnp.bfloat16)

        loop(3, body)
        self.weight_grad(COL_OUT, self.f, 3, plan)

    def attend_back(self, plan=None):
        lanes = lax.broadcasted_iota(jnp.int32, (TOKENS, 128), 1)

        def body(pair):
            queries = self.pair_of(pair, 0) * jnp.bfloat16(SCALE)
            keys, values = self.pair_of(pair, 1), self.pair_of(pair, 2)
            grads = self.a[:, columns(pair, 0, 128)]
            keys_turned = jnp.transpose(keys)
            grad_queries = []
            grad_keys = None
            for head in range(2):
                mine = (lanes < 64) if head == 0 else (lanes >= 64)
                masked = jnp.where(mine, queries, jnp.bfloat16(0))
                masked_grads = jnp.where(mine, grads, jnp.bfloat16(0))
                scores = dot(keys, masked, NT)
                probs = jnp.exp(scores - self.lse[pl.ds(pair * 2 + head, 1), :])
                value_part = dot(probs.astype(jnp.bfloat16), masked_grads)
                grad_probs = dot(values, masked_grads, NT)
                centre = jnp.sum(probs * grad_probs, axis=0, keepdims=True)
                grad_scores = (probs * (grad_probs - centre)).astype(jnp.bfloat16)
                key_part = dot(grad_scores, masked)
                grad_queries.append(dot(keys_turned[head * 64 : head * 64 + 64], grad_scores))
                if head == 0:
                    grad_keys, grad_values = key_part, value_part
                else:
                    grad_keys, grad_values = grad_keys + key_part, grad_values + value_part
            self.qkv[:, columns(pair, 0, 128)] = (
                jnp.transpose(jnp.concatenate(grad_queries, axis=0)) * SCALE
            ).astype(jnp.bfloat16)
            self.qkv[:, columns(pair, D, 128)] = grad_keys.astype(jnp.bfloat16)
            self.qkv[:, columns(pair, 2 * D, 128)] = grad_values.astype(jnp.bfloat16)

        loop(6, body, plan)

    def project_input(self, plan=None):
        self.first_norm()
        self.input_grad(self.qkv, 0, 3 * D, plan)
        self.turn(self.h)
        self.norm_back(self.x, self.r, 0, None, self.h)

    def project_weight(self, start, tiles, plan=None):
        def body(index):
            self.w[:, columns(index, start * TILE)] = dot(
                self.turned[...], self.qkv[:, columns(index, start * TILE)]
            ).astype(jnp.bfloat16)

        loop(tiles, body, plan)

    def vectors_back(self):
        packed = jnp.concatenate([self.vec_grad[...], jnp.zeros((120, D), jnp.float32)], axis=0)
        self.w[:, COL_VECTORS : COL_VECTORS + 128] = jnp.transpose(packed).astype(jnp.bfloat16)
        self.w[:, COL_QUERY : COL_QUERY + 128] = jnp.zeros((D, 128), jnp.bfloat16)


def spread_steps(steps, count):
    plan = {}
    for at, step in enumerate(steps):
        plan.setdefault(min(count - 1, at * count // max(len(steps), 1)), []).append(step)
    return plan


TOWER_REFS = (
    ("w", "x", "cap", "h", "qkv", "a", "r", "h2", "g", "gp", "y", "f", "kvp", "lse", "turned", "acc", "vec", "vec_grad", "small_own")
)


def layer_kernel(
    master, tokens, captions, vectors, labels, scalars,
    share_out, vector_out, facts, patch_out, *scratch,
):
    p = Place()
    t = Tower(**dict(zip(TOWER_REFS, scratch)))
    scratch = scratch[len(TOWER_REFS) :]
    stage, small, pair_a, pair_b, b_in, z_in, a_in, last, mine, everyone = scratch[:10]
    share, extra, caps, map_q, map_out, map_q_share, signs = scratch[10:17]
    swap_sems, token_sems, patch_sems, own_sems, send_sem, recv_sem, grant = scratch[17:24]
    gather_s, scatter_s = scratch[24:31], scratch[31:]
    map_q_at = 4 * D + 2 * FF
    map_q_copy = pltpu.make_async_copy(
        master.at[:, map_q_at : map_q_at + D], map_q, own_sems.at[0]
    )
    map_q_copy.start()
    greet_all(p)

    own_vectors = jnp.transpose(
        jnp.concatenate([vectors[...], jnp.zeros((121, 24), jnp.float32)], axis=0)
    )
    own_vectors = own_vectors.astype(jnp.bfloat16).astype(jnp.float32)
    map_q_copy.wait()
    map_q[...] = map_q[...].astype(jnp.bfloat16).astype(jnp.float32)
    part = jnp.sum(own_vectors[:, 6:7] * map_q[...], axis=0, keepdims=True)
    high = part.astype(jnp.bfloat16).astype(jnp.float32)
    for side in range(6):
        lanes = slice(side * 128, side * 128 + 128)
        extra[side : side + 1, 128:256] = high[:, lanes]
        extra[6 + side : 7 + side, 128:256] = (part - high)[:, lanes]
    extra[12:24, 128:256] = jnp.zeros((12, 128), jnp.float32)
    extra[:, 0:128] = own_vectors
    each = captions.shape[0]
    caps[...] = jnp.concatenate(
        [unit_rows(captions[...].astype(jnp.float32)), jnp.zeros((64 - each, D), jnp.float32)], axis=0
    ).astype(jnp.bfloat16)
    slot = lax.broadcasted_iota(jnp.int32, (8 * each, 512), 1)
    within = (slot >> 7) * 16 + (slot & 15)
    source = ((slot >> 5) & 3) * (2 * each) + ((slot >> 4) & 1) * each + within
    label = lax.broadcasted_iota(jnp.int32, (8 * each, 512), 0)
    pick = ((label == source) & (within < each)).astype(jnp.float32).astype(jnp.bfloat16)
    row = 2.0 * labels[pl.ds(p.blk, 1), :].astype(jnp.float32) - 1.0
    signs[...] = dot(jnp.broadcast_to(row, (16, 8 * each)).astype(jnp.bfloat16), pick)
    all_greeted()

    count = len(GATHER_SECTIONS)
    gathers, swaps = [], []
    pieces = (
        (master, 0, 0, 3 * D),
        (extra, 0, 3 * D, 256),
        (master, 3 * D, COL_OUT, D + 2 * FF),
        (master, map_q_at + D, COL_MAP_KV, 3 * D),
    )
    for number, (first, width, z_first) in enumerate(GATHER_SECTIONS):
        swaps.append(
            Swap(p, pieces, stage, 0, 24, first, width, first // 2, swap_sems.at[number])
        )
        swaps[-1].begin()
        gathers.append(
            Gather(p, t.w, CHIP_ROWS, first, width, z_first, [s.at[number] for s in gather_s])
        )
    own_caps = caps.at[pl.ds(aligned(p.blk * 16, 16), 16), :]
    swaps.append(
        Swap(p, ((own_caps, 0, 0, D),), t.cap, p.chip * 32, 16, 0, D, None, swap_sems.at[count])
    )
    swaps[-1].begin()
    gathers.append(Gather(p, t.cap, 32, 0, D, True, [s.at[count] for s in gather_s]))
    token_copies = []
    for step in range(1, 4):
        to = lax.rem(p.blk + step, 4)
        token_copies.append(
            remote(
                tokens.at[to],
                t.x.at[pl.ds(aligned(p.blk * 144, 144), 144), :],
                token_sems.at[0, step - 1],
                token_sems.at[1, step - 1],
                {"blk": to},
            )
        )
        token_copies[-1].start()
    own_tokens = pltpu.make_async_copy(
        tokens.at[p.blk], t.x.at[pl.ds(aligned(p.blk * 144, 144), 144), :], token_sems.at[0, 3]
    )
    own_tokens.start()

    def ready(number):
        swaps[number].finish()
        if number < count:
            first, width, _ = GATHER_SECTIONS[number]
            t.w[
                pl.ds(aligned(p.chip * 48, 48), 48), pl.ds(gathers[number].mine, width // 2)
            ] = stage[:, first // 2 : first // 2 + width // 2].astype(jnp.bfloat16)
        gathers[number].begin()

    order = []
    for number, gather in enumerate(gathers):
        for at, step in enumerate(gather.steps()):
            call = step if at else (lambda number=number: ready(number))
            order.append((gather_key(number, at), number, at, call))
    order.sort(key=lambda entry: entry[:3])
    ends = [
        max(i for i, entry in enumerate(order) if entry[1] <= number)
        for number in range(count + 1)
    ]

    def between(number):
        return [entry[3] for entry in order[ends[number - 1] + 1 : ends[number] + 1]]

    for entry in order[: ends[0] + 1]:
        entry[3]()
    for step in range(3):
        source = lax.rem(p.blk + 3 - step, 4)
        landed = t.x.at[pl.ds(aligned(source * 144, 144), 144), :]
        remote(
            landed, landed, token_sems.at[0, step], token_sems.at[1, step], {"blk": source}
        ).wait_recv()
    own_tokens.wait()
    gathers[0].finish()

    t.unpack()
    t.first_norm()
    t.project()
    t.attend(spread_steps(between(1), 6))
    gathers[1].finish()
    t.attend_out()
    t.feed_up(spread_steps(between(2), 12))
    gathers[2].finish()
    t.feed_down(spread_steps(between(3), 3))
    gathers[3].finish()
    t.pool_project(spread_steps(between(4), 6))
    gathers[4].finish()
    t.vec_grad[...] = jnp.zeros((8, D), jnp.float32)
    images = tokens.shape[0] * 8
    t.pool(signs[0:1, :], jnp.full((1, 512), scalars[0], jnp.float32), scalars[1], images)
    swap = Swap(
        p, ((t.small_own, 0, 0, D),), small, p.chip * 16, 8, 0, D, None, swap_sems.at[count + 1]
    )
    swap.begin()
    small_gather = Gather(p, small, 16, 0, D, True, [s.at[count + 1] for s in gather_s])
    small_steps = small_gather.steps()
    gathers[3].sent()

    sections = []
    for number, (first, width, z_first) in enumerate(SCATTER_SECTIONS):
        half = width // 2
        which, at = PAIR_PLACES[number]
        pair_in = (pair_a, pair_b)[which].at[:, at : at + half]
        if number < 4:
            others = (b_in[number], a_in[number], z_in[number])
        else:
            here = slice(LATE_PLACES[number - 4], LATE_PLACES[number - 4] + half)
            others = (
                t.g.at[0:384, here],
                t.g.at[384 : 432 if z_first else 576, here],
                t.gp.at[0 : 288 if z_first else 144, here],
            )
        bufs = (pair_in, *others, last[number])
        sections.append(
            Scatter(p, t.w, share, first, width, z_first, bufs, [s.at[number] for s in scatter_s])
        )

    def small_begin():
        swap.finish()
        small_steps[0]()

    links, program = Links(*LINK_SPEED), Program()
    timed = []

    def leaves(section, number):
        timed.append((section, program.now, SCATTER_SECTIONS[number][1]))

    leaves(sections[0], 0)
    program.want(zip((0.5, 1.5, 4.5, 7.0, 9.5, 12.0), [small_begin] + small_steps[1:]))
    program.gap(2.5)
    program.loop("down_first", 6, 0.75)
    leaves(sections[1], 1)
    program.loop("down_second", 6, 0.75)
    leaves(sections[2], 2)
    program.loop("up_input", 3, 1.4)
    program.gap(0.5)
    program.loop("up_first", 6, 0.46)
    leaves(sections[3], 3)
    program.loop("up_second", 6, 0.46)
    program.gap(1.7)
    leaves(sections[4], 4)
    program.loop("out", 3, 1.1)
    leaves(sections[5], 5)
    program.loop("attend", 6, 2.05)
    program.gap(1.0)
    program.loop("project_input", 3, 1.0)
    program.gap(2.2)
    program.loop("front", 5, 0.5)
    leaves(sections[6], 6)
    program.loop("end", 4, 0.5)
    program.gap(1.0)
    leaves(sections[7], 7)
    for entry in timed:
        program.want(links.steps(*entry))
    program.settle()
    plans = program.plans
    t.pool_back(None, sections[0].begin)
    t.turn(t.f)
    gathers[2].sent()
    t.down_back(0, 6, plans["down_first"])
    sections[1].begin()
    t.down_back(6, 6, plans["down_second"])
    sections[2].begin()
    t.up_input(plans["up_input"])
    t.turn(t.h2)
    gathers[1].sent()
    t.up_weight(0, 6, plans["up_first"])
    sections[3].begin()
    t.up_weight(6, 6, plans["up_second"])
    levels = [p.on_level(lax.rem(p.z + step, 4)) for step in range(1, 4)]
    for device in (p.sibling, p.a_near, p.b_near, *levels):
        pl.semaphore_signal(grant, inc=1, device_id=device, device_id_type=MESH)
    t.up_norm()
    pl.semaphore_wait(grant, 6)
    sections[4].begin()
    t.out_back(plans["out"])
    sections[5].begin()
    t.attend_back(plans["attend"])
    t.project_input(plans["project_input"])
    patch_copies = []
    for step in range(1, 4):
        to = lax.rem(p.blk + step, 4)
        patch_copies.append(
            remote(
                t.h.at[pl.ds(aligned(to * 144, 144), 144), :],
                patch_out.at[p.blk],
                patch_sems.at[0, step - 1],
                patch_sems.at[1, step - 1],
                {"blk": to},
            )
        )
        patch_copies[-1].start()
    own_patch = pltpu.make_async_copy(
        t.h.at[pl.ds(aligned(p.blk * 144, 144), 144), :], patch_out.at[p.blk], patch_sems.at[0, 3]
    )
    own_patch.start()
    gathers[0].sent()
    t.project_weight(0, 5, plans["front"])
    sections[6].begin()
    t.project_weight(5, 4, plans["end"])
    t.vectors_back()
    sections[7].begin()
    small_gather.finish()
    probe_share, square = small_tail(
        p, small, map_q[...], own_vectors[:, 6:7], map_out, map_q_share
    )
    small_gather.sent()
    gathers[4].sent()
    for copy in token_copies:
        copy.wait_send()
    outs = [
        pltpu.make_async_copy(source, share_out.at[:, target : target + D], own_sems.at[4 + number])
        for number, (source, target) in enumerate(
            ((map_q_share, map_q_at), (map_out, map_q_at + 3 * D))
        )
    ]
    for out in outs:
        out.start()
    for step in program.tail[:-2]:
        step()
    for step, copy in enumerate(patch_copies):
        source = lax.rem(p.blk + 3 - step, 4)
        landed = patch_out.at[source]
        remote(
            landed, landed, patch_sems.at[0, step], patch_sems.at[1, step], {"blk": source}
        ).wait_recv()
        copy.wait_send()
    own_patch.wait()
    square = square_share(share, square, COL_OUT // 256, SCATTER_COLS // 256)
    for step in program.tail[-2:]:
        step()
    spread = Spread(p, mine, everyone, send_sem, recv_sem)
    spread.begin(jnp.full((8, 128), square_share(share, square, 0, COL_OUT // 256), jnp.float32))
    for number, (source, target, width) in enumerate(
        ((0, 0, 3 * D), (COL_OUT, 3 * D, D + 2 * FF), (COL_MAP_KV, map_q_at + D, 2 * D))
    ):
        outs.append(
            pltpu.make_async_copy(
                share.at[:, source : source + width],
                share_out.at[:, target : target + width],
                own_sems.at[1 + number],
            )
        )
        outs[-1].start()
    lane = lax.broadcasted_iota(jnp.int32, (24, 128), 1)
    vector_out[...] = jnp.transpose(
        jnp.where(lane == 6, probe_share, share[:, COL_VECTORS : COL_VECTORS + 128])
    )[0:8]
    sums, norm = spread.finish(small)
    facts[...] = jnp.concatenate([jnp.broadcast_to(sums[:, :128], (7, 128)), norm[:1]], axis=0)
    for out in outs:
        out.wait()


def layer_call(master, tokens, captions, vectors, labels, scalars):
    dma = pltpu.SemaphoreType.DMA
    f32 = jnp.float32
    gathers = len(GATHER_SECTIONS) + 2
    count = len(SCATTER_SECTIONS)
    widths = [entry[1] // 2 for entry in SCATTER_SECTIONS]

    def vm(*shape, dt=jnp.bfloat16):
        return pltpu.VMEM(shape, dt)

    vmem = pl.BlockSpec(memory_space=pltpu.VMEM)
    return pl.pallas_call(
        layer_kernel,
        out_shape=(
            jax.ShapeDtypeStruct((24, 8 * D + 2 * FF), f32),
            jax.ShapeDtypeStruct((8, 24), f32),
            jax.ShapeDtypeStruct((8, 128), f32),
            jax.ShapeDtypeStruct((4, 144, D), jnp.bfloat16),
        ),
        in_specs=[
            pl.BlockSpec(memory_space=pl.ANY),
            pl.BlockSpec(memory_space=pl.ANY),
            vmem,
            vmem,
            vmem,
            pl.BlockSpec(memory_space=pltpu.SMEM),
        ],
        out_specs=(
            pl.BlockSpec(memory_space=pl.ANY),
            vmem,
            vmem,
            pl.BlockSpec(memory_space=pl.ANY),
        ),
        scratch_shapes=[
            vm(D, GATHER_COLS),
            vm(TOKENS, D),
            vm(512, D),
            vm(TOKENS, D),
            vm(TOKENS, 3 * D),
            vm(TOKENS, D),
            vm(TOKENS, D, dt=f32),
            vm(TOKENS, D),
            vm(TOKENS, FF),
            vm(TOKENS, FF),
            vm(TOKENS, D, dt=f32),
            vm(TOKENS, D),
            vm(TOKENS, 2 * D),
            vm(16, TOKENS, dt=f32),
            vm(D, TOKENS),
            vm(TOKENS, D, dt=f32),
            vm(16, D, dt=f32),
            vm(8, D, dt=f32),
            vm(8, D, dt=f32),
            vm(48, GATHER_COLS // 2, dt=f32),
            vm(256, D, dt=f32),
            vm(D, 1920),
            vm(D, 1536),
            [vm(384, w) for w in widths[:4]],
            [vm(288 if entry[2] else 144, entry[1] // 2) for entry in SCATTER_SECTIONS[:4]],
            [vm(48 if entry[2] else 192, entry[1] // 2) for entry in SCATTER_SECTIONS[:4]],
            [vm(48, w, dt=f32) for w in widths],
            vm(8, 128, dt=f32),
            vm(31, 8, 128, dt=f32),
            vm(24, SCATTER_COLS, dt=f32),
            vm(24, 256, dt=f32),
            vm(64, D),
            vm(24, D, dt=f32),
            vm(24, D, dt=f32),
            vm(24, D, dt=f32),
            vm(16, 512, dt=f32),
            dma((gathers, 4)),
            dma((2, 4)),
            dma((2, 4)),
            dma((6,)),
            dma,
            dma,
            pltpu.SemaphoreType.REGULAR,
            *gather_sems(gathers),
            dma((count, 2)),
            dma((count, 2, 2)),
            dma((count, 2)),
            dma((count, 2, 2, 3)),
            dma((count, 2)),
        ],
        compiler_params=pltpu.CompilerParams(
            collective_id=0, has_side_effects=True, vmem_limit_bytes=63 * 2**20
        ),
        name="layer_step",
    )(master, tokens, captions, vectors, labels, scalars)


def local_kernel(
    patch_tokens,
    captions,
    pair_labels,
    master_weights,
    first_moments,
    second_moments,
    master_vectors,
    vector_first,
    vector_second,
    loss_scalars,
    scalar_first,
    scalar_second,
):
    weight_share, vector_share, facts, patch_grad = layer_call(
        master_weights, patch_tokens, captions, master_vectors.T, pair_labels, loss_scalars
    )
    vector_share = vector_share[:7].T
    patch_grad = patch_grad.astype(jnp.float32)
    loss_total, scalar_total, grad_norm = facts[0, 0], facts[0, 1:3], facts[7, 0]
    factor = CLIP_AT / jnp.maximum(grad_norm, CLIP_AT)
    new_w, new_wm, new_wv = adamw(
        master_weights, weight_share * factor, first_moments, second_moments, 0.03, 0.1
    )
    new_v, new_vm, new_vv = adamw(
        master_vectors, vector_share * factor, vector_first, vector_second, 0.3, 0.0
    )
    new_s, new_sm, new_sv = adamw(
        loss_scalars, scalar_total * factor, scalar_first, scalar_second, 0.3, 0.0
    )
    return (
        loss_total,
        grad_norm,
        patch_grad,
        new_w,
        new_wm,
        new_wv,
        new_w.astype(jnp.bfloat16),
        new_v,
        new_vm,
        new_vv,
        new_v.astype(jnp.bfloat16),
        new_s,
        new_sm,
        new_sv,
    )


def solution(mesh):
    in_specs = (
        P("img", "blk", None),
        P("img", None),
        P("img", None),
        P(("blk", "img"), None),
        P(("blk", "img"), None),
        P(("blk", "img"), None),
        P(("blk", "img"), None),
        P(("blk", "img"), None),
        P(("blk", "img"), None),
        P(),
        P(),
        P(),
    )
    out_specs = (
        P(),
        P(),
        P("img", "blk", None),
        P(("blk", "img"), None),
        P(("blk", "img"), None),
        P(("blk", "img"), None),
        P(("blk", "img"), None),
        P(("blk", "img"), None),
        P(("blk", "img"), None),
        P(("blk", "img"), None),
        P(("blk", "img"), None),
        P(),
        P(),
        P(),
    )
    body = local_kernel if tuple(mesh.shape.values()) == (4, 8) else local
    return jax.shard_map(body, mesh=mesh, in_specs=in_specs, out_specs=out_specs, check_vma=False)
```

```python
import functools

import jax
import jax.numpy as jnp
from jax import lax
from jax.experimental import pallas as pl
from jax.experimental.pallas import tpu as pltpu
from jax.sharding import PartitionSpec as P

D = 768
HEADS = 12
HEAD_DIM = 64
FF = 3072
STEP = 10


BETA_ONE = 0.9
BETA_TWO = 0.999
EPS_ADAM = 1e-08
CLIP_AT = 1.0


def layer_norm(values, gain_vec, bias_vec):
    row_mean = jnp.mean(values, axis=-1, keepdims=True)
    centered = values - row_mean
    row_var = jnp.mean(centered * centered, axis=-1, keepdims=True)
    return centered * lax.rsqrt(row_var + 1e-06) * gain_vec + bias_vec


def unit_rows(pooled):
    return pooled * lax.rsqrt(jnp.sum(pooled * pooled, axis=-1, keepdims=True) + 1e-06)


def attend(queries, keys_all, values_all):
    scale = HEAD_DIM ** (-0.5)
    scores = (
        jnp.einsum("iqhe,ikhe->ihqk", queries, keys_all, preferred_element_type=jnp.float32) * scale
    )
    row_max = jnp.max(scores, axis=-1, keepdims=True)
    expos = jnp.exp(scores - row_max)
    row_sum = jnp.sum(expos, axis=-1, keepdims=True)
    attn_probs = (expos / row_sum).astype(jnp.bfloat16)
    mixed_out = jnp.einsum(
        "ihqk,ikhe->iqhe", attn_probs, values_all, preferred_element_type=jnp.float32
    )
    return (mixed_out.astype(jnp.bfloat16), row_max + jnp.log(row_sum))


def attend_back(queries, keys_all, values_all, log_norm, grad_mixed):
    scale = HEAD_DIM ** (-0.5)
    scores = (
        jnp.einsum("iqhe,ikhe->ihqk", queries, keys_all, preferred_element_type=jnp.float32) * scale
    )
    attn_probs = jnp.exp(scores - log_norm)
    grad_values = jnp.einsum(
        "ihqk,iqhe->ikhe",
        attn_probs.astype(jnp.bfloat16),
        grad_mixed,
        preferred_element_type=jnp.float32,
    )
    grad_probs = jnp.einsum(
        "iqhe,ikhe->ihqk", grad_mixed, values_all, preferred_element_type=jnp.float32
    )
    centre = jnp.sum(attn_probs * grad_probs, axis=-1, keepdims=True)
    grad_scores = (attn_probs * (grad_probs - centre)).astype(jnp.bfloat16)
    grad_queries = (
        jnp.einsum("ihqk,ikhe->iqhe", grad_scores, keys_all, preferred_element_type=jnp.float32)
        * scale
    )
    grad_keys = (
        jnp.einsum("ihqk,iqhe->ikhe", grad_scores, queries, preferred_element_type=jnp.float32)
        * scale
    )
    return (grad_queries, grad_keys, grad_values)


def adamw(parameter, gradient, moment_one, moment_two, step_rate, decay_rate):
    moment_one = BETA_ONE * moment_one + (1.0 - BETA_ONE) * gradient
    moment_two = BETA_TWO * moment_two + (1.0 - BETA_TWO) * gradient * gradient
    first_hat = moment_one / (1.0 - BETA_ONE**STEP)
    second_hat = moment_two / (1.0 - BETA_TWO**STEP)
    updated = parameter - step_rate * (
        first_hat / (jnp.sqrt(second_hat) + EPS_ADAM) + decay_rate * parameter
    )
    return (updated, moment_one, moment_two)


def local(
    patch_tokens,
    captions,
    pair_labels,
    master_weights,
    first_moments,
    second_moments,
    master_vectors,
    vector_first,
    vector_second,
    loss_scalars,
    scalar_first,
    scalar_second,
):
    blocks = lax.axis_size("blk")
    block = lax.axis_index("blk")
    all_images = patch_tokens.shape[0] * lax.axis_size("img")
    images = patch_tokens.shape[0] // blocks
    length = patch_tokens.shape[1] * blocks
    scale = HEAD_DIM ** (-0.5)
    both = ("blk", "img")
    rows = master_weights.shape[0]
    first_row = lax.axis_index(both) * rows
    patch_tokens = lax.all_to_all(patch_tokens, "blk", 0, 1, tiled=True)
    pair_labels = lax.dynamic_slice_in_dim(pair_labels, block * images, images, 0)
    rounded = master_weights.astype(jnp.bfloat16)
    full_vectors = lax.all_gather(master_vectors.astype(jnp.bfloat16), both, axis=0, tiled=True)
    vectors = full_vectors.astype(jnp.float32)

    def gather(start, stop):
        return lax.all_gather(rounded[:, start:stop], both, axis=0, tiled=True)

    w_front = gather(0, 4 * D)
    w_qkv = w_front[:, : 3 * D]
    w_out = w_front[:, 3 * D :]
    w_up = gather(4 * D, 4 * D + FF)
    w_down = gather(4 * D + FF, 4 * D + 2 * FF)
    own_map_q = rounded[:, 4 * D + 2 * FF : 5 * D + 2 * FF]
    w_map = gather(5 * D + 2 * FF, 8 * D + 2 * FF)
    w_map_kv = w_map[:, : 2 * D]
    w_map_out = w_map[:, 2 * D :]
    own_vectors = master_vectors.astype(jnp.bfloat16)
    tokens = patch_tokens.astype(jnp.float32)
    normed, norm_one_pull = jax.vjp(layer_norm, tokens, vectors[:, 0], vectors[:, 1])
    normed_b = normed.astype(jnp.bfloat16)
    qkv_b = jnp.einsum("ipd,dc->ipc", normed_b, w_qkv, preferred_element_type=jnp.float32).astype(
        jnp.bfloat16
    )
    queries = qkv_b[:, :, :D].reshape(images, length, HEADS, HEAD_DIM)
    keys_all = qkv_b[:, :, D : 2 * D].reshape(images, length, HEADS, HEAD_DIM)
    values_all = qkv_b[:, :, 2 * D :].reshape(images, length, HEADS, HEAD_DIM)
    mixed_heads, log_norm = attend(queries, keys_all, values_all)
    mixed_b = mixed_heads.reshape(images, length, D)
    residual = tokens + jnp.einsum(
        "ipd,dc->ipc", mixed_b, w_out, preferred_element_type=jnp.float32
    )
    hidden, norm_two_pull = jax.vjp(layer_norm, residual, vectors[:, 2], vectors[:, 3])
    hidden_b = hidden.astype(jnp.bfloat16)
    pre_act = jnp.einsum("ipd,df->ipf", hidden_b, w_up, preferred_element_type=jnp.float32)
    activation, gelu_pull = jax.vjp(jax.nn.gelu, pre_act)
    activation_b = activation.astype(jnp.bfloat16)
    layer_out = residual + jnp.einsum(
        "ipf,df->ipd", activation_b, w_down, preferred_element_type=jnp.float32
    )
    final_norm, norm_three_pull = jax.vjp(layer_norm, layer_out, vectors[:, 4], vectors[:, 5])
    final_b = final_norm.astype(jnp.bfloat16)
    map_kv = jnp.einsum("ipd,dc->ipc", final_b, w_map_kv, preferred_element_type=jnp.float32)
    map_kv = map_kv.astype(jnp.bfloat16).reshape(images, length, 2, HEADS, HEAD_DIM)
    probe_query = lax.psum(
        jnp.dot(own_vectors[:, 6], own_map_q, preferred_element_type=jnp.float32), both
    )
    probe_query = probe_query.astype(jnp.bfloat16).reshape(HEADS, HEAD_DIM)
    pool_scores = (
        jnp.einsum("he,iphe->ihp", probe_query, map_kv[:, :, 0], preferred_element_type=jnp.float32)
        * scale
    )
    row_max = jnp.max(pool_scores, axis=-1)
    row_sum = jnp.sum(jnp.exp(pool_scores - row_max[..., None]), axis=-1)
    pool_probs = jnp.exp(pool_scores - row_max[..., None]) / row_sum[..., None]
    map_values = map_kv[:, :, 1].astype(jnp.float32)
    pooled_part = jnp.einsum(
        "ihp,iphe->ihe", pool_probs, map_values, precision=lax.Precision.HIGHEST
    )
    pooled_heads = pooled_part.reshape(images, D)
    pooled_heads_b = pooled_heads.astype(jnp.bfloat16)
    pooled = jnp.dot(pooled_heads_b, w_map_out, preferred_element_type=jnp.float32)
    caption_all = lax.all_gather(captions, "img", axis=0, tiled=True).astype(jnp.float32)
    caption_unit = unit_rows(caption_all).astype(jnp.bfloat16)
    unit_image, unit_pull = jax.vjp(unit_rows, pooled)
    cosine = jnp.einsum(
        "id,cd->ic",
        unit_image.astype(jnp.bfloat16),
        caption_unit,
        preferred_element_type=jnp.float32,
    )
    signs = 2.0 * pair_labels.astype(jnp.float32) - 1.0

    def pair_loss(cosine_in, scalars_in):
        logits = jnp.exp(scalars_in[0]) * cosine_in + scalars_in[1]
        return jnp.sum(jax.nn.softplus(-signs * logits)) / all_images

    loss_local, loss_pull = jax.vjp(pair_loss, cosine, loss_scalars)
    grad_cosine, grad_scalars = loss_pull(jnp.ones((), jnp.float32))
    loss_total, scalar_total = lax.psum((loss_local, grad_scalars), both)
    grad_unit = jnp.einsum(
        "ic,cd->id",
        grad_cosine.astype(jnp.bfloat16),
        caption_unit,
        preferred_element_type=jnp.float32,
    )
    (grad_pooled,) = unit_pull(grad_unit)
    grad_pooled_b = grad_pooled.astype(jnp.bfloat16)
    pooled_all, grad_pooled_all = (
        lax.all_gather(pooled_heads_b, both, axis=0, tiled=True),
        lax.all_gather(grad_pooled_b, both, axis=0, tiled=True),
    )
    share_map_out = jnp.einsum(
        "id,ic->dc",
        lax.dynamic_slice_in_dim(pooled_all, first_row, rows, 1),
        grad_pooled_all,
        preferred_element_type=jnp.float32,
    )
    grad_heads_b = jnp.einsum(
        "ic,dc->id", grad_pooled_b, w_map_out, preferred_element_type=jnp.float32
    )
    grad_heads_b = grad_heads_b.astype(jnp.bfloat16).reshape(images, HEADS, HEAD_DIM)
    grad_heads = grad_heads_b.astype(jnp.float32)
    centre = jnp.sum(grad_heads * pooled_heads.reshape(images, HEADS, HEAD_DIM), axis=-1)
    grad_probs = jnp.einsum(
        "ihe,iphe->ihp", grad_heads_b, map_kv[:, :, 1], preferred_element_type=jnp.float32
    )
    grad_pool_scores = (pool_probs * (grad_probs - centre[..., None])).astype(jnp.bfloat16)
    grad_map_keys = (
        jnp.einsum(
            "ihp,he->iphe", grad_pool_scores, probe_query, preferred_element_type=jnp.float32
        )
        * scale
    )
    grad_map_values = jnp.einsum(
        "ihp,ihe->iphe", pool_probs, grad_heads, precision=lax.Precision.HIGHEST
    )
    grad_probe_query = (
        jnp.einsum(
            "ihp,iphe->he", grad_pool_scores, map_kv[:, :, 0], preferred_element_type=jnp.float32
        ).reshape(D)
        * scale
    )
    grad_map_kv = (
        jnp.stack([grad_map_keys, grad_map_values], axis=2)
        .astype(jnp.bfloat16)
        .reshape(images, length, 2 * D)
    )
    grad_w_map_kv = jnp.einsum(
        "ipd,ipc->dc", final_b, grad_map_kv, preferred_element_type=jnp.float32
    )
    grad_final = jnp.einsum(
        "ipc,dc->ipd", grad_map_kv, w_map_kv, preferred_element_type=jnp.float32
    )
    grad_layer_out, grad_gain_three, grad_bias_three = norm_three_pull(grad_final)
    probe_total = lax.psum(grad_probe_query, both)
    share_map_q = jnp.outer(own_vectors[:, 6].astype(jnp.float32), probe_total)
    share_probe = jnp.dot(
        own_map_q.astype(jnp.float32), probe_total, precision=lax.Precision.HIGHEST
    )
    grad_branch_two = grad_layer_out.astype(jnp.bfloat16)
    grad_w_down = jnp.einsum(
        "ipd,ipf->df", grad_branch_two, activation_b, preferred_element_type=jnp.float32
    )
    grad_activation = jnp.einsum(
        "ipd,df->ipf", grad_branch_two, w_down, preferred_element_type=jnp.float32
    )
    (grad_pre,) = gelu_pull(grad_activation)
    grad_pre_b = grad_pre.astype(jnp.bfloat16)
    grad_w_up = jnp.einsum("ipd,ipf->df", hidden_b, grad_pre_b, preferred_element_type=jnp.float32)
    grad_hidden = jnp.einsum("ipf,df->ipd", grad_pre_b, w_up, preferred_element_type=jnp.float32)
    grad_res_part, grad_gain_two, grad_bias_two = norm_two_pull(grad_hidden)
    grad_residual = grad_layer_out + grad_res_part
    grad_branch_one = grad_residual.astype(jnp.bfloat16)
    grad_w_out = jnp.einsum(
        "ipd,ipc->dc", mixed_b, grad_branch_one, preferred_element_type=jnp.float32
    )
    grad_mixed = jnp.einsum(
        "ipc,dc->ipd", grad_branch_one, w_out, preferred_element_type=jnp.float32
    )
    grad_mixed = grad_mixed.astype(jnp.bfloat16)
    grad_queries, grad_keys, grad_values = attend_back(
        queries, keys_all, values_all, log_norm, grad_mixed.reshape(images, length, HEADS, HEAD_DIM)
    )
    grad_qkv = jnp.concatenate(
        [
            grad_queries.reshape(images, length, D),
            grad_keys.reshape(images, length, D),
            grad_values.reshape(images, length, D),
        ],
        axis=-1,
    ).astype(jnp.bfloat16)
    grad_w_qkv = jnp.einsum("ipd,ipc->dc", normed_b, grad_qkv, preferred_element_type=jnp.float32)
    grad_normed = jnp.einsum("ipc,dc->ipd", grad_qkv, w_qkv, preferred_element_type=jnp.float32)
    grad_tok_part, grad_gain_one, grad_bias_one = norm_one_pull(grad_normed)
    patch_grad = lax.all_to_all(
        (grad_residual + grad_tok_part).astype(jnp.bfloat16), "blk", 1, 0, tiled=True
    ).astype(jnp.float32)
    grad_vectors = jnp.stack(
        [
            grad_gain_one,
            grad_bias_one,
            grad_gain_two,
            grad_bias_two,
            grad_gain_three,
            grad_bias_three,
        ],
        axis=1,
    )

    def scatter(part):
        return lax.psum_scatter(
            part.astype(jnp.bfloat16), both, scatter_dimension=0, tiled=True
        ).astype(jnp.float32)

    share_map_kv = scatter(grad_w_map_kv)
    share_down = scatter(grad_w_down)
    share_up = scatter(grad_w_up)
    share_front = scatter(jnp.concatenate([grad_w_qkv, grad_w_out], axis=1))
    weight_share = jnp.concatenate(
        [share_front, share_up, share_down, share_map_q, share_map_kv, share_map_out], axis=1
    )
    vector_share = jnp.concatenate(
        [
            lax.psum_scatter(grad_vectors, both, scatter_dimension=0, tiled=True),
            share_probe[:, None],
        ],
        axis=1,
    )
    squares = jnp.sum(weight_share * weight_share) + jnp.sum(vector_share * vector_share)
    square_total = lax.psum(squares, ("blk", "img"))
    grad_norm = jnp.sqrt(square_total + jnp.sum(scalar_total * scalar_total))
    factor = CLIP_AT / jnp.maximum(grad_norm, CLIP_AT)
    new_w, new_wm, new_wv = adamw(
        master_weights, weight_share * factor, first_moments, second_moments, 0.03, 0.1
    )
    new_v, new_vm, new_vv = adamw(
        master_vectors, vector_share * factor, vector_first, vector_second, 0.3, 0.0
    )
    new_s, new_sm, new_sv = adamw(
        loss_scalars, scalar_total * factor, scalar_first, scalar_second, 0.3, 0.0
    )
    return (
        loss_total,
        grad_norm,
        patch_grad,
        new_w,
        new_wm,
        new_wv,
        new_w.astype(jnp.bfloat16),
        new_v,
        new_vm,
        new_vv,
        new_v.astype(jnp.bfloat16),
        new_s,
        new_sm,
        new_sv,
    )


LINK_SPEED = (1.1, 5.0)


def gather_key(number, at):
    return 0 if at == 0 else at + number


MESH = pl.DeviceIdType.MESH
CHIP_ROWS = 48
GATHER_SECTIONS = ((0, 2560, False), (2560, 3840, True), (6400, 3072, False), (9472, 2304, False))
SCATTER_SECTIONS = (
    (9472, 1536, False),
    (6400, 1536, False),
    (7936, 1536, False),
    (3328, 1536, False),
    (4864, 1536, False),
    (2560, 768, False),
    (0, 1280, False),
    (1280, 1280, False),
)
PAIR_PLACES = ((0, 0), (0, 768), (1, 0), (1, 768), (0, 0), (0, 1536), (0, 768), (1, 0))
LATE_PLACES = (0, 768, 1152, 1792)
GATHER_COLS = 11776
SCATTER_COLS = 11008


def aligned(value, step):
    return pl.multiple_of(value, step)


class Place:
    def __init__(self):
        self.blk = lax.axis_index("blk")
        self.img = lax.axis_index("img")
        self.x = lax.rem(self.blk, 2)
        self.y = self.blk // 2
        self.z = self.img // 2
        self.c = lax.rem(self.img, 2)
        self.chip = self.blk * 4 + self.z
        self.sibling = {"img": self.z * 2 + 1 - self.c}
        self.up = {"img": self.img + 2}
        self.down = {"img": self.img - 2}
        self.a_near = {"blk": self.block(1, 0)}
        self.b_near = {"blk": self.block(0, 1)}

    def on_level(self, level):
        return {"img": level * 2 + self.c}

    def block(self, da, db):
        flip_x = da * (1 - self.c) + db * self.c
        flip_y = db * (1 - self.c) + da * self.c
        other_x = self.x + flip_x * (1 - 2 * self.x)
        other_y = self.y + flip_y * (1 - 2 * self.y)
        return other_y * 2 + other_x


def remote(src, dst, send_sem, recv_sem, device):
    return pltpu.make_async_remote_copy(
        src_ref=src,
        dst_ref=dst,
        send_sem=send_sem,
        recv_sem=recv_sem,
        device_id=device,
        device_id_type=MESH,
    )


def greet_all(place):
    barrier = pltpu.get_barrier_semaphore()
    me = place.blk * 8 + place.img

    def greet(step, carry):
        other = lax.rem(me + step, 32)
        pl.semaphore_signal(
            barrier,
            inc=1,
            device_id={"blk": other // 8, "img": lax.rem(other, 8)},
            device_id_type=MESH,
        )
        return carry

    lax.fori_loop(1, 32, greet, 0)


def all_greeted():
    pl.semaphore_wait(pltpu.get_barrier_semaphore(), 31)


class Gather:
    def __init__(self, place, buf, rows, first, width, z_first, sems):
        self.p, self.buf, self.rows, self.half = place, buf, rows, width // 2
        self.z_first = z_first
        self.mine = aligned(first + place.c * self.half, 128)
        self.theirs = aligned(first + (1 - place.c) * self.half, 128)
        self.near_recv, self.z_recv, self.b_recv, self.near_send, self.z_send, self.b_send, self.pair = sems

    def item(self, da, db, level):
        start = aligned((self.p.block(da, db) * 4 + level) * self.rows, self.rows)
        return self.buf.at[pl.ds(start, self.rows), pl.ds(self.mine, self.half)]

    def a_copy(self, level, da=0):
        part = self.item(da, 0, level)
        return remote(part, part, self.near_send.at[level], self.near_recv.at[level], self.p.a_near)

    def z_copy(self, da, level, up):
        part = self.item(da, 0, level)
        device = self.p.up if up else self.p.down
        return remote(part, part, self.z_send.at[up, da, level], self.z_recv.at[da, level], device)

    def b_copy(self, da, level):
        part = self.item(da, 0, level)
        return remote(part, part, self.b_send.at[da, level], self.b_recv.at[da, level], self.p.b_near)

    def pair_copy(self, da, db):
        start = aligned(self.p.block(da, db) * (4 * self.rows), 4 * self.rows)
        part = self.buf.at[pl.ds(start, 4 * self.rows), pl.ds(self.mine, self.half)]
        return remote(part, part, self.pair.at[0], self.pair.at[1], self.p.sibling)

    def onward(self, da, level, up, down):
        if self.z_first and da == 0:
            self.a_copy(level).start()
        self.b_copy(da, level).start()
        if up:
            pl.when(self.p.z < 3)(lambda: self.z_copy(da, level, 1).start())
        if down:
            pl.when(self.p.z > 0)(lambda: self.z_copy(da, level, 0).start())

    def begin(self):
        if not self.z_first:
            self.a_copy(self.p.z).start()
        self.onward(0, self.p.z, True, True)

    def near(self):
        z = self.p.z
        if not self.z_first:
            self.a_copy(z, 1).wait_recv()
            self.onward(1, z, True, True)
            return
        for step in range(4):
            level = lax.rem(z + step, 4)
            self.a_copy(level, 1).wait_recv()
            self.onward(1, level, False, False)
        self.pair_copy(1, 0).start()

    def level(self, distance):
        z = self.p.z
        sides = 1 if self.z_first else 2

        @pl.when(z >= distance)
        def from_below():
            for da in range(sides):
                self.z_copy(da, z - distance, 1).wait_recv()
                self.onward(da, z - distance, True, False)

        @pl.when(z + distance <= 3)
        def from_above():
            for da in range(sides):
                self.z_copy(da, z + distance, 0).wait_recv()
                self.onward(da, z + distance, False, True)

        if distance == 3:
            for da in range(sides):
                self.pair_copy(da, 0).start()

    def far(self):
        for da in range(2):
            for level in range(4):
                part = self.item(da, 1, level)
                remote(
                    part, part, self.b_send.at[da, level], self.b_recv.at[da, level], self.p.b_near
                ).wait_recv()
            self.pair_copy(da, 1).start()

    def finish(self):
        whole = self.buf.at[pl.ds(0, 16 * self.rows), pl.ds(self.theirs, self.half)]
        both = remote(whole, whole, self.pair.at[0], self.pair.at[1], self.p.sibling)
        both.wait_recv()

    def sent(self):
        z = self.p.z
        whole = self.buf.at[pl.ds(0, 16 * self.rows), pl.ds(self.mine, self.half)]
        remote(whole, whole, self.pair.at[0], self.pair.at[1], self.p.sibling).wait_send()
        if not self.z_first:
            self.a_copy(z).wait_send()
        for level in range(4):
            if self.z_first:
                self.a_copy(level).wait_send()
            for da in range(2):
                self.b_copy(da, level).wait_send()
            for da in range(1 if self.z_first else 2):
                if level < 3:
                    pl.when((z >= level) & (z < 3))(
                        lambda da=da, level=level: self.z_copy(da, level, 1).wait_send()
                    )
                if level > 0:
                    pl.when((z <= level) & (z > 0))(
                        lambda da=da, level=level: self.z_copy(da, level, 0).wait_send()
                    )

    def steps(self):
        levels = [functools.partial(self.level, distance) for distance in (1, 2, 3)]
        if self.z_first:
            return [self.begin, *levels, self.near, self.far]
        return [self.begin, self.near, *levels, self.far]


def gather_sems(count):
    dma = pltpu.SemaphoreType.DMA
    return [
        dma((count, 4)),
        dma((count, 2, 4)),
        dma((count, 2, 4)),
        dma((count, 4)),
        dma((count, 2, 2, 4)),
        dma((count, 2, 4)),
        dma((count, 2)),
    ]


class Scatter:
    def __init__(self, place, buf, share, first, width, z_first, bufs, sems):
        self.p, self.buf, self.share, self.half = place, buf, share, width // 2
        self.z_first = z_first
        self.mine = aligned(first + place.c * self.half, 128)
        self.theirs = aligned(first + (1 - place.c) * self.half, 128)
        self.pair_in, self.b_in, self.a_in, self.z_in, self.last = bufs
        self.pair, self.b_sem, self.a_sem, self.z_sem, self.end = sems

    def run_rows(self, da, db):
        return aligned(self.p.block(da, db) * 192, 192)

    def run(self, da, db):
        return self.buf.at[pl.ds(self.run_rows(da, db), 192), pl.ds(self.mine, self.half)]

    def level_rows(self, da, level):
        return aligned((self.p.block(da, 0) * 4 + level) * 48, 48)

    def part(self, da, level):
        return self.buf.at[pl.ds(self.level_rows(da, level), 48), pl.ds(self.mine, self.half)]

    def add(self, row, source, count, offset=0):
        def one(step, carry):
            here = aligned(row + step * 48, 48)
            there = aligned(offset + step * 48, 48)
            self.buf[pl.ds(here, 48), pl.ds(self.mine, self.half)] += source[pl.ds(there, 48), :]
            return carry

        if count == 1:
            one(0, 0)
        else:
            lax.fori_loop(0, count, one, 0)

    def pair_copy(self):
        return remote(
            self.buf.at[pl.ds(0, 768), pl.ds(self.theirs, self.half)],
            self.pair_in,
            self.pair.at[0],
            self.pair.at[1],
            self.p.sibling,
        )

    def b_copy(self, da):
        return remote(
            self.run(da, 1),
            self.b_in.at[da * 192 : da * 192 + 192, :],
            self.b_sem.at[0, da],
            self.b_sem.at[1, da],
            self.p.b_near,
        )

    def a_copy(self):
        source = self.part(1, self.p.z) if self.z_first else self.run(1, 0)
        return remote(source, self.a_in, self.a_sem.at[0], self.a_sem.at[1], self.p.a_near)

    def z_slot(self, da, step):
        return slice(da * 144 + (3 - step) * 48, da * 144 + (4 - step) * 48)

    def z_copy(self, da, step):
        level = lax.rem(self.p.z + step, 4)
        return remote(
            self.part(da, level),
            self.z_in.at[self.z_slot(da, step), :],
            self.z_sem.at[0, da, 3 - step],
            self.z_sem.at[1, da, 3 - step],
            self.p.on_level(level),
        )

    def z_start(self, da):
        for step in (2, 1, 3):
            self.z_copy(da, step).start()

    def z_total(self, da):
        total = self.buf[pl.ds(self.level_rows(da, self.p.z), 48), pl.ds(self.mine, self.half)]
        total = total.astype(jnp.float32)
        for step in (1, 3, 2):
            self.z_copy(da, step).wait_recv()
            total += self.z_in[self.z_slot(da, step), :].astype(jnp.float32)
        return total

    def end_copy(self):
        return remote(
            self.last.at[pl.ds(aligned((1 - self.p.c) * 24, 8), 24), :],
            self.share.at[:, pl.ds(self.mine, self.half)],
            self.end.at[0],
            self.end.at[1],
            self.p.sibling,
        )

    def begin(self):
        self.pair_copy().start()

    def pairs_far(self):
        self.pair_copy().wait_recv()
        for da in range(2):
            row = self.run_rows(da, 1)
            self.add(row, self.pair_in, 4, row)
            self.b_copy(da).start()

    def pairs_near(self):
        for da in range(2):
            row = self.run_rows(da, 0)
            self.add(row, self.pair_in, 4, row)

    def blocks(self):
        for da in (1, 0):
            self.b_copy(da).wait_recv()
            self.add(self.run_rows(da, 0), self.b_in, 4, da * 192)
            if self.z_first:
                self.z_start(da)
            elif da == 1:
                self.a_copy().start()

    def joined(self):
        if self.z_first:
            self.buf[pl.ds(self.level_rows(1, self.p.z), 48), pl.ds(self.mine, self.half)] = (
                self.z_total(1).astype(jnp.bfloat16)
            )
            self.a_copy().start()
        else:
            self.a_copy().wait_recv()
            self.add(self.run_rows(0, 0), self.a_in, 4)
            self.z_start(0)

    def close(self):
        total = self.z_total(0)
        if self.z_first:
            self.a_copy().wait_recv()
            total += self.a_in[...].astype(jnp.float32)
        self.last[...] = total
        self.end_copy().start()
        self.share[:, pl.ds(self.mine, self.half)] = self.last[
            pl.ds(aligned(self.p.c * 24, 8), 24), :
        ]

    def finish(self):
        theirs = self.share.at[:, pl.ds(self.theirs, self.half)]
        remote(theirs, theirs, self.end.at[0], self.end.at[1], self.p.sibling).wait_recv()
        self.end_copy().wait_send()
        self.a_copy().wait_send()
        self.pair_copy().wait_send()
        for da in range(2):
            self.b_copy(da).wait_send()
        for da in range(2 if self.z_first else 1):
            for step in range(1, 4):
                self.z_copy(da, step).wait_send()


class Links:
    def __init__(self, slow=1.0, hop=2.0):
        self.flat = self.high = 0.0
        self.slow, self.hop = slow, hop

    def use(self, name, start, time):
        start = max(start, getattr(self, name))
        setattr(self, name, start + time * self.slow)
        return start + time * self.slow + self.hop

    def steps(self, section, start, width):
        size = width / 256
        out = []
        now = start + 0.35 * size * self.slow + 1.0
        out += [(now, section.pairs_far), (now + 0.5, section.pairs_near)]
        now = self.use("flat", now + 0.5, 1.01 * size)
        out.append((now, section.blocks))
        if section.z_first:
            now = self.use("high", now, 2.02 * size)
            out.append((now, section.joined))
            now = self.use("flat", now, 0.13 * size)
        else:
            now = self.use("flat", now, 0.5 * size)
            out.append((now, section.joined))
            now = self.use("high", now, 1.01 * size)
        out += [(now, section.close), (now + 4.0, section.finish)]
        return out


class Program:
    def __init__(self):
        self.now, self.places, self.wanted = 0.0, [], []
        self.plans = {}
        self.tail = []

    def loop(self, name, count, each):
        self.plans[name] = {}
        for index in range(count):
            self.now += each
            self.places.append((self.now, name, index))

    def gap(self, time):
        self.now += time

    def want(self, steps):
        self.wanted += [(time, len(self.wanted) + n, step) for n, (time, step) in enumerate(steps)]

    def settle(self):
        for time, _, step in sorted(self.wanted, key=lambda entry: entry[:2]):
            for place, name, index in self.places:
                if place >= time:
                    self.plans[name].setdefault(index, []).append(step)
                    break
            else:
                self.tail.append(step)


class Swap:
    def __init__(self, place, pieces, buf, first_buf_row, rows, first, width, offset, sems):
        self.p, self.rows, self.half = place, rows, width // 2
        self.buf, self.sems = buf, sems
        self.row = aligned(first_buf_row + place.c * rows, rows)
        self.other_row = aligned(first_buf_row + (1 - place.c) * rows, rows)
        self.halves = []
        for core in range(2):
            low, here = first + core * self.half, []
            for array, source, target, size in pieces:
                start, stop = max(low, target), min(low + self.half, target + size)
                if start < stop:
                    at = start - low + offset if offset is not None else start
                    here.append((array, source + start - target, at, stop - start))
            self.halves.append(here)
        self.at = (
            pl.ds(aligned(first + place.c * self.half, 128), self.half)
            if offset is None
            else pl.ds(offset, self.half)
        )
        self.away_at = (
            pl.ds(aligned(first + (1 - place.c) * self.half, 128), self.half)
            if offset is None
            else pl.ds(offset, self.half)
        )

    def begin(self, late=None):
        for core in range(2):
            for array, source, at, size in self.halves[core]:
                if late is not None and (array is late[0]) != late[1]:
                    continue
                part = array.at[:, source : source + size]
                goal = self.buf.at[pl.ds(self.row, self.rows), at : at + size]

                @pl.when(self.p.c == core)
                def here(part=part, goal=goal):
                    pltpu.make_async_copy(part, goal, self.sems.at[2]).start()

                @pl.when(self.p.c != core)
                def away(part=part, goal=goal):
                    remote(part, goal, self.sems.at[0], self.sems.at[1], self.p.sibling).start()

    def finish(self):
        landed = self.buf.at[pl.ds(self.other_row, self.rows), self.at]
        own = self.buf.at[pl.ds(self.row, self.rows), self.at]
        gone = self.buf.at[pl.ds(self.row, self.rows), self.away_at]
        remote(landed, landed, self.sems.at[0], self.sems.at[1], self.p.sibling).wait_recv()
        pltpu.make_async_copy(own, own, self.sems.at[2]).wait()
        remote(gone, gone, self.sems.at[0], self.sems.at[1], self.p.sibling).wait_send()


class Spread:
    def __init__(self, place, mine, everyone, send_sem, recv_sem):
        self.p, self.mine, self.everyone = place, mine, everyone
        self.send_sem, self.recv_sem = send_sem, recv_sem
        self.me = place.blk * 8 + place.img

    def copy(self, step):
        other = lax.rem(self.me + step, 32)
        return remote(
            self.mine,
            self.everyone.at[step - 1],
            self.send_sem,
            self.recv_sem,
            {"blk": other // 8, "img": lax.rem(other, 8)},
        )

    def begin(self, tile):
        self.mine[...] = tile

        def start(step, carry):
            self.copy(step).start()
            return carry

        lax.fori_loop(1, 32, start, 0)

    def finish(self, small):
        scalars = jnp.sum(small[...].reshape(32, 8, 768), axis=0)[3:4]
        lane = lax.broadcasted_iota(jnp.int32, (1, 768), 1)
        square = jnp.sum(jnp.where((lane == 1) | (lane == 2), scalars * scalars, 0.0))
        return scalars, jnp.sqrt(self.total() + square)

    def total(self):
        remote(
            self.everyone, self.everyone, self.send_sem, self.recv_sem, self.p.sibling
        ).wait()
        return self.mine[...] + jnp.sum(self.everyone[...], axis=0)


def small_tail(p, small, map_q, probe, map_out_ref, map_q_ref):
    everything = small[...]
    as_rows = everything.astype(jnp.bfloat16)
    sums = jnp.sum(everything.reshape(32, 8, 768), axis=0)
    query = sums[2:3]
    device = lax.broadcasted_iota(jnp.int32, (32, 256), 0) * 8
    row = lax.broadcasted_iota(jnp.int32, (32, 256), 1)

    def rows_of(kind):
        pick = (row == device + kind).astype(jnp.float32).astype(jnp.bfloat16)
        return jnp.dot(pick, as_rows, preferred_element_type=jnp.float32).astype(jnp.bfloat16)

    pooled, grads = rows_of(0), rows_of(1)
    first = (p.blk * 8 + p.img) * 24
    picks = (
        lax.broadcasted_iota(jnp.int32, (24, 768), 1)
        == lax.broadcasted_iota(jnp.int32, (24, 768), 0) + first
    ).astype(jnp.float32).astype(jnp.bfloat16)
    rows = lax.dot_general(
        picks, pooled, (((1,), (1,)), ((), ())), preferred_element_type=jnp.float32
    ).astype(jnp.bfloat16)
    map_out = jnp.dot(rows, grads, preferred_element_type=jnp.float32)
    map_q_share = probe * query
    probe_share = jnp.sum(map_q * query, axis=1, keepdims=True)
    square = (
        jnp.sum(map_out * map_out)
        + jnp.sum(map_q_share * map_q_share)
        + jnp.sum(probe_share * probe_share)
    )
    map_out_ref[...], map_q_ref[...] = map_out, map_q_share
    return probe_share, square


def square_share(share, square, start, stop):
    def one(step, total):
        part = share[:, pl.ds(aligned(step * 256, 256), 256)]
        return total + jnp.sum(part * part)

    return lax.fori_loop(start, stop, one, square)


COL_VECTORS = 2304
COL_QUERY = 2432
COL_OUT = 2560
COL_UP = 3328
COL_DOWN = 6400
COL_MAP_KV = 9472
COL_MAP_OUT = 11008
TOKENS = 576
CHUNK = 96
TILE = 256
SCALE = 0.125
GELU_A = 0.7978845608028654
GELU_B = 0.044715
NT = (((1,), (1,)), ((), ()))
TN = (((0,), (0,)), ((), ()))


def dot(lhs, rhs, dims=(((1,), (0,)), ((), ()))):
    return lax.dot_general(lhs, rhs, dims, preferred_element_type=jnp.float32)


def loop(count, body, plan=None):
    def one(index, carry):
        body(index)
        for at, steps in (plan or {}).items():

            @pl.when(index == at)
            def run(steps=steps):
                for step in steps:
                    step()

        return carry

    lax.fori_loop(0, count, one, 0)


def columns(index, first=0, width=TILE):
    return pl.ds(aligned(first + index * width, 128), width)


def chunk_rows(index):
    return pl.ds(aligned(index * CHUNK, 32), CHUNK)


def normalize(values):
    row_mean = jnp.mean(values, axis=-1, keepdims=True)
    centered = values - row_mean
    row_var = jnp.mean(centered * centered, axis=-1, keepdims=True)
    rate = lax.rsqrt(row_var + 1e-06)
    return centered * rate, rate


def normalize_back(scaled, rate, grad, gain):
    inner = grad * gain
    first = jnp.mean(inner, axis=-1, keepdims=True)
    second = jnp.mean(inner * scaled, axis=-1, keepdims=True)
    return (
        rate * (inner - first - scaled * second),
        jnp.sum(grad * scaled, axis=0, keepdims=True),
        jnp.sum(grad, axis=0, keepdims=True),
    )


class Tower:
    def __init__(self, **refs):
        self.__dict__.update(refs)

    def unpack(self):
        turned = jnp.transpose(self.w[:, COL_VECTORS : COL_VECTORS + 128].astype(jnp.float32))
        self.vec[0:8, :] = turned[0:8]
        packed = self.w[:, COL_QUERY : COL_QUERY + 128].astype(jnp.float32)
        total = jnp.sum(packed.reshape(32, 24, 128), axis=0)
        query = total[0:6] + total[6:12]
        row = jnp.concatenate([query[i : i + 1] for i in range(6)], axis=1)
        self.vec[8:16, :] = jnp.broadcast_to(row, (8, 768)).astype(jnp.bfloat16).astype(jnp.float32)

    def norm(self, source, gain, bias, out):
        def body(index):
            rows = chunk_rows(index)
            scaled, _ = normalize(source[rows, :].astype(jnp.float32))
            out[rows, :] = (scaled * gain + bias).astype(jnp.bfloat16)

        loop(TOKENS // CHUNK, body)

    def first_norm(self):
        self.norm(self.x, self.vec[0:1, :], self.vec[1:2, :], self.h)

    def project(self, plan=None):
        def body(index):
            self.qkv[:, columns(index)] = dot(self.h[...], self.w[:, columns(index)]).astype(jnp.bfloat16)

        loop(9, body, plan)

    def pair_of(self, pair, which):
        return self.qkv[:, columns(pair, which * D, 128)]

    def attend(self, plan=None):
        lanes = lax.broadcasted_iota(jnp.int32, (TOKENS, 128), 1)

        def body(pair):
            queries = self.pair_of(pair, 0) * jnp.bfloat16(SCALE)
            keys = self.pair_of(pair, 1)
            values_turned = jnp.transpose(self.pair_of(pair, 2))
            mixed = []
            for head in range(2):
                mine = (lanes < 64) if head == 0 else (lanes >= 64)
                masked = jnp.where(mine, queries, jnp.bfloat16(0))
                scores = dot(keys, masked, NT)
                most = jnp.max(scores, axis=0, keepdims=True)
                expos = jnp.exp(scores - most)
                total = jnp.sum(expos, axis=0, keepdims=True)
                part = dot(values_turned[head * 64 : head * 64 + 64], expos.astype(jnp.bfloat16))
                mixed.append(part * (1.0 / total))
                self.lse[pl.ds(pair * 2 + head, 1), :] = most + jnp.log(total)
            self.a[:, columns(pair, 0, 128)] = jnp.transpose(
                jnp.concatenate(mixed, axis=0)
            ).astype(jnp.bfloat16)

        loop(6, body, plan)

    def attend_out(self, plan=None):
        def body(index):
            self.r[:, columns(index)] = self.x[:, columns(index)].astype(jnp.float32) + dot(
                self.a[...], self.w[:, columns(index, COL_OUT)]
            )

        loop(3, body, plan)
        self.norm(self.r, self.vec[2:3, :], self.vec[3:4, :], self.h2)

    def feed_up(self, plan=None):
        def body(index):
            value = dot(self.h2[...], self.w[:, columns(index, COL_UP)])
            square = value * value
            bend = jnp.tanh(GELU_A * value * (1.0 + GELU_B * square))
            half = 0.5 + 0.5 * bend
            self.g[:, columns(index)] = (value * half).astype(jnp.bfloat16)
            slope = half + 0.5 * value * (1.0 - bend * bend) * (
                GELU_A + 3.0 * GELU_A * GELU_B * square
            )
            self.gp[:, columns(index)] = slope.astype(jnp.bfloat16)

        loop(12, body, plan)

    def feed_down(self, plan=None):
        def body(index):
            self.y[:, columns(index)] = self.r[:, columns(index)] + dot(
                self.g[...], self.w[columns(index), COL_DOWN : COL_DOWN + FF], NT
            )

        loop(3, body, plan)
        self.norm(self.y, self.vec[4:5, :], self.vec[5:6, :], self.f)

    def pool_project(self, plan=None):
        def body(index):
            self.kvp[:, columns(index)] = dot(
                self.f[...], self.w[:, columns(index, COL_MAP_KV)]
            ).astype(jnp.bfloat16)

        loop(6, body, plan)

    def pool(self, signs, temperature, offset, images):
        head = lax.broadcasted_iota(jnp.int32, (16, D), 0)
        owner = lax.broadcasted_iota(jnp.int32, (16, D), 1) // HEAD_DIM
        own = head == owner
        heads_query = jnp.where(own, self.vec[8:9, :], 0.0).astype(jnp.bfloat16)
        keys, values = self.kvp[:, :D], self.kvp[:, D:]
        scores = dot(heads_query, keys, NT) * SCALE
        expos = jnp.exp(scores - jnp.max(scores, axis=1, keepdims=True))
        probs = expos / jnp.sum(expos, axis=1, keepdims=True)
        probs_high = probs.astype(jnp.bfloat16)
        probs_low = (probs - probs_high.astype(jnp.float32)).astype(jnp.bfloat16)
        spread = dot(probs_high, values) + dot(probs_low, values)
        pooled = jnp.sum(jnp.where(own, spread, 0.0), axis=0, keepdims=True)
        pooled_b = pooled.astype(jnp.bfloat16)
        w_out = self.w[:, COL_MAP_OUT : COL_MAP_OUT + D]
        many = jnp.broadcast_to(pooled, (16, D)).astype(jnp.bfloat16)
        embed = dot(many, w_out)[0:1]
        rate = lax.rsqrt(jnp.sum(embed * embed, axis=1, keepdims=True) + 1e-06)
        unit = jnp.broadcast_to(embed * rate, (16, D)).astype(jnp.bfloat16)
        cosine = dot(unit, self.cap[...], NT)[0:1]
        heat = jnp.exp(temperature)
        logits = heat * cosine + offset
        turned = -signs * logits
        losses = jnp.maximum(turned, 0.0) + jnp.log1p(jnp.exp(-jnp.abs(turned)))
        loss = jnp.sum(jnp.where(signs == 0.0, 0.0, losses), axis=1, keepdims=True) / images
        grad_logits = -signs * (1.0 / (1.0 + jnp.exp(-turned))) / images
        grad_heat = jnp.sum(grad_logits * cosine * heat, axis=1, keepdims=True)
        grad_offset = jnp.sum(grad_logits, axis=1, keepdims=True)
        grad_cosine = jnp.broadcast_to(grad_logits * heat, (16, cosine.shape[1])).astype(jnp.bfloat16)
        grad_unit = dot(grad_cosine, self.cap[...])[0:1]
        grad_embed = rate * grad_unit - embed * (
            rate * rate * rate * jnp.sum(grad_unit * embed, axis=1, keepdims=True)
        )
        grad_many = jnp.broadcast_to(grad_embed, (16, D)).astype(jnp.bfloat16)
        grad_pooled = dot(grad_many, w_out, NT).astype(jnp.bfloat16).astype(jnp.float32)
        heads_grad = jnp.where(own, grad_pooled, 0.0).astype(jnp.bfloat16)
        grad_probs = dot(heads_grad, values, NT)
        centre = jnp.sum(probs * grad_probs, axis=1, keepdims=True)
        grad_scores = (probs * (grad_probs - centre)).astype(jnp.bfloat16)
        query_spread = dot(grad_scores, keys) * SCALE
        grad_query = jnp.sum(jnp.where(own, query_spread, 0.0), axis=0, keepdims=True)
        self.small_own[0:1, :] = pooled_b.astype(jnp.float32)
        self.small_own[1:2, :] = grad_many[0:1].astype(jnp.float32)
        self.small_own[2:3, :] = grad_query
        lane = lax.broadcasted_iota(jnp.int32, (1, D), 1)
        self.small_own[3:4, :] = jnp.where(
            lane == 0, loss, jnp.where(lane == 1, grad_heat, jnp.where(lane == 2, grad_offset, 0.0))
        )
        self.small_own[4:8, :] = jnp.zeros((4, D), jnp.float32)
        self.kvp[:, :D] = (dot(grad_scores, heads_query, TN) * SCALE).astype(jnp.bfloat16)
        both_probs = jnp.concatenate([probs_high, probs_low], axis=0)
        both_grads = jnp.concatenate([heads_grad, heads_grad], axis=0)
        self.kvp[:, D:] = dot(both_probs, both_grads, TN).astype(jnp.bfloat16)

    def turn(self, source):
        def body(index):
            self.turned[columns(index), :] = jnp.transpose(source[:, columns(index)])

        loop(3, body)

    def weight_grad(self, first, source, tiles, plan=None):
        def body(index):
            self.w[:, columns(index, first)] = dot(
                self.turned[...], source[:, columns(index)]
            ).astype(jnp.bfloat16)

        loop(tiles, body, plan)

    def input_grad(self, source, first, width, plan=None):
        def body(index):
            self.acc[:, columns(index)] = dot(
                source[...], self.w[columns(index), first : first + width], NT
            )

        loop(3, body, plan)

    def norm_back(self, source, added, number, out, rounded):
        gain = self.vec[2 * number : 2 * number + 1, :]

        def body(index, carry):
            rows = chunk_rows(index)
            scaled, rate = normalize(source[rows, :].astype(jnp.float32))
            grad, grad_gain, grad_bias = normalize_back(scaled, rate, self.acc[rows, :], gain)
            if added is not None:
                grad = grad + added[rows, :]
            if out is not None:
                out[rows, :] = grad
            rounded[rows, :] = grad.astype(jnp.bfloat16)
            return carry[0] + grad_gain, carry[1] + grad_bias

        zero = jnp.zeros((1, D), jnp.float32)
        grad_gain, grad_bias = lax.fori_loop(0, TOKENS // CHUNK, body, (zero, zero))
        self.vec_grad[2 * number : 2 * number + 1, :] = grad_gain
        self.vec_grad[2 * number + 1 : 2 * number + 2, :] = grad_bias

    def pool_back(self, plan=None, after=None):
        self.input_grad(self.kvp, COL_MAP_KV, 2 * D)
        self.turn(self.f)
        self.weight_grad(COL_MAP_KV, self.kvp, 6, plan)
        if after is not None:
            after()
        self.norm_back(self.y, None, 2, self.y, self.f)

    def down_back(self, start, tiles, plan=None):
        def body(step):
            index = start + step
            here = columns(index)
            grad = dot(self.f[...], self.w[:, columns(index, COL_DOWN)])
            self.gp[:, here] = (grad * self.gp[:, here].astype(jnp.float32)).astype(jnp.bfloat16)
            self.w[:, columns(index, COL_DOWN)] = dot(self.turned[...], self.g[:, here]).astype(
                jnp.bfloat16
            )

        loop(tiles, body, plan)

    def up_input(self, plan=None):
        self.input_grad(self.gp, COL_UP, FF, plan)

    def up_weight(self, start, tiles, plan=None):
        def body(step):
            index = start + step
            self.w[:, columns(index, COL_UP)] = dot(
                self.turned[...], self.gp[:, columns(index)]
            ).astype(jnp.bfloat16)

        loop(tiles, body, plan)

    def up_norm(self):
        self.norm_back(self.r, self.y, 1, self.r, self.f)

    def out_back(self, plan=None):
        self.turn(self.a)

        def body(index):
            self.a[:, columns(index)] = dot(
                self.f[...], self.w[columns(index), COL_OUT : COL_OUT + D], NT
            ).astype(jnp.bfloat16)

        loop(3, body)
        self.weight_grad(COL_OUT, self.f, 3, plan)

    def attend_back(self, plan=None):
        lanes = lax.broadcasted_iota(jnp.int32, (TOKENS, 128), 1)

        def body(pair):
            queries = self.pair_of(pair, 0) * jnp.bfloat16(SCALE)
            keys, values = self.pair_of(pair, 1), self.pair_of(pair, 2)
            grads = self.a[:, columns(pair, 0, 128)]
            keys_turned = jnp.transpose(keys)
            grad_queries = []
            grad_keys = None
            for head in range(2):
                mine = (lanes < 64) if head == 0 else (lanes >= 64)
                masked = jnp.where(mine, queries, jnp.bfloat16(0))
                masked_grads = jnp.where(mine, grads, jnp.bfloat16(0))
                scores = dot(keys, masked, NT)
                probs = jnp.exp(scores - self.lse[pl.ds(pair * 2 + head, 1), :])
                value_part = dot(probs.astype(jnp.bfloat16), masked_grads)
                grad_probs = dot(values, masked_grads, NT)
                centre = jnp.sum(probs * grad_probs, axis=0, keepdims=True)
                grad_scores = (probs * (grad_probs - centre)).astype(jnp.bfloat16)
                key_part = dot(grad_scores, masked)
                grad_queries.append(dot(keys_turned[head * 64 : head * 64 + 64], grad_scores))
                if head == 0:
                    grad_keys, grad_values = key_part, value_part
                else:
                    grad_keys, grad_values = grad_keys + key_part, grad_values + value_part
            self.qkv[:, columns(pair, 0, 128)] = (
                jnp.transpose(jnp.concatenate(grad_queries, axis=0)) * SCALE
            ).astype(jnp.bfloat16)
            self.qkv[:, columns(pair, D, 128)] = grad_keys.astype(jnp.bfloat16)
            self.qkv[:, columns(pair, 2 * D, 128)] = grad_values.astype(jnp.bfloat16)

        loop(6, body, plan)

    def project_input(self, plan=None):
        self.first_norm()
        self.input_grad(self.qkv, 0, 3 * D, plan)
        self.turn(self.h)
        self.norm_back(self.x, self.r, 0, None, self.h)

    def project_weight(self, start, tiles, plan=None):
        def body(index):
            self.w[:, columns(index, start * TILE)] = dot(
                self.turned[...], self.qkv[:, columns(index, start * TILE)]
            ).astype(jnp.bfloat16)

        loop(tiles, body, plan)

    def vectors_back(self):
        packed = jnp.concatenate([self.vec_grad[...], jnp.zeros((120, D), jnp.float32)], axis=0)
        self.w[:, COL_VECTORS : COL_VECTORS + 128] = jnp.transpose(packed).astype(jnp.bfloat16)
        self.w[:, COL_QUERY : COL_QUERY + 128] = jnp.zeros((D, 128), jnp.bfloat16)


def spread_steps(steps, count):
    plan = {}
    for at, step in enumerate(steps):
        plan.setdefault(min(count - 1, at * count // max(len(steps), 1)), []).append(step)
    return plan


TOWER_REFS = (
    ("w", "x", "cap", "h", "qkv", "a", "r", "h2", "g", "gp", "y", "f", "kvp", "lse", "turned", "acc", "vec", "vec_grad", "small_own")
)


def layer_kernel(
    master, tokens, captions, vectors, labels, scalars,
    share_out, vector_out, facts, patch_out, *scratch,
):
    p = Place()
    t = Tower(**dict(zip(TOWER_REFS, scratch)))
    scratch = scratch[len(TOWER_REFS) :]
    stage, small, pair_a, pair_b, b_in, z_in, a_in, last, mine, everyone = scratch[:10]
    share, extra, caps, map_q, map_out, map_q_share, signs = scratch[10:17]
    swap_sems, token_sems, patch_sems, own_sems, send_sem, recv_sem, grant = scratch[17:24]
    gather_s, scatter_s = scratch[24:31], scratch[31:]
    map_q_at = 4 * D + 2 * FF
    map_q_copy = pltpu.make_async_copy(
        master.at[:, map_q_at : map_q_at + D], map_q, own_sems.at[0]
    )
    map_q_copy.start()
    greet_all(p)

    own_vectors = jnp.transpose(
        jnp.concatenate([vectors[...], jnp.zeros((121, 24), jnp.float32)], axis=0)
    )
    own_vectors = own_vectors.astype(jnp.bfloat16).astype(jnp.float32)
    map_q_copy.wait()
    map_q[...] = map_q[...].astype(jnp.bfloat16).astype(jnp.float32)
    part = jnp.sum(own_vectors[:, 6:7] * map_q[...], axis=0, keepdims=True)
    high = part.astype(jnp.bfloat16).astype(jnp.float32)
    for side in range(6):
        lanes = slice(side * 128, side * 128 + 128)
        extra[side : side + 1, 128:256] = high[:, lanes]
        extra[6 + side : 7 + side, 128:256] = (part - high)[:, lanes]
    extra[12:24, 128:256] = jnp.zeros((12, 128), jnp.float32)
    extra[:, 0:128] = own_vectors
    each = captions.shape[0]
    caps[...] = jnp.concatenate(
        [unit_rows(captions[...].astype(jnp.float32)), jnp.zeros((64 - each, D), jnp.float32)], axis=0
    ).astype(jnp.bfloat16)
    slot = lax.broadcasted_iota(jnp.int32, (8 * each, 512), 1)
    within = (slot >> 7) * 16 + (slot & 15)
    source = ((slot >> 5) & 3) * (2 * each) + ((slot >> 4) & 1) * each + within
    label = lax.broadcasted_iota(jnp.int32, (8 * each, 512), 0)
    pick = ((label == source) & (within < each)).astype(jnp.float32).astype(jnp.bfloat16)
    row = 2.0 * labels[pl.ds(p.blk, 1), :].astype(jnp.float32) - 1.0
    signs[...] = dot(jnp.broadcast_to(row, (16, 8 * each)).astype(jnp.bfloat16), pick)
    all_greeted()

    count = len(GATHER_SECTIONS)
    gathers, swaps = [], []
    pieces = (
        (master, 0, 0, 3 * D),
        (extra, 0, 3 * D, 256),
        (master, 3 * D, COL_OUT, D + 2 * FF),
        (master, map_q_at + D, COL_MAP_KV, 3 * D),
    )
    for number, (first, width, z_first) in enumerate(GATHER_SECTIONS):
        swaps.append(
            Swap(p, pieces, stage, 0, 24, first, width, first // 2, swap_sems.at[number])
        )
        swaps[-1].begin()
        gathers.append(
            Gather(p, t.w, CHIP_ROWS, first, width, z_first, [s.at[number] for s in gather_s])
        )
    own_caps = caps.at[pl.ds(aligned(p.blk * 16, 16), 16), :]
    swaps.append(
        Swap(p, ((own_caps, 0, 0, D),), t.cap, p.chip * 32, 16, 0, D, None, swap_sems.at[count])
    )
    swaps[-1].begin()
    gathers.append(Gather(p, t.cap, 32, 0, D, True, [s.at[count] for s in gather_s]))
    token_copies = []
    for step in range(1, 4):
        to = lax.rem(p.blk + step, 4)
        token_copies.append(
            remote(
                tokens.at[to],
                t.x.at[pl.ds(aligned(p.blk * 144, 144), 144), :],
                token_sems.at[0, step - 1],
                token_sems.at[1, step - 1],
                {"blk": to},
            )
        )
        token_copies[-1].start()
    own_tokens = pltpu.make_async_copy(
        tokens.at[p.blk], t.x.at[pl.ds(aligned(p.blk * 144, 144), 144), :], token_sems.at[0, 3]
    )
    own_tokens.start()

    def ready(number):
        swaps[number].finish()
        if number < count:
            first, width, _ = GATHER_SECTIONS[number]
            t.w[
                pl.ds(aligned(p.chip * 48, 48), 48), pl.ds(gathers[number].mine, width // 2)
            ] = stage[:, first // 2 : first // 2 + width // 2].astype(jnp.bfloat16)
        gathers[number].begin()

    order = []
    for number, gather in enumerate(gathers):
        for at, step in enumerate(gather.steps()):
            call = step if at else (lambda number=number: ready(number))
            order.append((gather_key(number, at), number, at, call))
    order.sort(key=lambda entry: entry[:3])
    ends = [
        max(i for i, entry in enumerate(order) if entry[1] <= number)
        for number in range(count + 1)
    ]

    def between(number):
        return [entry[3] for entry in order[ends[number - 1] + 1 : ends[number] + 1]]

    for entry in order[: ends[0] + 1]:
        entry[3]()
    for step in range(3):
        source = lax.rem(p.blk + 3 - step, 4)
        landed = t.x.at[pl.ds(aligned(source * 144, 144), 144), :]
        remote(
            landed, landed, token_sems.at[0, step], token_sems.at[1, step], {"blk": source}
        ).wait_recv()
    own_tokens.wait()
    gathers[0].finish()

    t.unpack()
    t.first_norm()
    t.project()
    t.attend(spread_steps(between(1), 6))
    gathers[1].finish()
    t.attend_out()
    t.feed_up(spread_steps(between(2), 12))
    gathers[2].finish()
    t.feed_down(spread_steps(between(3), 3))
    gathers[3].finish()
    t.pool_project(spread_steps(between(4), 6))
    gathers[4].finish()
    t.vec_grad[...] = jnp.zeros((8, D), jnp.float32)
    images = tokens.shape[0] * 8
    t.pool(signs[0:1, :], jnp.full((1, 512), scalars[0], jnp.float32), scalars[1], images)
    swap = Swap(
        p, ((t.small_own, 0, 0, D),), small, p.chip * 16, 8, 0, D, None, swap_sems.at[count + 1]
    )
    swap.begin()
    small_gather = Gather(p, small, 16, 0, D, True, [s.at[count + 1] for s in gather_s])
    small_steps = small_gather.steps()
    gathers[3].sent()

    sections = []
    for number, (first, width, z_first) in enumerate(SCATTER_SECTIONS):
        half = width // 2
        which, at = PAIR_PLACES[number]
        pair_in = (pair_a, pair_b)[which].at[:, at : at + half]
        if number < 4:
            others = (b_in[number], a_in[number], z_in[number])
        else:
            here = slice(LATE_PLACES[number - 4], LATE_PLACES[number - 4] + half)
            others = (
                t.g.at[0:384, here],
                t.g.at[384 : 432 if z_first else 576, here],
                t.gp.at[0 : 288 if z_first else 144, here],
            )
        bufs = (pair_in, *others, last[number])
        sections.append(
            Scatter(p, t.w, share, first, width, z_first, bufs, [s.at[number] for s in scatter_s])
        )

    def small_begin():
        swap.finish()
        small_steps[0]()

    links, program = Links(*LINK_SPEED), Program()
    timed = []

    def leaves(section, number):
        timed.append((section, program.now, SCATTER_SECTIONS[number][1]))

    leaves(sections[0], 0)
    program.want(zip((0.5, 1.5, 4.5, 7.0, 9.5, 12.0), [small_begin] + small_steps[1:]))
    program.gap(2.5)
    program.loop("down_first", 6, 0.75)
    leaves(sections[1], 1)
    program.loop("down_second", 6, 0.75)
    leaves(sections[2], 2)
    program.loop("up_input", 3, 1.4)
    program.gap(0.5)
    program.loop("up_first", 6, 0.46)
    leaves(sections[3], 3)
    program.loop("up_second", 6, 0.46)
    program.gap(1.7)
    leaves(sections[4], 4)
    program.loop("out", 3, 1.1)
    leaves(sections[5], 5)
    program.loop("attend", 6, 2.05)
    program.gap(1.0)
    program.loop("project_input", 3, 1.0)
    program.gap(2.2)
    program.loop("front", 5, 0.5)
    leaves(sections[6], 6)
    program.loop("end", 4, 0.5)
    program.gap(1.0)
    leaves(sections[7], 7)
    for entry in timed:
        program.want(links.steps(*entry))
    program.settle()
    plans = program.plans
    t.pool_back(None, sections[0].begin)
    t.turn(t.f)
    gathers[2].sent()
    t.down_back(0, 6, plans["down_first"])
    sections[1].begin()
    t.down_back(6, 6, plans["down_second"])
    sections[2].begin()
    t.up_input(plans["up_input"])
    t.turn(t.h2)
    gathers[1].sent()
    t.up_weight(0, 6, plans["up_first"])
    sections[3].begin()
    t.up_weight(6, 6, plans["up_second"])
    levels = [p.on_level(lax.rem(p.z + step, 4)) for step in range(1, 4)]
    for device in (p.sibling, p.a_near, p.b_near, *levels):
        pl.semaphore_signal(grant, inc=1, device_id=device, device_id_type=MESH)
    t.up_norm()
    pl.semaphore_wait(grant, 6)
    sections[4].begin()
    t.out_back(plans["out"])
    sections[5].begin()
    t.attend_back(plans["attend"])
    t.project_input(plans["project_input"])
    patch_copies = []
    for step in range(1, 4):
        to = lax.rem(p.blk + step, 4)
        patch_copies.append(
            remote(
                t.h.at[pl.ds(aligned(to * 144, 144), 144), :],
                patch_out.at[p.blk],
                patch_sems.at[0, step - 1],
                patch_sems.at[1, step - 1],
                {"blk": to},
            )
        )
        patch_copies[-1].start()
    own_patch = pltpu.make_async_copy(
        t.h.at[pl.ds(aligned(p.blk * 144, 144), 144), :], patch_out.at[p.blk], patch_sems.at[0, 3]
    )
    own_patch.start()
    gathers[0].sent()
    t.project_weight(0, 5, plans["front"])
    sections[6].begin()
    t.project_weight(5, 4, plans["end"])
    t.vectors_back()
    sections[7].begin()
    small_gather.finish()
    probe_share, square = small_tail(
        p, small, map_q[...], own_vectors[:, 6:7], map_out, map_q_share
    )
    small_gather.sent()
    gathers[4].sent()
    for copy in token_copies:
        copy.wait_send()
    outs = [
        pltpu.make_async_copy(source, share_out.at[:, target : target + D], own_sems.at[4 + number])
        for number, (source, target) in enumerate(
            ((map_q_share, map_q_at), (map_out, map_q_at + 3 * D))
        )
    ]
    for out in outs:
        out.start()
    for step in program.tail[:-2]:
        step()
    for step, copy in enumerate(patch_copies):
        source = lax.rem(p.blk + 3 - step, 4)
        landed = patch_out.at[source]
        remote(
            landed, landed, patch_sems.at[0, step], patch_sems.at[1, step], {"blk": source}
        ).wait_recv()
        copy.wait_send()
    own_patch.wait()
    square = square_share(share, square, COL_OUT // 256, SCATTER_COLS // 256)
    for step in program.tail[-2:]:
        step()
    spread = Spread(p, mine, everyone, send_sem, recv_sem)
    spread.begin(jnp.full((8, 128), square_share(share, square, 0, COL_OUT // 256), jnp.float32))
    for number, (source, target, width) in enumerate(
        ((0, 0, 3 * D), (COL_OUT, 3 * D, D + 2 * FF), (COL_MAP_KV, map_q_at + D, 2 * D))
    ):
        outs.append(
            pltpu.make_async_copy(
                share.at[:, source : source + width],
                share_out.at[:, target : target + width],
                own_sems.at[1 + number],
            )
        )
        outs[-1].start()
    lane = lax.broadcasted_iota(jnp.int32, (24, 128), 1)
    vector_out[...] = jnp.transpose(
        jnp.where(lane == 6, probe_share, share[:, COL_VECTORS : COL_VECTORS + 128])
    )[0:8]
    sums, norm = spread.finish(small)
    facts[...] = jnp.concatenate([jnp.broadcast_to(sums[:, :128], (7, 128)), norm[:1]], axis=0)
    for out in outs:
        out.wait()


def layer_call(master, tokens, captions, vectors, labels, scalars):
    dma = pltpu.SemaphoreType.DMA
    f32 = jnp.float32
    gathers = len(GATHER_SECTIONS) + 2
    count = len(SCATTER_SECTIONS)
    widths = [entry[1] // 2 for entry in SCATTER_SECTIONS]

    def vm(*shape, dt=jnp.bfloat16):
        return pltpu.VMEM(shape, dt)

    vmem = pl.BlockSpec(memory_space=pltpu.VMEM)
    return pl.pallas_call(
        layer_kernel,
        out_shape=(
            jax.ShapeDtypeStruct((24, 8 * D + 2 * FF), f32),
            jax.ShapeDtypeStruct((8, 24), f32),
            jax.ShapeDtypeStruct((8, 128), f32),
            jax.ShapeDtypeStruct((4, 144, D), jnp.bfloat16),
        ),
        in_specs=[
            pl.BlockSpec(memory_space=pl.ANY),
            pl.BlockSpec(memory_space=pl.ANY),
            vmem,
            vmem,
            vmem,
            pl.BlockSpec(memory_space=pltpu.SMEM),
        ],
        out_specs=(
            pl.BlockSpec(memory_space=pl.ANY),
            vmem,
            vmem,
            pl.BlockSpec(memory_space=pl.ANY),
        ),
        scratch_shapes=[
            vm(D, GATHER_COLS),
            vm(TOKENS, D),
            vm(512, D),
            vm(TOKENS, D),
            vm(TOKENS, 3 * D),
            vm(TOKENS, D),
            vm(TOKENS, D, dt=f32),
            vm(TOKENS, D),
            vm(TOKENS, FF),
            vm(TOKENS, FF),
            vm(TOKENS, D, dt=f32),
            vm(TOKENS, D),
            vm(TOKENS, 2 * D),
            vm(16, TOKENS, dt=f32),
            vm(D, TOKENS),
            vm(TOKENS, D, dt=f32),
            vm(16, D, dt=f32),
            vm(8, D, dt=f32),
            vm(8, D, dt=f32),
            vm(48, GATHER_COLS // 2, dt=f32),
            vm(256, D, dt=f32),
            vm(D, 1920),
            vm(D, 1536),
            [vm(384, w) for w in widths[:4]],
            [vm(288 if entry[2] else 144, entry[1] // 2) for entry in SCATTER_SECTIONS[:4]],
            [vm(48 if entry[2] else 192, entry[1] // 2) for entry in SCATTER_SECTIONS[:4]],
            [vm(48, w, dt=f32) for w in widths],
            vm(8, 128, dt=f32),
            vm(31, 8, 128, dt=f32),
            vm(24, SCATTER_COLS, dt=f32),
            vm(24, 256, dt=f32),
            vm(64, D),
            vm(24, D, dt=f32),
            vm(24, D, dt=f32),
            vm(24, D, dt=f32),
            vm(16, 512, dt=f32),
            dma((gathers, 4)),
            dma((2, 4)),
            dma((2, 4)),
            dma((6,)),
            dma,
            dma,
            pltpu.SemaphoreType.REGULAR,
            *gather_sems(gathers),
            dma((count, 2)),
            dma((count, 2, 2)),
            dma((count, 2)),
            dma((count, 2, 2, 3)),
            dma((count, 2)),
        ],
        compiler_params=pltpu.CompilerParams(
            collective_id=0, has_side_effects=True, vmem_limit_bytes=63 * 2**20
        ),
        name="layer_step",
    )(master, tokens, captions, vectors, labels, scalars)


def local_kernel(
    patch_tokens,
    captions,
    pair_labels,
    master_weights,
    first_moments,
    second_moments,
    master_vectors,
    vector_first,
    vector_second,
    loss_scalars,
    scalar_first,
    scalar_second,
):
    weight_share, vector_share, facts, patch_grad = layer_call(
        master_weights, patch_tokens, captions, master_vectors.T, pair_labels, loss_scalars
    )
    vector_share = vector_share[:7].T
    patch_grad = patch_grad.astype(jnp.float32)
    loss_total, scalar_total, grad_norm = facts[0, 0], facts[0, 1:3], facts[7, 0]
    factor = CLIP_AT / jnp.maximum(grad_norm, CLIP_AT)
    new_w, new_wm, new_wv = adamw(
        master_weights, weight_share * factor, first_moments, second_moments, 0.03, 0.1
    )
    new_v, new_vm, new_vv = adamw(
        master_vectors, vector_share * factor, vector_first, vector_second, 0.3, 0.0
    )
    new_s, new_sm, new_sv = adamw(
        loss_scalars, scalar_total * factor, scalar_first, scalar_second, 0.3, 0.0
    )
    return (
        loss_total,
        grad_norm,
        patch_grad,
        new_w,
        new_wm,
        new_wv,
        new_w.astype(jnp.bfloat16),
        new_v,
        new_vm,
        new_vv,
        new_v.astype(jnp.bfloat16),
        new_s,
        new_sm,
        new_sv,
    )


def solution(mesh):
    in_specs = (
        P("img", "blk", None),
        P("img", None),
        P("img", None),
        P(("blk", "img"), None),
        P(("blk", "img"), None),
        P(("blk", "img"), None),
        P(("blk", "img"), None),
        P(("blk", "img"), None),
        P(("blk", "img"), None),
        P(),
        P(),
        P(),
    )
    out_specs = (
        P(),
        P(),
        P("img", "blk", None),
        P(("blk", "img"), None),
        P(("blk", "img"), None),
        P(("blk", "img"), None),
        P(("blk", "img"), None),
        P(("blk", "img"), None),
        P(("blk", "img"), None),
        P(("blk", "img"), None),
        P(("blk", "img"), None),
        P(),
        P(),
        P(),
    )
    body = local_kernel if tuple(mesh.shape.values()) == (4, 8) else local
    return jax.shard_map(body, mesh=mesh, in_specs=in_specs, out_specs=out_specs, check_vma=False)
```
